32 devices in a mesh: dp: 8 (over z, y), mp: 4 (over x, core).
Axes of the slice: x: 2, y: 2, z: 4, core: 2. Of those that a mesh axis runs over, the one named last changes fastest.
Arguments:
- tokens_in: bfloat16 [4096, 1024], P('dp'), may hold values from -6 to 6
- masked_positions: int32 [8, 96], P('dp'), may hold values from 0 to 512, as said below
- replace_choice: int32 [8, 96], P('dp'), may hold values from 0 to 33
- replace_table: bfloat16 [34, 1024], replicated, may hold values from -6 to 6
- masked_cotangent: bfloat16 [8, 96, 1024], P('dp'), may hold values from -6 to 6
- attend: float32 [1024, 3, 1024], P('dp', None, 'mp'), may hold values from -0.1875 to 0.1875
- attend_mean: float32 [1024, 3, 1024], P('dp', None, 'mp'), may hold values from -1 to 1
- attend_square: float32 [1024, 3, 1024], P('dp', None, 'mp'), may hold values from 0.004096 to 0.016384
- attend_shadow: float32 [1024, 3, 1024], P('dp', None, 'mp'), may hold values from -0.0009765625 to 0.0009765625
- rejoin: float32 [1024, 1024], P('dp', 'mp'), may hold values from -0.75 to 0.75
- rejoin_mean: float32 [1024, 1024], P('dp', 'mp'), may hold values from -1 to 1
- rejoin_square: float32 [1024, 1024], P('dp', 'mp'), may hold values from 0.004096 to 0.016384
- rejoin_shadow: float32 [1024, 1024], P('dp', 'mp'), may hold values from -0.00390625 to 0.00390625
- expand: float32 [1024, 4096], P('dp', 'mp'), may hold values from -0.1875 to 0.1875
- expand_mean: float32 [1024, 4096], P('dp', 'mp'), may hold values from -1 to 1
- expand_square: float32 [1024, 4096], P('dp', 'mp'), may hold values from 0.004096 to 0.016384
- expand_shadow: float32 [1024, 4096], P('dp', 'mp'), may hold values from -0.0009765625 to 0.0009765625
- narrow: float32 [1024, 4096], P('dp', 'mp'), may hold values from -0.09375 to 0.09375
- narrow_mean: float32 [1024, 4096], P('dp', 'mp'), may hold values from -1 to 1
- narrow_square: float32 [1024, 4096], P('dp', 'mp'), may hold values from 0.004096 to 0.016384
- narrow_shadow: float32 [1024, 4096], P('dp', 'mp'), may hold values from -0.00048828125 to 0.00048828125
- vectors: float32 [1024, 12], P('dp', 'mp')
- vectors_mean: float32 [1024, 12], P('dp', 'mp'), may hold values from -3 to 3
- vectors_square: float32 [1024, 12], P('dp', 'mp'), may hold values from 0.036864 to 0.147456
- vectors_shadow: float32 [1024, 12], P('dp', 'mp'), may hold values from -0.0234375 to 0.0234375
Outputs:
- activations: float32 [4096, 1024], P('dp')
- input_gradient: float32 [4096, 1024], P('dp')
- gradient_norm: float32 [], replicated
- next_attend: float32 [1024, 3, 1024], P('dp', None, 'mp')
- momentum_attend: float32 [1024, 3, 1024], P('dp', None, 'mp')
- variance_attend: float32 [1024, 3, 1024], P('dp', None, 'mp')
- average_attend: float32 [1024, 3, 1024], P('dp', None, 'mp')
- copy_attend: bfloat16 [1024, 3, 1024], P('dp', None, 'mp')
- next_rejoin: float32 [1024, 1024], P('dp', 'mp')
- momentum_rejoin: float32 [1024, 1024], P('dp', 'mp')
- variance_rejoin: float32 [1024, 1024], P('dp', 'mp')
- average_rejoin: float32 [1024, 1024], P('dp', 'mp')
- copy_rejoin: bfloat16 [1024, 1024], P('dp', 'mp')
- next_expand: float32 [1024, 4096], P('dp', 'mp')
- momentum_expand: float32 [1024, 4096], P('dp', 'mp')
- variance_expand: float32 [1024, 4096], P('dp', 'mp')
- average_expand: float32 [1024, 4096], P('dp', 'mp')
- copy_expand: bfloat16 [1024, 4096], P('dp', 'mp')
- next_narrow: float32 [1024, 4096], P('dp', 'mp')
- momentum_narrow: float32 [1024, 4096], P('dp', 'mp')
- variance_narrow: float32 [1024, 4096], P('dp', 'mp')
- average_narrow: float32 [1024, 4096], P('dp', 'mp')
- copy_narrow: bfloat16 [1024, 4096], P('dp', 'mp')
- next_vectors: float32 [1024, 12], P('dp', 'mp')
- momentum_vectors: float32 [1024, 12], P('dp', 'mp')
- variance_vectors: float32 [1024, 12], P('dp', 'mp')
- average_vectors: float32 [1024, 12], P('dp', 'mp')
- copy_vectors: bfloat16 [1024, 12], P('dp', 'mp')
The draws below stay inside these ranges and needn't reach their ends.
Inputs may be any that keep to these rules, and one draw needn't show every extreme that they name: `masked_positions`: row s lists the masked positions of sequence s: its first entries are distinct positions below 512, the remaining entries equal 512 and mark empty slots. Each row has 48 to 96 positions; some row has 96 and some row 48.
All inputs are finite; a program needn't handle non-finite values.
Results may differ from the reference program's by a relative error of at most 0.035.
Values may be sent and summed in bfloat16 or wider, within the bound.
A program may use at most 128 MiB of HBM per device.

```python
import math
import jax
import jax.numpy as jnp
from jax import lax

D = 1024
HEADS = 16
HEAD_DIM = 64
FF = 4096
REPL_ROWS = 34
SEQ_LEN = 512
MCAP = 96
DEPTH = 2
STEP = 7
SEQS = 8
TOKENS = 4096


def draw_masked_positions(key, part):
    shuffle_key, count_key, full_key = jax.random.split(key, 3)
    row_keys = jax.random.split(shuffle_key, SEQS)

    def shuffle_row(row_key):
        return jax.random.permutation(row_key, SEQ_LEN)[:MCAP]
    shuffled = jax.vmap(shuffle_row)(row_keys).astype(jnp.int32)
    counts = jax.random.randint(count_key, (SEQS,), MCAP // 2, MCAP + 1)
    fullest = jax.random.randint(full_key, (), 0, SEQS)
    sparsest = (fullest + 1) % SEQS
    row_index = jnp.arange(SEQS)
    counts = jnp.where(row_index == fullest, MCAP, counts)
    counts = jnp.where(row_index == sparsest, MCAP // 2, counts)
    slot_index = jnp.arange(MCAP)[None, :]
    return jnp.where(slot_index < counts[:, None], shuffled, SEQ_LEN).astype(jnp.int32)


def draw_vectors(key, part):
    noise_key, factor_key = jax.random.split(key)
    along = jnp.arange(D, dtype=jnp.float32)[:, None] / (D - 1)
    column = jnp.arange(12)[None, :]
    noise = 0.5 * jax.random.normal(noise_key, (D, 12), jnp.float32)
    rising = 0.6 * 3.0 ** along
    factor = jax.random.uniform(factor_key, (D, 12), jnp.float32, 0.85, 1.15)
    gain_column = (column == 4) | (column == 6)
    return jnp.where(gain_column, rising * factor, noise)


def plant(values, rng, low, largest):
    longest = values.shape.index(max(values.shape))
    spots = []
    for shift in (0, 1):
        where = [jax.random.randint(jax.random.fold_in(rng, axis), (), 0, length) for axis, length in enumerate(values.shape)]
        where[longest] = (where[longest] + shift) % values.shape[longest]
        spots.append(tuple(where))
    return values.at[spots[0]].set(low).at[spots[1]].set(largest)


def steps_of(stream_key, extent, pieces, low, top_value):
    gain = 1.0
    for position, blocks in pieces:
        draws = jax.random.uniform(jax.random.fold_in(jax.random.fold_in(stream_key, 6), position), (blocks,), jnp.float32, low / len(pieces), top_value / len(pieces))
        gain = gain * jnp.repeat(jnp.exp(draws), extent[position] // blocks).reshape((-1,) + (1,) * (len(extent) - 1 - position))
    return gain


def gaussian(rng, shape, deviation, bound, pieces=(), held_as=jnp.bfloat16):
    factor_of = steps_of(rng, shape, pieces, -0.22, 0.18) if pieces else 1.0
    result = jax.random.normal(rng, shape, jnp.float32) * deviation * factor_of
    return jnp.minimum(jnp.maximum(result, -bound), bound).astype(held_as)


def setup_inputs(seed: int = 0) -> dict:
    seeds = jax.random.split(jax.random.key(seed), 26)
    tokens_in = gaussian(seeds[0], (TOKENS, D), 1.0, 6.0, ((0, 8),))
    masked_positions = draw_masked_positions(jax.random.fold_in(seeds[25], 71), 0)
    replace_choice = plant(jax.random.randint(seeds[2], (SEQS, MCAP), 0, REPL_ROWS), jax.random.fold_in(seeds[2], 1), 0, REPL_ROWS - 1).astype(jnp.int32)
    replace_table = gaussian(seeds[3], (REPL_ROWS, D), 1.0, 6.0)
    masked_cotangent = gaussian(seeds[4], (SEQS, MCAP, D), 1.0, 6.0, ((0, 8),))
    attend = gaussian(seeds[5], (D, 3, D), D ** -0.5, 0.1875, ((0, 8), (2, 4)), jnp.float32)
    attend_mean = gaussian(seeds[6], (D, 3, D), (0.001 * TOKENS ** 0.5), 1.0, ((0, 8), (2, 4)), jnp.float32)
    attend_square = jnp.clip(jnp.exp(math.log(0.016384) - 1.3862944 * jax.random.uniform(seeds[7], (D, 3, D), jnp.float32) ** steps_of(seeds[7], (D, 3, D), ((0, 8), (2, 4)), -0.2, 0.2)), 0.004096, 0.016384)
    attend_shadow = gaussian(seeds[8], (D, 3, D), (0.002 * D ** -0.5), 0.0009765625, ((0, 8), (2, 4)), jnp.float32)
    rejoin = gaussian(seeds[9], (D, D), (D // 16) ** -0.5, 0.75, ((0, 8), (1, 4)), jnp.float32)
    rejoin_mean = gaussian(seeds[10], (D, D), (0.001 * TOKENS ** 0.5), 1.0, ((0, 8), (1, 4)), jnp.float32)
    rejoin_square = jnp.clip(jnp.exp(math.log(0.016384) - 1.3862944 * jax.random.uniform(seeds[11], (D, D), jnp.float32) ** steps_of(seeds[11], (D, D), ((0, 8), (1, 4)), -0.2, 0.2)), 0.004096, 0.016384)
    rejoin_shadow = gaussian(seeds[12], (D, D), (0.002 * (D // 16) ** -0.5), 0.00390625, ((0, 8), (1, 4)), jnp.float32)
    expand = gaussian(seeds[13], (D, FF), D ** -0.5, 0.1875, ((0, 8), (1, 4)), jnp.float32)
    expand_mean = gaussian(seeds[14], (D, FF), (0.001 * TOKENS ** 0.5), 1.0, ((0, 8), (1, 4)), jnp.float32)
    expand_square = jnp.clip(jnp.exp(math.log(0.016384) - 1.3862944 * jax.random.uniform(seeds[15], (D, FF), jnp.float32) ** steps_of(seeds[15], (D, FF), ((0, 8), (1, 4)), -0.2, 0.2)), 0.004096, 0.016384)
    expand_shadow = gaussian(seeds[16], (D, FF), (0.002 * D ** -0.5), 0.0009765625, ((0, 8), (1, 4)), jnp.float32)
    narrow = gaussian(seeds[17], (D, FF), FF ** -0.5, 0.09375, ((0, 8), (1, 4)), jnp.float32)
    narrow_mean = gaussian(seeds[18], (D, FF), (0.001 * TOKENS ** 0.5), 1.0, ((0, 8), (1, 4)), jnp.float32)
    narrow_square = jnp.clip(jnp.exp(math.log(0.016384) - 1.3862944 * jax.random.uniform(seeds[19], (D, FF), jnp.float32) ** steps_of(seeds[19], (D, FF), ((0, 8), (1, 4)), -0.2, 0.2)), 0.004096, 0.016384)
    narrow_shadow = gaussian(seeds[20], (D, FF), (0.002 * FF ** -0.5), 0.00048828125, ((0, 8), (1, 4)), jnp.float32)
    vectors = draw_vectors(jax.random.fold_in(seeds[25], 71), 0)
    vectors_mean = gaussian(seeds[22], (D, 12), (0.003 * TOKENS ** 0.5), 3.0, ((0, 8), (1, 4)), jnp.float32)
    vectors_square = jnp.clip(jnp.exp(math.log(0.147456) - 1.3862944 * jax.random.uniform(seeds[23], (D, 12), jnp.float32) ** steps_of(seeds[23], (D, 12), ((0, 8), (1, 4)), -0.2, 0.2)), 0.036864, 0.147456)
    vectors_shadow = gaussian(seeds[24], (D, 12), 0.0015, 0.0234375, ((0, 8), (1, 4)), jnp.float32)
    return dict(tokens_in=tokens_in, masked_positions=masked_positions, replace_choice=replace_choice, replace_table=replace_table, masked_cotangent=masked_cotangent, attend=attend, attend_mean=attend_mean, attend_square=attend_square, attend_shadow=attend_shadow, rejoin=rejoin, rejoin_mean=rejoin_mean, rejoin_square=rejoin_square, rejoin_shadow=rejoin_shadow, expand=expand, expand_mean=expand_mean, expand_square=expand_square, expand_shadow=expand_shadow, narrow=narrow, narrow_mean=narrow_mean, narrow_square=narrow_square, narrow_shadow=narrow_shadow, vectors=vectors, vectors_mean=vectors_mean, vectors_square=vectors_square, vectors_shadow=vectors_shadow)


@jax.custom_vjp
def low(v):
    return lax.optimization_barrier(v.astype(jnp.bfloat16)).astype(jnp.float32)

@jax.custom_vjp
def low_back(v):
    return v

def low_keep(v):
    return (low(v), None)

def low_pass(kept, grad):
    return (grad,)

def back_keep(v):
    return (v, None)

def back_low(kept, grad):
    return (low(grad),)
low.defvjp(low_keep, low_pass)
low_back.defvjp(back_keep, back_low)
highest = lax.Precision.HIGHEST
norm_eps = 1e-05

def matmul(former, latter):
    return jnp.dot(former, latter, precision=highest, preferred_element_type=jnp.float32)

def layer_norm(tensor, norm_gain, norm_shift):
    centred = tensor - lax.optimization_barrier(jnp.mean(tensor, axis=-1, keepdims=True))
    spread = lax.rsqrt(lax.optimization_barrier(jnp.mean(centred * centred, axis=-1, keepdims=True)) + norm_eps)
    return centred * spread * norm_gain + norm_shift

def activate(tensor):
    return jax.nn.gelu(tensor, approximate=True)

def attention(segment):
    queries, key_rows, value_rows = segment
    length = queries.shape[0]
    query_heads = queries.reshape(length, HEADS, HEAD_DIM)
    key_heads = key_rows.reshape(length, HEADS, HEAD_DIM)
    value_heads = value_rows.reshape(length, HEADS, HEAD_DIM)
    scores = jnp.einsum('qhd,khd->hqk', query_heads, key_heads, precision=highest) * HEAD_DIM ** (-0.5)
    shares = low(jax.nn.softmax(low_back(scores), axis=-1))
    context = jnp.einsum('hqk,khd->qhd', shares, value_heads, precision=highest)
    return context.reshape(length, D)

def depth_step(inputs, params):
    attend, rejoin, expand, narrow, vectors = params
    row_count = inputs.shape[0]
    lowered = low(inputs)
    projected = matmul(lowered, attend.reshape(D, 3 * D)).reshape(row_count, 3, D)
    queries = low(low_back(projected[:, 0] + vectors[:, 0]))
    key_rows = low(low_back(projected[:, 1]))
    value_rows = low(low_back(projected[:, 2] + vectors[:, 1]))
    sequences = row_count // SEQ_LEN
    row_shape = (sequences, SEQ_LEN, D)
    context = lax.map(jax.checkpoint(attention), (queries.reshape(row_shape), key_rows.reshape(row_shape), value_rows.reshape(row_shape)))
    context = low(low_back(context.reshape(row_count, D)))
    mixed_sum = low_back(matmul(context, rejoin.T))
    residual_one = inputs + (mixed_sum + vectors[:, 2])
    normed = layer_norm(residual_one, vectors[:, 4], vectors[:, 5])
    hidden = low(normed)
    expanded = matmul(hidden, expand) + vectors[:, 8:12].T.reshape(FF)
    active = low(activate(low_back(expanded)))
    reduced = low_back(matmul(active, narrow.T))
    residual_two = normed + (reduced + vectors[:, 3])
    return layer_norm(residual_two, vectors[:, 6], vectors[:, 7])

def forward(embedded, params):
    lowered_params = tuple((low(tensor) for tensor in params))
    stream = embedded
    for depth_index in range(DEPTH):
        stream = depth_step(stream, lowered_params)
    return stream

def apply_update(weight, first_moment, second_moment, shadow, gradient, step_rate):
    momentum = 0.5 * first_moment + 0.5 * gradient
    variance = 0.5 * second_moment + 0.5 * gradient * gradient
    bias_fix = 1.0 - 0.5 ** STEP
    updated = weight - step_rate * (momentum / bias_fix / (jnp.sqrt(variance / bias_fix) + 1e-08) + 0.01 * weight)
    average = 0.999 * shadow + 0.001 * updated
    return (updated, momentum, variance, average, updated.astype(jnp.bfloat16))

def reference(tokens_in, masked_positions, replace_choice, replace_table, masked_cotangent, attend, attend_mean, attend_square, attend_shadow, rejoin, rejoin_mean, rejoin_square, rejoin_shadow, expand, expand_mean, expand_square, expand_shadow, narrow, narrow_mean, narrow_square, narrow_shadow, vectors, vectors_mean, vectors_square, vectors_shadow):
    positions = jnp.arange(SEQ_LEN, dtype=jnp.int32)
    slot_match = (masked_positions[:, :, None] == positions[None, None, :]).astype(jnp.float32)
    masked_flag = lax.optimization_barrier(jnp.sum(slot_match, axis=1))
    replace_hot = (replace_choice[:, :, None] == jnp.arange(REPL_ROWS, dtype=jnp.int32)[None, None, :]).astype(jnp.float32)
    replacements = jnp.einsum('sjr,rd->sjd', replace_hot, replace_table.astype(jnp.float32), precision=highest)
    placed_rows = jnp.einsum('sjp,sjd->spd', slot_match, replacements, precision=highest)
    kept_flag = (1.0 - masked_flag)[:, :, None]
    embedded = tokens_in.astype(jnp.float32).reshape(SEQS, SEQ_LEN, D) * kept_flag + placed_rows
    cotangent = jnp.einsum('sjp,sjd->spd', slot_match, masked_cotangent.astype(jnp.float32), precision=highest)
    params = (attend, rejoin, expand, narrow, vectors)
    per_group = math.gcd(SEQS, max(1, 4096 // SEQ_LEN))
    group_count = SEQS // per_group
    group_rows = per_group * SEQ_LEN

    def visit_group(totals, group_pair):
        inputs, upstream = group_pair
        outputs, pullback = jax.vjp(forward, inputs, params)
        input_back, param_back = pullback(upstream)
        return (jax.tree.map(jnp.add, totals, param_back), (outputs, input_back))
    zero_grads = tuple((jnp.zeros_like(tensor) for tensor in params))
    gradients, (outputs, input_backs) = lax.scan(visit_group, zero_grads, (embedded.reshape(group_count, group_rows, D), cotangent.reshape(group_count, group_rows, D)))
    activations = outputs.reshape(TOKENS, D)
    input_gradient = (input_backs.reshape(SEQS, SEQ_LEN, D) * kept_flag).reshape(TOKENS, D)
    squares = sum((jnp.sum(tensor * tensor) for tensor in gradients))
    gradient_norm = jnp.sqrt(squares)
    param_count = 4 * D * D + 2 * D * FF + 12 * D
    clip_limit = 0.001 * math.sqrt(param_count * TOKENS)
    factor = jnp.minimum(1.0, clip_limit / (gradient_norm + 1e-06))
    attend_out = apply_update(attend, attend_mean, attend_square, attend_shadow, gradients[0] * factor, 0.04)
    rejoin_out = apply_update(rejoin, rejoin_mean, rejoin_square, rejoin_shadow, gradients[1] * factor, 0.16)
    expand_out = apply_update(expand, expand_mean, expand_square, expand_shadow, gradients[2] * factor, 0.04)
    narrow_out = apply_update(narrow, narrow_mean, narrow_square, narrow_shadow, gradients[3] * factor, 0.04)
    vectors_out = apply_update(vectors, vectors_mean, vectors_square, vectors_shadow, gradients[4] * factor, 0.5)
    return (activations, input_gradient, gradient_norm, attend_out[0], attend_out[1], attend_out[2], attend_out[3], attend_out[4], rejoin_out[0], rejoin_out[1], rejoin_out[2], rejoin_out[3], rejoin_out[4], expand_out[0], expand_out[1], expand_out[2], expand_out[3], expand_out[4], narrow_out[0], narrow_out[1], narrow_out[2], narrow_out[3], narrow_out[4], vectors_out[0], vectors_out[1], vectors_out[2], vectors_out[3], vectors_out[4])
```

```python
import math
from types import SimpleNamespace

import jax
import jax.numpy as jnp
from jax import lax
from jax.experimental import pallas as pl
from jax.experimental.pallas import tpu as pltpu
from jax.sharding import PartitionSpec as P

HEAD_DIM = 64
SEQ_LEN = 512
DEPTH = 2
STEP = 7
EPS = 1e-05
BF = jnp.bfloat16
F32 = jnp.float32
MESH = pl.DeviceIdType.MESH
LANES = 128
TILE = 256
SLOTS = 128
CHUNKS = 2
SUB = 64
VEC, ATT, REJ, EXP, NAR = range(5)
GELU_A = 0.7978845608028654
GELU_B = 0.044715


def nn(former, latter):
    return jnp.dot(former, latter, preferred_element_type=F32)


def nt(former, latter):
    return lax.dot_general(former, latter, (((1,), (1,)), ((), ())), preferred_element_type=F32)


def low_transpose(block):
    return jnp.transpose(block.astype(F32), (1, 0)).astype(BF)


def loop(count, body):
    def step(index, carry):
        body(index)
        return carry

    lax.fori_loop(0, count, step, 0)


def each(first, last, body):
    if last - first <= 8:
        for index in range(first, last):
            body(index)
    else:

        def step(index, carry):
            body(index)
            return carry

        lax.fori_loop(first, last, step, 0)


def aligned(index, size):
    return pl.ds(pl.multiple_of(index, size), size)


def layer_kernel(names, sizes, *refs):
    r = SimpleNamespace(**dict(zip(names, refs, strict=True)))
    n, d_model, rows, hw, uw, vr = sizes
    half = rows // 2
    ch = half // CHUNKS
    lines = n // 2
    heads = hw // HEAD_DIM
    slot_half = SLOTS // 2

    d = lax.axis_index("dp")
    m = lax.axis_index("mp")
    z, y = d // 2, d % 2
    core = m % 2
    core_peer = (d, m + 1 - 2 * core)
    x_peer = (d, (m + 2) % 4)
    y_peer = (d + 1 - 2 * y, m)
    own0 = core * half
    oth0 = half - own0

    weights = (r.wv, r.wa, r.wr, r.we, r.wn)
    grads = (r.gsv, r.gsa, r.gsr, r.gse, r.gsn)
    from_y = (r.yv, r.ya, r.yr, r.ye, r.yn)
    from_z = (r.zv, r.za, r.zr, r.ze, r.zn)

    def z_peer(step):
        return (((z + step) % lines) * 2 + y, m)

    def z_from(step):
        return ((z + lines - step) % lines) * 2 + y

    def block(ref, region, index):
        where = aligned(index * vr, vr)
        return ref.at[:, where, :] if region == ATT else ref.at[where, :]

    def remote(source, target, send, recv, device):
        return pltpu.make_async_remote_copy(
            src_ref=source,
            dst_ref=target,
            send_sem=send,
            recv_sem=recv,
            device_id=device,
            device_id_type=MESH,
        )

    barrier = pltpu.get_barrier_semaphore()
    for peer in (core_peer, x_peer, y_peer):
        pl.semaphore_signal(barrier, inc=1, device_id=peer, device_id_type=MESH)
    each(
        1,
        lines,
        lambda s: pl.semaphore_signal(barrier, inc=1, device_id=z_peer(s), device_id_type=MESH),
    )
    pl.semaphore_wait(barrier, 3 + lines - 1)

    def gather_z(region, step):
        piece = block(weights[region], region, d)
        return remote(
            piece, piece, r.agzs.at[region, step], r.agzr.at[region, step], z_peer(step)
        )

    def gather_z_arrival(region, step):
        piece = block(weights[region], region, z_from(step))
        return remote(
            piece, piece, r.agzs.at[region, step], r.agzr.at[region, step], z_peer(step)
        )

    def gather_y(region, step):
        piece = block(weights[region], region, z_from(step))
        return remote(piece, piece, r.agys.at[region, step], r.agyr.at[region, step], y_peer)

    def gather_y_arrival(region, step):
        piece = block(weights[region], region, z_from(step) + 1 - 2 * y)
        return remote(piece, piece, r.agys.at[region, step], r.agyr.at[region, step], y_peer)

    def gather_start(region):
        each(1, lines, lambda s: gather_z(region, s).start())
        gather_y(region, 0).start()

    def gather_pass(region):
        def one(step):
            gather_z_arrival(region, step).wait_recv()
            gather_y(region, step).start()

        each(1, lines, one)

    def gather_wait(region):
        each(0, lines, lambda s: gather_y_arrival(region, s).wait_recv())

    def gather_close(region):
        each(1, lines, lambda s: gather_z(region, s).wait_send())
        each(0, lines, lambda s: gather_y(region, s).wait_send())

    def scatter_y(region, step):
        owner = ((z + step) % lines) * 2 + 1 - y
        return remote(
            block(grads[region], region, owner),
            from_y[region].at[step],
            r.rsys.at[region, step],
            r.rsyr.at[region, step],
            y_peer,
        )

    def scatter_z(region, step):
        owner = ((z + step) % lines) * 2 + y
        return remote(
            block(grads[region], region, owner),
            from_z[region].at[step - 1],
            r.rszs.at[region, step],
            r.rszr.at[region, step],
            z_peer(step),
        )

    def scatter_start(region):
        def one(step):
            scatter_y(region, step).start()

        each(1, lines, one)
        one(0)

    def scatter_pass(region, step):
        scatter_y(region, step).wait_recv()
        piece = block(grads[region], region, ((z + step) % lines) * 2 + y)
        piece[...] = (piece[...].astype(F32) + from_y[region][step].astype(F32)).astype(BF)
        scatter_z(region, step).start()

    def scatter_finish(region, out_ref):
        scatter_y(region, 0).wait_recv()
        piece = block(grads[region], region, d)
        out_ref[...] = piece[...].astype(F32) + from_y[region][0].astype(F32)

        def one(step):
            scatter_z(region, step).wait_recv()
            out_ref[...] += from_z[region][step - 1].astype(F32)

        each(1, lines, one)

    def scatter_close(region):
        each(0, lines, lambda s: scatter_y(region, s).wait_send())
        each(1, lines, lambda s: scatter_z(region, s).wait_send())

    def core_copy(k, q, count):
        b = k % 2
        return remote(
            r.cs.at[b, q, :count],
            r.cr.at[b, q, :count],
            r.arcs.at[k, q],
            r.arcr.at[k, q],
            core_peer,
        )

    def x_copy(k, q, count):
        b = k % 2
        return remote(
            r.xs.at[b, q, :count],
            r.xr.at[b, q, :count],
            r.arxs.at[k, q],
            r.arxr.at[k, q],
            x_peer,
        )

    def sum_begin(k, q, tile_of, count):
        b = k % 2

        def one(j):
            cols = aligned(j * TILE, TILE)
            part = tile_of(cols)
            r.cs[b, q, :count, cols] = part[:count].astype(BF)
            r.acc[:count, cols] = part[count:]

        loop(d_model // TILE, one)
        copy = core_copy(k, q, count)
        copy.start()
        copy.wait_recv()
        r.xs[b, q, :count] = (r.acc[:count] + r.cr[b, q, :count].astype(F32)).astype(BF)
        x_copy(k, q, count).start()

    def sum_end(k, q, count):
        x_copy(k, q, count).wait()
        core_copy(k, q, count).wait_send()

    def sum_rows(k, q, where):
        b = k % 2
        return r.xs[b, q, where].astype(F32) + r.xr[b, q, where].astype(F32)

    def share(k, ref, q):
        where = aligned(own0 + q * ch, ch)
        return remote(ref.at[where], ref.at[where], r.shs.at[k, q], r.shr.at[k, q], core_peer)

    def share_arrival(k, ref, q):
        where = aligned(oth0 + q * ch, ch)
        return remote(ref.at[where], ref.at[where], r.shs.at[k, q], r.shr.at[k, q], core_peer)

    def share_wait(k, ref, q):
        share(k, ref, q).wait_send()
        share_arrival(k, ref, q).wait_recv()

    def both(ref, q, cols=slice(None)):
        return jnp.concatenate(
            [ref[aligned(oth0 + q * ch, ch), cols], ref[aligned(own0 + q * ch, ch), cols]],
            axis=0,
        )

    def put_both(ref, q, cols, value):
        ref[aligned(oth0 + q * ch, ch), cols] = value[:ch]
        ref[aligned(own0 + q * ch, ch), cols] = value[ch:]

    r.vb[0] = r.vin[...].astype(BF)
    swap = remote(r.vb.at[0], r.vb.at[1], r.vxs.at[0], r.vxr.at[0], core_peer)
    swap.start()
    mine = aligned(d * vr, vr)
    r.wa[:, mine, :] = r.attend[...].astype(BF)
    gather_start(ATT)
    r.wr[mine, :] = r.rejoin[...].astype(BF)
    swap.wait_recv()
    r.vb[2] = r.vb[0] + r.vb[1]
    swap_x = remote(r.vb.at[2], r.vb.at[3], r.vxs.at[1], r.vxr.at[1], x_peer)
    swap_x.start()
    r.we[mine, :] = r.expand[...].astype(BF)
    r.wn[mine, :] = r.narrow[...].astype(BF)
    swap_x.wait_recv()
    r.wv[mine, :] = r.vb[2] + r.vb[3]
    gather_start(VEC)
    gather_start(REJ)

    r.pb[...] = jnp.full(r.pb.shape, SEQ_LEN, jnp.int32)
    slots = r.pos.shape[1]
    r.pb[0:1, 0:slots] = r.pos[...]
    r.pb[8:9, 0:slots] = r.cho[...]
    pos_row = jnp.broadcast_to(r.pb[0:1, :], (SLOTS, SLOTS))
    cho_row = jnp.broadcast_to(r.pb[8:9, :], (SLOTS, SLOTS))
    pos_col = jnp.transpose(pos_row.astype(F32), (1, 0)).astype(jnp.int32)
    cho_col = jnp.transpose(cho_row.astype(F32), (1, 0)).astype(jnp.int32)
    lane_iota = lax.broadcasted_iota(jnp.int32, (SLOTS, LANES), 1)
    row_iota = lax.broadcasted_iota(jnp.int32, (SLOTS, LANES), 0)
    for j in range(rows // LANES):
        r.oh[:, j * LANES : (j + 1) * LANES] = jnp.where(
            pos_col == lane_iota + j * LANES, 1.0, 0.0
        ).astype(BF)
        r.oht[j * LANES : (j + 1) * LANES, :] = jnp.where(
            pos_row == row_iota + j * LANES, 1.0, 0.0
        ).astype(BF)
    r.low2c[...] = jnp.zeros(r.low2c.shape, BF)
    r.low2c[0 : r.table.shape[0], :] = r.table[...]
    choice = jnp.where(cho_col == lane_iota, 1.0, 0.0).astype(BF)
    for j in range(d_model // TILE):
        r.slt[:, j * TILE : (j + 1) * TILE] = nn(
            choice, r.low2c[:, j * TILE : (j + 1) * TILE]
        ).astype(BF)
    r.mc[...] = jnp.zeros(r.mc.shape, BF)
    r.mc[0:slots, :] = r.mcot[...].reshape(slots, d_model)
    r.vg[...] = jnp.zeros(r.vg.shape, F32)

    def embed(i):
        where = aligned(i * SUB, SUB)
        hot = r.oht[where, :]
        keep = 1.0 - jnp.sum(hot.astype(F32), axis=1, keepdims=True)
        r.keep[where, :] = keep
        r.xl[where, :] = (r.tok[where, :].astype(F32) * keep + nn(hot, r.slt[...])).astype(BF)

    loop(rows // SUB, embed)
    r.st[...] = r.xl[aligned(own0, half), :].astype(F32)

    def transpose_into(target, lane0, source, row0, count):
        for i in range(count // LANES):
            target[:, lane0 + i * LANES : lane0 + (i + 1) * LANES] = low_transpose(
                source[row0 + i * LANES : row0 + (i + 1) * LANES, :]
            )

    transpose_into(r.xt, 0, r.xl, 0, rows)

    gather_pass(ATT)
    gather_start(EXP)
    gather_pass(VEC)
    gather_wait(ATT)
    gather_wait(VEC)
    for j in range(d_model // LANES):
        r.vt[:, j * LANES : (j + 1) * LANES] = jnp.transpose(
            r.wv[j * LANES : (j + 1) * LANES, :].astype(F32), (1, 0)
        )[0:16, :]

    def head_bias(row):
        return r.vt[row : row + 1, aligned(m * hw, hw)]

    half_mask = lax.broadcasted_iota(jnp.int32, (1, LANES), 1) < HEAD_DIM

    def lane_half(value, head):
        return jnp.where(half_mask if head % 2 == 0 else jnp.logical_not(half_mask), value, 0)

    def put_heads(ref, q, value):
        for head in range(heads):
            pair = (head // 2) * LANES
            piece = lane_half(value[:, pair : pair + LANES], head)
            ref[head, aligned(oth0 + q * ch, ch), :] = piece[:ch]
            ref[head, aligned(own0 + q * ch, ch), :] = piece[ch:]

    def put_heads_across(ref, q, across):
        for head in range(heads):
            at = (head % 2) * HEAD_DIM
            piece = across[head * HEAD_DIM : (head + 1) * HEAD_DIM, :]
            ref[head, at : at + HEAD_DIM, aligned(oth0 + q * ch, ch)] = piece[:, :ch]
            ref[head, at : at + HEAD_DIM, aligned(own0 + q * ch, ch)] = piece[:, ch:]

    def put_across(ref, q, across):
        ref[:, aligned(oth0 + q * ch, ch)] = across[:, :ch]
        ref[:, aligned(own0 + q * ch, ch)] = across[:, ch:]

    for ref in (r.qzt, r.dozt):
        ref[...] = jnp.zeros(ref.shape, BF)

    def share_block(layer, head, lane0):
        if layer == 0:
            return r.p0.at[head, :, aligned(lane0, TILE)]
        return r.gse.at[
            aligned((head // 2) * rows, rows), aligned((head % 2) * rows + lane0, TILE)
        ]

    def project(layer, q):
        x = both(r.xl, q)
        queries = (nn(x, r.wa[0]) + head_bias(0)).astype(BF) * jnp.asarray(0.125, BF)
        put_heads(r.qz.at[layer], q, queries)
        put_heads_across(r.qzt.at[layer], q, low_transpose(queries))
        keys = nn(x, r.wa[1]).astype(BF)
        put_both(r.kn.at[layer], q, slice(None), keys)
        put_across(r.kt.at[layer], q, low_transpose(keys))
        values = (nn(x, r.wa[2]) + head_bias(1)).astype(BF)
        put_both(r.vn.at[layer], q, slice(None), values)
        put_across(r.vvt, q, low_transpose(values))

    def attend_forward(layer):
        def one(i):
            head, lane0 = i // 2, (i % 2) * TILE
            pair = aligned((head // 2) * LANES, LANES)
            lanes = aligned(lane0, TILE)
            scores = nn(r.kn[layer, :, pair], r.qzt[layer, head, :, lanes])
            raised = jnp.exp(scores - jnp.max(scores, axis=0, keepdims=True))
            total = jnp.sum(raised, axis=0, keepdims=True)
            low = (raised * (1.0 / total)).astype(BF)
            share_block(layer, head, lane0)[...] = low
            where = aligned(head * HEAD_DIM, HEAD_DIM)
            r.ct[layer, where, lanes] = nn(r.vvt[where, :], low).astype(BF)

        loop(heads * (rows // TILE), one)
        target, row0 = (r.ctx, 0) if layer == 0 else (r.ctx1, 0)
        for i in range(rows // LANES):
            target[row0 + i * LANES : row0 + (i + 1) * LANES, :] = low_transpose(
                r.ct[layer, :, i * LANES : (i + 1) * LANES]
            )

    def first_norm(layer, q):
        def one(i):
            at = aligned(q * ch + i * SUB, SUB)
            total = sum_rows(2 * layer, q, aligned(i * SUB, SUB))
            res = r.st[at, :] + (total + r.vt[2:3, :])
            cen = res - jnp.mean(res, axis=1, keepdims=True)
            spread = lax.rsqrt(jnp.mean(cen * cen, axis=1, keepdims=True) + EPS)
            hat = cen * spread
            r.xh1[layer, at, :] = hat
            r.rs1[layer, at, :] = spread
            normed = hat * r.vt[4:5, :] + r.vt[5:6, :]
            r.st[at, :] = normed
            r.normed[aligned(own0 + q * ch + i * SUB, SUB), :] = normed.astype(BF)

        loop(ch // SUB, one)

    def second_norm(layer, q):
        def one(i):
            at = aligned(q * ch + i * SUB, SUB)
            total = sum_rows(2 * layer + 1, q, aligned(i * SUB, SUB))
            res = r.st[at, :] + (total + r.vt[3:4, :])
            cen = res - jnp.mean(res, axis=1, keepdims=True)
            spread = lax.rsqrt(jnp.mean(cen * cen, axis=1, keepdims=True) + EPS)
            hat = cen * spread
            r.xh2[layer, at, :] = hat
            r.rs2[layer, at, :] = spread
            out = hat * r.vt[6:7, :] + r.vt[7:8, :]
            r.st[at, :] = out
            if layer < DEPTH - 1:
                r.xl[aligned(own0 + q * ch + i * SUB, SUB), :] = out.astype(BF)

        loop(ch // SUB, one)

    def unit_act(layer):
        return r.act0 if layer == 0 else r.gsn

    def unit_slope(layer):
        return (r.slope0, 0) if layer == 0 else (r.gsn, rows)

    def widen(layer, q):
        act = unit_act(layer)
        slope, slope0 = unit_slope(layer)

        def one(j):
            cols = aligned(j * TILE, TILE)
            v = nn(both(r.normed, q), r.we[:, cols]) + r.vt[pl.ds(8 + m, 1), cols]
            square = v * v
            t = jnp.tanh(GELU_A * v * (1.0 + GELU_B * square))
            gate = 0.5 * (1.0 + t)
            put_both(act, q, cols, (v * gate).astype(BF))
            bend = gate + (0.5 * GELU_A) * v * (1.0 - t * t) * (1.0 + (3.0 * GELU_B) * square)
            bend = bend.astype(BF)
            slope[aligned(slope0 + oth0 + q * ch, ch), cols] = bend[:ch]
            slope[aligned(slope0 + own0 + q * ch, ch), cols] = bend[ch:]

        loop(uw // TILE, one)

    def rejoin_sum(layer, q):
        ctx = r.ctx if layer == 0 else r.ctx1
        sum_begin(2 * layer, q, lambda cols: nt(both(ctx, q), r.wr[cols, :]), ch)

    def narrow_sum(layer, q):
        act = unit_act(layer)
        sum_begin(2 * layer + 1, q, lambda cols: nt(both(act, q), r.wn[cols, :]), ch)

    for layer in range(DEPTH):
        for q in range(CHUNKS):
            if layer > 0:
                share_wait(2 * layer - 1, r.xl, q)
            project(layer, q)
        if layer == 0:
            gather_pass(REJ)
        attend_forward(layer)
        if layer == 0:
            gather_wait(REJ)
        for q in range(CHUNKS):
            rejoin_sum(layer, q)
        if layer == 0:
            gather_start(NAR)
            gather_pass(EXP)
        else:
            transpose_into(r.xt, rows, r.xl, 0, rows)
        for q in range(CHUNKS):
            sum_end(2 * layer, q, ch)
            first_norm(layer, q)
            share(2 * layer, r.normed, q).start()
            if layer == 0 and q == 0:
                gather_wait(EXP)
            share_wait(2 * layer, r.normed, q)
            widen(layer, q)
            if layer == 0 and q == 0:
                gather_pass(NAR)
                gather_wait(NAR)
            narrow_sum(layer, q)
        if layer == 0:
            transpose_into(r.nt, 0, r.normed, 0, rows)
        for q in range(CHUNKS):
            sum_end(2 * layer + 1, q, ch)
            second_norm(layer, q)
            if layer < DEPTH - 1:
                share(2 * layer + 1, r.xl, q).start()

    own_rows = aligned(own0, half)
    out_here = pltpu.make_async_copy(r.st, r.act.at[own_rows], r.osem.at[0])
    out_there = remote(r.st, r.act.at[own_rows], r.osem.at[1], r.osem.at[2], core_peer)
    out_arrival = remote(
        r.st, r.act.at[aligned(oth0, half)], r.osem.at[1], r.osem.at[2], core_peer
    )
    out_here.start()
    out_there.start()

    def add_rows(row, value):
        r.vg[row : row + 1, :] += jnp.sum(value, axis=0, keepdims=True)

    def norm_pull(g, hat, spread, gain):
        scaled = g * gain
        mean = jnp.mean(scaled, axis=1, keepdims=True)
        inner = jnp.mean(scaled * hat, axis=1, keepdims=True)
        return spread * (scaled - mean - hat * inner)

    def second_pull(layer, q, gradient):
        def one(i):
            at = aligned(q * ch + i * SUB, SUB)
            g = gradient(i, at)
            hat = r.xh2[layer, at, :]
            add_rows(6, g * hat)
            add_rows(7, g)
            back = norm_pull(g, hat, r.rs2[layer, at, :], r.vt[6:7, :])
            add_rows(3, back)
            r.gb[at, :] = back
            r.low2[aligned(own0 + q * ch + i * SUB, SUB), :] = back.astype(BF)

        loop(ch // SUB, one)

    def first_pull(layer, q, gradient):
        def one(i):
            at = aligned(q * ch + i * SUB, SUB)
            g = gradient(i, at)
            hat = r.xh1[layer, at, :]
            add_rows(4, g * hat)
            add_rows(5, g)
            back = norm_pull(g, hat, r.rs1[layer, at, :], r.vt[4:5, :])
            add_rows(2, back)
            r.gb[at, :] = back
            r.xl[aligned(own0 + q * ch + i * SUB, SUB), :] = back.astype(BF)

        loop(ch // SUB, one)

    def hot_rows(at_start):
        return r.oht[aligned(own0 + at_start, SUB), :]

    def bias_sums(row0):
        for kind, row in ((0, 0), (2, 1)):
            cols = aligned(m * hw, hw)
            r.vg[row : row + 1, cols] += jnp.sum(
                r.dp[kind, row0 : row0 + rows, :].astype(F32), axis=0, keepdims=True
            )

    for q in range(CHUNKS):
        second_pull(1, q, lambda i, at: nn(hot_rows(q * ch + i * SUB), r.mc[...]))
        share(4, r.low2, q).start()
    hot = r.oh[...]

    def pick(target, row0, source, source0, width):
        def one(j):
            cols = aligned(j * TILE, TILE)
            target[row0 : row0 + SLOTS, cols] = nn(
                hot, source[source0 : source0 + rows, cols]
            ).astype(BF)

        loop(width // TILE, one)

    pick(r.act0, rows, r.gsn, 0, uw)
    pick(r.slc, 0, r.gsn, rows, uw)
    pick(r.low2c, 0, r.normed, 0, d_model)
    transpose_into(r.nt, rows, r.low2c, 0, SLOTS)
    pick(r.ctx, rows, r.ctx1, 0, hw)
    for q in range(CHUNKS):
        share_wait(4, r.low2, q)
    pick(r.low2c, 0, r.low2, 0, d_model)

    def slot_units(j):
        cols = aligned(j * TILE, TILE)
        back = nn(r.low2c[...], r.wn[:, cols]) * r.slc[:, cols].astype(F32)
        back = back.astype(BF)
        r.be[rows : rows + SLOTS, cols] = back
        r.vg[pl.ds(8 + m, 1), cols] += jnp.sum(back.astype(F32), axis=0, keepdims=True)

    loop(uw // TILE, slot_units)
    slot_own = core * slot_half
    slot_oth = slot_half - slot_own

    def slot_tile(cols):
        part = nt(r.be[rows : rows + SLOTS, :], r.we[cols, :])
        r.part[...] = part
        return jnp.concatenate(
            [
                r.part[aligned(slot_oth, slot_half), :],
                r.part[aligned(slot_own, slot_half), :],
            ],
            axis=0,
        )

    sum_begin(4, 0, slot_tile, slot_half)
    transpose_into(r.l2t, rows, r.low2c, 0, SLOTS)
    sum_end(4, 0, slot_half)
    mine_slots = r.slt.at[aligned(slot_own, slot_half)]
    mine_slots[...] = sum_rows(4, 0, slice(0, slot_half)).astype(BF)
    slots_out = remote(mine_slots, mine_slots, r.osem.at[3], r.osem.at[4], core_peer)
    slots_in_ref = r.slt.at[aligned(slot_oth, slot_half)]
    slots_in = remote(slots_in_ref, slots_in_ref, r.osem.at[3], r.osem.at[4], core_peer)
    slots_out.start()
    slots_in.wait_recv()
    for q in range(CHUNKS):
        first_pull(
            1, q, lambda i, at: r.gb[at, :] + nn(hot_rows(q * ch + i * SUB), r.slt[...])
        )
        share(5, r.xl, q).start()

    for head in range(heads):
        r.qc[head] = nn(hot, r.qz[1, head]).astype(BF)
        source = r.gse[
            (head // 2) * rows : (head // 2 + 1) * rows,
            (head % 2) * rows : (head % 2 + 1) * rows,
        ]
        r.pc[head] = nn(source, r.oht[...]).astype(BF)
    r.cct[...] = nn(r.ct[1], r.oht[...]).astype(BF)
    for q in range(CHUNKS):
        share_wait(5, r.xl, q)
    pick(r.low2c, 0, r.xl, 0, d_model)
    transpose_into(r.l1t, rows, r.low2c, 0, SLOTS)
    low_ctx = nn(r.low2c[...], r.wr[...]).astype(BF)
    across = low_transpose(low_ctx)
    dq_across = []
    for pair in range(heads // 2):
        lanes = slice(pair * LANES, (pair + 1) * LANES)
        dv = jnp.zeros((rows, LANES), F32)
        dk = jnp.zeros((rows, LANES), F32)
        for head in (2 * pair, 2 * pair + 1):
            where = slice(head * HEAD_DIM, (head + 1) * HEAD_DIM)
            at = (head % 2) * HEAD_DIM
            r.dozt[head, at : at + HEAD_DIM, 0:SLOTS] = across[where, :]
            low = r.pc[head]
            dv += nn(low, lane_half(low_ctx[:, lanes], head))
            dp = nn(r.vn[1, :, lanes], r.dozt[head, :, 0:SLOTS])
            delta = jnp.sum(
                across[where, :].astype(F32) * r.cct[where, :].astype(F32), axis=0, keepdims=True
            )
            ds = (low.astype(F32) * (dp - delta)).astype(BF)
            dk += nn(ds, r.qc[head])
            dq_across.append(nn(r.kt[1, where, :], ds) * 0.125)
        r.dp[1, rows : 2 * rows, lanes] = dk.astype(BF)
        r.dp[2, rows : 2 * rows, lanes] = dv.astype(BF)
    dq = low_transpose(jnp.concatenate(dq_across, axis=0))
    r.dp[0, rows : 2 * rows, :] = nn(r.oht[...], dq).astype(BF)
    bias_sums(rows)

    def layer_rows(k, q, row0):
        def tile_of(cols):
            total = None
            for kind in range(3):
                lhs = jnp.concatenate(
                    [
                        r.dp[kind, aligned(row0 + oth0 + q * ch, ch), :],
                        r.dp[kind, aligned(row0 + own0 + q * ch, ch), :],
                    ],
                    axis=0,
                )
                part = nt(lhs, r.wa[kind, cols, :])
                total = part if total is None else total + part
            return total

        sum_begin(k, q, tile_of, ch)

    for q in range(CHUNKS):
        layer_rows(5, q, rows)

    for q in range(CHUNKS):
        sum_end(5, q, ch)
        second_pull(
            0, q, lambda i, at: r.gb[at, :] + sum_rows(5, q, aligned(i * SUB, SUB))
        )
        share(6, r.low2, q).start()
        share_wait(6, r.low2, q)

        def units(j, q=q):
            cols = aligned(j * TILE, TILE)
            slope = both(r.slope0, q, cols).astype(F32)
            back = (nn(both(r.low2, q), r.wn[:, cols]) * slope).astype(BF)
            put_both(r.be, q, cols, back)
            r.vg[pl.ds(8 + m, 1), cols] += jnp.sum(back.astype(F32), axis=0, keepdims=True)

        loop(uw // TILE, units)
        sum_begin(6, q, lambda cols, q=q: nt(both(r.be, q), r.we[cols, :]), ch)

    def weight_grad(target, across, latter, width):
        def one(t):
            i, j = t // (width // TILE), t % (width // TILE)
            at, cols = aligned(i * TILE, TILE), aligned(j * TILE, TILE)
            target[at, cols] = nn(across[at, :], latter[:, cols]).astype(BF)

        loop((d_model // TILE) * (width // TILE), one)

    transpose_into(r.l2t, 0, r.low2, 0, rows)
    weight_grad(r.gsn, r.l2t, r.act0, uw)
    scatter_start(NAR)
    weight_grad(r.gse, r.nt, r.be, uw)
    scatter_start(EXP)
    for q in range(CHUNKS):
        sum_end(6, q, ch)
        first_pull(
            0, q, lambda i, at: r.gb[at, :] + sum_rows(6, q, aligned(i * SUB, SUB))
        )
        share(7, r.xl, q).start()
    scatter_pass(NAR, 1) if lines > 1 else None
    for q in range(CHUNKS):
        share_wait(7, r.xl, q)
        back = nn(both(r.xl, q), r.wr[...]).astype(BF)
        put_heads(r.doz, q, back)
        put_heads_across(r.dozt, q, low_transpose(back))

    def head_pair(pair):
        lanes = aligned(pair * LANES, LANES)
        dv = jnp.zeros((rows, LANES), F32)
        dk = jnp.zeros((rows, LANES), F32)
        for side in range(2):
            head = 2 * pair + side
            where = aligned(head * HEAD_DIM, HEAD_DIM)
            for part in range(rows // TILE):
                some = slice(part * TILE, (part + 1) * TILE)
                low = r.p0[head, :, some]
                dv += nn(low, r.doz[head, some, :])
                inner = r.dozt[head, side * HEAD_DIM : (side + 1) * HEAD_DIM, some]
                delta = jnp.sum(
                    inner.astype(F32) * r.ct[0, where, some].astype(F32), axis=0, keepdims=True
                )
                dp = nn(r.vn[0, :, lanes], r.dozt[head, :, some])
                ds = (low.astype(F32) * (dp - delta)).astype(BF)
                dk += nn(ds, r.qz[0, head, some, :])
                r.dqt[where, some] = (nn(r.kt[0, where, :], ds) * 0.125).astype(BF)
        r.dp[1, 0:rows, lanes] = dk.astype(BF)
        r.dp[2, 0:rows, lanes] = dv.astype(BF)

    loop(heads // 2, head_pair)
    for i in range(rows // LANES):
        some = slice(i * LANES, (i + 1) * LANES)
        r.dp[0, some, :] = low_transpose(r.dqt[:, some])
    for q in range(CHUNKS):
        layer_rows(7, q, 0)
    bias_sums(0)
    transpose_into(r.l1t, 0, r.xl, 0, rows)
    weight_grad(r.gsr, r.l1t, r.ctx, hw)
    scatter_start(REJ)
    first_of_x = jnp.where(m < 2, 1.0, 0.0)
    r.vg[2:8, :] = r.vg[2:8, :] * first_of_x
    for j in range(d_model // LANES):
        tall = jnp.concatenate(
            [r.vg[:, j * LANES : (j + 1) * LANES], jnp.zeros((LANES - 16, LANES), F32)], axis=0
        )
        r.gsv[j * LANES : (j + 1) * LANES, :] = jnp.transpose(tall, (1, 0)).astype(BF)
    scatter_start(VEC)
    for kind in range(3):
        weight_grad(r.gsa.at[kind], r.xt, r.dp.at[kind], hw)
    scatter_start(ATT)
    each(2, lines, lambda s: scatter_pass(NAR, s))
    out_here.wait()
    out_there.wait_send()
    for q in range(CHUNKS):
        sum_end(7, q, ch)

        def last(i, q=q):
            at = aligned(q * ch + i * SUB, SUB)
            g = r.gb[at, :] + sum_rows(7, q, aligned(i * SUB, SUB))
            r.st[at, :] = g * r.keep[aligned(own0 + q * ch + i * SUB, SUB), :]

        loop(ch // SUB, last)
    in_here = pltpu.make_async_copy(r.st, r.ing.at[own_rows], r.osem.at[5])
    in_there = remote(r.st, r.ing.at[own_rows], r.osem.at[6], r.osem.at[7], core_peer)
    in_arrival = remote(r.st, r.ing.at[aligned(oth0, half)], r.osem.at[6], r.osem.at[7], core_peer)
    in_here.start()
    in_there.start()

    each(1, lines, lambda s: scatter_pass(EXP, s))
    each(1, lines, lambda s: scatter_pass(REJ, s))
    each(1, lines, lambda s: scatter_pass(VEC, s))
    each(1, lines, lambda s: scatter_pass(ATT, s))

    def squares(value):
        value = value * value
        if value.ndim == 3:
            value = jnp.sum(value, axis=0)
        value = jnp.sum(value, axis=0, keepdims=True)
        return jnp.sum(value, axis=1, keepdims=True)

    scatter_finish(NAR, r.gn)
    scatter_finish(EXP, r.ge)
    scatter_finish(REJ, r.gr)
    total = squares(r.gn[...]) + squares(r.ge[...]) + squares(r.gr[...])
    scatter_finish(VEC, r.vf.at[0])
    swap_v = remote(r.vf.at[0], r.vf.at[1], r.vxs.at[2], r.vxr.at[2], core_peer)
    swap_v.start()
    swap_v.wait_recv()
    r.vf[2] = r.vf[0] + r.vf[1]
    swap_w = remote(r.vf.at[2], r.vf.at[3], r.vxs.at[3], r.vxr.at[3], x_peer)
    swap_w.start()
    swap_w.wait_recv()
    r.gv[...] = r.vf[2] + r.vf[3]
    lane = lax.broadcasted_iota(jnp.int32, r.gv.shape, 1)
    own_lanes = jnp.logical_and(lane >= 3 * m, lane < 3 * m + 3)
    total = total + squares(jnp.where(own_lanes, r.gv[...], 0.0))
    scatter_finish(ATT, r.ga)
    total = total + squares(r.ga[...])

    r.ns[0] = jnp.broadcast_to(total, (8, LANES))
    for step, peer in enumerate((core_peer, x_peer, y_peer)):
        swap_n = remote(r.ns.at[step], r.nr.at[step], r.nss.at[step], r.nsr.at[step], peer)
        swap_n.start()
        swap_n.wait_recv()
        r.ns[step + 1] = r.ns[step] + r.nr[step]
    r.nz[z] = r.ns[3]

    def norm_copy(step):
        return remote(
            r.ns.at[3], r.nz.at[z], r.nzs.at[step], r.nzr.at[step], z_peer(step)
        )

    def norm_arrival(step):
        return remote(
            r.ns.at[3],
            r.nz.at[(z + lines - step) % lines],
            r.nzs.at[step],
            r.nzr.at[step],
            z_peer(step),
        )

    each(1, lines, lambda s: norm_copy(s).start())
    each(1, lines, lambda s: norm_arrival(s).wait_recv())
    r.norm[...] = jnp.sqrt(jnp.sum(r.nz[...], axis=0))

    each(1, lines, lambda s: norm_copy(s).wait_send())
    for step, peer in enumerate((core_peer, x_peer, y_peer)):
        remote(
            r.ns.at[step], r.nr.at[step], r.nss.at[step], r.nsr.at[step], peer
        ).wait_send()
    swap.wait_send()
    swap_x.wait_send()
    swap_v.wait_send()
    swap_w.wait_send()
    slots_out.wait_send()
    for region in range(5):
        gather_close(region)
        scatter_close(region)
    out_arrival.wait_recv()
    in_here.wait()
    in_there.wait_send()
    in_arrival.wait_recv()


def run_layers(
    n, tok, pos, cho, table, mcot, attend, rejoin, expand, narrow, vin
):
    rows, d_model = tok.shape
    vr = rejoin.shape[0]
    hw = rejoin.shape[1]
    uw = expand.shape[1]
    lines = n // 2
    ways = max(lines - 1, 1)
    half = rows // 2
    ch = half // CHUNKS
    heads = hw // HEAD_DIM
    wide = rows + SLOTS
    inputs = [
        ("tok", tok),
        ("pos", pos),
        ("cho", cho),
        ("table", table),
        ("mcot", mcot),
        ("attend", attend),
        ("rejoin", rejoin),
        ("expand", expand),
        ("narrow", narrow),
        ("vin", vin),
    ]
    outputs = [
        ("act", (rows, d_model), pl.ANY),
        ("ing", (rows, d_model), pl.ANY),
        ("ga", (3, vr, hw), pltpu.VMEM),
        ("gr", (vr, hw), pltpu.VMEM),
        ("ge", (vr, uw), pltpu.VMEM),
        ("gn", (vr, uw), pltpu.VMEM),
        ("gv", (vr, LANES), pltpu.VMEM),
        ("norm", (8, LANES), pltpu.VMEM),
    ]
    low = [
        ("wv", (d_model, LANES)),
        ("wa", (3, d_model, hw)),
        ("wr", (d_model, hw)),
        ("we", (d_model, uw)),
        ("wn", (d_model, uw)),
        ("gsv", (d_model, LANES)),
        ("gsa", (3, d_model, hw)),
        ("gsr", (d_model, hw)),
        ("gse", (d_model, uw)),
        ("gsn", (d_model, uw)),
        ("yv", (lines, vr, LANES)),
        ("ya", (lines, 3, vr, hw)),
        ("yr", (lines, vr, hw)),
        ("ye", (lines, vr, uw)),
        ("yn", (lines, vr, uw)),
        ("zv", (ways, vr, LANES)),
        ("za", (ways, 3, vr, hw)),
        ("zr", (ways, vr, hw)),
        ("ze", (ways, vr, uw)),
        ("zn", (ways, vr, uw)),
        ("cs", (2, CHUNKS, ch, d_model)),
        ("cr", (2, CHUNKS, ch, d_model)),
        ("xs", (2, CHUNKS, ch, d_model)),
        ("xr", (2, CHUNKS, ch, d_model)),
        ("vb", (4, vr, LANES)),
        ("oh", (SLOTS, rows)),
        ("oht", (rows, SLOTS)),
        ("mc", (SLOTS, d_model)),
        ("xl", (rows, d_model)),
        ("normed", (rows, d_model)),
        ("low2", (rows, d_model)),
        ("xt", (d_model, 2 * rows)),
        ("nt", (d_model, wide)),
        ("l2t", (d_model, wide)),
        ("l1t", (d_model, wide)),
        ("act0", (wide, uw)),
        ("slope0", (rows, uw)),
        ("be", (wide, uw)),
        ("ctx", (wide, hw)),
        ("ctx1", (rows, hw)),
        ("dp", (3, 2 * rows, hw)),
        ("qz", (2, heads, rows, LANES)),
        ("qzt", (2, heads, LANES, rows)),
        ("kn", (2, rows, hw)),
        ("kt", (2, hw, rows)),
        ("vn", (2, rows, hw)),
        ("vvt", (hw, rows)),
        ("ct", (2, hw, rows)),
        ("p0", (heads, rows, rows)),
        ("doz", (heads, rows, LANES)),
        ("dozt", (heads, LANES, rows)),
        ("dqt", (hw, rows)),
        ("slc", (SLOTS, uw)),
        ("low2c", (SLOTS, d_model)),
        ("slt", (SLOTS, d_model)),
        ("qc", (heads, SLOTS, LANES)),
        ("pc", (heads, rows, SLOTS)),
        ("cct", (hw, SLOTS)),
    ]
    full = [
        ("vt", (16, d_model)),
        ("vg", (16, d_model)),
        ("keep", (rows, 1)),
        ("st", (half, d_model)),
        ("gb", (half, d_model)),
        ("xh1", (2, half, d_model)),
        ("xh2", (2, half, d_model)),
        ("rs1", (2, half, 1)),
        ("rs2", (2, half, 1)),
        ("acc", (ch, d_model)),
        ("part", (SLOTS, TILE)),
        ("vf", (4, vr, LANES)),
        ("ns", (4, 8, LANES)),
        ("nr", (3, 8, LANES)),
        ("nz", (lines, 8, LANES)),
    ]
    sems = [
        ("agzs", (5, lines)),
        ("agzr", (5, lines)),
        ("agys", (5, lines)),
        ("agyr", (5, lines)),
        ("rsys", (5, lines)),
        ("rsyr", (5, lines)),
        ("rszs", (5, lines)),
        ("rszr", (5, lines)),
        ("arcs", (8, CHUNKS)),
        ("arcr", (8, CHUNKS)),
        ("arxs", (8, CHUNKS)),
        ("arxr", (8, CHUNKS)),
        ("shs", (8, CHUNKS)),
        ("shr", (8, CHUNKS)),
        ("vxs", (4,)),
        ("vxr", (4,)),
        ("osem", (8,)),
        ("nss", (3,)),
        ("nsr", (3,)),
        ("nzs", (lines,)),
        ("nzr", (lines,)),
    ]
    names = (
        [name for name, _ in inputs]
        + [name for name, _, _ in outputs]
        + [name for name, _ in low]
        + [name for name, _ in full]
        + ["pb"]
        + [name for name, _ in sems]
    )
    sizes = (n, d_model, rows, hw, uw, vr)

    def body(*refs):
        layer_kernel(names, sizes, *refs)

    return pl.pallas_call(
        body,
        out_shape=[jax.ShapeDtypeStruct(shape, F32) for _, shape, _ in outputs],
        in_specs=[pl.BlockSpec(memory_space=pltpu.VMEM)] * len(inputs),
        out_specs=[pl.BlockSpec(memory_space=space) for _, _, space in outputs],
        scratch_shapes=[pltpu.VMEM(shape, BF) for _, shape in low]
        + [pltpu.VMEM(shape, F32) for _, shape in full]
        + [pltpu.VMEM((16, LANES), jnp.int32)]
        + [pltpu.SemaphoreType.DMA(shape) for _, shape in sems],
        compiler_params=pltpu.CompilerParams(
            collective_id=0, has_side_effects=True, vmem_limit_bytes=61 * 1024 * 1024
        ),
        cost_estimate=pl.CostEstimate(
            flops=20_000_000_000, bytes_accessed=20_000_000, transcendentals=4_000_000
        ),
    )(*[value for _, value in inputs])


def apply_update(weight, first_moment, second_moment, shadow, gradient, step_rate):
    momentum = 0.5 * first_moment + 0.5 * gradient
    variance = 0.5 * second_moment + 0.5 * gradient * gradient
    bias_fix = 1.0 - 0.5**STEP
    updated = weight - step_rate * (
        momentum / bias_fix / (jnp.sqrt(variance / bias_fix) + 1e-08) + 0.01 * weight
    )
    average = 0.999 * shadow + 0.001 * updated
    return (updated, momentum, variance, average, updated.astype(BF))


def per_device(
    tokens_in,
    masked_positions,
    replace_choice,
    replace_table,
    masked_cotangent,
    attend,
    attend_mean,
    attend_square,
    attend_shadow,
    rejoin,
    rejoin_mean,
    rejoin_square,
    rejoin_shadow,
    expand,
    expand_mean,
    expand_square,
    expand_shadow,
    narrow,
    narrow_mean,
    narrow_square,
    narrow_shadow,
    vectors,
    vectors_mean,
    vectors_square,
    vectors_shadow,
):
    n = lax.axis_size("dp")
    m = lax.axis_index("mp")
    vector_rows, vector_width = vectors.shape
    placed_vectors = lax.dynamic_update_slice(
        jnp.zeros((vector_rows, LANES), F32), vectors, (0, m * vector_width)
    )
    act, ing, ga, gr, ge, gn, gv, norm = run_layers(
        n,
        tokens_in,
        masked_positions,
        replace_choice,
        replace_table,
        masked_cotangent,
        attend.transpose(1, 0, 2),
        rejoin,
        expand,
        narrow,
        placed_vectors,
    )
    gradient_norm = norm[0, 0]
    d_model = tokens_in.shape[1]
    param_count = 4 * d_model * d_model + 2 * d_model * expand.shape[1] * 4 + 12 * d_model
    clip_limit = 0.001 * math.sqrt(param_count * tokens_in.shape[0] * n)
    factor = jnp.minimum(1.0, clip_limit / (gradient_norm + 1e-06))
    gv = lax.dynamic_slice(gv, (0, m * vector_width), (vector_rows, vector_width))
    results = [act, ing, gradient_norm]
    for group in (
        (attend, attend_mean, attend_square, attend_shadow, ga.transpose(1, 0, 2), 0.04),
        (rejoin, rejoin_mean, rejoin_square, rejoin_shadow, gr, 0.16),
        (expand, expand_mean, expand_square, expand_shadow, ge, 0.04),
        (narrow, narrow_mean, narrow_square, narrow_shadow, gn, 0.04),
        (vectors, vectors_mean, vectors_square, vectors_shadow, gv, 0.5),
    ):
        results.extend(apply_update(*group[:4], group[4] * factor, group[5]))
    return tuple(results)


def solution(mesh):
    row = P("dp", None)
    cube = P("dp", None, "mp")
    flat = P("dp", "mp")
    return jax.shard_map(
        per_device,
        mesh=mesh,
        in_specs=(row, row, row, P(), P("dp", None, None)) + (cube,) * 4 + (flat,) * 16,
        out_specs=(row, row, P()) + (cube,) * 5 + (flat,) * 20,
        check_vma=False,
    )
```

```python
import math
from types import SimpleNamespace

import jax
import jax.numpy as jnp
from jax import lax
from jax.experimental import pallas as pl
from jax.experimental.pallas import tpu as pltpu
from jax.sharding import PartitionSpec as P

HEAD_DIM = 64
SEQ_LEN = 512
DEPTH = 2
STEP = 7
EPS = 1e-05
BF = jnp.bfloat16
F32 = jnp.float32
MESH = pl.DeviceIdType.MESH
LANES = 128
TILE = 256
SLOTS = 128
CHUNKS = 2
SUB = 64
VEC, ATT, REJ, EXP, NAR = range(5)
GELU_A = 0.7978845608028654
GELU_B = 0.044715


def nn(former, latter):
    return jnp.dot(former, latter, preferred_element_type=F32)


def nt(former, latter):
    return lax.dot_general(former, latter, (((1,), (1,)), ((), ())), preferred_element_type=F32)


def low_transpose(block):
    return jnp.transpose(block.astype(F32), (1, 0)).astype(BF)


def loop(count, body):
    def step(index, carry):
        body(index)
        return carry

    lax.fori_loop(0, count, step, 0)


def each(first, last, body):
    if last - first <= 8:
        for index in range(first, last):
            body(index)
    else:

        def step(index, carry):
            body(index)
            return carry

        lax.fori_loop(first, last, step, 0)


def aligned(index, size):
    return pl.ds(pl.multiple_of(index, size), size)


def layer_kernel(names, sizes, *refs):
    r = SimpleNamespace(**dict(zip(names, refs, strict=True)))
    n, d_model, rows, hw, uw, vr = sizes
    half = rows // 2
    ch = half // CHUNKS
    lines = n // 2
    heads = hw // HEAD_DIM
    slot_half = SLOTS // 2

    d = lax.axis_index("dp")
    m = lax.axis_index("mp")
    z, y = d // 2, d % 2
    core = m % 2
    core_peer = (d, m + 1 - 2 * core)
    x_peer = (d, (m + 2) % 4)
    y_peer = (d + 1 - 2 * y, m)
    model_peers = (core_peer, x_peer, (d, 3 - m))
    own0 = core * half
    oth0 = half - own0

    weights = (r.wv, r.wa, r.wr, r.we, r.wn)
    grads = (r.gsv, r.gsa, r.gsr, r.gse, r.gsn)
    from_y = (r.yv, r.ya, r.yr, r.ye, r.yn)
    from_z = (r.zv, r.za, r.zr, r.ze, r.zn)

    def z_peer(step):
        return (((z + step) % lines) * 2 + y, m)

    def zy_peer(step):
        return (((z + step) % lines) * 2 + 1 - y, m)

    def z_from(step):
        return ((z + lines - step) % lines) * 2 + y

    def block(ref, region, index):
        where = aligned(index * vr, vr)
        return ref.at[:, where, :] if region == ATT else ref.at[where, :]

    def remote(source, target, send, recv, device):
        return pltpu.make_async_remote_copy(
            src_ref=source,
            dst_ref=target,
            send_sem=send,
            recv_sem=recv,
            device_id=device,
            device_id_type=MESH,
        )

    barrier = pltpu.get_barrier_semaphore()

    def greet(peer):
        pl.semaphore_signal(barrier, inc=1, device_id=peer, device_id_type=MESH)

    for peer in model_peers:
        greet(peer)
    each(1, lines, lambda s: greet(z_peer(s)))
    each(0, lines, lambda s: greet(zy_peer(s)))
    pl.semaphore_wait(barrier, len(model_peers) + n - 1)

    def gather_z(region, step):
        piece = block(weights[region], region, d)
        return remote(
            piece, piece, r.agzs.at[region, step], r.agzr.at[region, step], z_peer(step)
        )

    def gather_z_arrival(region, step):
        piece = block(weights[region], region, z_from(step))
        return remote(
            piece, piece, r.agzs.at[region, step], r.agzr.at[region, step], z_peer(step)
        )

    def gather_y(region, step):
        piece = block(weights[region], region, z_from(step))
        return remote(piece, piece, r.agys.at[region, step], r.agyr.at[region, step], y_peer)

    def gather_y_arrival(region, step):
        piece = block(weights[region], region, z_from(step) + 1 - 2 * y)
        return remote(piece, piece, r.agys.at[region, step], r.agyr.at[region, step], y_peer)

    def gather_start(region):
        each(1, lines, lambda s: gather_z(region, s).start())
        gather_y(region, 0).start()

    def gather_pass(region, only=None):
        def one(step):
            gather_z_arrival(region, step).wait_recv()
            gather_y(region, step).start()

        if only is None:
            each(1, lines, one)
        else:
            one(only)

    def gather_wait(region):
        each(0, lines, lambda s: gather_y_arrival(region, s).wait_recv())

    def gather_close(region):
        each(1, lines, lambda s: gather_z(region, s).wait_send())
        each(0, lines, lambda s: gather_y(region, s).wait_send())

    def scatter_y(region, step):
        owner = ((z + step) % lines) * 2 + 1 - y
        return remote(
            block(grads[region], region, owner),
            from_y[region].at[step],
            r.rsys.at[region, step],
            r.rsyr.at[region, step],
            y_peer,
        )

    def scatter_z(region, step):
        owner = ((z + step) % lines) * 2 + y
        return remote(
            block(grads[region], region, owner),
            from_z[region].at[step - 1],
            r.rszs.at[region, step],
            r.rszr.at[region, step],
            z_peer(step),
        )

    def scatter_start(region):
        def one(step):
            scatter_y(region, step).start()

        each(1, lines, one)
        one(0)

    def scatter_pass(region, step):
        scatter_y(region, step).wait_recv()
        piece = block(grads[region], region, ((z + step) % lines) * 2 + y)
        piece[...] = (piece[...].astype(F32) + from_y[region][step].astype(F32)).astype(BF)
        scatter_z(region, step).start()

    def scatter_finish(region, out_ref):
        scatter_y(region, 0).wait_recv()
        piece = block(grads[region], region, d)
        out_ref[...] = piece[...].astype(F32) + from_y[region][0].astype(F32)

        def one(step):
            scatter_z(region, step).wait_recv()
            out_ref[...] += from_z[region][step - 1].astype(F32)

        each(1, lines, one)

    def scatter_close(region):
        each(0, lines, lambda s: scatter_y(region, s).wait_send())
        each(1, lines, lambda s: scatter_z(region, s).wait_send())

    def core_copy(k, q, count):
        b = k % 2
        return remote(
            r.cs.at[b, q, :count],
            r.cr.at[b, q, :count],
            r.arcs.at[k, q],
            r.arcr.at[k, q],
            core_peer,
        )

    def x_copy(k, q, count):
        b = k % 2
        return remote(
            r.xs.at[b, q, :count],
            r.xr.at[b, q, :count],
            r.arxs.at[k, q],
            r.arxr.at[k, q],
            x_peer,
        )

    def sum_begin(k, q, tile_of, count):
        b = k % 2

        def one(j):
            cols = aligned(j * TILE, TILE)
            part = tile_of(cols)
            r.cs[b, q, :count, cols] = part[:count].astype(BF)
            r.acc[:count, cols] = part[count:]

        loop(d_model // TILE, one)
        copy = core_copy(k, q, count)
        copy.start()
        copy.wait_recv()
        r.xs[b, q, :count] = (r.acc[:count] + r.cr[b, q, :count].astype(F32)).astype(BF)
        x_copy(k, q, count).start()

    def sum_end(k, q, count):
        x_copy(k, q, count).wait()
        core_copy(k, q, count).wait_send()

    def sum_rows(k, q, where):
        b = k % 2
        return r.xs[b, q, where].astype(F32) + r.xr[b, q, where].astype(F32)

    def share(k, ref, q):
        where = aligned(own0 + q * ch, ch)
        return remote(ref.at[where], ref.at[where], r.shs.at[k, q], r.shr.at[k, q], core_peer)

    def share_arrival(k, ref, q):
        where = aligned(oth0 + q * ch, ch)
        return remote(ref.at[where], ref.at[where], r.shs.at[k, q], r.shr.at[k, q], core_peer)

    def share_wait(k, ref, q):
        share(k, ref, q).wait_send()
        share_arrival(k, ref, q).wait_recv()

    def both(ref, q, cols=slice(None)):
        return jnp.concatenate(
            [ref[aligned(oth0 + q * ch, ch), cols], ref[aligned(own0 + q * ch, ch), cols]],
            axis=0,
        )

    def put_both(ref, q, cols, value):
        ref[aligned(oth0 + q * ch, ch), cols] = value[:ch]
        ref[aligned(own0 + q * ch, ch), cols] = value[ch:]

    columns = r.vin.shape[0]
    r.vs[...] = jnp.zeros(r.vs.shape, F32)
    r.vs[pl.ds(columns * m, columns), :] = r.vin[...]
    r.vb[0] = low_transpose(r.vs[...])
    swap = remote(r.vb.at[0], r.vb.at[1], r.vxs.at[0], r.vxr.at[0], core_peer)
    swap.start()
    mine = aligned(d * vr, vr)
    r.wa[:, mine, :] = r.attend[...].astype(BF)
    gather_start(ATT)
    r.wr[mine, :] = r.rejoin[...].astype(BF)
    swap.wait_recv()
    r.vb[2] = r.vb[0] + r.vb[1]
    swap_x = remote(r.vb.at[2], r.vb.at[3], r.vxs.at[1], r.vxr.at[1], x_peer)
    swap_x.start()
    r.we[mine, :] = r.expand[...].astype(BF)
    r.wn[mine, :] = r.narrow[...].astype(BF)
    swap_x.wait_recv()
    r.wv[mine, :] = r.vb[2] + r.vb[3]
    gather_start(VEC)
    gather_start(REJ)

    r.pb[...] = jnp.full(r.pb.shape, SEQ_LEN, jnp.int32)
    slots = r.pos.shape[1]
    r.pb[0:1, 0:slots] = r.pos[...]
    r.pb[8:9, 0:slots] = r.cho[...]
    pos_row = jnp.broadcast_to(r.pb[0:1, :], (SLOTS, SLOTS))
    cho_row = jnp.broadcast_to(r.pb[8:9, :], (SLOTS, SLOTS))
    pos_col = jnp.transpose(pos_row.astype(F32), (1, 0)).astype(jnp.int32)
    cho_col = jnp.transpose(cho_row.astype(F32), (1, 0)).astype(jnp.int32)
    lane_iota = lax.broadcasted_iota(jnp.int32, (SLOTS, LANES), 1)
    row_iota = lax.broadcasted_iota(jnp.int32, (SLOTS, LANES), 0)
    for j in range(rows // LANES):
        r.oh[:, j * LANES : (j + 1) * LANES] = jnp.where(
            pos_col == lane_iota + j * LANES, 1.0, 0.0
        ).astype(BF)
        r.oht[j * LANES : (j + 1) * LANES, :] = jnp.where(
            pos_row == row_iota + j * LANES, 1.0, 0.0
        ).astype(BF)
    r.low2c[...] = jnp.zeros(r.low2c.shape, BF)
    r.low2c[0 : r.table.shape[0], :] = r.table[...]
    choice = jnp.where(cho_col == lane_iota, 1.0, 0.0).astype(BF)
    for j in range(d_model // TILE):
        r.slt[:, j * TILE : (j + 1) * TILE] = nn(
            choice, r.low2c[:, j * TILE : (j + 1) * TILE]
        ).astype(BF)
    r.mc[...] = jnp.zeros(r.mc.shape, BF)
    r.mc[0:slots, :] = r.mcot[...].reshape(slots, d_model)
    r.vg[...] = jnp.zeros(r.vg.shape, F32)

    def embed(i):
        where = aligned(i * SUB, SUB)
        hot = r.oht[where, :]
        keep = 1.0 - jnp.sum(hot.astype(F32), axis=1, keepdims=True)
        r.keep[where, :] = keep
        r.xl[where, :] = (r.tok[where, :].astype(F32) * keep + nn(hot, r.slt[...])).astype(BF)

    loop(rows // SUB, embed)
    r.st[...] = r.xl[aligned(own0, half), :].astype(F32)

    def transpose_into(target, lane0, source, row0, count):
        for i in range(count // LANES):
            target[:, lane0 + i * LANES : lane0 + (i + 1) * LANES] = low_transpose(
                source[row0 + i * LANES : row0 + (i + 1) * LANES, :]
            )

    transpose_into(r.xt, 0, r.xl, 0, rows)

    gather_pass(ATT)
    gather_start(EXP)
    gather_pass(VEC)
    gather_wait(ATT)
    gather_wait(VEC)
    for j in range(d_model // LANES):
        r.vt[:, j * LANES : (j + 1) * LANES] = jnp.transpose(
            r.wv[j * LANES : (j + 1) * LANES, :].astype(F32), (1, 0)
        )[0:16, :]

    def head_bias(row):
        return r.vt[row : row + 1, aligned(m * hw, hw)]

    half_mask = lax.broadcasted_iota(jnp.int32, (1, LANES), 1) < HEAD_DIM

    def lane_half(value, head):
        return jnp.where(half_mask if head % 2 == 0 else jnp.logical_not(half_mask), value, 0)

    def put_heads(ref, q, value):
        for head in range(heads):
            pair = (head // 2) * LANES
            piece = lane_half(value[:, pair : pair + LANES], head)
            ref[head, aligned(oth0 + q * ch, ch), :] = piece[:ch]
            ref[head, aligned(own0 + q * ch, ch), :] = piece[ch:]

    def put_heads_across(ref, q, across):
        for head in range(heads):
            at = (head % 2) * HEAD_DIM
            piece = across[head * HEAD_DIM : (head + 1) * HEAD_DIM, :]
            ref[head, at : at + HEAD_DIM, aligned(oth0 + q * ch, ch)] = piece[:, :ch]
            ref[head, at : at + HEAD_DIM, aligned(own0 + q * ch, ch)] = piece[:, ch:]

    def put_across(ref, q, across):
        ref[:, aligned(oth0 + q * ch, ch)] = across[:, :ch]
        ref[:, aligned(own0 + q * ch, ch)] = across[:, ch:]

    for ref in (r.qzt, r.dozt):
        ref[...] = jnp.zeros(ref.shape, BF)

    def share_block(layer, head, lane0, width):
        if layer == 0:
            return r.p0.at[head, :, aligned(lane0, width)]
        return r.gse.at[
            (head // 2) * rows : (head // 2 + 1) * rows,
            aligned((head % 2) * rows + lane0, width),
        ]

    def both_lanes(ref, where, q):
        return jnp.concatenate(
            [ref[where, aligned(oth0 + q * ch, ch)], ref[where, aligned(own0 + q * ch, ch)]],
            axis=1,
        )

    def project(layer, q):
        x = both(r.xl, q)
        queries = (nn(x, r.wa[0]) + head_bias(0)).astype(BF) * jnp.asarray(0.125, BF)
        put_heads(r.qz.at[layer], q, queries)
        put_heads_across(r.qzt.at[layer], q, low_transpose(queries))
        keys = nn(x, r.wa[1]).astype(BF)
        put_both(r.kn.at[layer], q, slice(None), keys)
        put_across(r.kt.at[layer], q, low_transpose(keys))
        values = (nn(x, r.wa[2]) + head_bias(1)).astype(BF)
        put_both(r.vn.at[layer], q, slice(None), values)
        put_across(r.vvt, q, low_transpose(values))

    def attend_forward(layer, q):
        for head in range(heads):
            pair = slice((head // 2) * LANES, (head // 2 + 1) * LANES)
            across = both_lanes(r.qzt.at[layer, head], slice(None), q)
            scores = nn(r.kn[layer, :, pair], across)
            raised = jnp.exp(scores - jnp.max(scores, axis=0, keepdims=True))
            total = jnp.sum(raised, axis=0, keepdims=True)
            low = (raised * (1.0 / total)).astype(BF)
            share_block(layer, head, oth0 + q * ch, ch)[...] = low[:, :ch]
            share_block(layer, head, own0 + q * ch, ch)[...] = low[:, ch:]
            where = slice(head * HEAD_DIM, (head + 1) * HEAD_DIM)
            context = nn(r.vvt[where, :], low).astype(BF)
            r.ct[layer, where, aligned(oth0 + q * ch, ch)] = context[:, :ch]
            r.ct[layer, where, aligned(own0 + q * ch, ch)] = context[:, ch:]
        target = r.ctx if layer == 0 else r.ctx1
        put_both(target, q, slice(None), low_transpose(both_lanes(r.ct.at[layer], slice(None), q)))

    def first_norm(layer, q):
        def one(i):
            at = aligned(q * ch + i * SUB, SUB)
            total = sum_rows(2 * layer, q, aligned(i * SUB, SUB))
            res = r.st[at, :] + (total + r.vt[2:3, :])
            cen = res - jnp.mean(res, axis=1, keepdims=True)
            spread = lax.rsqrt(jnp.mean(cen * cen, axis=1, keepdims=True) + EPS)
            hat = cen * spread
            r.xh1[layer, at, :] = hat
            r.rs1[layer, at, :] = spread
            normed = hat * r.vt[4:5, :] + r.vt[5:6, :]
            r.st[at, :] = normed
            r.normed[aligned(own0 + q * ch + i * SUB, SUB), :] = normed.astype(BF)

        loop(ch // SUB, one)

    def second_norm(layer, q):
        def one(i):
            at = aligned(q * ch + i * SUB, SUB)
            total = sum_rows(2 * layer + 1, q, aligned(i * SUB, SUB))
            res = r.st[at, :] + (total + r.vt[3:4, :])
            cen = res - jnp.mean(res, axis=1, keepdims=True)
            spread = lax.rsqrt(jnp.mean(cen * cen, axis=1, keepdims=True) + EPS)
            hat = cen * spread
            r.xh2[layer, at, :] = hat
            r.rs2[layer, at, :] = spread
            out = hat * r.vt[6:7, :] + r.vt[7:8, :]
            r.st[at, :] = out
            if layer < DEPTH - 1:
                r.xl[aligned(own0 + q * ch + i * SUB, SUB), :] = out.astype(BF)

        loop(ch // SUB, one)

    def unit_act(layer):
        return r.act0 if layer == 0 else r.gsn

    def unit_slope(layer):
        return (r.slope0, 0) if layer == 0 else (r.gsn, rows)

    def widen(layer, q):
        act = unit_act(layer)
        slope, slope0 = unit_slope(layer)

        def one(j):
            cols = aligned(j * TILE, TILE)
            v = nn(both(r.normed, q), r.we[:, cols]) + r.vt[pl.ds(8 + m, 1), cols]
            square = v * v
            t = jnp.tanh(GELU_A * v * (1.0 + GELU_B * square))
            gate = 0.5 * (1.0 + t)
            put_both(act, q, cols, (v * gate).astype(BF))
            bend = gate + (0.5 * GELU_A) * v * (1.0 - t * t) * (1.0 + (3.0 * GELU_B) * square)
            bend = bend.astype(BF)
            slope[aligned(slope0 + oth0 + q * ch, ch), cols] = bend[:ch]
            slope[aligned(slope0 + own0 + q * ch, ch), cols] = bend[ch:]

        loop(uw // TILE, one)

    def rejoin_sum(layer, q):
        ctx = r.ctx if layer == 0 else r.ctx1
        sum_begin(2 * layer, q, lambda cols: nt(both(ctx, q), r.wr[cols, :]), ch)

    def narrow_sum(layer, q):
        act = unit_act(layer)
        sum_begin(2 * layer + 1, q, lambda cols: nt(both(act, q), r.wn[cols, :]), ch)

    hot = r.oh[...]

    def pick(target, row0, source, source0, width):
        def one(j):
            cols = aligned(j * TILE, TILE)
            target[row0 : row0 + SLOTS, cols] = nn(
                hot, source[source0 : source0 + rows, cols]
            ).astype(BF)

        loop(width // TILE, one)

    by_columns = (2 * vr) % LANES == 0

    def column_core(step):
        cols = aligned((z_from(step) - y) * vr, 2 * vr)
        return remote(
            r.cs.at[1, :, :, cols],
            r.cr.at[1, :, :, cols],
            r.ccs.at[step],
            r.ccr.at[step],
            core_peer,
        )

    def column_x(step):
        cols = aligned((z_from(step) - y) * vr, 2 * vr)
        return remote(
            r.xs.at[1, :, :, cols], r.xr.at[1, :, :, cols], r.cxs.at[step], r.cxr.at[step], x_peer
        )

    def column_sum(step):
        cols = aligned((z_from(step) - y) * vr, 2 * vr)
        weight = r.wn[cols, :]
        away = nt(r.act0[aligned(oth0, half), :], weight).astype(BF)
        for q in range(CHUNKS):
            r.cs[1, q, :, cols] = away[q * ch : (q + 1) * ch]
        column_core(step).start()
        here = nt(r.act0[aligned(own0, half), :], weight)
        column_core(step).wait_recv()
        for q in range(CHUNKS):
            r.xs[1, q, :, cols] = (
                here[q * ch : (q + 1) * ch] + r.cr[1, q, :, cols].astype(F32)
            ).astype(BF)
        column_x(step).start()

    for layer in range(DEPTH):
        for q in range(CHUNKS):
            if layer > 0:
                share_wait(2 * layer - 1, r.xl, q)
            project(layer, q)
        if layer == 0:
            gather_pass(REJ)
        for q in range(CHUNKS):
            attend_forward(layer, q)
            if layer == 0 and q == 0:
                gather_wait(REJ)
            rejoin_sum(layer, q)
        if layer == 0:
            gather_start(NAR)
            gather_pass(EXP)
        else:
            transpose_into(r.xt, rows, r.xl, 0, rows)
        for q in range(CHUNKS):
            sum_end(2 * layer, q, ch)
            first_norm(layer, q)
            share(2 * layer, r.normed, q).start()
            if layer == 0 and q == 0:
                gather_wait(EXP)
            share_wait(2 * layer, r.normed, q)
            widen(layer, q)
            if layer > 0:
                narrow_sum(layer, q)
        if layer == 0:
            transpose_into(r.nt, 0, r.normed, 0, rows)
            if by_columns:
                for step in range(lines):
                    if step < lines - 1:
                        gather_pass(NAR, step + 1)
                    gather_y_arrival(NAR, step).wait_recv()
                    column_sum(step)
                for step in range(lines):
                    column_x(step).wait()
                    column_core(step).wait_send()
            else:
                gather_pass(NAR)
                gather_wait(NAR)
                for q in range(CHUNKS):
                    narrow_sum(layer, q)
        else:
            pick(r.act0, rows, r.gsn, 0, uw)
            pick(r.slc, 0, r.gsn, rows, uw)
            for head in range(heads):
                r.qc[head] = nn(hot, r.qz[1, head]).astype(BF)
                source = r.gse[
                    (head // 2) * rows : (head // 2 + 1) * rows,
                    (head % 2) * rows : (head % 2 + 1) * rows,
                ]
                r.pc[head] = nn(source, r.oht[...]).astype(BF)
        for q in range(CHUNKS):
            if not (layer == 0 and by_columns):
                sum_end(2 * layer + 1, q, ch)
            second_norm(layer, q)
            if layer < DEPTH - 1:
                share(2 * layer + 1, r.xl, q).start()
            elif q == 0:
                pick(r.low2c, 0, r.normed, 0, d_model)
                transpose_into(r.nt, rows, r.low2c, 0, SLOTS)
                pick(r.ctx, rows, r.ctx1, 0, hw)
                r.cct[...] = nn(r.ct[1], r.oht[...]).astype(BF)

    own_rows = aligned(own0, half)
    out_here = pltpu.make_async_copy(r.st, r.act.at[own_rows], r.osem.at[0])
    out_there = remote(r.st, r.act.at[own_rows], r.osem.at[1], r.osem.at[2], core_peer)
    out_arrival = remote(
        r.st, r.act.at[aligned(oth0, half)], r.osem.at[1], r.osem.at[2], core_peer
    )
    out_here.start()
    out_there.start()

    def add_rows(row, value):
        r.vg[row : row + 1, :] += jnp.sum(value, axis=0, keepdims=True)

    def norm_pull(g, hat, spread, gain):
        scaled = g * gain
        mean = jnp.mean(scaled, axis=1, keepdims=True)
        inner = jnp.mean(scaled * hat, axis=1, keepdims=True)
        return spread * (scaled - mean - hat * inner)

    def second_pull(layer, q, gradient):
        def one(i):
            at = aligned(q * ch + i * SUB, SUB)
            g = gradient(i, at)
            hat = r.xh2[layer, at, :]
            add_rows(6, g * hat)
            add_rows(7, g)
            back = norm_pull(g, hat, r.rs2[layer, at, :], r.vt[6:7, :])
            add_rows(3, back)
            r.gb[at, :] = back
            r.low2[aligned(own0 + q * ch + i * SUB, SUB), :] = back.astype(BF)

        loop(ch // SUB, one)

    def first_pull(layer, q, gradient):
        def one(i):
            at = aligned(q * ch + i * SUB, SUB)
            g = gradient(i, at)
            hat = r.xh1[layer, at, :]
            add_rows(4, g * hat)
            add_rows(5, g)
            back = norm_pull(g, hat, r.rs1[layer, at, :], r.vt[4:5, :])
            add_rows(2, back)
            r.gb[at, :] = back
            r.xl[aligned(own0 + q * ch + i * SUB, SUB), :] = back.astype(BF)

        loop(ch // SUB, one)

    def hot_rows(at_start):
        return r.oht[aligned(own0 + at_start, SUB), :]

    def bias_sums(row0):
        for kind, row in ((0, 0), (2, 1)):
            cols = aligned(m * hw, hw)
            r.vg[row : row + 1, cols] += jnp.sum(
                r.dp[kind, row0 : row0 + rows, :].astype(F32), axis=0, keepdims=True
            )

    for q in range(CHUNKS):
        second_pull(1, q, lambda i, at: nn(hot_rows(q * ch + i * SUB), r.mc[...]))
        share(4, r.low2, q).start()
    for q in range(CHUNKS):
        share_wait(4, r.low2, q)
    pick(r.low2c, 0, r.low2, 0, d_model)

    def slot_units(j):
        cols = aligned(j * TILE, TILE)
        back = nn(r.low2c[...], r.wn[:, cols]) * r.slc[:, cols].astype(F32)
        back = back.astype(BF)
        r.be[rows : rows + SLOTS, cols] = back
        r.vg[pl.ds(8 + m, 1), cols] += jnp.sum(back.astype(F32), axis=0, keepdims=True)

    loop(uw // TILE, slot_units)
    slot_own = core * slot_half
    slot_oth = slot_half - slot_own

    def slot_tile(cols):
        part = nt(r.be[rows : rows + SLOTS, :], r.we[cols, :])
        r.part[...] = part
        return jnp.concatenate(
            [
                r.part[aligned(slot_oth, slot_half), :],
                r.part[aligned(slot_own, slot_half), :],
            ],
            axis=0,
        )

    sum_begin(4, 0, slot_tile, slot_half)
    transpose_into(r.l2t, rows, r.low2c, 0, SLOTS)
    sum_end(4, 0, slot_half)
    mine_slots = r.slt.at[aligned(slot_own, slot_half)]
    mine_slots[...] = sum_rows(4, 0, slice(0, slot_half)).astype(BF)
    slots_out = remote(mine_slots, mine_slots, r.osem.at[3], r.osem.at[4], core_peer)
    slots_in_ref = r.slt.at[aligned(slot_oth, slot_half)]
    slots_in = remote(slots_in_ref, slots_in_ref, r.osem.at[3], r.osem.at[4], core_peer)
    slots_out.start()
    slots_in.wait_recv()
    for q in range(CHUNKS):
        first_pull(
            1, q, lambda i, at: r.gb[at, :] + nn(hot_rows(q * ch + i * SUB), r.slt[...])
        )
        share(5, r.xl, q).start()

    for q in range(CHUNKS):
        share_wait(5, r.xl, q)
    pick(r.low2c, 0, r.xl, 0, d_model)
    transpose_into(r.l1t, rows, r.low2c, 0, SLOTS)
    low_ctx = nn(r.low2c[...], r.wr[...]).astype(BF)
    across = low_transpose(low_ctx)
    dq_across = []
    for pair in range(heads // 2):
        lanes = slice(pair * LANES, (pair + 1) * LANES)
        dv = jnp.zeros((rows, LANES), F32)
        dk = jnp.zeros((rows, LANES), F32)
        for head in (2 * pair, 2 * pair + 1):
            where = slice(head * HEAD_DIM, (head + 1) * HEAD_DIM)
            at = (head % 2) * HEAD_DIM
            r.dozt[head, at : at + HEAD_DIM, 0:SLOTS] = across[where, :]
            low = r.pc[head]
            dv += nn(low, lane_half(low_ctx[:, lanes], head))
            dp = nn(r.vn[1, :, lanes], r.dozt[head, :, 0:SLOTS])
            delta = jnp.sum(
                across[where, :].astype(F32) * r.cct[where, :].astype(F32), axis=0, keepdims=True
            )
            ds = (low.astype(F32) * (dp - delta)).astype(BF)
            dk += nn(ds, r.qc[head])
            dq_across.append(nn(r.kt[1, where, :], ds) * 0.125)
        r.dp[1, rows : 2 * rows, lanes] = dk.astype(BF)
        r.dp[2, rows : 2 * rows, lanes] = dv.astype(BF)
    dq = low_transpose(jnp.concatenate(dq_across, axis=0))
    r.dp[0, rows : 2 * rows, :] = nn(r.oht[...], dq).astype(BF)
    bias_sums(rows)

    def layer_rows(k, q, row0):
        def tile_of(cols):
            total = None
            for kind in range(3):
                lhs = jnp.concatenate(
                    [
                        r.dp[kind, aligned(row0 + oth0 + q * ch, ch), :],
                        r.dp[kind, aligned(row0 + own0 + q * ch, ch), :],
                    ],
                    axis=0,
                )
                part = nt(lhs, r.wa[kind, cols, :])
                total = part if total is None else total + part
            return total

        sum_begin(k, q, tile_of, ch)

    for q in range(CHUNKS):
        layer_rows(5, q, rows)

    def weight_grad_rows(target, across, latter, width, row0, count):
        at = aligned(row0, count)

        def one(j):
            cols = aligned(j * TILE, TILE)
            target[at, cols] = nn(across[at, :], latter[:, cols]).astype(BF)

        loop(width // TILE, one)

    def weight_grad(target, across, latter, width):
        loop(
            d_model // TILE,
            lambda i: weight_grad_rows(target, across, latter, width, i * TILE, TILE),
        )

    def transpose_both(target, source, q):
        for row0 in (oth0 + q * ch, own0 + q * ch):
            target[:, aligned(row0, ch)] = low_transpose(source[aligned(row0, ch), :])

    for q in range(CHUNKS):
        sum_end(5, q, ch)
        second_pull(
            0, q, lambda i, at: r.gb[at, :] + sum_rows(5, q, aligned(i * SUB, SUB))
        )
        share(6, r.low2, q).start()
        share_wait(6, r.low2, q)
        transpose_both(r.l2t, r.low2, q)
        if q == CHUNKS - 1:
            if by_columns:

                def first_rows(step):
                    owner = ((z + step) % lines) * 2 + 1 - y
                    weight_grad_rows(r.gsn, r.l2t, r.act0, uw, owner * vr, vr)
                    scatter_y(NAR, step).start()

                each(1, lines, first_rows)
                first_rows(0)
            else:
                weight_grad(r.gsn, r.l2t, r.act0, uw)
                scatter_start(NAR)

        def units(j, q=q):
            cols = aligned(j * TILE, TILE)
            slope = both(r.slope0, q, cols).astype(F32)
            back = (nn(both(r.low2, q), r.wn[:, cols]) * slope).astype(BF)
            put_both(r.be, q, cols, back)
            r.vg[pl.ds(8 + m, 1), cols] += jnp.sum(back.astype(F32), axis=0, keepdims=True)

        loop(uw // TILE, units)
        sum_begin(6, q, lambda cols, q=q: nt(both(r.be, q), r.we[cols, :]), ch)

    if by_columns:
        each(
            0,
            lines,
            lambda s: weight_grad_rows(
                r.gsn, r.l2t, r.act0, uw, (((z + s) % lines) * 2 + y) * vr, vr
            ),
        )
    weight_grad(r.gse, r.nt, r.be, uw)
    scatter_start(EXP)
    passes = [lambda s=s: scatter_pass(NAR, s) for s in range(1, lines)]
    passes += [lambda s=s: scatter_pass(EXP, s) for s in range(1, lines)]

    def pump(count=1):
        for _ in range(min(count, len(passes))):
            passes.pop(0)()

    pump()
    for q in range(CHUNKS):
        sum_end(6, q, ch)
        first_pull(
            0, q, lambda i, at: r.gb[at, :] + sum_rows(6, q, aligned(i * SUB, SUB))
        )
        share(7, r.xl, q).start()
    pump()
    for q in range(CHUNKS):
        share_wait(7, r.xl, q)
        back = nn(both(r.xl, q), r.wr[...]).astype(BF)
        put_heads(r.doz, q, back)
        put_heads_across(r.dozt, q, low_transpose(back))

    def head_pair(pair):
        lanes = aligned(pair * LANES, LANES)
        dv = jnp.zeros((rows, LANES), F32)
        dk = jnp.zeros((rows, LANES), F32)
        for side in range(2):
            head = 2 * pair + side
            where = aligned(head * HEAD_DIM, HEAD_DIM)
            for part in range(rows // TILE):
                some = slice(part * TILE, (part + 1) * TILE)
                low = r.p0[head, :, some]
                dv += nn(low, r.doz[head, some, :])
                inner = r.dozt[head, side * HEAD_DIM : (side + 1) * HEAD_DIM, some]
                delta = jnp.sum(
                    inner.astype(F32) * r.ct[0, where, some].astype(F32), axis=0, keepdims=True
                )
                dp = nn(r.vn[0, :, lanes], r.dozt[head, :, some])
                ds = (low.astype(F32) * (dp - delta)).astype(BF)
                dk += nn(ds, r.qz[0, head, some, :])
                r.dqt[where, some] = (nn(r.kt[0, where, :], ds) * 0.125).astype(BF)
        r.dp[1, 0:rows, lanes] = dk.astype(BF)
        r.dp[2, 0:rows, lanes] = dv.astype(BF)

    loop(heads // 2, head_pair)
    for i in range(rows // LANES):
        some = slice(i * LANES, (i + 1) * LANES)
        r.dp[0, some, :] = low_transpose(r.dqt[:, some])
    for q in range(CHUNKS):
        layer_rows(7, q, 0)
    pump()
    bias_sums(0)
    transpose_into(r.l1t, 0, r.xl, 0, rows)
    weight_grad(r.gsr, r.l1t, r.ctx, hw)
    scatter_start(REJ)
    first_of_x = jnp.where(m < 2, 1.0, 0.0)
    r.vg[2:8, :] = r.vg[2:8, :] * first_of_x
    for j in range(d_model // LANES):
        tall = jnp.concatenate(
            [r.vg[:, j * LANES : (j + 1) * LANES], jnp.zeros((LANES - 16, LANES), F32)], axis=0
        )
        r.gsv[j * LANES : (j + 1) * LANES, :] = jnp.transpose(tall, (1, 0)).astype(BF)
    scatter_start(VEC)
    for kind in range(3):
        weight_grad(r.gsa.at[kind], r.xt, r.dp.at[kind], hw)
    scatter_start(ATT)
    pump()
    out_here.wait()
    out_there.wait_send()
    for q in range(CHUNKS):
        sum_end(7, q, ch)

        def last(i, q=q):
            at = aligned(q * ch + i * SUB, SUB)
            g = r.gb[at, :] + sum_rows(7, q, aligned(i * SUB, SUB))
            r.st[at, :] = g * r.keep[aligned(own0 + q * ch + i * SUB, SUB), :]

        loop(ch // SUB, last)
    in_here = pltpu.make_async_copy(r.st, r.ing.at[own_rows], r.osem.at[5])
    in_there = remote(r.st, r.ing.at[own_rows], r.osem.at[6], r.osem.at[7], core_peer)
    in_arrival = remote(r.st, r.ing.at[aligned(oth0, half)], r.osem.at[6], r.osem.at[7], core_peer)
    in_here.start()
    in_there.start()

    pump(len(passes))
    each(1, lines, lambda s: scatter_pass(REJ, s))
    each(1, lines, lambda s: scatter_pass(VEC, s))
    each(1, lines, lambda s: scatter_pass(ATT, s))

    def squares(value):
        value = value * value
        if value.ndim == 3:
            value = jnp.sum(value, axis=0)
        value = jnp.sum(value, axis=0, keepdims=True)
        return jnp.sum(value, axis=1, keepdims=True)

    scatter_finish(NAR, r.gn)
    scatter_finish(EXP, r.ge)
    scatter_finish(REJ, r.gr)
    total = squares(r.gn[...]) + squares(r.ge[...]) + squares(r.gr[...])
    scatter_finish(VEC, r.vf.at[0])
    swap_v = remote(r.vf.at[0], r.vf.at[1], r.vxs.at[2], r.vxr.at[2], core_peer)
    swap_v.start()
    swap_v.wait_recv()
    r.vf[2] = r.vf[0] + r.vf[1]
    swap_w = remote(r.vf.at[2], r.vf.at[3], r.vxs.at[3], r.vxr.at[3], x_peer)
    swap_w.start()
    swap_w.wait_recv()
    r.vs[...] = jnp.transpose(r.vf[2] + r.vf[3], (1, 0))
    r.gv[...] = r.vs[pl.ds(columns * m, columns), :]
    total = total + squares(r.gv[...])
    scatter_finish(ATT, r.ga)
    total = total + squares(r.ga[...])

    r.nm[m] = jnp.broadcast_to(total, (8, LANES))

    def model_copy(k, slot):
        return remote(r.nm.at[slot], r.nm.at[slot], r.nms.at[k], r.nmr.at[k], model_peers[k])

    for k in range(3):
        model_copy(k, m).start()
    for k in range(3):
        model_copy(k, model_peers[k][1]).wait_recv()
    r.nz[d] = jnp.sum(r.nm[...], axis=0)

    def line_copy(step, slot):
        here = r.nz.at[slot]
        return remote(here, here, r.nzs.at[0, step], r.nzr.at[0, step], z_peer(step))

    def cross_copy(step, slot):
        here = r.nz.at[slot]
        return remote(here, here, r.nzs.at[1, step], r.nzr.at[1, step], zy_peer(step))

    each(0, lines, lambda s: cross_copy(s, d).start())
    each(1, lines, lambda s: line_copy(s, d).start())
    each(0, lines, lambda s: cross_copy(s, z_from(s) + 1 - 2 * y).wait_recv())
    each(1, lines, lambda s: line_copy(s, z_from(s)).wait_recv())
    r.norm[...] = jnp.sqrt(jnp.sum(r.nz[...], axis=0))

    each(0, lines, lambda s: cross_copy(s, d).wait_send())
    each(1, lines, lambda s: line_copy(s, d).wait_send())
    for k in range(3):
        model_copy(k, m).wait_send()
    swap.wait_send()
    swap_x.wait_send()
    swap_v.wait_send()
    swap_w.wait_send()
    slots_out.wait_send()
    for region in range(5):
        gather_close(region)
        scatter_close(region)
    out_arrival.wait_recv()
    in_here.wait()
    in_there.wait_send()
    in_arrival.wait_recv()


def run_layers(
    n, tok, pos, cho, table, mcot, attend, rejoin, expand, narrow, vin
):
    rows, d_model = tok.shape
    vr = rejoin.shape[0]
    hw = rejoin.shape[1]
    uw = expand.shape[1]
    lines = n // 2
    ways = max(lines - 1, 1)
    half = rows // 2
    ch = half // CHUNKS
    heads = hw // HEAD_DIM
    wide = rows + SLOTS
    inputs = [
        ("tok", tok),
        ("pos", pos),
        ("cho", cho),
        ("table", table),
        ("mcot", mcot),
        ("attend", attend),
        ("rejoin", rejoin),
        ("expand", expand),
        ("narrow", narrow),
        ("vin", vin),
    ]
    outputs = [
        ("act", (rows, d_model), pl.ANY),
        ("ing", (rows, d_model), pl.ANY),
        ("ga", (3, vr, hw), pltpu.VMEM),
        ("gr", (vr, hw), pltpu.VMEM),
        ("ge", (vr, uw), pltpu.VMEM),
        ("gn", (vr, uw), pltpu.VMEM),
        ("gv", vin.shape, pltpu.VMEM),
        ("norm", (8, LANES), pltpu.VMEM),
    ]
    low = [
        ("wv", (d_model, LANES)),
        ("wa", (3, d_model, hw)),
        ("wr", (d_model, hw)),
        ("we", (d_model, uw)),
        ("wn", (d_model, uw)),
        ("gsv", (d_model, LANES)),
        ("gsa", (3, d_model, hw)),
        ("gsr", (d_model, hw)),
        ("gse", (d_model, uw)),
        ("gsn", (d_model, uw)),
        ("yv", (lines, vr, LANES)),
        ("ya", (lines, 3, vr, hw)),
        ("yr", (lines, vr, hw)),
        ("ye", (lines, vr, uw)),
        ("yn", (lines, vr, uw)),
        ("zv", (ways, vr, LANES)),
        ("za", (ways, 3, vr, hw)),
        ("zr", (ways, vr, hw)),
        ("ze", (ways, vr, uw)),
        ("zn", (ways, vr, uw)),
        ("cs", (2, CHUNKS, ch, d_model)),
        ("cr", (2, CHUNKS, ch, d_model)),
        ("xs", (2, CHUNKS, ch, d_model)),
        ("xr", (2, CHUNKS, ch, d_model)),
        ("vb", (4, vr, LANES)),
        ("oh", (SLOTS, rows)),
        ("oht", (rows, SLOTS)),
        ("mc", (SLOTS, d_model)),
        ("xl", (rows, d_model)),
        ("normed", (rows, d_model)),
        ("low2", (rows, d_model)),
        ("xt", (d_model, 2 * rows)),
        ("nt", (d_model, wide)),
        ("l2t", (d_model, wide)),
        ("l1t", (d_model, wide)),
        ("act0", (wide, uw)),
        ("slope0", (rows, uw)),
        ("be", (wide, uw)),
        ("ctx", (wide, hw)),
        ("ctx1", (rows, hw)),
        ("dp", (3, 2 * rows, hw)),
        ("qz", (2, heads, rows, LANES)),
        ("qzt", (2, heads, LANES, rows)),
        ("kn", (2, rows, hw)),
        ("kt", (2, hw, rows)),
        ("vn", (2, rows, hw)),
        ("vvt", (hw, rows)),
        ("ct", (2, hw, rows)),
        ("p0", (heads, rows, rows)),
        ("doz", (heads, rows, LANES)),
        ("dozt", (heads, LANES, rows)),
        ("dqt", (hw, rows)),
        ("slc", (SLOTS, uw)),
        ("low2c", (SLOTS, d_model)),
        ("slt", (SLOTS, d_model)),
        ("qc", (heads, SLOTS, LANES)),
        ("pc", (heads, rows, SLOTS)),
        ("cct", (hw, SLOTS)),
    ]
    full = [
        ("vt", (16, d_model)),
        ("vg", (16, d_model)),
        ("keep", (rows, 1)),
        ("st", (half, d_model)),
        ("gb", (half, d_model)),
        ("xh1", (2, half, d_model)),
        ("xh2", (2, half, d_model)),
        ("rs1", (2, half, 1)),
        ("rs2", (2, half, 1)),
        ("acc", (ch, d_model)),
        ("part", (SLOTS, TILE)),
        ("vf", (4, vr, LANES)),
        ("vs", (LANES, vr)),
        ("nm", (4, 8, LANES)),
        ("nz", (n, 8, LANES)),
    ]
    sems = [
        ("agzs", (5, lines)),
        ("agzr", (5, lines)),
        ("agys", (5, lines)),
        ("agyr", (5, lines)),
        ("rsys", (5, lines)),
        ("rsyr", (5, lines)),
        ("rszs", (5, lines)),
        ("rszr", (5, lines)),
        ("arcs", (8, CHUNKS)),
        ("arcr", (8, CHUNKS)),
        ("arxs", (8, CHUNKS)),
        ("arxr", (8, CHUNKS)),
        ("shs", (8, CHUNKS)),
        ("shr", (8, CHUNKS)),
        ("vxs", (4,)),
        ("vxr", (4,)),
        ("osem", (8,)),
        ("nms", (3,)),
        ("nmr", (3,)),
        ("nzs", (2, lines)),
        ("nzr", (2, lines)),
        ("ccs", (lines,)),
        ("ccr", (lines,)),
        ("cxs", (lines,)),
        ("cxr", (lines,)),
    ]
    names = (
        [name for name, _ in inputs]
        + [name for name, _, _ in outputs]
        + [name for name, _ in low]
        + [name for name, _ in full]
        + ["pb"]
        + [name for name, _ in sems]
    )
    sizes = (n, d_model, rows, hw, uw, vr)

    def body(*refs):
        layer_kernel(names, sizes, *refs)

    return pl.pallas_call(
        body,
        out_shape=[jax.ShapeDtypeStruct(shape, F32) for _, shape, _ in outputs],
        in_specs=[pl.BlockSpec(memory_space=pltpu.VMEM)] * len(inputs),
        out_specs=[pl.BlockSpec(memory_space=space) for _, _, space in outputs],
        scratch_shapes=[pltpu.VMEM(shape, BF) for _, shape in low]
        + [pltpu.VMEM(shape, F32) for _, shape in full]
        + [pltpu.VMEM((16, LANES), jnp.int32)]
        + [pltpu.SemaphoreType.DMA(shape) for _, shape in sems],
        compiler_params=pltpu.CompilerParams(
            collective_id=0, has_side_effects=True, vmem_limit_bytes=61 * 1024 * 1024
        ),
        cost_estimate=pl.CostEstimate(
            flops=20_000_000_000, bytes_accessed=20_000_000, transcendentals=4_000_000
        ),
    )(*[value for _, value in inputs])


def apply_update(weight, first_moment, second_moment, shadow, gradient, step_rate):
    momentum = 0.5 * first_moment + 0.5 * gradient
    variance = 0.5 * second_moment + 0.5 * gradient * gradient
    bias_fix = 1.0 - 0.5**STEP
    updated = weight - step_rate * (
        momentum / bias_fix / (jnp.sqrt(variance / bias_fix) + 1e-08) + 0.01 * weight
    )
    average = 0.999 * shadow + 0.001 * updated
    return (updated, momentum, variance, average, updated.astype(BF))


def update_kernel(rates, clip_limit, norm, act, ing, *refs):
    *refs, norm_out, act_out, ing_out = refs
    act_out[...] = act[...]
    ing_out[...] = ing[...]
    norm_out[...] = norm[0:1, 0:1]
    factor = jnp.minimum(1.0, clip_limit / (norm[0:1, 0:1] + 1e-06))
    ins, outs = refs[: 5 * len(rates)], refs[5 * len(rates) :]
    for index, rate in enumerate(rates):
        weight, first, second, shadow, gradient = ins[5 * index : 5 * index + 5]
        targets = outs[5 * index : 5 * index + 5]
        for part in range(weight.shape[0]) if len(weight.shape) == 3 else (slice(None),):
            results = apply_update(
                weight[part],
                first[part],
                second[part],
                shadow[part],
                gradient[part] * factor,
                rate,
            )
            for target, value in zip(targets, results, strict=True):
                target[part] = value


def run_update(groups, rates, norm, clip_limit, act, ing):
    vr = groups[1][0].shape[0]
    step = min(vr, 32)

    def spec(shape, whole):
        if whole:
            return pl.BlockSpec(shape, lambda i: (0, 0))
        if len(shape) == 3:
            return pl.BlockSpec((shape[0], step, shape[2]), lambda i: (0, i, 0))
        return pl.BlockSpec((step, shape[1]), lambda i: (i, 0))

    last = len(groups) - 1
    passed = pl.BlockSpec((act.shape[0] * step // vr, act.shape[1]), lambda i: (i, 0))
    specs = [spec(group[0].shape, k == last) for k, group in enumerate(groups)]

    def body(*refs):
        update_kernel(rates, clip_limit, *refs)

    flat = [value for group in groups for value in group]
    size = sum(value.size for value in flat) * 4
    outs = pl.pallas_call(
        body,
        grid=(vr // step,),
        in_specs=[spec(norm.shape, True)]
        + [passed] * 2
        + [one for one in specs for _ in range(5)],
        out_specs=[one for one in specs for _ in range(5)]
        + [spec((1, 1), True)]
        + [passed] * 2,
        out_shape=[
            jax.ShapeDtypeStruct(group[0].shape, kind)
            for group in groups
            for kind in (F32, F32, F32, F32, BF)
        ]
        + [jax.ShapeDtypeStruct(shape, F32) for shape in ((1, 1), act.shape, ing.shape)],
        compiler_params=pltpu.CompilerParams(vmem_limit_bytes=60 * 1024 * 1024),
        cost_estimate=pl.CostEstimate(flops=size, bytes_accessed=2 * size, transcendentals=0),
    )(norm, act, ing, *flat)
    groups_out = [outs[5 * k : 5 * k + 5] for k in range(len(groups))]
    return groups_out, outs[-3].reshape(()), *outs[-2:]


def per_device(
    tokens_in,
    masked_positions,
    replace_choice,
    replace_table,
    masked_cotangent,
    attend,
    attend_mean,
    attend_square,
    attend_shadow,
    rejoin,
    rejoin_mean,
    rejoin_square,
    rejoin_shadow,
    expand,
    expand_mean,
    expand_square,
    expand_shadow,
    narrow,
    narrow_mean,
    narrow_square,
    narrow_shadow,
    vectors,
    vectors_mean,
    vectors_square,
    vectors_shadow,
):
    n = lax.axis_size("dp")
    act, ing, ga, gr, ge, gn, gv, norm = run_layers(
        n,
        tokens_in,
        masked_positions,
        replace_choice,
        replace_table,
        masked_cotangent,
        attend.transpose(1, 0, 2),
        rejoin,
        expand,
        narrow,
        vectors.T,
    )
    d_model = tokens_in.shape[1]
    param_count = 4 * d_model * d_model + 2 * d_model * expand.shape[1] * 4 + 12 * d_model
    clip_limit = 0.001 * math.sqrt(param_count * tokens_in.shape[0] * n)
    cubes = [x.transpose(1, 0, 2) for x in (attend, attend_mean, attend_square, attend_shadow)]
    rows_of = [x.T for x in (vectors, vectors_mean, vectors_square, vectors_shadow)]
    new, gradient_norm, act, ing = run_update(
        (
            (*cubes, ga),
            (rejoin, rejoin_mean, rejoin_square, rejoin_shadow, gr),
            (expand, expand_mean, expand_square, expand_shadow, ge),
            (narrow, narrow_mean, narrow_square, narrow_shadow, gn),
            (*rows_of, gv),
        ),
        (0.04, 0.16, 0.04, 0.04, 0.5),
        norm,
        clip_limit,
        act,
        ing,
    )
    results = [act, ing, gradient_norm]
    results.extend(x.transpose(1, 0, 2) for x in new[0])
    for group in new[1:4]:
        results.extend(group)
    results.extend(x.T for x in new[4])
    return tuple(results)


def solution(mesh):
    row = P("dp", None)
    cube = P("dp", None, "mp")
    flat = P("dp", "mp")
    return jax.shard_map(
        per_device,
        mesh=mesh,
        in_specs=(row, row, row, P(), P("dp", None, None)) + (cube,) * 4 + (flat,) * 16,
        out_specs=(row, row, P()) + (cube,) * 5 + (flat,) * 20,
        check_vma=False,
    )
```

```python
import math
from types import SimpleNamespace

import jax
import jax.numpy as jnp
from jax import lax
from jax.experimental import pallas as pl
from jax.experimental.pallas import tpu as pltpu
from jax.sharding import PartitionSpec as P

HEAD_DIM = 64
SEQ_LEN = 512
DEPTH = 2
STEP = 7
EPS = 1e-05
BF = jnp.bfloat16
F32 = jnp.float32
MESH = pl.DeviceIdType.MESH
LANES = 128
TILE = 256
SLOTS = 128
CHUNKS = 2
SUB = 64
VEC, ATT, REJ, EXP, NAR = range(5)
GELU_A = 0.7978845608028654
GELU_B = 0.044715


def nn(former, latter):
    return jnp.dot(former, latter, preferred_element_type=F32)


def nt(former, latter):
    return lax.dot_general(former, latter, (((1,), (1,)), ((), ())), preferred_element_type=F32)


def low_transpose(block):
    return jnp.transpose(block.astype(F32), (1, 0)).astype(BF)


def loop(count, body):
    def step(index, carry):
        body(index)
        return carry

    lax.fori_loop(0, count, step, 0)


def each(first, last, body):
    if last - first <= 8:
        for index in range(first, last):
            body(index)
    else:

        def step(index, carry):
            body(index)
            return carry

        lax.fori_loop(first, last, step, 0)


def aligned(index, size):
    return pl.ds(pl.multiple_of(index, size), size)


def layer_kernel(names, sizes, *refs):
    r = SimpleNamespace(**dict(zip(names, refs, strict=True)))
    n, d_model, rows, hw, uw, vr = sizes
    r.doz, r.dozt = r.qz.at[1], r.qzt.at[1]
    half = rows // 2
    ch = half // CHUNKS
    lines = n // 2
    heads = hw // HEAD_DIM
    slot_half = SLOTS // 2

    d = lax.axis_index("dp")
    m = lax.axis_index("mp")
    z, y = d // 2, d % 2
    core = m % 2
    core_peer = (d, m + 1 - 2 * core)
    x_peer = (d, (m + 2) % 4)
    y_peer = (d + 1 - 2 * y, m)
    model_peers = (core_peer, x_peer, (d, 3 - m))
    own0 = core * half
    oth0 = half - own0

    weights = (r.wv, r.wa, r.wr, r.we, r.wn)
    grads = (r.gsv, r.gsa, r.gsr, r.gse, r.gsn)
    from_y = (r.yv, r.ya, r.yr, r.ye, r.yn)
    from_z = (r.zv, r.za, r.zr, r.ze, r.zn)

    def z_peer(step):
        return (((z + step) % lines) * 2 + y, m)

    def zy_peer(step):
        return (((z + step) % lines) * 2 + 1 - y, m)

    def z_from(step):
        return ((z + lines - step) % lines) * 2 + y

    def block(ref, region, index):
        where = aligned(index * vr, vr)
        return ref.at[:, where, :] if region == ATT else ref.at[where, :]

    def remote(source, target, send, recv, device):
        return pltpu.make_async_remote_copy(
            src_ref=source,
            dst_ref=target,
            send_sem=send,
            recv_sem=recv,
            device_id=device,
            device_id_type=MESH,
        )

    barrier = pltpu.get_barrier_semaphore()

    def greet(peer):
        pl.semaphore_signal(barrier, inc=1, device_id=peer, device_id_type=MESH)

    for peer in model_peers:
        greet(peer)
    each(1, lines, lambda s: greet(z_peer(s)))
    each(0, lines, lambda s: greet(zy_peer(s)))
    pl.semaphore_wait(barrier, len(model_peers) + n - 1)

    relay = lines == 4
    crossing = (VEC, REJ)
    last_line = lines - 1
    inner = jnp.logical_and(z > 0, z < last_line)
    far_end = (jnp.where(z == 1, 0, last_line) * 2 + y, m)
    near_mid = (jnp.where(z == 0, 1, last_line - 1) * 2 + y, m)

    def gather_z(region, step):
        piece = block(weights[region], region, d)
        return remote(
            piece, piece, r.agzs.at[region, step], r.agzr.at[region, step], z_peer(step)
        )

    def gather_z_arrival(region, step):
        piece = block(weights[region], region, z_from(step))
        return remote(
            piece, piece, r.agzs.at[region, step], r.agzr.at[region, step], z_peer(step)
        )

    def gather_relay(region):
        piece = block(weights[region], region, z_from(2))
        arrives_as = jnp.where(z == 1, 1, last_line)
        return remote(
            piece, piece, r.agzs.at[region, lines], r.agzr.at[region, arrives_as], far_end
        )

    def gather_y(region, step):
        piece = block(weights[region], region, z_from(step))
        return remote(piece, piece, r.agys.at[region, step], r.agyr.at[region, step], y_peer)

    def gather_cross(region, step):
        piece = block(weights[region], region, d + 1 - 2 * y)
        return remote(
            piece, piece, r.agys.at[region, step], r.agyr.at[region, step], z_peer(step)
        )

    def gather_y_arrival(region, step):
        piece = block(weights[region], region, z_from(step) + 1 - 2 * y)
        return remote(piece, piece, r.agys.at[region, step], r.agyr.at[region, step], y_peer)

    def near(region, step, body):
        if not relay or region in crossing or step == 2:
            body()
        else:
            pl.when(z < last_line if step == 1 else z > 0)(body)

    def gather_start_z(region):
        order = (1, 3, 2) if relay else range(1, lines)
        for step in order:
            near(region, step, lambda: gather_z(region, step).start())

    def gather_start_y(region):
        gather_y(region, 0).start()

    def gather_pass(region, turn):
        step = jnp.where(z == 0, lines - turn, turn) if relay else turn
        gather_z_arrival(region, step).wait_recv()
        if relay and turn == 2:
            pl.when(inner)(lambda: gather_relay(region).start())
        gather_y(region, step).start()

    def gather_turn(region):
        gather_y_arrival(region, 0).wait_recv()
        each(1, lines, lambda s: gather_cross(region, s).start())

    def gather_wait(region):
        if region in crossing:
            each(1, lines, lambda s: gather_z_arrival(region, s).wait_recv())
            each(1, lines, lambda s: gather_y_arrival(region, s).wait_recv())
        else:
            each(0, lines, lambda s: gather_y_arrival(region, s).wait_recv())

    def gather_close(region):
        for step in range(1, lines):
            near(region, step, lambda: gather_z(region, step).wait_send())
        if relay and region not in crossing:
            pl.when(inner)(lambda: gather_relay(region).wait_send())
        each(0, lines, lambda s: gather_y(region, s).wait_send())

    def scatter_y(region, step):
        owner = ((z + step) % lines) * 2 + 1 - y
        return remote(
            block(grads[region], region, owner),
            from_y[region].at[step],
            r.rsys.at[region, step],
            r.rsyr.at[region, step],
            y_peer,
        )

    def scatter_cross(region, step):
        owner = ((z + step) % lines) * 2 + 1 - y
        return remote(
            block(grads[region], region, owner),
            from_y[region].at[step],
            r.rsys.at[region, step],
            r.rsyr.at[region, step],
            z_peer(step),
        )

    def scatter_z(region, step):
        owner = ((z + step) % lines) * 2 + y
        return remote(
            block(grads[region], region, owner),
            from_z[region].at[step],
            r.rszs.at[region, step],
            r.rszr.at[region, step],
            z_peer(step),
        )

    def scatter_far(region, step):
        owner = ((z + step) % lines) * 2 + y
        return remote(
            block(grads[region], region, owner),
            from_z[region].at[0],
            r.rszs.at[region, step],
            r.rszr.at[region, 0],
            near_mid,
        )

    def scatter_order(turn):
        if not relay:
            return turn % lines
        if turn == 1:
            return jnp.where(z == 0, last_line, 1)
        if turn == 2:
            return jnp.where(z == 0, 1, last_line)
        return 2 if turn == 3 else 0

    def scatter_start(region):
        if region in crossing:
            each(1, lines, lambda s: scatter_z(region, s).start())
            each(1, lines, lambda s: scatter_cross(region, s).start())
        else:
            each(1, lines + 1, lambda t: scatter_y(region, scatter_order(t)).start())

    def scatter_pass(region, turn):
        step = scatter_order(turn)
        scatter_y(region, step).wait_recv()
        piece = block(grads[region], region, ((z + step) % lines) * 2 + y)
        total = piece[...].astype(F32) + from_y[region][step].astype(F32)
        piece[...] = total.astype(BF)
        if not relay:
            scatter_z(region, step).start()
        elif turn == 1:
            pl.when(inner)(lambda: scatter_z(region, step).start())
            pl.when(jnp.logical_not(inner))(lambda: scatter_far(region, step).start())
        elif turn == 2:
            scatter_z(region, step).start()
        else:

            @pl.when(inner)
            def _():
                scatter_far(region, 0).wait_recv()
                piece[...] = (total + from_z[region][0].astype(F32)).astype(BF)

            scatter_z(region, step).start()

    def scatter_turn(region):
        piece = block(grads[region], region, d + 1 - 2 * y)
        total = piece[...].astype(F32)
        for step in range(1, lines):
            scatter_cross(region, step).wait_recv()
            total = total + from_y[region][step].astype(F32)
        piece[...] = total.astype(BF)
        scatter_y(region, 0).start()

    def scatter_finish(region, out_ref):
        def one(step):
            scatter_z(region, step).wait_recv()
            out_ref[...] += from_z[region][step].astype(F32)

        scatter_y(region, 0).wait_recv()
        piece = block(grads[region], region, d)
        out_ref[...] = piece[...].astype(F32) + from_y[region][0].astype(F32)
        for step in range(1, lines):
            if not relay or region in crossing or step == 2:
                one(step)
            else:
                pl.when(z > 0 if step == 1 else z < last_line)(lambda: one(step))

    def scatter_close(region):
        each(0, lines, lambda s: scatter_y(region, s).wait_send())
        each(1, lines, lambda s: scatter_z(region, s).wait_send())

    def core_copy(k, q, count):
        b = k % 2
        return remote(
            r.cs.at[b, q, :count],
            r.cr.at[b, q, :count],
            r.arcs.at[k, q],
            r.arcr.at[k, q],
            core_peer,
        )

    def x_copy(k, q, count):
        b = k % 2
        return remote(
            r.xs.at[b, q, :count],
            r.xr.at[b, q, :count],
            r.arxs.at[k, q],
            r.arxr.at[k, q],
            x_peer,
        )

    def sum_begin(k, q, tile_of, count):
        b = k % 2

        def one(j):
            cols = aligned(j * TILE, TILE)
            part = tile_of(cols)
            r.cs[b, q, :count, cols] = part[:count].astype(BF)
            r.acc[:count, cols] = part[count:]

        loop(d_model // TILE, one)
        copy = core_copy(k, q, count)
        copy.start()
        copy.wait_recv()
        r.xs[b, q, :count] = (r.acc[:count] + r.cr[b, q, :count].astype(F32)).astype(BF)
        x_copy(k, q, count).start()

    def sum_end(k, q, count):
        x_copy(k, q, count).wait()
        core_copy(k, q, count).wait_send()

    def sum_rows(k, q, where):
        b = k % 2
        return r.xs[b, q, where].astype(F32) + r.xr[b, q, where].astype(F32)

    def share(k, ref, q):
        where = aligned(own0 + q * ch, ch)
        return remote(ref.at[where], ref.at[where], r.shs.at[k, q], r.shr.at[k, q], core_peer)

    def share_arrival(k, ref, q):
        where = aligned(oth0 + q * ch, ch)
        return remote(ref.at[where], ref.at[where], r.shs.at[k, q], r.shr.at[k, q], core_peer)

    def share_wait(k, ref, q):
        share(k, ref, q).wait_send()
        share_arrival(k, ref, q).wait_recv()

    def both(ref, q, cols=slice(None)):
        return jnp.concatenate(
            [ref[aligned(oth0 + q * ch, ch), cols], ref[aligned(own0 + q * ch, ch), cols]],
            axis=0,
        )

    def put_both(ref, q, cols, value):
        ref[aligned(oth0 + q * ch, ch), cols] = value[:ch]
        ref[aligned(own0 + q * ch, ch), cols] = value[ch:]

    columns = r.vin.shape[0]
    r.vs[...] = jnp.zeros(r.vs.shape, F32)
    r.vs[pl.ds(columns * m, columns), :] = r.vin[...]
    r.vb[0] = low_transpose(r.vs[...])
    swap = remote(r.vb.at[0], r.vb.at[1], r.vxs.at[0], r.vxr.at[0], core_peer)
    swap.start()
    mine = aligned(d * vr, vr)
    r.wa[:, mine, :] = r.attend[...].astype(BF)
    gather_start_y(ATT)
    gather_start_z(ATT)
    r.wr[mine, :] = r.rejoin[...].astype(BF)
    gather_start_y(REJ)
    swap.wait_recv()
    r.vb[2] = r.vb[0] + r.vb[1]
    swap_x = remote(r.vb.at[2], r.vb.at[3], r.vxs.at[1], r.vxr.at[1], x_peer)
    swap_x.start()
    r.we[mine, :] = r.expand[...].astype(BF)
    gather_start_y(EXP)
    r.wn[mine, :] = r.narrow[...].astype(BF)
    swap_x.wait_recv()
    r.wv[mine, :] = r.vb[2] + r.vb[3]
    gather_start_y(VEC)
    gather_start_y(NAR)
    gather_start_z(VEC)
    gather_start_z(REJ)

    r.pb[...] = jnp.full(r.pb.shape, SEQ_LEN, jnp.int32)
    slots = r.pos.shape[1]
    r.pb[0:1, 0:slots] = r.pos[...]
    r.pb[8:9, 0:slots] = r.cho[...]
    pos_row = jnp.broadcast_to(r.pb[0:1, :], (SLOTS, SLOTS))
    cho_row = jnp.broadcast_to(r.pb[8:9, :], (SLOTS, SLOTS))
    pos_col = jnp.transpose(pos_row.astype(F32), (1, 0)).astype(jnp.int32)
    cho_col = jnp.transpose(cho_row.astype(F32), (1, 0)).astype(jnp.int32)
    lane_iota = lax.broadcasted_iota(jnp.int32, (SLOTS, LANES), 1)
    row_iota = lax.broadcasted_iota(jnp.int32, (SLOTS, LANES), 0)
    for j in range(rows // LANES):
        r.oh[:, j * LANES : (j + 1) * LANES] = jnp.where(
            pos_col == lane_iota + j * LANES, 1.0, 0.0
        ).astype(BF)
        r.oht[j * LANES : (j + 1) * LANES, :] = jnp.where(
            pos_row == row_iota + j * LANES, 1.0, 0.0
        ).astype(BF)
    r.low2c[...] = jnp.zeros(r.low2c.shape, BF)
    r.low2c[0 : r.table.shape[0], :] = r.table[...]
    choice = jnp.where(cho_col == lane_iota, 1.0, 0.0).astype(BF)
    for j in range(d_model // TILE):
        r.slt[:, j * TILE : (j + 1) * TILE] = nn(
            choice, r.low2c[:, j * TILE : (j + 1) * TILE]
        ).astype(BF)
    r.mc[...] = jnp.zeros(r.mc.shape, BF)
    r.mc[0:slots, :] = r.mcot[...].reshape(slots, d_model)
    r.vg[...] = jnp.zeros(r.vg.shape, F32)

    if relay:
        gather_pass(ATT, 1)

    def embed(i):
        where = aligned(i * SUB, SUB)
        hot = r.oht[where, :]
        keep = 1.0 - jnp.sum(hot.astype(F32), axis=1, keepdims=True)
        r.keep[where, :] = keep
        r.xl[where, :] = (r.tok[where, :].astype(F32) * keep + nn(hot, r.slt[...])).astype(BF)

    loop(rows // SUB, embed)
    r.st[...] = r.xl[aligned(own0, half), :].astype(F32)

    def transpose_into(target, lane0, source, row0, count):
        for i in range(count // LANES):
            target[:, lane0 + i * LANES : lane0 + (i + 1) * LANES] = low_transpose(
                source[row0 + i * LANES : row0 + (i + 1) * LANES, :]
            )

    gather_turn(REJ)
    gather_turn(VEC)
    for turn in range(2 if relay else 1, lines):
        gather_pass(ATT, turn)
    gather_start_z(EXP)
    gather_wait(ATT)
    gather_wait(VEC)
    for j in range(d_model // LANES):
        r.vt[:, j * LANES : (j + 1) * LANES] = jnp.transpose(
            r.wv[j * LANES : (j + 1) * LANES, :].astype(F32), (1, 0)
        )[0:16, :]

    def head_bias(row):
        return r.vt[row : row + 1, aligned(m * hw, hw)]

    half_mask = lax.broadcasted_iota(jnp.int32, (1, LANES), 1) < HEAD_DIM

    def lane_half(value, head):
        return jnp.where(half_mask if head % 2 == 0 else jnp.logical_not(half_mask), value, 0)

    def put_heads(ref, q, value):
        for head in range(heads):
            pair = (head // 2) * LANES
            piece = lane_half(value[:, pair : pair + LANES], head)
            ref[head, aligned(oth0 + q * ch, ch), :] = piece[:ch]
            ref[head, aligned(own0 + q * ch, ch), :] = piece[ch:]

    def put_heads_across(ref, q, across):
        for head in range(heads):
            at = (head % 2) * HEAD_DIM
            piece = across[head * HEAD_DIM : (head + 1) * HEAD_DIM, :]
            ref[head, at : at + HEAD_DIM, aligned(oth0 + q * ch, ch)] = piece[:, :ch]
            ref[head, at : at + HEAD_DIM, aligned(own0 + q * ch, ch)] = piece[:, ch:]

    def put_across(ref, q, across):
        ref[:, aligned(oth0 + q * ch, ch)] = across[:, :ch]
        ref[:, aligned(own0 + q * ch, ch)] = across[:, ch:]

    r.qzt[...] = jnp.zeros(r.qzt.shape, BF)

    def share_block(layer, head, lane0, width):
        if layer == 0:
            return r.p0.at[head, :, aligned(lane0, width)]
        return r.gse.at[
            (head // 2) * rows : (head // 2 + 1) * rows,
            aligned((head % 2) * rows + lane0, width),
        ]

    def both_lanes(ref, where, q):
        return jnp.concatenate(
            [ref[where, aligned(oth0 + q * ch, ch)], ref[where, aligned(own0 + q * ch, ch)]],
            axis=1,
        )

    def project(layer, q):
        x = both(r.xl, q)
        queries = (nn(x, r.wa[0]) + head_bias(0)).astype(BF) * jnp.asarray(0.125, BF)
        put_heads(r.qz.at[layer], q, queries)
        put_heads_across(r.qzt.at[layer], q, low_transpose(queries))
        keys = nn(x, r.wa[1]).astype(BF)
        put_both(r.kn.at[layer], q, slice(None), keys)
        put_across(r.kt.at[layer], q, low_transpose(keys))
        values = (nn(x, r.wa[2]) + head_bias(1)).astype(BF)
        put_both(r.vn.at[layer], q, slice(None), values)
        put_across(r.vvt, q, low_transpose(values))

    def attend_forward(layer, q):
        for head in range(heads):
            pair = slice((head // 2) * LANES, (head // 2 + 1) * LANES)
            across = both_lanes(r.qzt.at[layer, head], slice(None), q)
            scores = nn(r.kn[layer, :, pair], across)
            raised = jnp.exp(scores - jnp.max(scores, axis=0, keepdims=True))
            total = jnp.sum(raised, axis=0, keepdims=True)
            low = (raised * (1.0 / total)).astype(BF)
            share_block(layer, head, oth0 + q * ch, ch)[...] = low[:, :ch]
            share_block(layer, head, own0 + q * ch, ch)[...] = low[:, ch:]
            where = slice(head * HEAD_DIM, (head + 1) * HEAD_DIM)
            context = nn(r.vvt[where, :], low).astype(BF)
            r.ct[layer, where, aligned(oth0 + q * ch, ch)] = context[:, :ch]
            r.ct[layer, where, aligned(own0 + q * ch, ch)] = context[:, ch:]
        target = r.ctx if layer == 0 else r.ctx1
        put_both(target, q, slice(None), low_transpose(both_lanes(r.ct.at[layer], slice(None), q)))

    def first_norm(layer, q):
        def one(i):
            at = aligned(q * ch + i * SUB, SUB)
            total = sum_rows(2 * layer, q, aligned(i * SUB, SUB))
            res = r.st[at, :] + (total + r.vt[2:3, :])
            cen = res - jnp.mean(res, axis=1, keepdims=True)
            spread = lax.rsqrt(jnp.mean(cen * cen, axis=1, keepdims=True) + EPS)
            hat = cen * spread
            r.xh1[layer, at, :] = hat
            r.rs1[layer, at, :] = spread
            normed = hat * r.vt[4:5, :] + r.vt[5:6, :]
            r.st[at, :] = normed
            r.normed[aligned(own0 + q * ch + i * SUB, SUB), :] = normed.astype(BF)

        loop(ch // SUB, one)

    def second_norm(layer, q):
        def one(i):
            at = aligned(q * ch + i * SUB, SUB)
            total = sum_rows(2 * layer + 1, q, aligned(i * SUB, SUB))
            res = r.st[at, :] + (total + r.vt[3:4, :])
            cen = res - jnp.mean(res, axis=1, keepdims=True)
            spread = lax.rsqrt(jnp.mean(cen * cen, axis=1, keepdims=True) + EPS)
            hat = cen * spread
            r.xh2[layer, at, :] = hat
            r.rs2[layer, at, :] = spread
            out = hat * r.vt[6:7, :] + r.vt[7:8, :]
            r.st[at, :] = out
            if layer < DEPTH - 1:
                r.xl[aligned(own0 + q * ch + i * SUB, SUB), :] = out.astype(BF)

        loop(ch // SUB, one)

    def unit_act(layer):
        return r.act0 if layer == 0 else r.gsn

    def unit_slope(layer):
        return (r.slope0, 0) if layer == 0 else (r.gsn, rows)

    def widen(layer, q):
        act = unit_act(layer)
        slope, slope0 = unit_slope(layer)

        def one(j):
            cols = aligned(j * TILE, TILE)
            v = nn(both(r.normed, q), r.we[:, cols]) + r.vt[pl.ds(8 + m, 1), cols]
            square = v * v
            t = jnp.tanh(GELU_A * v * (1.0 + GELU_B * square))
            gate = 0.5 * (1.0 + t)
            put_both(act, q, cols, (v * gate).astype(BF))
            bend = gate + (0.5 * GELU_A) * v * (1.0 - t * t) * (1.0 + (3.0 * GELU_B) * square)
            bend = bend.astype(BF)
            slope[aligned(slope0 + oth0 + q * ch, ch), cols] = bend[:ch]
            slope[aligned(slope0 + own0 + q * ch, ch), cols] = bend[ch:]

        loop(uw // TILE, one)

    def rejoin_sum(layer, q):
        ctx = r.ctx if layer == 0 else r.ctx1
        sum_begin(2 * layer, q, lambda cols: nt(both(ctx, q), r.wr[cols, :]), ch)

    def narrow_sum(layer, q):
        act = unit_act(layer)
        sum_begin(2 * layer + 1, q, lambda cols: nt(both(act, q), r.wn[cols, :]), ch)

    hot = r.oh[...]

    def pick(target, row0, source, source0, width):
        def one(j):
            cols = aligned(j * TILE, TILE)
            target[row0 : row0 + SLOTS, cols] = nn(
                hot, source[source0 : source0 + rows, cols]
            ).astype(BF)

        loop(width // TILE, one)

    by_columns = (2 * vr) % LANES == 0

    def column_core(step):
        cols = aligned((z_from(step) - y) * vr, 2 * vr)
        return remote(
            r.cs.at[1, :, :, cols],
            r.cr.at[1, :, :, cols],
            r.ccs.at[step],
            r.ccr.at[step],
            core_peer,
        )

    def column_x(step):
        cols = aligned((z_from(step) - y) * vr, 2 * vr)
        return remote(
            r.xs.at[1, :, :, cols], r.xr.at[1, :, :, cols], r.cxs.at[step], r.cxr.at[step], x_peer
        )

    def column_sum(step):
        cols = aligned((z_from(step) - y) * vr, 2 * vr)
        weight = r.wn[cols, :]
        away = nt(r.act0[aligned(oth0, half), :], weight).astype(BF)
        for q in range(CHUNKS):
            r.cs[1, q, :, cols] = away[q * ch : (q + 1) * ch]
        column_core(step).start()
        here = nt(r.act0[aligned(own0, half), :], weight)
        column_core(step).wait_recv()
        for q in range(CHUNKS):
            r.xs[1, q, :, cols] = (
                here[q * ch : (q + 1) * ch] + r.cr[1, q, :, cols].astype(F32)
            ).astype(BF)
        column_x(step).start()

    for layer in range(DEPTH):
        for q in range(CHUNKS):
            if layer > 0:
                share_wait(2 * layer - 1, r.xl, q)
            project(layer, q)
        for q in range(CHUNKS):
            attend_forward(layer, q)
            if layer == 0 and q == 0:
                gather_pass(EXP, 1)
                gather_start_z(NAR)
                gather_wait(REJ)
            rejoin_sum(layer, q)
        if layer == 0:
            for turn in range(2, lines):
                gather_pass(EXP, turn)
            transpose_into(r.xt, 0, r.xl, 0, rows)
        else:
            transpose_into(r.xt, rows, r.xl, 0, rows)
        for q in range(CHUNKS):
            sum_end(2 * layer, q, ch)
            first_norm(layer, q)
            share(2 * layer, r.normed, q).start()
            if layer == 0 and q == 0:
                gather_wait(EXP)
            share_wait(2 * layer, r.normed, q)
            widen(layer, q)
            if layer > 0:
                narrow_sum(layer, q)
            elif q == 0:
                gather_pass(NAR, 1)
        if layer == 0:
            transpose_into(r.nt, 0, r.normed, 0, rows)
            if by_columns:
                for turn in range(lines):
                    if 0 < turn < lines - 1:
                        gather_pass(NAR, turn + 1)
                    step = jnp.where(z == 0, (lines - turn) % lines, turn) if relay else turn
                    gather_y_arrival(NAR, step).wait_recv()
                    column_sum(step)
                for step in range(lines):
                    column_x(step).wait()
                    column_core(step).wait_send()
            else:
                for turn in range(2, lines):
                    gather_pass(NAR, turn)
                gather_wait(NAR)
                for q in range(CHUNKS):
                    narrow_sum(layer, q)
        else:
            pick(r.act0, rows, r.gsn, 0, uw)
            pick(r.slc, 0, r.gsn, rows, uw)
            for head in range(heads):
                r.qc[head] = nn(hot, r.qz[1, head]).astype(BF)
                source = r.gse[
                    (head // 2) * rows : (head // 2 + 1) * rows,
                    (head % 2) * rows : (head % 2 + 1) * rows,
                ]
                r.pc[head] = nn(source, r.oht[...]).astype(BF)
        for q in range(CHUNKS):
            if not (layer == 0 and by_columns):
                sum_end(2 * layer + 1, q, ch)
            second_norm(layer, q)
            if layer < DEPTH - 1:
                share(2 * layer + 1, r.xl, q).start()
            elif q == 0:
                pick(r.low2c, 0, r.normed, 0, d_model)
                transpose_into(r.nt, rows, r.low2c, 0, SLOTS)
                pick(r.ctx, rows, r.ctx1, 0, hw)
                r.cct[...] = nn(r.ct[1], r.oht[...]).astype(BF)

    own_rows = aligned(own0, half)
    out_here = pltpu.make_async_copy(r.st, r.act.at[own_rows], r.osem.at[0])
    out_there = remote(r.st, r.act.at[own_rows], r.osem.at[1], r.osem.at[2], core_peer)
    out_arrival = remote(
        r.st, r.act.at[aligned(oth0, half)], r.osem.at[1], r.osem.at[2], core_peer
    )
    out_here.start()
    out_there.start()

    def add_rows(row, value):
        r.vg[row : row + 1, :] += jnp.sum(value, axis=0, keepdims=True)

    def norm_pull(g, hat, spread, gain):
        scaled = g * gain
        mean = jnp.mean(scaled, axis=1, keepdims=True)
        inner = jnp.mean(scaled * hat, axis=1, keepdims=True)
        return spread * (scaled - mean - hat * inner)

    def second_pull(layer, q, gradient):
        def one(i):
            at = aligned(q * ch + i * SUB, SUB)
            g = gradient(i, at)
            hat = r.xh2[layer, at, :]
            add_rows(6, g * hat)
            add_rows(7, g)
            back = norm_pull(g, hat, r.rs2[layer, at, :], r.vt[6:7, :])
            add_rows(3, back)
            r.gb[at, :] = back
            r.low2[aligned(own0 + q * ch + i * SUB, SUB), :] = back.astype(BF)

        loop(ch // SUB, one)

    def first_pull(layer, q, gradient):
        def one(i):
            at = aligned(q * ch + i * SUB, SUB)
            g = gradient(i, at)
            hat = r.xh1[layer, at, :]
            add_rows(4, g * hat)
            add_rows(5, g)
            back = norm_pull(g, hat, r.rs1[layer, at, :], r.vt[4:5, :])
            add_rows(2, back)
            r.gb[at, :] = back
            r.xl[aligned(own0 + q * ch + i * SUB, SUB), :] = back.astype(BF)

        loop(ch // SUB, one)

    def hot_rows(at_start):
        return r.oht[aligned(own0 + at_start, SUB), :]

    def bias_sums(row0):
        for kind, row in ((0, 0), (2, 1)):
            cols = aligned(m * hw, hw)
            r.vg[row : row + 1, cols] += jnp.sum(
                r.dp[kind, row0 : row0 + rows, :].astype(F32), axis=0, keepdims=True
            )

    for q in range(CHUNKS):
        second_pull(1, q, lambda i, at: nn(hot_rows(q * ch + i * SUB), r.mc[...]))
        share(4, r.low2, q).start()
    for q in range(CHUNKS):
        share_wait(4, r.low2, q)
    pick(r.low2c, 0, r.low2, 0, d_model)

    def slot_units(j):
        cols = aligned(j * TILE, TILE)
        back = nn(r.low2c[...], r.wn[:, cols]) * r.slc[:, cols].astype(F32)
        back = back.astype(BF)
        r.be[rows : rows + SLOTS, cols] = back
        r.vg[pl.ds(8 + m, 1), cols] += jnp.sum(back.astype(F32), axis=0, keepdims=True)

    loop(uw // TILE, slot_units)
    slot_own = core * slot_half
    slot_oth = slot_half - slot_own

    def slot_tile(cols):
        part = nt(r.be[rows : rows + SLOTS, :], r.we[cols, :])
        r.part[...] = part
        return jnp.concatenate(
            [
                r.part[aligned(slot_oth, slot_half), :],
                r.part[aligned(slot_own, slot_half), :],
            ],
            axis=0,
        )

    sum_begin(4, 0, slot_tile, slot_half)
    transpose_into(r.l2t, rows, r.low2c, 0, SLOTS)
    sum_end(4, 0, slot_half)
    mine_slots = r.slt.at[aligned(slot_own, slot_half)]
    mine_slots[...] = sum_rows(4, 0, slice(0, slot_half)).astype(BF)
    slots_out = remote(mine_slots, mine_slots, r.osem.at[3], r.osem.at[4], core_peer)
    slots_in_ref = r.slt.at[aligned(slot_oth, slot_half)]
    slots_in = remote(slots_in_ref, slots_in_ref, r.osem.at[3], r.osem.at[4], core_peer)
    slots_out.start()
    slots_in.wait_recv()
    for q in range(CHUNKS):
        first_pull(
            1, q, lambda i, at: r.gb[at, :] + nn(hot_rows(q * ch + i * SUB), r.slt[...])
        )
        share(5, r.xl, q).start()

    for q in range(CHUNKS):
        share_wait(5, r.xl, q)
    pick(r.low2c, 0, r.xl, 0, d_model)
    transpose_into(r.l1t, rows, r.low2c, 0, SLOTS)
    low_ctx = nn(r.low2c[...], r.wr[...]).astype(BF)
    across = low_transpose(low_ctx)
    dq_across = []
    for pair in range(heads // 2):
        lanes = slice(pair * LANES, (pair + 1) * LANES)
        dv = jnp.zeros((rows, LANES), F32)
        dk = jnp.zeros((rows, LANES), F32)
        for head in (2 * pair, 2 * pair + 1):
            where = slice(head * HEAD_DIM, (head + 1) * HEAD_DIM)
            at = (head % 2) * HEAD_DIM
            r.dozt[head, at : at + HEAD_DIM, 0:SLOTS] = across[where, :]
            low = r.pc[head]
            dv += nn(low, lane_half(low_ctx[:, lanes], head))
            dp = nn(r.vn[1, :, lanes], r.dozt[head, :, 0:SLOTS])
            delta = jnp.sum(
                across[where, :].astype(F32) * r.cct[where, :].astype(F32), axis=0, keepdims=True
            )
            ds = (low.astype(F32) * (dp - delta)).astype(BF)
            dk += nn(ds, r.qc[head])
            dq_across.append(nn(r.kt[1, where, :], ds) * 0.125)
        r.dp[1, rows : 2 * rows, lanes] = dk.astype(BF)
        r.dp[2, rows : 2 * rows, lanes] = dv.astype(BF)
    dq = low_transpose(jnp.concatenate(dq_across, axis=0))
    r.dp[0, rows : 2 * rows, :] = nn(r.oht[...], dq).astype(BF)
    bias_sums(rows)

    def layer_rows(k, q, row0):
        def tile_of(cols):
            total = None
            for kind in range(3):
                lhs = jnp.concatenate(
                    [
                        r.dp[kind, aligned(row0 + oth0 + q * ch, ch), :],
                        r.dp[kind, aligned(row0 + own0 + q * ch, ch), :],
                    ],
                    axis=0,
                )
                part = nt(lhs, r.wa[kind, cols, :])
                total = part if total is None else total + part
            return total

        sum_begin(k, q, tile_of, ch)

    for q in range(CHUNKS):
        layer_rows(5, q, rows)

    def weight_grad_rows(target, across, latter, width, row0, count):
        at = aligned(row0, count)

        def one(j):
            cols = aligned(j * TILE, TILE)
            target[at, cols] = nn(across[at, :], latter[:, cols]).astype(BF)

        loop(width // TILE, one)

    def weight_grad(target, across, latter, width):
        loop(
            d_model // TILE,
            lambda i: weight_grad_rows(target, across, latter, width, i * TILE, TILE),
        )

    def transpose_both(target, source, q):
        for row0 in (oth0 + q * ch, own0 + q * ch):
            target[:, aligned(row0, ch)] = low_transpose(source[aligned(row0, ch), :])

    for q in range(CHUNKS):
        sum_end(5, q, ch)
        second_pull(
            0, q, lambda i, at: r.gb[at, :] + sum_rows(5, q, aligned(i * SUB, SUB))
        )
        share(6, r.low2, q).start()
        share_wait(6, r.low2, q)
        transpose_both(r.l2t, r.low2, q)
        if q == CHUNKS - 1:
            if by_columns:

                def first_rows(turn):
                    step = scatter_order(turn)
                    owner = ((z + step) % lines) * 2 + 1 - y
                    weight_grad_rows(r.gsn, r.l2t, r.act0, uw, owner * vr, vr)
                    scatter_y(NAR, step).start()

                each(1, lines + 1, first_rows)
            else:
                weight_grad(r.gsn, r.l2t, r.act0, uw)
                scatter_start(NAR)

        def units(j, q=q):
            cols = aligned(j * TILE, TILE)
            slope = both(r.slope0, q, cols).astype(F32)
            back = (nn(both(r.low2, q), r.wn[:, cols]) * slope).astype(BF)
            put_both(r.be, q, cols, back)
            r.vg[pl.ds(8 + m, 1), cols] += jnp.sum(back.astype(F32), axis=0, keepdims=True)

        loop(uw // TILE, units)
        sum_begin(6, q, lambda cols, q=q: nt(both(r.be, q), r.we[cols, :]), ch)

    if by_columns:
        each(
            0,
            lines,
            lambda s: weight_grad_rows(
                r.gsn, r.l2t, r.act0, uw, (((z + s) % lines) * 2 + y) * vr, vr
            ),
        )
    weight_grad(r.gse, r.nt, r.be, uw)
    scatter_start(EXP)
    passes = [lambda s=s: scatter_pass(NAR, s) for s in range(1, lines)]
    passes += [lambda s=s: scatter_pass(EXP, s) for s in range(1, lines)]

    def pump(count=1):
        for _ in range(min(count, len(passes))):
            passes.pop(0)()

    pump()
    for q in range(CHUNKS):
        sum_end(6, q, ch)
        first_pull(
            0, q, lambda i, at: r.gb[at, :] + sum_rows(6, q, aligned(i * SUB, SUB))
        )
        share(7, r.xl, q).start()
    pump()
    for q in range(CHUNKS):
        share_wait(7, r.xl, q)
        back = nn(both(r.xl, q), r.wr[...]).astype(BF)
        put_heads(r.doz, q, back)
        put_heads_across(r.dozt, q, low_transpose(back))

    def head_pair(pair):
        lanes = aligned(pair * LANES, LANES)
        dv = jnp.zeros((rows, LANES), F32)
        dk = jnp.zeros((rows, LANES), F32)
        for side in range(2):
            head = 2 * pair + side
            where = aligned(head * HEAD_DIM, HEAD_DIM)
            for part in range(rows // TILE):
                some = slice(part * TILE, (part + 1) * TILE)
                low = r.p0[head, :, some]
                dv += nn(low, r.doz[head, some, :])
                inner = r.dozt[head, side * HEAD_DIM : (side + 1) * HEAD_DIM, some]
                delta = jnp.sum(
                    inner.astype(F32) * r.ct[0, where, some].astype(F32), axis=0, keepdims=True
                )
                dp = nn(r.vn[0, :, lanes], r.dozt[head, :, some])
                ds = (low.astype(F32) * (dp - delta)).astype(BF)
                dk += nn(ds, r.qz[0, head, some, :])
                r.dqt[where, some] = (nn(r.kt[0, where, :], ds) * 0.125).astype(BF)
        r.dp[1, 0:rows, lanes] = dk.astype(BF)
        r.dp[2, 0:rows, lanes] = dv.astype(BF)

    loop(heads // 2, head_pair)
    for i in range(rows // LANES):
        some = slice(i * LANES, (i + 1) * LANES)
        r.dp[0, some, :] = low_transpose(r.dqt[:, some])
    for q in range(CHUNKS):
        layer_rows(7, q, 0)
    pump()
    bias_sums(0)
    transpose_into(r.l1t, 0, r.xl, 0, rows)
    weight_grad(r.gsr, r.l1t, r.ctx, hw)
    scatter_start(REJ)
    first_of_x = jnp.where(m < 2, 1.0, 0.0)
    r.vg[2:8, :] = r.vg[2:8, :] * first_of_x
    for j in range(d_model // LANES):
        tall = jnp.concatenate(
            [r.vg[:, j * LANES : (j + 1) * LANES], jnp.zeros((LANES - 16, LANES), F32)], axis=0
        )
        r.gsv[j * LANES : (j + 1) * LANES, :] = jnp.transpose(tall, (1, 0)).astype(BF)
    scatter_start(VEC)
    for kind in range(3):
        weight_grad(r.gsa.at[kind], r.xt, r.dp.at[kind], hw)
    scatter_start(ATT)
    pump()
    out_here.wait()
    out_there.wait_send()
    for q in range(CHUNKS):
        sum_end(7, q, ch)

        def last(i, q=q):
            at = aligned(q * ch + i * SUB, SUB)
            g = r.gb[at, :] + sum_rows(7, q, aligned(i * SUB, SUB))
            r.st[at, :] = g * r.keep[aligned(own0 + q * ch + i * SUB, SUB), :]

        loop(ch // SUB, last)
    in_here = pltpu.make_async_copy(r.st, r.ing.at[own_rows], r.osem.at[5])
    in_there = remote(r.st, r.ing.at[own_rows], r.osem.at[6], r.osem.at[7], core_peer)
    in_arrival = remote(r.st, r.ing.at[aligned(oth0, half)], r.osem.at[6], r.osem.at[7], core_peer)
    in_here.start()
    in_there.start()

    pump()
    scatter_turn(REJ)
    scatter_turn(VEC)
    pump(len(passes))
    for turn in range(1, lines):
        scatter_pass(ATT, turn)

    def squares(value):
        value = value * value
        if value.ndim == 3:
            value = jnp.sum(value, axis=0)
        value = jnp.sum(value, axis=0, keepdims=True)
        return jnp.sum(value, axis=1, keepdims=True)

    scatter_finish(NAR, r.gn)
    scatter_finish(EXP, r.ge)
    scatter_finish(REJ, r.gr)
    total = squares(r.gn[...]) + squares(r.ge[...]) + squares(r.gr[...])
    scatter_finish(VEC, r.vf.at[0])
    swap_v = remote(r.vf.at[0], r.vf.at[1], r.vxs.at[2], r.vxr.at[2], core_peer)
    swap_v.start()
    swap_v.wait_recv()
    r.vf[2] = r.vf[0] + r.vf[1]
    swap_w = remote(r.vf.at[2], r.vf.at[3], r.vxs.at[3], r.vxr.at[3], x_peer)
    swap_w.start()
    swap_w.wait_recv()
    r.vs[...] = jnp.transpose(r.vf[2] + r.vf[3], (1, 0))
    r.gv[...] = r.vs[pl.ds(columns * m, columns), :]
    total = total + squares(r.gv[...])
    scatter_finish(ATT, r.ga)
    total = total + squares(r.ga[...])

    r.nm[m] = jnp.broadcast_to(total, (8, LANES))

    def model_copy(k, slot):
        return remote(r.nm.at[slot], r.nm.at[slot], r.nms.at[k], r.nmr.at[k], model_peers[k])

    for k in range(3):
        model_copy(k, m).start()
    for k in range(3):
        model_copy(k, model_peers[k][1]).wait_recv()
    r.nz[d] = jnp.sum(r.nm[...], axis=0)

    def line_copy(step, slot):
        here = r.nz.at[slot]
        return remote(here, here, r.nzs.at[0, step], r.nzr.at[0, step], z_peer(step))

    def cross_copy(step, slot):
        here = r.nz.at[slot]
        return remote(here, here, r.nzs.at[1, step], r.nzr.at[1, step], zy_peer(step))

    each(0, lines, lambda s: cross_copy(s, d).start())
    each(1, lines, lambda s: line_copy(s, d).start())
    each(0, lines, lambda s: cross_copy(s, z_from(s) + 1 - 2 * y).wait_recv())
    each(1, lines, lambda s: line_copy(s, z_from(s)).wait_recv())
    r.norm[...] = jnp.sqrt(jnp.sum(r.nz[...], axis=0))

    each(0, lines, lambda s: cross_copy(s, d).wait_send())
    each(1, lines, lambda s: line_copy(s, d).wait_send())
    for k in range(3):
        model_copy(k, m).wait_send()
    swap.wait_send()
    swap_x.wait_send()
    swap_v.wait_send()
    swap_w.wait_send()
    slots_out.wait_send()
    for region in range(5):
        gather_close(region)
        scatter_close(region)
    out_arrival.wait_recv()
    in_here.wait()
    in_there.wait_send()
    in_arrival.wait_recv()


def run_layers(
    n, tok, pos, cho, table, mcot, attend, rejoin, expand, narrow, vin
):
    rows, d_model = tok.shape
    vr = rejoin.shape[0]
    hw = rejoin.shape[1]
    uw = expand.shape[1]
    lines = n // 2
    half = rows // 2
    ch = half // CHUNKS
    heads = hw // HEAD_DIM
    wide = rows + SLOTS
    inputs = [
        ("tok", tok),
        ("pos", pos),
        ("cho", cho),
        ("table", table),
        ("mcot", mcot),
        ("attend", attend),
        ("rejoin", rejoin),
        ("expand", expand),
        ("narrow", narrow),
        ("vin", vin),
    ]
    outputs = [
        ("act", (rows, d_model), pl.ANY),
        ("ing", (rows, d_model), pl.ANY),
        ("ga", (3, vr, hw), pltpu.VMEM),
        ("gr", (vr, hw), pltpu.VMEM),
        ("ge", (vr, uw), pltpu.VMEM),
        ("gn", (vr, uw), pltpu.VMEM),
        ("gv", vin.shape, pltpu.VMEM),
        ("norm", (8, LANES), pltpu.VMEM),
    ]
    low = [
        ("wv", (d_model, LANES)),
        ("wa", (3, d_model, hw)),
        ("wr", (d_model, hw)),
        ("we", (d_model, uw)),
        ("wn", (d_model, uw)),
        ("gsv", (d_model, LANES)),
        ("gsa", (3, d_model, hw)),
        ("gsr", (d_model, hw)),
        ("gse", (d_model, uw)),
        ("gsn", (d_model, uw)),
        ("yv", (lines, vr, LANES)),
        ("ya", (lines, 3, vr, hw)),
        ("yr", (lines, vr, hw)),
        ("ye", (lines, vr, uw)),
        ("yn", (lines, vr, uw)),
        ("zv", (lines, vr, LANES)),
        ("za", (lines, 3, vr, hw)),
        ("zr", (lines, vr, hw)),
        ("ze", (lines, vr, uw)),
        ("zn", (lines, vr, uw)),
        ("cs", (2, CHUNKS, ch, d_model)),
        ("cr", (2, CHUNKS, ch, d_model)),
        ("xs", (2, CHUNKS, ch, d_model)),
        ("xr", (2, CHUNKS, ch, d_model)),
        ("vb", (4, vr, LANES)),
        ("oh", (SLOTS, rows)),
        ("oht", (rows, SLOTS)),
        ("mc", (SLOTS, d_model)),
        ("xl", (rows, d_model)),
        ("normed", (rows, d_model)),
        ("low2", (rows, d_model)),
        ("xt", (d_model, 2 * rows)),
        ("nt", (d_model, wide)),
        ("l2t", (d_model, wide)),
        ("l1t", (d_model, wide)),
        ("act0", (wide, uw)),
        ("slope0", (rows, uw)),
        ("be", (wide, uw)),
        ("ctx", (wide, hw)),
        ("ctx1", (rows, hw)),
        ("dp", (3, 2 * rows, hw)),
        ("qz", (2, heads, rows, LANES)),
        ("qzt", (2, heads, LANES, rows)),
        ("kn", (2, rows, hw)),
        ("kt", (2, hw, rows)),
        ("vn", (2, rows, hw)),
        ("vvt", (hw, rows)),
        ("ct", (2, hw, rows)),
        ("p0", (heads, rows, rows)),
        ("dqt", (hw, rows)),
        ("slc", (SLOTS, uw)),
        ("low2c", (SLOTS, d_model)),
        ("slt", (SLOTS, d_model)),
        ("qc", (heads, SLOTS, LANES)),
        ("pc", (heads, rows, SLOTS)),
        ("cct", (hw, SLOTS)),
    ]
    full = [
        ("vt", (16, d_model)),
        ("vg", (16, d_model)),
        ("keep", (rows, 1)),
        ("st", (half, d_model)),
        ("gb", (half, d_model)),
        ("xh1", (2, half, d_model)),
        ("xh2", (2, half, d_model)),
        ("rs1", (2, half, 1)),
        ("rs2", (2, half, 1)),
        ("acc", (ch, d_model)),
        ("part", (SLOTS, TILE)),
        ("vf", (4, vr, LANES)),
        ("vs", (LANES, vr)),
        ("nm", (4, 8, LANES)),
        ("nz", (n, 8, LANES)),
    ]
    sems = [
        ("agzs", (5, lines + 1)),
        ("agzr", (5, lines)),
        ("agys", (5, lines)),
        ("agyr", (5, lines)),
        ("rsys", (5, lines)),
        ("rsyr", (5, lines)),
        ("rszs", (5, lines)),
        ("rszr", (5, lines)),
        ("arcs", (8, CHUNKS)),
        ("arcr", (8, CHUNKS)),
        ("arxs", (8, CHUNKS)),
        ("arxr", (8, CHUNKS)),
        ("shs", (8, CHUNKS)),
        ("shr", (8, CHUNKS)),
        ("vxs", (4,)),
        ("vxr", (4,)),
        ("osem", (8,)),
        ("nms", (3,)),
        ("nmr", (3,)),
        ("nzs", (2, lines)),
        ("nzr", (2, lines)),
        ("ccs", (lines,)),
        ("ccr", (lines,)),
        ("cxs", (lines,)),
        ("cxr", (lines,)),
    ]
    names = (
        [name for name, _ in inputs]
        + [name for name, _, _ in outputs]
        + [name for name, _ in low]
        + [name for name, _ in full]
        + ["pb"]
        + [name for name, _ in sems]
    )
    sizes = (n, d_model, rows, hw, uw, vr)

    def body(*refs):
        layer_kernel(names, sizes, *refs)

    return pl.pallas_call(
        body,
        out_shape=[jax.ShapeDtypeStruct(shape, F32) for _, shape, _ in outputs],
        in_specs=[pl.BlockSpec(memory_space=pltpu.VMEM)] * len(inputs),
        out_specs=[pl.BlockSpec(memory_space=space) for _, _, space in outputs],
        scratch_shapes=[pltpu.VMEM(shape, BF) for _, shape in low]
        + [pltpu.VMEM(shape, F32) for _, shape in full]
        + [pltpu.VMEM((16, LANES), jnp.int32)]
        + [pltpu.SemaphoreType.DMA(shape) for _, shape in sems],
        compiler_params=pltpu.CompilerParams(
            collective_id=0, has_side_effects=True, vmem_limit_bytes=61 * 1024 * 1024
        ),
        cost_estimate=pl.CostEstimate(
            flops=20_000_000_000, bytes_accessed=20_000_000, transcendentals=4_000_000
        ),
    )(*[value for _, value in inputs])


def apply_update(weight, first_moment, second_moment, shadow, gradient, step_rate):
    momentum = 0.5 * first_moment + 0.5 * gradient
    variance = 0.5 * second_moment + 0.5 * gradient * gradient
    bias_fix = 1.0 - 0.5**STEP
    updated = weight - step_rate * (
        momentum / bias_fix / (jnp.sqrt(variance / bias_fix) + 1e-08) + 0.01 * weight
    )
    average = 0.999 * shadow + 0.001 * updated
    return (updated, momentum, variance, average, updated.astype(BF))


def update_kernel(rates, clip_limit, norm, act, ing, *refs):
    *refs, norm_out, act_out, ing_out = refs
    act_out[...] = act[...]
    ing_out[...] = ing[...]
    norm_out[...] = norm[0:1, 0:1]
    factor = jnp.minimum(1.0, clip_limit / (norm[0:1, 0:1] + 1e-06))
    ins, outs = refs[: 5 * len(rates)], refs[5 * len(rates) :]
    for index, rate in enumerate(rates):
        weight, first, second, shadow, gradient = ins[5 * index : 5 * index + 5]
        targets = outs[5 * index : 5 * index + 5]
        for part in range(weight.shape[0]) if len(weight.shape) == 3 else (slice(None),):
            results = apply_update(
                weight[part],
                first[part],
                second[part],
                shadow[part],
                gradient[part] * factor,
                rate,
            )
            for target, value in zip(targets, results, strict=True):
                target[part] = value


def run_update(groups, rates, norm, clip_limit, act, ing):
    vr = groups[1][0].shape[0]
    step = min(vr, 32)

    def spec(shape, whole):
        if whole:
            return pl.BlockSpec(shape, lambda i: (0, 0))
        if len(shape) == 3:
            return pl.BlockSpec((shape[0], step, shape[2]), lambda i: (0, i, 0))
        return pl.BlockSpec((step, shape[1]), lambda i: (i, 0))

    last = len(groups) - 1
    passed = pl.BlockSpec((act.shape[0] * step // vr, act.shape[1]), lambda i: (i, 0))
    specs = [spec(group[0].shape, k == last) for k, group in enumerate(groups)]

    def body(*refs):
        update_kernel(rates, clip_limit, *refs)

    flat = [value for group in groups for value in group]
    size = sum(value.size for value in flat) * 4
    outs = pl.pallas_call(
        body,
        grid=(vr // step,),
        in_specs=[spec(norm.shape, True)]
        + [passed] * 2
        + [one for one in specs for _ in range(5)],
        out_specs=[one for one in specs for _ in range(5)]
        + [spec((1, 1), True)]
        + [passed] * 2,
        out_shape=[
            jax.ShapeDtypeStruct(group[0].shape, kind)
            for group in groups
            for kind in (F32, F32, F32, F32, BF)
        ]
        + [jax.ShapeDtypeStruct(shape, F32) for shape in ((1, 1), act.shape, ing.shape)],
        compiler_params=pltpu.CompilerParams(vmem_limit_bytes=60 * 1024 * 1024),
        cost_estimate=pl.CostEstimate(flops=size, bytes_accessed=2 * size, transcendentals=0),
    )(norm, act, ing, *flat)
    groups_out = [outs[5 * k : 5 * k + 5] for k in range(len(groups))]
    return groups_out, outs[-3].reshape(()), *outs[-2:]


def per_device(
    tokens_in,
    masked_positions,
    replace_choice,
    replace_table,
    masked_cotangent,
    attend,
    attend_mean,
    attend_square,
    attend_shadow,
    rejoin,
    rejoin_mean,
    rejoin_square,
    rejoin_shadow,
    expand,
    expand_mean,
    expand_square,
    expand_shadow,
    narrow,
    narrow_mean,
    narrow_square,
    narrow_shadow,
    vectors,
    vectors_mean,
    vectors_square,
    vectors_shadow,
):
    n = lax.axis_size("dp")
    act, ing, ga, gr, ge, gn, gv, norm = run_layers(
        n,
        tokens_in,
        masked_positions,
        replace_choice,
        replace_table,
        masked_cotangent,
        attend.transpose(1, 0, 2),
        rejoin,
        expand,
        narrow,
        vectors.T,
    )
    d_model = tokens_in.shape[1]
    param_count = 4 * d_model * d_model + 2 * d_model * expand.shape[1] * 4 + 12 * d_model
    clip_limit = 0.001 * math.sqrt(param_count * tokens_in.shape[0] * n)
    cubes = [x.transpose(1, 0, 2) for x in (attend, attend_mean, attend_square, attend_shadow)]
    rows_of = [x.T for x in (vectors, vectors_mean, vectors_square, vectors_shadow)]
    new, gradient_norm, act, ing = run_update(
        (
            (*cubes, ga),
            (rejoin, rejoin_mean, rejoin_square, rejoin_shadow, gr),
            (expand, expand_mean, expand_square, expand_shadow, ge),
            (narrow, narrow_mean, narrow_square, narrow_shadow, gn),
            (*rows_of, gv),
        ),
        (0.04, 0.16, 0.04, 0.04, 0.5),
        norm,
        clip_limit,
        act,
        ing,
    )
    results = [act, ing, gradient_norm]
    results.extend(x.transpose(1, 0, 2) for x in new[0])
    for group in new[1:4]:
        results.extend(group)
    results.extend(x.T for x in new[4])
    return tuple(results)


def solution(mesh):
    row = P("dp", None)
    cube = P("dp", None, "mp")
    flat = P("dp", "mp")
    return jax.shard_map(
        per_device,
        mesh=mesh,
        in_specs=(row, row, row, P(), P("dp", None, None)) + (cube,) * 4 + (flat,) * 16,
        out_specs=(row, row, P()) + (cube,) * 5 + (flat,) * 20,
        check_vma=False,
    )
```

```python
import math
from types import SimpleNamespace

import jax
import jax.numpy as jnp
from jax import lax
from jax.experimental import pallas as pl
from jax.experimental.pallas import tpu as pltpu
from jax.sharding import PartitionSpec as P

HEAD_DIM = 64
SEQ_LEN = 512
DEPTH = 2
STEP = 7
EPS = 1e-05
BF = jnp.bfloat16
F32 = jnp.float32
MESH = pl.DeviceIdType.MESH
LANES = 128
TILE = 256
SLOTS = 128
CHUNKS = 2
SUB = 64
VEC, ATT, REJ, EXP, NAR = range(5)
GELU_A = 0.7978845608028654
GELU_B = 0.044715


def nn(former, latter):
    return jnp.dot(former, latter, preferred_element_type=F32)


def nt(former, latter):
    return lax.dot_general(former, latter, (((1,), (1,)), ((), ())), preferred_element_type=F32)


def low_transpose(block):
    return jnp.transpose(block.astype(F32), (1, 0)).astype(BF)


def loop(count, body):
    def step(index, carry):
        body(index)
        return carry

    lax.fori_loop(0, count, step, 0)


def each(first, last, body):
    if last - first <= 8:
        for index in range(first, last):
            body(index)
    else:

        def step(index, carry):
            body(index)
            return carry

        lax.fori_loop(first, last, step, 0)


def aligned(index, size):
    return pl.ds(pl.multiple_of(index, size), size)


def layer_kernel(names, sizes, *refs):
    r = SimpleNamespace(**dict(zip(names, refs, strict=True)))
    n, d_model, rows, hw, uw, vr = sizes
    r.doz, r.dozt = r.qz.at[1], r.qzt.at[1]
    half = rows // 2
    ch = half // CHUNKS
    lines = n // 2
    heads = hw // HEAD_DIM
    slot_half = SLOTS // 2

    d = lax.axis_index("dp")
    m = lax.axis_index("mp")
    z, y = d // 2, d % 2
    core = m % 2
    core_peer = (d, m + 1 - 2 * core)
    x_peer = (d, (m + 2) % 4)
    y_peer = (d + 1 - 2 * y, m)
    model_peers = (core_peer, x_peer, (d, 3 - m))
    own0 = core * half
    oth0 = half - own0

    weights = (r.wv, r.wa, r.wr, r.we, r.wn)
    grads = (r.gsv, r.gsa, r.gsr, r.gse, r.gsn)
    from_y = (r.yv, r.ya, r.yr, r.ye, r.yn)
    from_z = (r.zv, r.za, r.zr, r.ze, r.zn)

    def z_peer(step):
        return (((z + step) % lines) * 2 + y, m)

    def zy_peer(step):
        return (((z + step) % lines) * 2 + 1 - y, m)

    def z_from(step):
        return ((z + lines - step) % lines) * 2 + y

    def block(ref, region, index):
        where = aligned(index * vr, vr)
        return ref.at[:, where, :] if region == ATT else ref.at[where, :]

    def remote(source, target, send, recv, device):
        return pltpu.make_async_remote_copy(
            src_ref=source,
            dst_ref=target,
            send_sem=send,
            recv_sem=recv,
            device_id=device,
            device_id_type=MESH,
        )

    barrier = pltpu.get_barrier_semaphore()

    def greet(peer):
        pl.semaphore_signal(barrier, inc=1, device_id=peer, device_id_type=MESH)

    for peer in model_peers:
        greet(peer)
    each(1, lines, lambda s: greet(z_peer(s)))
    each(0, lines, lambda s: greet(zy_peer(s)))
    pl.semaphore_wait(barrier, len(model_peers) + n - 1)

    relay = lines == 4
    last_line = lines - 1
    inner = jnp.logical_and(z > 0, z < last_line)
    far_end = (jnp.where(z == 1, 0, last_line) * 2 + y, m)
    near_mid = (jnp.where(z == 0, 1, last_line - 1) * 2 + y, m)

    def gather_z(region, step):
        piece = block(weights[region], region, d)
        return remote(
            piece, piece, r.agzs.at[region, step], r.agzr.at[region, step], z_peer(step)
        )

    def gather_z_arrival(region, step):
        piece = block(weights[region], region, z_from(step))
        return remote(
            piece, piece, r.agzs.at[region, step], r.agzr.at[region, step], z_peer(step)
        )

    def gather_onward(region, turn):
        piece = block(weights[region], region, z_from(gather_order(turn)))
        if turn == 3:
            target = far_end
            arrives_as = jnp.where(z == 1, 1, last_line)
        else:
            target = ((z + 3 - 2 * turn) * 2 + y, m)
            arrives_as = 2
        return remote(
            piece,
            piece,
            r.agzs.at[region, last_line + turn],
            r.agzr.at[region, arrives_as],
            target,
        )

    def gather_y(region, step):
        piece = block(weights[region], region, z_from(step))
        return remote(piece, piece, r.agys.at[region, step], r.agyr.at[region, step], y_peer)

    def gather_y_arrival(region, step):
        piece = block(weights[region], region, z_from(step) + 1 - 2 * y)
        return remote(piece, piece, r.agys.at[region, step], r.agyr.at[region, step], y_peer)

    def near(step, body):
        if not relay:
            body()
        elif step != 2:
            pl.when(z < last_line if step == 1 else z > 0)(body)

    def gather_start_z(region):
        for step in range(1, lines):
            near(step, lambda: gather_z(region, step).start())

    def gather_start_y(region):
        gather_y(region, 0).start()

    def gather_order(turn):
        if not relay or turn == 0:
            return turn
        if turn == 1:
            return jnp.where(z == 0, last_line, 1)
        if turn == 2:
            return jnp.where(inner, last_line, 2)
        return jnp.where(inner, 2, jnp.where(z == 0, 1, last_line))

    def gather_pass(region, turn):
        step = gather_order(turn)
        gather_z_arrival(region, step).wait_recv()
        if relay:
            pl.when(inner)(lambda: gather_onward(region, turn).start())
        gather_y(region, step).start()

    def gather_wait(region):
        each(0, lines, lambda s: gather_y_arrival(region, s).wait_recv())

    def gather_close(region):
        for step in range(1, lines):
            near(step, lambda: gather_z(region, step).wait_send())
        if relay:
            for turn in range(1, lines):
                pl.when(inner)(lambda: gather_onward(region, turn).wait_send())
        each(0, lines, lambda s: gather_y(region, s).wait_send())

    def scatter_y(region, step):
        owner = ((z + step) % lines) * 2 + 1 - y
        return remote(
            block(grads[region], region, owner),
            from_y[region].at[step],
            r.rsys.at[region, step],
            r.rsyr.at[region, step],
            y_peer,
        )

    def scatter_z(region, step):
        owner = ((z + step) % lines) * 2 + y
        return remote(
            block(grads[region], region, owner),
            from_z[region].at[step],
            r.rszs.at[region, step],
            r.rszr.at[region, step],
            z_peer(step),
        )

    def scatter_far(region, step):
        owner = ((z + step) % lines) * 2 + y
        return remote(
            block(grads[region], region, owner),
            from_z[region].at[0],
            r.rszs.at[region, step],
            r.rszr.at[region, 0],
            near_mid,
        )

    def scatter_order(turn):
        if not relay:
            return turn % lines
        if turn == 1:
            return jnp.where(z == 0, last_line, 1)
        if turn == 2:
            return jnp.where(z == 0, 1, last_line)
        return 2 if turn == 3 else 0

    def scatter_start(region):
        ready.append(region)
        scatter_next()

    ready = []
    order = (NAR, EXP, REJ, VEC, ATT)
    queue = [(region, turn) for region in order for turn in range(1, lines + 1)]
    under_way = []
    weight_of = {NAR: 4, EXP: 4, ATT: 3, REJ: 1, VEC: 1}

    def scatter_next():
        while queue and queue[0][0] in ready:
            if sum(weight_of[region] for region, _ in under_way) > 4:
                break
            region, turn = queue.pop(0)
            scatter_y(region, scatter_order(turn)).start()
            under_way.append((region, turn))

    def scatter_pass():
        region, turn = under_way[0]
        step = scatter_order(turn)
        scatter_y(region, step).wait_recv()
        under_way.pop(0)
        scatter_next()
        if turn == lines:
            return
        piece = block(grads[region], region, ((z + step) % lines) * 2 + y)
        total = piece[...].astype(F32) + from_y[region][step].astype(F32)
        piece[...] = total.astype(BF)
        if not relay:
            scatter_z(region, step).start()
        elif turn == 1:
            pl.when(inner)(lambda: scatter_z(region, step).start())
            pl.when(jnp.logical_not(inner))(lambda: scatter_far(region, step).start())
        elif turn == 2:
            scatter_z(region, step).start()
        else:

            @pl.when(inner)
            def _():
                scatter_far(region, 0).wait_recv()
                piece[...] = (total + from_z[region][0].astype(F32)).astype(BF)

            scatter_z(region, step).start()

    def scatter_finish(region, out_ref):
        def one(step):
            scatter_z(region, step).wait_recv()
            out_ref[...] += from_z[region][step].astype(F32)

        piece = block(grads[region], region, d)
        out_ref[...] = piece[...].astype(F32) + from_y[region][0].astype(F32)
        for step in range(1, lines):
            if not relay or step == 2:
                one(step)
            else:
                pl.when(z > 0 if step == 1 else z < last_line)(lambda: one(step))

    def scatter_close(region):
        each(0, lines, lambda s: scatter_y(region, s).wait_send())
        each(1, lines, lambda s: scatter_z(region, s).wait_send())

    def core_copy(k, q, count):
        b = k % 2
        return remote(
            r.cs.at[b, q, :count],
            r.cr.at[b, q, :count],
            r.arcs.at[k, q],
            r.arcr.at[k, q],
            core_peer,
        )

    def x_copy(k, q, count):
        b = k % 2
        return remote(
            r.xs.at[b, q, :count],
            r.xr.at[b, q, :count],
            r.arxs.at[k, q],
            r.arxr.at[k, q],
            x_peer,
        )

    def sum_begin(k, q, tile_of, count):
        b = k % 2

        def one(j):
            cols = aligned(j * TILE, TILE)
            part = tile_of(cols)
            r.cs[b, q, :count, cols] = part[:count].astype(BF)
            r.acc[:count, cols] = part[count:]

        loop(d_model // TILE, one)
        copy = core_copy(k, q, count)
        copy.start()
        copy.wait_recv()
        r.xs[b, q, :count] = (r.acc[:count] + r.cr[b, q, :count].astype(F32)).astype(BF)
        x_copy(k, q, count).start()

    def sum_end(k, q, count):
        x_copy(k, q, count).wait()
        core_copy(k, q, count).wait_send()

    def sum_rows(k, q, where):
        b = k % 2
        return r.xs[b, q, where].astype(F32) + r.xr[b, q, where].astype(F32)

    def share(k, ref, q):
        where = aligned(own0 + q * ch, ch)
        return remote(ref.at[where], ref.at[where], r.shs.at[k, q], r.shr.at[k, q], core_peer)

    def share_arrival(k, ref, q):
        where = aligned(oth0 + q * ch, ch)
        return remote(ref.at[where], ref.at[where], r.shs.at[k, q], r.shr.at[k, q], core_peer)

    def share_wait(k, ref, q):
        share(k, ref, q).wait_send()
        share_arrival(k, ref, q).wait_recv()

    def both(ref, q, cols=slice(None)):
        return jnp.concatenate(
            [ref[aligned(oth0 + q * ch, ch), cols], ref[aligned(own0 + q * ch, ch), cols]],
            axis=0,
        )

    def put_both(ref, q, cols, value):
        ref[aligned(oth0 + q * ch, ch), cols] = value[:ch]
        ref[aligned(own0 + q * ch, ch), cols] = value[ch:]

    columns = r.vin.shape[0]
    r.vs[...] = jnp.zeros(r.vs.shape, F32)
    r.vs[pl.ds(columns * m, columns), :] = r.vin[...]
    r.vb[0] = low_transpose(r.vs[...])
    swap = remote(r.vb.at[0], r.vb.at[1], r.vxs.at[0], r.vxr.at[0], core_peer)
    swap.start()
    mine = aligned(d * vr, vr)
    r.wa[:, mine, :] = r.attend[...].astype(BF)
    gather_start_y(ATT)
    gather_start_z(ATT)
    r.wr[mine, :] = r.rejoin[...].astype(BF)
    gather_start_y(REJ)
    swap.wait_recv()
    r.vb[2] = r.vb[0] + r.vb[1]
    swap_x = remote(r.vb.at[2], r.vb.at[3], r.vxs.at[1], r.vxr.at[1], x_peer)
    swap_x.start()
    r.we[mine, :] = r.expand[...].astype(BF)
    r.wn[mine, :] = r.narrow[...].astype(BF)
    swap_x.wait_recv()
    r.wv[mine, :] = r.vb[2] + r.vb[3]
    gather_start_y(VEC)

    r.pb[...] = jnp.full(r.pb.shape, SEQ_LEN, jnp.int32)
    slots = r.pos.shape[1]
    r.pb[0:1, 0:slots] = r.pos[...]
    r.pb[8:9, 0:slots] = r.cho[...]
    pos_row = jnp.broadcast_to(r.pb[0:1, :], (SLOTS, SLOTS))
    cho_row = jnp.broadcast_to(r.pb[8:9, :], (SLOTS, SLOTS))
    pos_col = jnp.transpose(pos_row.astype(F32), (1, 0)).astype(jnp.int32)
    cho_col = jnp.transpose(cho_row.astype(F32), (1, 0)).astype(jnp.int32)
    lane_iota = lax.broadcasted_iota(jnp.int32, (SLOTS, LANES), 1)
    row_iota = lax.broadcasted_iota(jnp.int32, (SLOTS, LANES), 0)
    for j in range(rows // LANES):
        r.oh[:, j * LANES : (j + 1) * LANES] = jnp.where(
            pos_col == lane_iota + j * LANES, 1.0, 0.0
        ).astype(BF)
        r.oht[j * LANES : (j + 1) * LANES, :] = jnp.where(
            pos_row == row_iota + j * LANES, 1.0, 0.0
        ).astype(BF)
    r.low2c[...] = jnp.zeros(r.low2c.shape, BF)
    r.low2c[0 : r.table.shape[0], :] = r.table[...]
    choice = jnp.where(cho_col == lane_iota, 1.0, 0.0).astype(BF)
    for j in range(d_model // TILE):
        r.slt[:, j * TILE : (j + 1) * TILE] = nn(
            choice, r.low2c[:, j * TILE : (j + 1) * TILE]
        ).astype(BF)
    r.mc[...] = jnp.zeros(r.mc.shape, BF)
    r.mc[0:slots, :] = r.mcot[...].reshape(slots, d_model)
    r.vg[...] = jnp.zeros(r.vg.shape, F32)

    gather_pass(ATT, 1)
    gather_start_y(EXP)

    def embed(i):
        where = aligned(i * SUB, SUB)
        hot = r.oht[where, :]
        keep = 1.0 - jnp.sum(hot.astype(F32), axis=1, keepdims=True)
        r.keep[where, :] = keep
        r.xl[where, :] = (r.tok[where, :].astype(F32) * keep + nn(hot, r.slt[...])).astype(BF)

    loop(rows // SUB, embed)
    r.st[...] = r.xl[aligned(own0, half), :].astype(F32)

    def transpose_into(target, lane0, source, row0, count):
        for i in range(count // LANES):
            target[:, lane0 + i * LANES : lane0 + (i + 1) * LANES] = low_transpose(
                source[row0 + i * LANES : row0 + (i + 1) * LANES, :]
            )

    for turn in range(2, lines - 1):
        gather_pass(ATT, turn)
    gather_start_z(VEC)
    gather_start_z(REJ)
    gather_pass(ATT, lines - 1)
    gather_start_z(EXP)
    for turn in range(1, lines):
        gather_pass(VEC, turn)
    for turn in range(1, lines):
        gather_pass(REJ, turn)
    gather_wait(VEC)
    gather_pass(EXP, 1)
    gather_wait(ATT)
    gather_start_y(NAR)
    gather_pass(EXP, 2)
    for j in range(d_model // LANES):
        r.vt[:, j * LANES : (j + 1) * LANES] = jnp.transpose(
            r.wv[j * LANES : (j + 1) * LANES, :].astype(F32), (1, 0)
        )[0:16, :]

    def head_bias(row):
        return r.vt[row : row + 1, aligned(m * hw, hw)]

    half_mask = lax.broadcasted_iota(jnp.int32, (1, LANES), 1) < HEAD_DIM

    def lane_half(value, head):
        return jnp.where(half_mask if head % 2 == 0 else jnp.logical_not(half_mask), value, 0)

    def put_heads(ref, q, value):
        for head in range(heads):
            pair = (head // 2) * LANES
            piece = lane_half(value[:, pair : pair + LANES], head)
            ref[head, aligned(oth0 + q * ch, ch), :] = piece[:ch]
            ref[head, aligned(own0 + q * ch, ch), :] = piece[ch:]

    def put_heads_across(ref, q, across):
        for head in range(heads):
            at = (head % 2) * HEAD_DIM
            piece = across[head * HEAD_DIM : (head + 1) * HEAD_DIM, :]
            ref[head, at : at + HEAD_DIM, aligned(oth0 + q * ch, ch)] = piece[:, :ch]
            ref[head, at : at + HEAD_DIM, aligned(own0 + q * ch, ch)] = piece[:, ch:]

    def put_across(ref, q, across):
        ref[:, aligned(oth0 + q * ch, ch)] = across[:, :ch]
        ref[:, aligned(own0 + q * ch, ch)] = across[:, ch:]

    r.qzt[...] = jnp.zeros(r.qzt.shape, BF)

    def share_block(layer, head, lane0, width):
        if layer == 0:
            return r.p0.at[head, :, aligned(lane0, width)]
        return r.gse.at[
            (head // 2) * rows : (head // 2 + 1) * rows,
            aligned((head % 2) * rows + lane0, width),
        ]

    def both_lanes(ref, where, q):
        return jnp.concatenate(
            [ref[where, aligned(oth0 + q * ch, ch)], ref[where, aligned(own0 + q * ch, ch)]],
            axis=1,
        )

    def project(layer, q):
        x = both(r.xl, q)
        queries = (nn(x, r.wa[0]) + head_bias(0)).astype(BF) * jnp.asarray(0.125, BF)
        put_heads(r.qz.at[layer], q, queries)
        put_heads_across(r.qzt.at[layer], q, low_transpose(queries))
        keys = nn(x, r.wa[1]).astype(BF)
        put_both(r.kn.at[layer], q, slice(None), keys)
        put_across(r.kt.at[layer], q, low_transpose(keys))
        values = (nn(x, r.wa[2]) + head_bias(1)).astype(BF)
        put_both(r.vn.at[layer], q, slice(None), values)
        put_across(r.vvt, q, low_transpose(values))

    def attend_forward(layer, q):
        for head in range(heads):
            pair = slice((head // 2) * LANES, (head // 2 + 1) * LANES)
            across = both_lanes(r.qzt.at[layer, head], slice(None), q)
            scores = nn(r.kn[layer, :, pair], across)
            raised = jnp.exp(scores - jnp.max(scores, axis=0, keepdims=True))
            total = jnp.sum(raised, axis=0, keepdims=True)
            low = (raised * (1.0 / total)).astype(BF)
            share_block(layer, head, oth0 + q * ch, ch)[...] = low[:, :ch]
            share_block(layer, head, own0 + q * ch, ch)[...] = low[:, ch:]
            where = slice(head * HEAD_DIM, (head + 1) * HEAD_DIM)
            context = nn(r.vvt[where, :], low).astype(BF)
            r.ct[layer, where, aligned(oth0 + q * ch, ch)] = context[:, :ch]
            r.ct[layer, where, aligned(own0 + q * ch, ch)] = context[:, ch:]
        target = r.ctx if layer == 0 else r.ctx1
        put_both(target, q, slice(None), low_transpose(both_lanes(r.ct.at[layer], slice(None), q)))

    def first_norm(layer, q):
        def one(i):
            at = aligned(q * ch + i * SUB, SUB)
            total = sum_rows(2 * layer, q, aligned(i * SUB, SUB))
            res = r.st[at, :] + (total + r.vt[2:3, :])
            cen = res - jnp.mean(res, axis=1, keepdims=True)
            spread = lax.rsqrt(jnp.mean(cen * cen, axis=1, keepdims=True) + EPS)
            hat = cen * spread
            r.xh1[layer, at, :] = hat
            r.rs1[layer, at, :] = spread
            normed = hat * r.vt[4:5, :] + r.vt[5:6, :]
            r.st[at, :] = normed
            r.normed[aligned(own0 + q * ch + i * SUB, SUB), :] = normed.astype(BF)

        loop(ch // SUB, one)

    def second_norm(layer, q):
        def one(i):
            at = aligned(q * ch + i * SUB, SUB)
            total = sum_rows(2 * layer + 1, q, aligned(i * SUB, SUB))
            res = r.st[at, :] + (total + r.vt[3:4, :])
            cen = res - jnp.mean(res, axis=1, keepdims=True)
            spread = lax.rsqrt(jnp.mean(cen * cen, axis=1, keepdims=True) + EPS)
            hat = cen * spread
            r.xh2[layer, at, :] = hat
            r.rs2[layer, at, :] = spread
            out = hat * r.vt[6:7, :] + r.vt[7:8, :]
            r.st[at, :] = out
            if layer < DEPTH - 1:
                r.xl[aligned(own0 + q * ch + i * SUB, SUB), :] = out.astype(BF)

        loop(ch // SUB, one)

    def unit_act(layer):
        return r.act0 if layer == 0 else r.gsn

    def gelu(v):
        square = v * v
        t = jnp.tanh(GELU_A * v * (1.0 + GELU_B * square))
        return 0.5 * (1.0 + t), t, square

    def gelu_slope(v, gate, t, square):
        return gate + (0.5 * GELU_A) * v * (1.0 - t * t) * (1.0 + (3.0 * GELU_B) * square)

    def widen(layer, q):
        act = unit_act(layer)

        def one(j):
            cols = aligned(j * TILE, TILE)
            v = nn(both(r.normed, q), r.we[:, cols]) + r.vt[pl.ds(8 + m, 1), cols]
            gate, t, square = gelu(v)
            put_both(act, q, cols, (v * gate).astype(BF))
            if layer == 0:
                put_both(r.slope0, q, cols, gelu_slope(v, gate, t, square).astype(BF))

        loop(uw // TILE, one)

    def widen_slots():
        def one(j):
            cols = aligned(j * TILE, TILE)
            v = nn(r.low2c[...], r.we[:, cols]) + r.vt[pl.ds(8 + m, 1), cols]
            gate, t, square = gelu(v)
            r.act0[rows : rows + SLOTS, cols] = (v * gate).astype(BF)
            r.slc[:, cols] = gelu_slope(v, gate, t, square).astype(BF)

        loop(uw // TILE, one)

    def rejoin_sum(layer, q):
        ctx = r.ctx if layer == 0 else r.ctx1
        sum_begin(2 * layer, q, lambda cols: nt(both(ctx, q), r.wr[cols, :]), ch)

    def narrow_sum(layer, q):
        act = unit_act(layer)
        sum_begin(2 * layer + 1, q, lambda cols: nt(both(act, q), r.wn[cols, :]), ch)

    hot = r.oh[...]

    def pick(target, row0, source, source0, width):
        def one(j):
            cols = aligned(j * TILE, TILE)
            target[row0 : row0 + SLOTS, cols] = nn(
                hot, source[source0 : source0 + rows, cols]
            ).astype(BF)

        loop(width // TILE, one)

    by_columns = (2 * vr) % LANES == 0

    def column_core(step):
        cols = aligned((z_from(step) - y) * vr, 2 * vr)
        return remote(
            r.cs.at[1, :, :, cols],
            r.cr.at[1, :, :, cols],
            r.ccs.at[step],
            r.ccr.at[step],
            core_peer,
        )

    def column_x(step):
        cols = aligned((z_from(step) - y) * vr, 2 * vr)
        return remote(
            r.xs.at[1, :, :, cols], r.xr.at[1, :, :, cols], r.cxs.at[step], r.cxr.at[step], x_peer
        )

    def column_sum(step):
        cols = aligned((z_from(step) - y) * vr, 2 * vr)
        weight = r.wn[cols, :]
        away = nt(r.act0[aligned(oth0, half), :], weight).astype(BF)
        for q in range(CHUNKS):
            r.cs[1, q, :, cols] = away[q * ch : (q + 1) * ch]
        column_core(step).start()
        here = nt(r.act0[aligned(own0, half), :], weight)
        column_core(step).wait_recv()
        for q in range(CHUNKS):
            r.xs[1, q, :, cols] = (
                here[q * ch : (q + 1) * ch] + r.cr[1, q, :, cols].astype(F32)
            ).astype(BF)
        column_x(step).start()

    for layer in range(DEPTH):
        for q in range(CHUNKS):
            if layer > 0:
                share_wait(2 * layer - 1, r.xl, q)
            project(layer, q)
        for q in range(CHUNKS):
            attend_forward(layer, q)
            if layer > 0:
                rejoin_sum(layer, q)
            elif q == 0:
                for turn in range(3, lines):
                    gather_pass(EXP, turn)
                gather_start_z(NAR)
        if layer == 0:
            gather_wait(REJ)
            for q in range(CHUNKS):
                rejoin_sum(layer, q)
            gather_pass(NAR, 1)
            transpose_into(r.xt, 0, r.xl, 0, rows)
        else:
            transpose_into(r.xt, rows, r.xl, 0, rows)
        for q in range(CHUNKS):
            sum_end(2 * layer, q, ch)
            first_norm(layer, q)
            share(2 * layer, r.normed, q).start()
            if layer == 0:
                gather_pass(NAR, q + 2)
                if q == 0:
                    gather_wait(EXP)
            share_wait(2 * layer, r.normed, q)
            widen(layer, q)
            if layer > 0:
                narrow_sum(layer, q)
        if layer == 0:
            for turn in range(CHUNKS + 2, lines):
                gather_pass(NAR, turn)
            if by_columns:
                for turn in range(lines):
                    step = gather_order(turn)
                    gather_y_arrival(NAR, step).wait_recv()
                    column_sum(step)
                transpose_into(r.nt, 0, r.normed, 0, rows)
                for step in range(lines):
                    column_x(step).wait()
                    column_core(step).wait_send()
            else:
                transpose_into(r.nt, 0, r.normed, 0, rows)
                gather_wait(NAR)
                for q in range(CHUNKS):
                    narrow_sum(layer, q)
        else:
            pick(r.low2c, 0, r.normed, 0, d_model)
            widen_slots()
            transpose_into(r.nt, rows, r.low2c, 0, SLOTS)
        for q in range(CHUNKS):
            if not (layer == 0 and by_columns):
                sum_end(2 * layer + 1, q, ch)
            second_norm(layer, q)
            if layer < DEPTH - 1:
                share(2 * layer + 1, r.xl, q).start()

    own_rows = aligned(own0, half)
    out_here = pltpu.make_async_copy(r.st, r.act.at[own_rows], r.osem.at[0])
    out_there = remote(r.st, r.act.at[own_rows], r.osem.at[1], r.osem.at[2], core_peer)
    out_arrival = remote(
        r.st, r.act.at[aligned(oth0, half)], r.osem.at[1], r.osem.at[2], core_peer
    )
    out_here.start()
    out_there.start()

    def add_rows(row, value):
        r.vg[row : row + 1, :] += jnp.sum(value, axis=0, keepdims=True)

    def norm_pull(g, hat, spread, gain):
        scaled = g * gain
        mean = jnp.mean(scaled, axis=1, keepdims=True)
        inner = jnp.mean(scaled * hat, axis=1, keepdims=True)
        return spread * (scaled - mean - hat * inner)

    def second_pull(layer, q, gradient):
        def one(i):
            at = aligned(q * ch + i * SUB, SUB)
            g = gradient(i, at)
            hat = r.xh2[layer, at, :]
            add_rows(6, g * hat)
            add_rows(7, g)
            back = norm_pull(g, hat, r.rs2[layer, at, :], r.vt[6:7, :])
            add_rows(3, back)
            r.gb[at, :] = back
            r.low2[aligned(own0 + q * ch + i * SUB, SUB), :] = back.astype(BF)

        loop(ch // SUB, one)

    def first_pull(layer, q, gradient):
        def one(i):
            at = aligned(q * ch + i * SUB, SUB)
            g = gradient(i, at)
            hat = r.xh1[layer, at, :]
            add_rows(4, g * hat)
            add_rows(5, g)
            back = norm_pull(g, hat, r.rs1[layer, at, :], r.vt[4:5, :])
            add_rows(2, back)
            r.gb[at, :] = back
            r.xl[aligned(own0 + q * ch + i * SUB, SUB), :] = back.astype(BF)

        loop(ch // SUB, one)

    def hot_rows(at_start):
        return r.oht[aligned(own0 + at_start, SUB), :]

    def bias_sums(row0):
        for kind, row in ((0, 0), (2, 1)):
            cols = aligned(m * hw, hw)
            r.vg[row : row + 1, cols] += jnp.sum(
                r.dp[kind, row0 : row0 + rows, :].astype(F32), axis=0, keepdims=True
            )

    for q in range(CHUNKS):
        second_pull(1, q, lambda i, at: nn(hot_rows(q * ch + i * SUB), r.mc[...]))
        share(4, r.low2, q).start()
    for q in range(CHUNKS):
        share_wait(4, r.low2, q)
    pick(r.low2c, 0, r.low2, 0, d_model)

    def slot_units(j):
        cols = aligned(j * TILE, TILE)
        back = nn(r.low2c[...], r.wn[:, cols]) * r.slc[:, cols].astype(F32)
        back = back.astype(BF)
        r.be[rows : rows + SLOTS, cols] = back
        r.vg[pl.ds(8 + m, 1), cols] += jnp.sum(back.astype(F32), axis=0, keepdims=True)

    loop(uw // TILE, slot_units)
    slot_own = core * slot_half
    slot_oth = slot_half - slot_own

    def slot_tile(cols):
        part = nt(r.be[rows : rows + SLOTS, :], r.we[cols, :])
        r.part[...] = part
        return jnp.concatenate(
            [
                r.part[aligned(slot_oth, slot_half), :],
                r.part[aligned(slot_own, slot_half), :],
            ],
            axis=0,
        )

    sum_begin(4, 0, slot_tile, slot_half)
    transpose_into(r.l2t, rows, r.low2c, 0, SLOTS)
    for head in range(heads):
        r.qc[head] = nn(hot, r.qz[1, head]).astype(BF)
        source = r.gse[
            (head // 2) * rows : (head // 2 + 1) * rows,
            (head % 2) * rows : (head % 2 + 1) * rows,
        ]
        r.pc[head] = nn(source, r.oht[...]).astype(BF)
    r.cct[...] = nn(r.ct[1], r.oht[...]).astype(BF)
    sum_end(4, 0, slot_half)
    mine_slots = r.slt.at[aligned(slot_own, slot_half)]
    mine_slots[...] = sum_rows(4, 0, slice(0, slot_half)).astype(BF)
    slots_out = remote(mine_slots, mine_slots, r.osem.at[3], r.osem.at[4], core_peer)
    slots_in_ref = r.slt.at[aligned(slot_oth, slot_half)]
    slots_in = remote(slots_in_ref, slots_in_ref, r.osem.at[3], r.osem.at[4], core_peer)
    slots_out.start()
    slots_in.wait_recv()
    for q in range(CHUNKS):
        first_pull(
            1, q, lambda i, at: r.gb[at, :] + nn(hot_rows(q * ch + i * SUB), r.slt[...])
        )
        share(5, r.xl, q).start()

    for q in range(CHUNKS):
        share_wait(5, r.xl, q)
    pick(r.low2c, 0, r.xl, 0, d_model)
    low_ctx = nn(r.low2c[...], r.wr[...]).astype(BF)
    across = low_transpose(low_ctx)
    dq_across = []
    for pair in range(heads // 2):
        lanes = slice(pair * LANES, (pair + 1) * LANES)
        dv = jnp.zeros((rows, LANES), F32)
        dk = jnp.zeros((rows, LANES), F32)
        for head in (2 * pair, 2 * pair + 1):
            where = slice(head * HEAD_DIM, (head + 1) * HEAD_DIM)
            at = (head % 2) * HEAD_DIM
            r.dozt[head, at : at + HEAD_DIM, 0:SLOTS] = across[where, :]
            low = r.pc[head]
            dv += nn(low, lane_half(low_ctx[:, lanes], head))
            dp = nn(r.vn[1, :, lanes], r.dozt[head, :, 0:SLOTS])
            delta = jnp.sum(
                across[where, :].astype(F32) * r.cct[where, :].astype(F32), axis=0, keepdims=True
            )
            ds = (low.astype(F32) * (dp - delta)).astype(BF)
            dk += nn(ds, r.qc[head])
            dq_across.append(nn(r.kt[1, where, :], ds) * 0.125)
        r.dp[1, rows : 2 * rows, lanes] = dk.astype(BF)
        r.dp[2, rows : 2 * rows, lanes] = dv.astype(BF)
    dq = low_transpose(jnp.concatenate(dq_across, axis=0))
    r.dp[0, rows : 2 * rows, :] = nn(r.oht[...], dq).astype(BF)
    bias_sums(rows)

    def layer_rows(k, q, row0):
        def tile_of(cols):
            total = None
            for kind in range(3):
                lhs = jnp.concatenate(
                    [
                        r.dp[kind, aligned(row0 + oth0 + q * ch, ch), :],
                        r.dp[kind, aligned(row0 + own0 + q * ch, ch), :],
                    ],
                    axis=0,
                )
                part = nt(lhs, r.wa[kind, cols, :])
                total = part if total is None else total + part
            return total

        sum_begin(k, q, tile_of, ch)

    for q in range(CHUNKS):
        layer_rows(5, q, rows)
    transpose_into(r.l1t, rows, r.low2c, 0, SLOTS)

    def weight_grad_rows(target, across, latter, width, row0, count):
        at = aligned(row0, count)

        def one(j):
            cols = aligned(j * TILE, TILE)
            target[at, cols] = nn(across[at, :], latter[:, cols]).astype(BF)

        loop(width // TILE, one)

    def weight_grad(target, across, latter, width):
        loop(
            d_model // TILE,
            lambda i: weight_grad_rows(target, across, latter, width, i * TILE, TILE),
        )

    def transpose_both(target, source, q):
        for row0 in (oth0 + q * ch, own0 + q * ch):
            target[:, aligned(row0, ch)] = low_transpose(source[aligned(row0, ch), :])

    def units_back(q):
        def one(j):
            cols = aligned(j * TILE, TILE)
            slope = both(r.slope0, q, cols).astype(F32)
            back = (nn(both(r.low2, q), r.wn[:, cols]) * slope).astype(BF)
            put_both(r.be, q, cols, back)
            r.vg[pl.ds(8 + m, 1), cols] += jnp.sum(back.astype(F32), axis=0, keepdims=True)

        loop(uw // TILE, one)

    for q in range(CHUNKS):
        sum_end(5, q, ch)
        second_pull(
            0, q, lambda i, at: r.gb[at, :] + sum_rows(5, q, aligned(i * SUB, SUB))
        )
        share(6, r.low2, q).start()
        share_wait(6, r.low2, q)
        transpose_both(r.l2t, r.low2, q)
        if q == 0:
            units_back(q)
    if by_columns:
        for turn in range(1, lines + 1):
            owner = ((z + scatter_order(turn)) % lines) * 2 + 1 - y
            weight_grad_rows(r.gsn, r.l2t, r.act0, uw, owner * vr, vr)
            if turn <= 2:
                scatter_y(NAR, scatter_order(turn)).start()
                under_way.append(queue.pop(0))
        ready.append(NAR)
    else:
        weight_grad(r.gsn, r.l2t, r.act0, uw)
        scatter_start(NAR)
    for q in range(CHUNKS):
        if q > 0:
            units_back(q)
        sum_begin(6, q, lambda cols, q=q: nt(both(r.be, q), r.we[cols, :]), ch)
    if by_columns:
        each(
            0,
            lines,
            lambda s: weight_grad_rows(
                r.gsn, r.l2t, r.act0, uw, (((z + s) % lines) * 2 + y) * vr, vr
            ),
        )
    pick(r.ctx, rows, r.ctx1, 0, hw)
    weight_grad(r.gse, r.nt, r.be, uw)
    scatter_start(EXP)
    scatter_pass()
    for q in range(CHUNKS):
        sum_end(6, q, ch)
        first_pull(
            0, q, lambda i, at: r.gb[at, :] + sum_rows(6, q, aligned(i * SUB, SUB))
        )
        share(7, r.xl, q).start()
    scatter_pass()
    for q in range(CHUNKS):
        share_wait(7, r.xl, q)
        back = nn(both(r.xl, q), r.wr[...]).astype(BF)
        put_heads(r.doz, q, back)
        put_heads_across(r.dozt, q, low_transpose(back))

    def head_pair(pair):
        lanes = aligned(pair * LANES, LANES)
        dv = jnp.zeros((rows, LANES), F32)
        dk = jnp.zeros((rows, LANES), F32)
        for side in range(2):
            head = 2 * pair + side
            where = aligned(head * HEAD_DIM, HEAD_DIM)
            for part in range(rows // TILE):
                some = slice(part * TILE, (part + 1) * TILE)
                low = r.p0[head, :, some]
                dv += nn(low, r.doz[head, some, :])
                inner = r.dozt[head, side * HEAD_DIM : (side + 1) * HEAD_DIM, some]
                delta = jnp.sum(
                    inner.astype(F32) * r.ct[0, where, some].astype(F32), axis=0, keepdims=True
                )
                dp = nn(r.vn[0, :, lanes], r.dozt[head, :, some])
                ds = (low.astype(F32) * (dp - delta)).astype(BF)
                dk += nn(ds, r.qz[0, head, some, :])
                r.dqt[where, some] = (nn(r.kt[0, where, :], ds) * 0.125).astype(BF)
        r.dp[1, 0:rows, lanes] = dk.astype(BF)
        r.dp[2, 0:rows, lanes] = dv.astype(BF)

    for pair in range(heads // 2):
        head_pair(pair)
        if under_way[0][0] != REJ:
            scatter_pass()
    for i in range(rows // LANES):
        some = slice(i * LANES, (i + 1) * LANES)
        r.dp[0, some, :] = low_transpose(r.dqt[:, some])
    for q in range(CHUNKS):
        layer_rows(7, q, 0)
    if under_way[0][0] != REJ:
        scatter_pass()
    bias_sums(0)
    transpose_into(r.l1t, 0, r.xl, 0, rows)
    weight_grad(r.gsr, r.l1t, r.ctx, hw)
    scatter_start(REJ)
    first_of_x = jnp.where(m < 2, 1.0, 0.0)
    r.vg[2:8, :] = r.vg[2:8, :] * first_of_x
    for j in range(d_model // LANES):
        tall = jnp.concatenate(
            [r.vg[:, j * LANES : (j + 1) * LANES], jnp.zeros((LANES - 16, LANES), F32)], axis=0
        )
        r.gsv[j * LANES : (j + 1) * LANES, :] = jnp.transpose(tall, (1, 0)).astype(BF)
    scatter_start(VEC)
    for kind in range(3):
        weight_grad(r.gsa.at[kind], r.xt, r.dp.at[kind], hw)
    scatter_start(ATT)
    scatter_pass()
    out_here.wait()
    out_there.wait_send()
    for q in range(CHUNKS):
        sum_end(7, q, ch)

        def last(i, q=q):
            at = aligned(q * ch + i * SUB, SUB)
            g = r.gb[at, :] + sum_rows(7, q, aligned(i * SUB, SUB))
            r.st[at, :] = g * r.keep[aligned(own0 + q * ch + i * SUB, SUB), :]

        loop(ch // SUB, last)
    in_here = pltpu.make_async_copy(r.st, r.ing.at[own_rows], r.osem.at[5])
    in_there = remote(r.st, r.ing.at[own_rows], r.osem.at[6], r.osem.at[7], core_peer)
    in_arrival = remote(r.st, r.ing.at[aligned(oth0, half)], r.osem.at[6], r.osem.at[7], core_peer)
    in_here.start()
    in_there.start()

    scatter_pass()
    def squares(value):
        value = value * value
        if value.ndim == 3:
            value = jnp.sum(value, axis=0)
        value = jnp.sum(value, axis=0, keepdims=True)
        return jnp.sum(value, axis=1, keepdims=True)

    swap_v = remote(r.vf.at[0], r.vf.at[1], r.vxs.at[2], r.vxr.at[2], core_peer)
    swap_w = remote(r.vf.at[2], r.vf.at[3], r.vxs.at[3], r.vxr.at[3], x_peer)
    total = jnp.zeros((1, 1), F32)
    while under_way:
        turn = under_way[0][1] if under_way[0][0] == ATT else 0
        if turn == 1:
            scatter_finish(NAR, r.gn)
            total = total + squares(r.gn[...])
        elif turn == 2:
            scatter_finish(VEC, r.vf.at[0])
            swap_v.start()
            scatter_finish(REJ, r.gr)
            total = total + squares(r.gr[...])
        elif turn == 3:
            swap_v.wait_recv()
            r.vf[2] = r.vf[0] + r.vf[1]
            swap_w.start()
            scatter_finish(EXP, r.ge)
            total = total + squares(r.ge[...])
        elif turn == 4:
            swap_w.wait_recv()
            r.vs[...] = jnp.transpose(r.vf[2] + r.vf[3], (1, 0))
            r.gv[...] = r.vs[pl.ds(columns * m, columns), :]
            total = total + squares(r.gv[...])
        scatter_pass()
    scatter_finish(ATT, r.ga)
    total = total + squares(r.ga[...])

    r.nm[m] = jnp.broadcast_to(total, (8, LANES))

    def model_copy(k, slot):
        return remote(r.nm.at[slot], r.nm.at[slot], r.nms.at[k], r.nmr.at[k], model_peers[k])

    for k in range(3):
        model_copy(k, m).start()
    for k in range(3):
        model_copy(k, model_peers[k][1]).wait_recv()
    r.nz[d] = jnp.sum(r.nm[...], axis=0)

    def line_copy(step, slot):
        here = r.nz.at[slot]
        return remote(here, here, r.nzs.at[0, step], r.nzr.at[0, step], z_peer(step))

    def cross_copy(step, slot):
        here = r.nz.at[slot]
        return remote(here, here, r.nzs.at[1, step], r.nzr.at[1, step], zy_peer(step))

    each(0, lines, lambda s: cross_copy(s, d).start())
    each(1, lines, lambda s: line_copy(s, d).start())
    each(0, lines, lambda s: cross_copy(s, z_from(s) + 1 - 2 * y).wait_recv())
    each(1, lines, lambda s: line_copy(s, z_from(s)).wait_recv())
    r.norm[...] = jnp.sqrt(jnp.sum(r.nz[...], axis=0))

    each(0, lines, lambda s: cross_copy(s, d).wait_send())
    each(1, lines, lambda s: line_copy(s, d).wait_send())
    for k in range(3):
        model_copy(k, m).wait_send()
    swap.wait_send()
    swap_x.wait_send()
    swap_v.wait_send()
    swap_w.wait_send()
    slots_out.wait_send()
    for region in range(5):
        gather_close(region)
        scatter_close(region)
    out_arrival.wait_recv()
    in_here.wait()
    in_there.wait_send()
    in_arrival.wait_recv()


def run_layers(
    n, tok, pos, cho, table, mcot, attend, rejoin, expand, narrow, vin
):
    rows, d_model = tok.shape
    vr = rejoin.shape[0]
    hw = rejoin.shape[1]
    uw = expand.shape[1]
    lines = n // 2
    half = rows // 2
    ch = half // CHUNKS
    heads = hw // HEAD_DIM
    wide = rows + SLOTS
    inputs = [
        ("tok", tok),
        ("pos", pos),
        ("cho", cho),
        ("table", table),
        ("mcot", mcot),
        ("attend", attend),
        ("rejoin", rejoin),
        ("expand", expand),
        ("narrow", narrow),
        ("vin", vin),
    ]
    outputs = [
        ("act", (rows, d_model), pl.ANY),
        ("ing", (rows, d_model), pl.ANY),
        ("ga", (3, vr, hw), pltpu.VMEM),
        ("gr", (vr, hw), pltpu.VMEM),
        ("ge", (vr, uw), pltpu.VMEM),
        ("gn", (vr, uw), pltpu.VMEM),
        ("gv", vin.shape, pltpu.VMEM),
        ("norm", (8, LANES), pltpu.VMEM),
    ]
    low = [
        ("wv", (d_model, LANES)),
        ("wa", (3, d_model, hw)),
        ("wr", (d_model, hw)),
        ("we", (d_model, uw)),
        ("wn", (d_model, uw)),
        ("gsv", (d_model, LANES)),
        ("gsa", (3, d_model, hw)),
        ("gsr", (d_model, hw)),
        ("gse", (d_model, uw)),
        ("gsn", (d_model, uw)),
        ("yv", (lines, vr, LANES)),
        ("ya", (lines, 3, vr, hw)),
        ("yr", (lines, vr, hw)),
        ("ye", (lines, vr, uw)),
        ("yn", (lines, vr, uw)),
        ("zv", (lines, vr, LANES)),
        ("za", (lines, 3, vr, hw)),
        ("zr", (lines, vr, hw)),
        ("ze", (lines, vr, uw)),
        ("zn", (lines, vr, uw)),
        ("cs", (2, CHUNKS, ch, d_model)),
        ("cr", (2, CHUNKS, ch, d_model)),
        ("xs", (2, CHUNKS, ch, d_model)),
        ("xr", (2, CHUNKS, ch, d_model)),
        ("vb", (4, vr, LANES)),
        ("oh", (SLOTS, rows)),
        ("oht", (rows, SLOTS)),
        ("mc", (SLOTS, d_model)),
        ("xl", (rows, d_model)),
        ("normed", (rows, d_model)),
        ("low2", (rows, d_model)),
        ("xt", (d_model, 2 * rows)),
        ("nt", (d_model, wide)),
        ("l2t", (d_model, wide)),
        ("l1t", (d_model, wide)),
        ("act0", (wide, uw)),
        ("slope0", (rows, uw)),
        ("be", (wide, uw)),
        ("ctx", (wide, hw)),
        ("ctx1", (rows, hw)),
        ("dp", (3, 2 * rows, hw)),
        ("qz", (2, heads, rows, LANES)),
        ("qzt", (2, heads, LANES, rows)),
        ("kn", (2, rows, hw)),
        ("kt", (2, hw, rows)),
        ("vn", (2, rows, hw)),
        ("vvt", (hw, rows)),
        ("ct", (2, hw, rows)),
        ("p0", (heads, rows, rows)),
        ("dqt", (hw, rows)),
        ("slc", (SLOTS, uw)),
        ("low2c", (SLOTS, d_model)),
        ("slt", (SLOTS, d_model)),
        ("qc", (heads, SLOTS, LANES)),
        ("pc", (heads, rows, SLOTS)),
        ("cct", (hw, SLOTS)),
    ]
    full = [
        ("vt", (16, d_model)),
        ("vg", (16, d_model)),
        ("keep", (rows, 1)),
        ("st", (half, d_model)),
        ("gb", (half, d_model)),
        ("xh1", (2, half, d_model)),
        ("xh2", (2, half, d_model)),
        ("rs1", (2, half, 1)),
        ("rs2", (2, half, 1)),
        ("acc", (ch, d_model)),
        ("part", (SLOTS, TILE)),
        ("vf", (4, vr, LANES)),
        ("vs", (LANES, vr)),
        ("nm", (4, 8, LANES)),
        ("nz", (n, 8, LANES)),
    ]
    sems = [
        ("agzs", (5, lines + 3)),
        ("agzr", (5, lines)),
        ("agys", (5, lines)),
        ("agyr", (5, lines)),
        ("rsys", (5, lines)),
        ("rsyr", (5, lines)),
        ("rszs", (5, lines)),
        ("rszr", (5, lines)),
        ("arcs", (8, CHUNKS)),
        ("arcr", (8, CHUNKS)),
        ("arxs", (8, CHUNKS)),
        ("arxr", (8, CHUNKS)),
        ("shs", (8, CHUNKS)),
        ("shr", (8, CHUNKS)),
        ("vxs", (4,)),
        ("vxr", (4,)),
        ("osem", (8,)),
        ("nms", (3,)),
        ("nmr", (3,)),
        ("nzs", (2, lines)),
        ("nzr", (2, lines)),
        ("ccs", (lines,)),
        ("ccr", (lines,)),
        ("cxs", (lines,)),
        ("cxr", (lines,)),
    ]
    names = (
        [name for name, _ in inputs]
        + [name for name, _, _ in outputs]
        + [name for name, _ in low]
        + [name for name, _ in full]
        + ["pb"]
        + [name for name, _ in sems]
    )
    sizes = (n, d_model, rows, hw, uw, vr)

    def body(*refs):
        layer_kernel(names, sizes, *refs)

    return pl.pallas_call(
        body,
        out_shape=[jax.ShapeDtypeStruct(shape, F32) for _, shape, _ in outputs],
        in_specs=[pl.BlockSpec(memory_space=pltpu.VMEM)] * len(inputs),
        out_specs=[pl.BlockSpec(memory_space=space) for _, _, space in outputs],
        scratch_shapes=[pltpu.VMEM(shape, BF) for _, shape in low]
        + [pltpu.VMEM(shape, F32) for _, shape in full]
        + [pltpu.VMEM((16, LANES), jnp.int32)]
        + [pltpu.SemaphoreType.DMA(shape) for _, shape in sems],
        compiler_params=pltpu.CompilerParams(
            collective_id=0, has_side_effects=True, vmem_limit_bytes=61 * 1024 * 1024
        ),
        cost_estimate=pl.CostEstimate(
            flops=20_000_000_000, bytes_accessed=20_000_000, transcendentals=4_000_000
        ),
    )(*[value for _, value in inputs])


def apply_update(weight, first_moment, second_moment, shadow, gradient, step_rate):
    momentum = 0.5 * first_moment + 0.5 * gradient
    variance = 0.5 * second_moment + 0.5 * gradient * gradient
    bias_fix = 1.0 - 0.5**STEP
    updated = weight - step_rate * (
        momentum / bias_fix / (jnp.sqrt(variance / bias_fix) + 1e-08) + 0.01 * weight
    )
    average = 0.999 * shadow + 0.001 * updated
    return (updated, momentum, variance, average, updated.astype(BF))


def update_kernel(rates, clip_limit, norm, act, ing, *refs):
    *refs, norm_out, act_out, ing_out = refs
    act_out[...] = act[...]
    ing_out[...] = ing[...]
    norm_out[...] = norm[0:1, 0:1]
    factor = jnp.minimum(1.0, clip_limit / (norm[0:1, 0:1] + 1e-06))
    ins, outs = refs[: 5 * len(rates)], refs[5 * len(rates) :]
    for index, rate in enumerate(rates):
        weight, first, second, shadow, gradient = ins[5 * index : 5 * index + 5]
        targets = outs[5 * index : 5 * index + 5]
        for part in range(weight.shape[0]) if len(weight.shape) == 3 else (slice(None),):
            results = apply_update(
                weight[part],
                first[part],
                second[part],
                shadow[part],
                gradient[part] * factor,
                rate,
            )
            for target, value in zip(targets, results, strict=True):
                target[part] = value


def run_update(groups, rates, norm, clip_limit, act, ing):
    vr = groups[1][0].shape[0]
    step = min(vr, 32)

    def spec(shape, whole):
        if whole:
            return pl.BlockSpec(shape, lambda i: (0, 0))
        if len(shape) == 3:
            return pl.BlockSpec((shape[0], step, shape[2]), lambda i: (0, i, 0))
        return pl.BlockSpec((step, shape[1]), lambda i: (i, 0))

    last = len(groups) - 1
    passed = pl.BlockSpec((act.shape[0] * step // vr, act.shape[1]), lambda i: (i, 0))
    specs = [spec(group[0].shape, k == last) for k, group in enumerate(groups)]

    def body(*refs):
        update_kernel(rates, clip_limit, *refs)

    flat = [value for group in groups for value in group]
    size = sum(value.size for value in flat) * 4
    outs = pl.pallas_call(
        body,
        grid=(vr // step,),
        in_specs=[spec(norm.shape, True)]
        + [passed] * 2
        + [one for one in specs for _ in range(5)],
        out_specs=[one for one in specs for _ in range(5)]
        + [spec((1, 1), True)]
        + [passed] * 2,
        out_shape=[
            jax.ShapeDtypeStruct(group[0].shape, kind)
            for group in groups
            for kind in (F32, F32, F32, F32, BF)
        ]
        + [jax.ShapeDtypeStruct(shape, F32) for shape in ((1, 1), act.shape, ing.shape)],
        compiler_params=pltpu.CompilerParams(vmem_limit_bytes=60 * 1024 * 1024),
        cost_estimate=pl.CostEstimate(flops=size, bytes_accessed=2 * size, transcendentals=0),
    )(norm, act, ing, *flat)
    groups_out = [outs[5 * k : 5 * k + 5] for k in range(len(groups))]
    return groups_out, outs[-3].reshape(()), *outs[-2:]


def per_device(
    tokens_in,
    masked_positions,
    replace_choice,
    replace_table,
    masked_cotangent,
    attend,
    attend_mean,
    attend_square,
    attend_shadow,
    rejoin,
    rejoin_mean,
    rejoin_square,
    rejoin_shadow,
    expand,
    expand_mean,
    expand_square,
    expand_shadow,
    narrow,
    narrow_mean,
    narrow_square,
    narrow_shadow,
    vectors,
    vectors_mean,
    vectors_square,
    vectors_shadow,
):
    n = lax.axis_size("dp")
    act, ing, ga, gr, ge, gn, gv, norm = run_layers(
        n,
        tokens_in,
        masked_positions,
        replace_choice,
        replace_table,
        masked_cotangent,
        attend.transpose(1, 0, 2),
        rejoin,
        expand,
        narrow,
        vectors.T,
    )
    d_model = tokens_in.shape[1]
    param_count = 4 * d_model * d_model + 2 * d_model * expand.shape[1] * 4 + 12 * d_model
    clip_limit = 0.001 * math.sqrt(param_count * tokens_in.shape[0] * n)
    cubes = [x.transpose(1, 0, 2) for x in (attend, attend_mean, attend_square, attend_shadow)]
    rows_of = [x.T for x in (vectors, vectors_mean, vectors_square, vectors_shadow)]
    new, gradient_norm, act, ing = run_update(
        (
            (*cubes, ga),
            (rejoin, rejoin_mean, rejoin_square, rejoin_shadow, gr),
            (expand, expand_mean, expand_square, expand_shadow, ge),
            (narrow, narrow_mean, narrow_square, narrow_shadow, gn),
            (*rows_of, gv),
        ),
        (0.04, 0.16, 0.04, 0.04, 0.5),
        norm,
        clip_limit,
        act,
        ing,
    )
    results = [act, ing, gradient_norm]
    results.extend(x.transpose(1, 0, 2) for x in new[0])
    for group in new[1:4]:
        results.extend(group)
    results.extend(x.T for x in new[4])
    return tuple(results)


def solution(mesh):
    row = P("dp", None)
    cube = P("dp", None, "mp")
    flat = P("dp", "mp")
    return jax.shard_map(
        per_device,
        mesh=mesh,
        in_specs=(row, row, row, P(), P("dp", None, None)) + (cube,) * 4 + (flat,) * 16,
        out_specs=(row, row, P()) + (cube,) * 5 + (flat,) * 20,
        check_vma=False,
    )
```

```python
import math
from types import SimpleNamespace

import jax
import jax.numpy as jnp
from jax import lax
from jax.experimental import pallas as pl
from jax.experimental.pallas import tpu as pltpu
from jax.sharding import PartitionSpec as P

HEAD_DIM = 64
SEQ_LEN = 512
DEPTH = 2
STEP = 7
EPS = 1e-05
BF = jnp.bfloat16
F32 = jnp.float32
MESH = pl.DeviceIdType.MESH
LANES = 128
TILE = 256
SLOTS = 128
CHUNKS = 2
SUB = 64
VEC, ATT, REJ, EXP, NAR = range(5)
GELU_A = 0.7978845608028654
GELU_B = 0.044715


def nn(former, latter):
    return jnp.dot(former, latter, preferred_element_type=F32)


def nt(former, latter):
    return lax.dot_general(former, latter, (((1,), (1,)), ((), ())), preferred_element_type=F32)


def low_transpose(block):
    return jnp.transpose(block.astype(F32), (1, 0)).astype(BF)


def loop(count, body):
    def step(index, carry):
        body(index)
        return carry

    lax.fori_loop(0, count, step, 0)


def each(first, last, body):
    if last - first <= 8:
        for index in range(first, last):
            body(index)
    else:

        def step(index, carry):
            body(index)
            return carry

        lax.fori_loop(first, last, step, 0)


def aligned(index, size):
    return pl.ds(pl.multiple_of(index, size), size)


def layer_kernel(names, sizes, *refs):
    r = SimpleNamespace(**dict(zip(names, refs, strict=True)))
    n, d_model, rows, hw, uw, vr = sizes
    r.doz, r.dozt = r.qz.at[1], r.qzt.at[1]
    half = rows // 2
    ch = half // CHUNKS
    lines = n // 2
    heads = hw // HEAD_DIM
    slot_half = SLOTS // 2

    d = lax.axis_index("dp")
    m = lax.axis_index("mp")
    z, y = d // 2, d % 2
    core = m % 2
    core_peer = (d, m + 1 - 2 * core)
    x_peer = (d, (m + 2) % 4)
    y_peer = (d + 1 - 2 * y, m)
    model_peers = (core_peer, x_peer, (d, 3 - m))
    own0 = core * half
    oth0 = half - own0

    weights = (r.wv, r.wa, r.wr, r.we, r.wn)
    grads = (r.gsv, r.gsa, r.gsr, r.gse, r.gsn)
    from_y = (r.yv, r.ya, r.yr, r.ye, r.yn)
    from_z = (r.zv, r.za, r.zr, r.ze, r.zn)

    def z_peer(step):
        return (((z + step) % lines) * 2 + y, m)

    def zy_peer(step):
        return (((z + step) % lines) * 2 + 1 - y, m)

    def z_from(step):
        return ((z + lines - step) % lines) * 2 + y

    def block(ref, region, index):
        if region == VEC:
            return ref.at[index]
        where = aligned(index * vr, vr)
        return ref.at[:, where, :] if region == ATT else ref.at[where, :]

    def remote(source, target, send, recv, device):
        return pltpu.make_async_remote_copy(
            src_ref=source,
            dst_ref=target,
            send_sem=send,
            recv_sem=recv,
            device_id=device,
            device_id_type=MESH,
        )

    barrier = pltpu.get_barrier_semaphore()

    def greet(peer):
        pl.semaphore_signal(barrier, inc=1, device_id=peer, device_id_type=MESH)

    for peer in model_peers:
        greet(peer)
    each(1, lines, lambda s: greet(z_peer(s)))
    each(0, lines, lambda s: greet(zy_peer(s)))
    pl.semaphore_wait(barrier, len(model_peers) + n - 1)

    relay = lines == 4
    last_line = lines - 1
    inner = jnp.logical_and(z > 0, z < last_line)
    far_end = (jnp.where(z == 1, 0, last_line) * 2 + y, m)
    near_mid = (jnp.where(z == 0, 1, last_line - 1) * 2 + y, m)

    def gather_z(region, step):
        piece = block(weights[region], region, d)
        return remote(
            piece, piece, r.agzs.at[region, step], r.agzr.at[region, step], z_peer(step)
        )

    def gather_z_arrival(region, step):
        piece = block(weights[region], region, z_from(step))
        return remote(
            piece, piece, r.agzs.at[region, step], r.agzr.at[region, step], z_peer(step)
        )

    def gather_onward(region, turn):
        piece = block(weights[region], region, z_from(gather_order(turn)))
        if turn == 3:
            target = far_end
            arrives_as = jnp.where(z == 1, 1, last_line)
        else:
            target = ((z + 3 - 2 * turn) * 2 + y, m)
            arrives_as = 2
        return remote(
            piece,
            piece,
            r.agzs.at[region, last_line + turn],
            r.agzr.at[region, arrives_as],
            target,
        )

    def gather_y(region, step):
        piece = block(weights[region], region, z_from(step))
        return remote(piece, piece, r.agys.at[region, step], r.agyr.at[region, step], y_peer)

    def gather_y_arrival(region, step):
        piece = block(weights[region], region, z_from(step) + 1 - 2 * y)
        return remote(piece, piece, r.agys.at[region, step], r.agyr.at[region, step], y_peer)

    def near(step, body):
        if not relay:
            body()
        elif step != 2:
            pl.when(z < last_line if step == 1 else z > 0)(body)

    def gather_start_z(region):
        for step in range(1, lines):
            near(step, lambda: gather_z(region, step).start())

    def gather_start_y(region):
        gather_y(region, 0).start()

    def gather_order(turn):
        if not relay or turn == 0:
            return turn
        if turn == 1:
            return jnp.where(z == 0, last_line, 1)
        if turn == 2:
            return jnp.where(inner, last_line, 2)
        return jnp.where(inner, 2, jnp.where(z == 0, 1, last_line))

    def gather_pass(region, turn):
        step = gather_order(turn)
        gather_z_arrival(region, step).wait_recv()
        if relay:
            pl.when(inner)(lambda: gather_onward(region, turn).start())
        gather_y(region, step).start()

    def gather_wait(region):
        each(0, lines, lambda s: gather_y_arrival(region, s).wait_recv())

    def gather_close(region):
        for step in range(1, lines):
            near(step, lambda: gather_z(region, step).wait_send())
        if relay:
            for turn in range(1, lines):
                pl.when(inner)(lambda: gather_onward(region, turn).wait_send())
        each(0, lines, lambda s: gather_y(region, s).wait_send())

    def scatter_y(region, step):
        owner = ((z + step) % lines) * 2 + 1 - y
        return remote(
            block(grads[region], region, owner),
            from_y[region].at[step],
            r.rsys.at[region, step],
            r.rsyr.at[region, step],
            y_peer,
        )

    def scatter_z(region, step):
        owner = ((z + step) % lines) * 2 + y
        return remote(
            block(grads[region], region, owner),
            from_z[region].at[step],
            r.rszs.at[region, step],
            r.rszr.at[region, step],
            z_peer(step),
        )

    def scatter_far(region, step):
        owner = ((z + step) % lines) * 2 + y
        return remote(
            block(grads[region], region, owner),
            from_z[region].at[0],
            r.rszs.at[region, step],
            r.rszr.at[region, 0],
            near_mid,
        )

    def scatter_order(turn):
        if not relay:
            return turn % lines
        if turn == 1:
            return jnp.where(z == 0, last_line, 1)
        if turn == 2:
            return jnp.where(z == 0, 1, last_line)
        return 2 if turn == 3 else 0

    def scatter_start(region):
        ready.append(region)
        scatter_next()

    ready = []
    order = (NAR, EXP, REJ, VEC, ATT)
    queue = [(region, turn) for region in order for turn in range(1, lines + 1)]
    under_way = []
    weight_of = {NAR: 4, EXP: 4, ATT: 3, REJ: 1, VEC: 1}

    def scatter_next():
        while queue and queue[0][0] in ready:
            if sum(weight_of[region] for region, _ in under_way) > 4:
                break
            region, turn = queue.pop(0)
            scatter_y(region, scatter_order(turn)).start()
            under_way.append((region, turn))

    def scatter_pass():
        region, turn = under_way[0]
        step = scatter_order(turn)
        scatter_y(region, step).wait_recv()
        under_way.pop(0)
        scatter_next()
        if turn == lines:
            return
        piece = block(grads[region], region, ((z + step) % lines) * 2 + y)
        total = piece[...].astype(F32) + from_y[region][step].astype(F32)
        piece[...] = total.astype(BF)
        if not relay:
            scatter_z(region, step).start()
        elif turn == 1:
            pl.when(inner)(lambda: scatter_z(region, step).start())
            pl.when(jnp.logical_not(inner))(lambda: scatter_far(region, step).start())
        elif turn == 2:
            scatter_z(region, step).start()
        else:

            @pl.when(inner)
            def _():
                scatter_far(region, 0).wait_recv()
                piece[...] = (total + from_z[region][0].astype(F32)).astype(BF)

            scatter_z(region, step).start()

    def scatter_finish(region, out_ref):
        def one(step):
            scatter_z(region, step).wait_recv()
            out_ref[...] += from_z[region][step].astype(F32)

        piece = block(grads[region], region, d)
        out_ref[...] = piece[...].astype(F32) + from_y[region][0].astype(F32)
        for step in range(1, lines):
            if not relay or step == 2:
                one(step)
            else:
                pl.when(z > 0 if step == 1 else z < last_line)(lambda: one(step))

    def scatter_close(region):
        each(0, lines, lambda s: scatter_y(region, s).wait_send())
        each(1, lines, lambda s: scatter_z(region, s).wait_send())

    tiles = d_model // TILE

    def core_copy(k, q, count, j):
        where = (k % 2, q, slice(0, count), aligned(j * TILE, TILE))
        return remote(
            r.cs.at[where], r.cr.at[where], r.arcs.at[k, q, j], r.arcr.at[k, q, j], core_peer
        )

    def x_copy(k, q, count, j):
        where = (k % 2, q, slice(0, count), aligned(j * TILE, TILE))
        return remote(
            r.xs.at[where], r.xr.at[where], r.arxs.at[k, q, j], r.arxr.at[k, q, j], x_peer
        )

    def sum_begin(k, q, tile_of, count):
        b = k % 2

        def onward(j):
            cols = aligned(j * TILE, TILE)
            core_copy(k, q, count, j).wait_recv()
            r.xs[b, q, :count, cols] = (
                r.acc[:count, cols] + r.cr[b, q, :count, cols].astype(F32)
            ).astype(BF)
            x_copy(k, q, count, j).start()

        def one(j):
            cols = aligned(j * TILE, TILE)
            part = tile_of(cols)
            r.cs[b, q, :count, cols] = part[:count].astype(BF)
            core_copy(k, q, count, j).start()
            r.acc[:count, cols] = part[count:]
            pl.when(j > 0)(lambda: onward(j - 1))

        loop(tiles, one)
        onward(tiles - 1)

    def sum_end(k, q, count):
        for j in range(tiles):
            x_copy(k, q, count, j).wait()
            core_copy(k, q, count, j).wait_send()

    def sum_rows(k, q, where):
        b = k % 2
        return r.xs[b, q, where].astype(F32) + r.xr[b, q, where].astype(F32)

    def share(k, ref, q):
        where = aligned(own0 + q * ch, ch)
        return remote(ref.at[where], ref.at[where], r.shs.at[k, q], r.shr.at[k, q], core_peer)

    def share_arrival(k, ref, q):
        where = aligned(oth0 + q * ch, ch)
        return remote(ref.at[where], ref.at[where], r.shs.at[k, q], r.shr.at[k, q], core_peer)

    def share_wait(k, ref, q):
        share(k, ref, q).wait_send()
        share_arrival(k, ref, q).wait_recv()

    def both(ref, q, cols=slice(None)):
        return jnp.concatenate(
            [ref[aligned(oth0 + q * ch, ch), cols], ref[aligned(own0 + q * ch, ch), cols]],
            axis=0,
        )

    def put_both(ref, q, cols, value):
        ref[aligned(oth0 + q * ch, ch), cols] = value[:ch]
        ref[aligned(own0 + q * ch, ch), cols] = value[ch:]

    columns = r.vin.shape[0]
    r.vs[...] = jnp.zeros(r.vs.shape, F32)
    r.vs[pl.ds(columns * m, columns), :] = r.vin[...]
    r.vb[0] = r.vs[...].astype(BF)
    swap = remote(r.vb.at[0], r.vb.at[1], r.vxs.at[0], r.vxr.at[0], core_peer)
    swap.start()
    mine = aligned(d * vr, vr)
    r.wa[:, mine, :] = r.attend[...].astype(BF)
    gather_start_y(ATT)
    gather_start_z(ATT)
    r.wr[mine, :] = r.rejoin[...].astype(BF)
    gather_start_y(REJ)
    swap.wait_recv()
    r.vb[2] = r.vb[0] + r.vb[1]
    swap_x = remote(r.vb.at[2], r.vb.at[3], r.vxs.at[1], r.vxr.at[1], x_peer)
    swap_x.start()
    r.we[mine, :] = r.expand[...].astype(BF)
    r.wn[mine, :] = r.narrow[...].astype(BF)
    swap_x.wait_recv()
    r.wv[d] = r.vb[2] + r.vb[3]
    gather_start_y(VEC)

    r.pb[...] = jnp.full(r.pb.shape, SEQ_LEN, jnp.int32)
    slots = r.pos.shape[1]
    r.pb[0:1, 0:slots] = r.pos[...]
    r.pb[8:9, 0:slots] = r.cho[...]
    pos_row = jnp.broadcast_to(r.pb[0:1, :], (SLOTS, SLOTS))
    cho_row = jnp.broadcast_to(r.pb[8:9, :], (SLOTS, SLOTS))
    pos_col = jnp.transpose(pos_row.astype(F32), (1, 0)).astype(jnp.int32)
    cho_col = jnp.transpose(cho_row.astype(F32), (1, 0)).astype(jnp.int32)
    lane_iota = lax.broadcasted_iota(jnp.int32, (SLOTS, LANES), 1)
    row_iota = lax.broadcasted_iota(jnp.int32, (SLOTS, LANES), 0)
    for j in range(rows // LANES):
        r.oh[:, j * LANES : (j + 1) * LANES] = jnp.where(
            pos_col == lane_iota + j * LANES, 1.0, 0.0
        ).astype(BF)
        r.oht[j * LANES : (j + 1) * LANES, :] = jnp.where(
            pos_row == row_iota + j * LANES, 1.0, 0.0
        ).astype(BF)
    r.low2c[...] = jnp.zeros(r.low2c.shape, BF)
    r.low2c[0 : r.table.shape[0], :] = r.table[...]
    choice = jnp.where(cho_col == lane_iota, 1.0, 0.0).astype(BF)
    for j in range(d_model // TILE):
        r.slt[:, j * TILE : (j + 1) * TILE] = nn(
            choice, r.low2c[:, j * TILE : (j + 1) * TILE]
        ).astype(BF)
    r.mc[...] = jnp.zeros(r.mc.shape, BF)
    r.mc[0:slots, :] = r.mcot[...].reshape(slots, d_model)
    r.vg[...] = jnp.zeros(r.vg.shape, F32)

    gather_pass(ATT, 1)
    gather_start_y(EXP)

    def embed(i):
        where = aligned(i * SUB, SUB)
        hot = r.oht[where, :]
        keep = 1.0 - jnp.sum(hot.astype(F32), axis=1, keepdims=True)
        r.keep[where, :] = keep
        r.xl[where, :] = (r.tok[where, :].astype(F32) * keep + nn(hot, r.slt[...])).astype(BF)

    loop(rows // SUB, embed)
    r.st[...] = r.xl[aligned(own0, half), :].astype(F32)

    def transpose_into(target, lane0, source, row0, count):
        for i in range(count // LANES):
            target[:, lane0 + i * LANES : lane0 + (i + 1) * LANES] = low_transpose(
                source[row0 + i * LANES : row0 + (i + 1) * LANES, :]
            )

    for turn in range(2, lines - 1):
        gather_pass(ATT, turn)
    gather_start_z(VEC)
    gather_start_z(REJ)
    gather_pass(ATT, lines - 1)
    gather_start_z(EXP)
    for turn in range(1, lines):
        gather_pass(VEC, turn)
    for turn in range(1, lines):
        gather_pass(REJ, turn)
    gather_wait(VEC)
    gather_pass(EXP, 1)
    gather_wait(ATT)
    gather_start_y(NAR)
    gather_pass(EXP, 2)
    for j in range(n):
        r.vt[:, j * vr : (j + 1) * vr] = r.wv[j].astype(F32)

    def head_bias(row):
        return r.vt[row : row + 1, aligned(m * hw, hw)]

    half_mask = lax.broadcasted_iota(jnp.int32, (1, LANES), 1) < HEAD_DIM

    def lane_half(value, head):
        return jnp.where(half_mask if head % 2 == 0 else jnp.logical_not(half_mask), value, 0)

    def put_heads(ref, q, value):
        for head in range(heads):
            pair = (head // 2) * LANES
            piece = lane_half(value[:, pair : pair + LANES], head)
            ref[head, aligned(oth0 + q * ch, ch), :] = piece[:ch]
            ref[head, aligned(own0 + q * ch, ch), :] = piece[ch:]

    def put_heads_across(ref, q, across):
        for head in range(heads):
            at = (head % 2) * HEAD_DIM
            piece = across[head * HEAD_DIM : (head + 1) * HEAD_DIM, :]
            ref[head, at : at + HEAD_DIM, aligned(oth0 + q * ch, ch)] = piece[:, :ch]
            ref[head, at : at + HEAD_DIM, aligned(own0 + q * ch, ch)] = piece[:, ch:]

    def put_across(ref, q, across):
        ref[:, aligned(oth0 + q * ch, ch)] = across[:, :ch]
        ref[:, aligned(own0 + q * ch, ch)] = across[:, ch:]

    r.qzt[...] = jnp.zeros(r.qzt.shape, BF)

    def share_block(layer, head, lane0, width):
        if layer == 0:
            return r.p0.at[head, :, aligned(lane0, width)]
        return r.gse.at[
            (head // 2) * rows : (head // 2 + 1) * rows,
            aligned((head % 2) * rows + lane0, width),
        ]

    def both_lanes(ref, where, q):
        return jnp.concatenate(
            [ref[where, aligned(oth0 + q * ch, ch)], ref[where, aligned(own0 + q * ch, ch)]],
            axis=1,
        )

    def project(layer, q):
        x = both(r.xl, q)
        queries = (nn(x, r.wa[0]) + head_bias(0)).astype(BF) * jnp.asarray(0.125, BF)
        put_heads(r.qz.at[layer], q, queries)
        put_heads_across(r.qzt.at[layer], q, low_transpose(queries))
        keys = nn(x, r.wa[1]).astype(BF)
        put_both(r.kn.at[layer], q, slice(None), keys)
        put_across(r.kt.at[layer], q, low_transpose(keys))
        values = (nn(x, r.wa[2]) + head_bias(1)).astype(BF)
        put_both(r.vn.at[layer], q, slice(None), values)
        put_across(r.vvt, q, low_transpose(values))

    def attend_forward(layer, q):
        for head in range(heads):
            pair = slice((head // 2) * LANES, (head // 2 + 1) * LANES)
            across = both_lanes(r.qzt.at[layer, head], slice(None), q)
            scores = nn(r.kn[layer, :, pair], across)
            raised = jnp.exp(scores - jnp.max(scores, axis=0, keepdims=True))
            total = jnp.sum(raised, axis=0, keepdims=True)
            low = (raised * (1.0 / total)).astype(BF)
            share_block(layer, head, oth0 + q * ch, ch)[...] = low[:, :ch]
            share_block(layer, head, own0 + q * ch, ch)[...] = low[:, ch:]
            where = slice(head * HEAD_DIM, (head + 1) * HEAD_DIM)
            context = nn(r.vvt[where, :], low).astype(BF)
            r.ct[layer, where, aligned(oth0 + q * ch, ch)] = context[:, :ch]
            r.ct[layer, where, aligned(own0 + q * ch, ch)] = context[:, ch:]
        target = r.ctx if layer == 0 else r.ctx1
        put_both(target, q, slice(None), low_transpose(both_lanes(r.ct.at[layer], slice(None), q)))

    def first_norm(layer, q):
        def one(i):
            at = aligned(q * ch + i * SUB, SUB)
            total = sum_rows(2 * layer, q, aligned(i * SUB, SUB))
            res = r.st[at, :] + (total + r.vt[2:3, :])
            cen = res - jnp.mean(res, axis=1, keepdims=True)
            spread = lax.rsqrt(jnp.mean(cen * cen, axis=1, keepdims=True) + EPS)
            hat = cen * spread
            r.xh1[layer, at, :] = hat
            r.rs1[layer, at, :] = spread
            normed = hat * r.vt[4:5, :] + r.vt[5:6, :]
            r.st[at, :] = normed
            r.normed[aligned(own0 + q * ch + i * SUB, SUB), :] = normed.astype(BF)

        loop(ch // SUB, one)

    def second_norm(layer, q):
        def one(i):
            at = aligned(q * ch + i * SUB, SUB)
            total = sum_rows(2 * layer + 1, q, aligned(i * SUB, SUB))
            res = r.st[at, :] + (total + r.vt[3:4, :])
            cen = res - jnp.mean(res, axis=1, keepdims=True)
            spread = lax.rsqrt(jnp.mean(cen * cen, axis=1, keepdims=True) + EPS)
            hat = cen * spread
            r.xh2[layer, at, :] = hat
            r.rs2[layer, at, :] = spread
            out = hat * r.vt[6:7, :] + r.vt[7:8, :]
            r.st[at, :] = out
            if layer < DEPTH - 1:
                r.xl[aligned(own0 + q * ch + i * SUB, SUB), :] = out.astype(BF)

        loop(ch // SUB, one)

    def unit_act(layer):
        return r.act0 if layer == 0 else r.gsn

    def gelu(v):
        square = v * v
        t = jnp.tanh(GELU_A * v * (1.0 + GELU_B * square))
        return 0.5 * (1.0 + t), t, square

    def gelu_slope(v, gate, t, square):
        return gate + (0.5 * GELU_A) * v * (1.0 - t * t) * (1.0 + (3.0 * GELU_B) * square)

    def widen(layer, q):
        act = unit_act(layer)

        def one(j):
            cols = aligned(j * TILE, TILE)
            v = nn(both(r.normed, q), r.we[:, cols]) + r.vt[pl.ds(8 + m, 1), cols]
            gate, t, square = gelu(v)
            put_both(act, q, cols, (v * gate).astype(BF))
            if layer == 0:
                put_both(r.slope0, q, cols, gelu_slope(v, gate, t, square).astype(BF))

        loop(uw // TILE, one)

    def widen_slots():
        def one(j):
            cols = aligned(j * TILE, TILE)
            v = nn(r.low2c[...], r.we[:, cols]) + r.vt[pl.ds(8 + m, 1), cols]
            gate, t, square = gelu(v)
            r.act0[rows : rows + SLOTS, cols] = (v * gate).astype(BF)
            r.slc[:, cols] = gelu_slope(v, gate, t, square).astype(BF)

        loop(uw // TILE, one)

    def rejoin_sum(layer, q):
        ctx = r.ctx if layer == 0 else r.ctx1
        sum_begin(2 * layer, q, lambda cols: nt(both(ctx, q), r.wr[cols, :]), ch)

    def narrow_sum(layer, q):
        act = unit_act(layer)
        sum_begin(2 * layer + 1, q, lambda cols: nt(both(act, q), r.wn[cols, :]), ch)

    hot = r.oh[...]

    def pick(target, row0, source, source0, width):
        def one(j):
            cols = aligned(j * TILE, TILE)
            target[row0 : row0 + SLOTS, cols] = nn(
                hot, source[source0 : source0 + rows, cols]
            ).astype(BF)

        loop(width // TILE, one)

    by_columns = (2 * vr) % LANES == 0

    def column_core(step):
        cols = aligned((z_from(step) - y) * vr, 2 * vr)
        return remote(
            r.cs.at[1, :, :, cols],
            r.cr.at[1, :, :, cols],
            r.ccs.at[step],
            r.ccr.at[step],
            core_peer,
        )

    def column_x(step):
        cols = aligned((z_from(step) - y) * vr, 2 * vr)
        return remote(
            r.xs.at[1, :, :, cols], r.xr.at[1, :, :, cols], r.cxs.at[step], r.cxr.at[step], x_peer
        )

    def column_sum(step):
        cols = aligned((z_from(step) - y) * vr, 2 * vr)
        weight = r.wn[cols, :]
        away = nt(r.act0[aligned(oth0, half), :], weight).astype(BF)
        for q in range(CHUNKS):
            r.cs[1, q, :, cols] = away[q * ch : (q + 1) * ch]
        column_core(step).start()
        here = nt(r.act0[aligned(own0, half), :], weight)
        column_core(step).wait_recv()
        for q in range(CHUNKS):
            r.xs[1, q, :, cols] = (
                here[q * ch : (q + 1) * ch] + r.cr[1, q, :, cols].astype(F32)
            ).astype(BF)
        column_x(step).start()

    for layer in range(DEPTH):
        for q in range(CHUNKS):
            if layer > 0:
                share_wait(2 * layer - 1, r.xl, q)
            project(layer, q)
        for q in range(CHUNKS):
            attend_forward(layer, q)
            if layer > 0:
                rejoin_sum(layer, q)
            elif q == 0:
                for turn in range(3, lines):
                    gather_pass(EXP, turn)
                gather_start_z(NAR)
        if layer == 0:
            gather_wait(REJ)
            for q in range(CHUNKS):
                rejoin_sum(layer, q)
            gather_pass(NAR, 1)
            transpose_into(r.xt, 0, r.xl, 0, rows)
        else:
            transpose_into(r.xt, rows, r.xl, 0, rows)
        for q in range(CHUNKS):
            sum_end(2 * layer, q, ch)
            first_norm(layer, q)
            share(2 * layer, r.normed, q).start()
            if layer == 0:
                gather_pass(NAR, q + 2)
                if q == 0:
                    gather_wait(EXP)
            share_wait(2 * layer, r.normed, q)
            widen(layer, q)
            if layer > 0:
                narrow_sum(layer, q)
        if layer == 0:
            for turn in range(CHUNKS + 2, lines):
                gather_pass(NAR, turn)
            if by_columns:
                for turn in range(lines):
                    step = gather_order(turn)
                    gather_y_arrival(NAR, step).wait_recv()
                    column_sum(step)
                transpose_into(r.nt, 0, r.normed, 0, rows)
                for step in range(lines):
                    column_x(step).wait()
                    column_core(step).wait_send()
            else:
                transpose_into(r.nt, 0, r.normed, 0, rows)
                gather_wait(NAR)
                for q in range(CHUNKS):
                    narrow_sum(layer, q)
        else:
            pick(r.low2c, 0, r.normed, 0, d_model)
            widen_slots()
            transpose_into(r.nt, rows, r.low2c, 0, SLOTS)
        for q in range(CHUNKS):
            if not (layer == 0 and by_columns):
                sum_end(2 * layer + 1, q, ch)
            second_norm(layer, q)
            if layer < DEPTH - 1:
                share(2 * layer + 1, r.xl, q).start()

    own_rows = aligned(own0, half)
    out_here = pltpu.make_async_copy(r.st, r.act.at[own_rows], r.osem.at[0])
    out_there = remote(r.st, r.act.at[own_rows], r.osem.at[1], r.osem.at[2], core_peer)
    out_arrival = remote(
        r.st, r.act.at[aligned(oth0, half)], r.osem.at[1], r.osem.at[2], core_peer
    )
    out_here.start()
    out_there.start()

    def add_rows(row, value):
        r.vg[row : row + 1, :] += jnp.sum(value, axis=0, keepdims=True)

    def norm_pull(g, hat, spread, gain):
        scaled = g * gain
        mean = jnp.mean(scaled, axis=1, keepdims=True)
        inner = jnp.mean(scaled * hat, axis=1, keepdims=True)
        return spread * (scaled - mean - hat * inner)

    def second_pull(layer, q, gradient):
        def one(i):
            at = aligned(q * ch + i * SUB, SUB)
            g = gradient(i, at)
            hat = r.xh2[layer, at, :]
            add_rows(6, g * hat)
            add_rows(7, g)
            back = norm_pull(g, hat, r.rs2[layer, at, :], r.vt[6:7, :])
            add_rows(3, back)
            r.gb[at, :] = back
            r.low2[aligned(own0 + q * ch + i * SUB, SUB), :] = back.astype(BF)

        loop(ch // SUB, one)

    def first_pull(layer, q, gradient):
        def one(i):
            at = aligned(q * ch + i * SUB, SUB)
            g = gradient(i, at)
            hat = r.xh1[layer, at, :]
            add_rows(4, g * hat)
            add_rows(5, g)
            back = norm_pull(g, hat, r.rs1[layer, at, :], r.vt[4:5, :])
            add_rows(2, back)
            r.gb[at, :] = back
            r.xl[aligned(own0 + q * ch + i * SUB, SUB), :] = back.astype(BF)

        loop(ch // SUB, one)

    def hot_rows(at_start):
        return r.oht[aligned(own0 + at_start, SUB), :]

    def bias_sums(row0):
        for kind, row in ((0, 0), (2, 1)):
            cols = aligned(m * hw, hw)
            r.vg[row : row + 1, cols] += jnp.sum(
                r.dp[kind, row0 : row0 + rows, :].astype(F32), axis=0, keepdims=True
            )

    for q in range(CHUNKS):
        second_pull(1, q, lambda i, at: nn(hot_rows(q * ch + i * SUB), r.mc[...]))
        share(4, r.low2, q).start()
    for q in range(CHUNKS):
        share_wait(4, r.low2, q)
    pick(r.low2c, 0, r.low2, 0, d_model)

    def slot_units(j):
        cols = aligned(j * TILE, TILE)
        back = nn(r.low2c[...], r.wn[:, cols]) * r.slc[:, cols].astype(F32)
        back = back.astype(BF)
        r.be[rows : rows + SLOTS, cols] = back
        r.vg[pl.ds(8 + m, 1), cols] += jnp.sum(back.astype(F32), axis=0, keepdims=True)

    loop(uw // TILE, slot_units)
    slot_own = core * slot_half
    slot_oth = slot_half - slot_own

    def slot_tile(cols):
        part = nt(r.be[rows : rows + SLOTS, :], r.we[cols, :])
        r.part[...] = part
        return jnp.concatenate(
            [
                r.part[aligned(slot_oth, slot_half), :],
                r.part[aligned(slot_own, slot_half), :],
            ],
            axis=0,
        )

    sum_begin(4, 0, slot_tile, slot_half)
    transpose_into(r.l2t, rows, r.low2c, 0, SLOTS)
    for head in range(heads):
        r.qc[head] = nn(hot, r.qz[1, head]).astype(BF)
        source = r.gse[
            (head // 2) * rows : (head // 2 + 1) * rows,
            (head % 2) * rows : (head % 2 + 1) * rows,
        ]
        r.pc[head] = nn(source, r.oht[...]).astype(BF)
    r.cct[...] = nn(r.ct[1], r.oht[...]).astype(BF)
    sum_end(4, 0, slot_half)
    mine_slots = r.slt.at[aligned(slot_own, slot_half)]
    mine_slots[...] = sum_rows(4, 0, slice(0, slot_half)).astype(BF)
    slots_out = remote(mine_slots, mine_slots, r.osem.at[3], r.osem.at[4], core_peer)
    slots_in_ref = r.slt.at[aligned(slot_oth, slot_half)]
    slots_in = remote(slots_in_ref, slots_in_ref, r.osem.at[3], r.osem.at[4], core_peer)
    slots_out.start()
    slots_in.wait_recv()
    for q in range(CHUNKS):
        first_pull(
            1, q, lambda i, at: r.gb[at, :] + nn(hot_rows(q * ch + i * SUB), r.slt[...])
        )
        share(5, r.xl, q).start()

    for q in range(CHUNKS):
        share_wait(5, r.xl, q)
    pick(r.low2c, 0, r.xl, 0, d_model)
    low_ctx = nn(r.low2c[...], r.wr[...]).astype(BF)
    across = low_transpose(low_ctx)
    dq_across = []
    for pair in range(heads // 2):
        lanes = slice(pair * LANES, (pair + 1) * LANES)
        dv = jnp.zeros((rows, LANES), F32)
        dk = jnp.zeros((rows, LANES), F32)
        for head in (2 * pair, 2 * pair + 1):
            where = slice(head * HEAD_DIM, (head + 1) * HEAD_DIM)
            at = (head % 2) * HEAD_DIM
            r.dozt[head, at : at + HEAD_DIM, 0:SLOTS] = across[where, :]
            low = r.pc[head]
            dv += nn(low, lane_half(low_ctx[:, lanes], head))
            dp = nn(r.vn[1, :, lanes], r.dozt[head, :, 0:SLOTS])
            delta = jnp.sum(
                across[where, :].astype(F32) * r.cct[where, :].astype(F32), axis=0, keepdims=True
            )
            ds = (low.astype(F32) * (dp - delta)).astype(BF)
            dk += nn(ds, r.qc[head])
            dq_across.append(nn(r.kt[1, where, :], ds) * 0.125)
        r.dp[1, rows : 2 * rows, lanes] = dk.astype(BF)
        r.dp[2, rows : 2 * rows, lanes] = dv.astype(BF)
    dq = low_transpose(jnp.concatenate(dq_across, axis=0))
    r.dp[0, rows : 2 * rows, :] = nn(r.oht[...], dq).astype(BF)
    bias_sums(rows)

    def layer_rows(k, q, row0):
        def tile_of(cols):
            total = None
            for kind in range(3):
                lhs = jnp.concatenate(
                    [
                        r.dp[kind, aligned(row0 + oth0 + q * ch, ch), :],
                        r.dp[kind, aligned(row0 + own0 + q * ch, ch), :],
                    ],
                    axis=0,
                )
                part = nt(lhs, r.wa[kind, cols, :])
                total = part if total is None else total + part
            return total

        sum_begin(k, q, tile_of, ch)

    for q in range(CHUNKS):
        layer_rows(5, q, rows)
    transpose_into(r.l1t, rows, r.low2c, 0, SLOTS)

    def weight_grad_rows(target, across, latter, width, row0, count):
        at = aligned(row0, count)

        def one(j):
            cols = aligned(j * TILE, TILE)
            target[at, cols] = nn(across[at, :], latter[:, cols]).astype(BF)

        loop(width // TILE, one)

    def weight_grad(target, across, latter, width):
        loop(
            d_model // TILE,
            lambda i: weight_grad_rows(target, across, latter, width, i * TILE, TILE),
        )

    def transpose_both(target, source, q):
        for row0 in (oth0 + q * ch, own0 + q * ch):
            target[:, aligned(row0, ch)] = low_transpose(source[aligned(row0, ch), :])

    def units_back(q):
        def one(j):
            cols = aligned(j * TILE, TILE)
            slope = both(r.slope0, q, cols).astype(F32)
            back = (nn(both(r.low2, q), r.wn[:, cols]) * slope).astype(BF)
            put_both(r.be, q, cols, back)
            r.vg[pl.ds(8 + m, 1), cols] += jnp.sum(back.astype(F32), axis=0, keepdims=True)

        loop(uw // TILE, one)

    for q in range(CHUNKS):
        sum_end(5, q, ch)
        second_pull(
            0, q, lambda i, at: r.gb[at, :] + sum_rows(5, q, aligned(i * SUB, SUB))
        )
        share(6, r.low2, q).start()
        share_wait(6, r.low2, q)
        transpose_both(r.l2t, r.low2, q)
        if q == 0:
            units_back(q)
    if by_columns:
        for turn in range(1, lines + 1):
            owner = ((z + scatter_order(turn)) % lines) * 2 + 1 - y
            weight_grad_rows(r.gsn, r.l2t, r.act0, uw, owner * vr, vr)
            if turn <= 2:
                scatter_y(NAR, scatter_order(turn)).start()
                under_way.append(queue.pop(0))
        ready.append(NAR)
    else:
        weight_grad(r.gsn, r.l2t, r.act0, uw)
        scatter_start(NAR)
    for q in range(CHUNKS):
        if q > 0:
            units_back(q)
        sum_begin(6, q, lambda cols, q=q: nt(both(r.be, q), r.we[cols, :]), ch)
    if by_columns:
        each(
            0,
            lines,
            lambda s: weight_grad_rows(
                r.gsn, r.l2t, r.act0, uw, (((z + s) % lines) * 2 + y) * vr, vr
            ),
        )
    pick(r.ctx, rows, r.ctx1, 0, hw)
    weight_grad(r.gse, r.nt, r.be, uw)
    scatter_start(EXP)
    scatter_pass()
    for q in range(CHUNKS):
        sum_end(6, q, ch)
        first_pull(
            0, q, lambda i, at: r.gb[at, :] + sum_rows(6, q, aligned(i * SUB, SUB))
        )
        share(7, r.xl, q).start()
    scatter_pass()
    for q in range(CHUNKS):
        share_wait(7, r.xl, q)
        back = nn(both(r.xl, q), r.wr[...]).astype(BF)
        put_heads(r.doz, q, back)
        put_heads_across(r.dozt, q, low_transpose(back))

    def head_pair(pair):
        lanes = aligned(pair * LANES, LANES)
        dv = jnp.zeros((rows, LANES), F32)
        dk = jnp.zeros((rows, LANES), F32)
        for side in range(2):
            head = 2 * pair + side
            where = aligned(head * HEAD_DIM, HEAD_DIM)
            for part in range(rows // TILE):
                some = slice(part * TILE, (part + 1) * TILE)
                low = r.p0[head, :, some]
                dv += nn(low, r.doz[head, some, :])
                inner = r.dozt[head, side * HEAD_DIM : (side + 1) * HEAD_DIM, some]
                delta = jnp.sum(
                    inner.astype(F32) * r.ct[0, where, some].astype(F32), axis=0, keepdims=True
                )
                dp = nn(r.vn[0, :, lanes], r.dozt[head, :, some])
                ds = (low.astype(F32) * (dp - delta)).astype(BF)
                dk += nn(ds, r.qz[0, head, some, :])
                r.dqt[where, some] = (nn(r.kt[0, where, :], ds) * 0.125).astype(BF)
        r.dp[1, 0:rows, lanes] = dk.astype(BF)
        r.dp[2, 0:rows, lanes] = dv.astype(BF)

    for pair in range(heads // 2):
        head_pair(pair)
        if under_way[0][0] != REJ:
            scatter_pass()
    for i in range(rows // LANES):
        some = slice(i * LANES, (i + 1) * LANES)
        r.dp[0, some, :] = low_transpose(r.dqt[:, some])
    for q in range(CHUNKS):
        layer_rows(7, q, 0)
    if under_way[0][0] != REJ:
        scatter_pass()
    bias_sums(0)
    transpose_into(r.l1t, 0, r.xl, 0, rows)
    weight_grad(r.gsr, r.l1t, r.ctx, hw)
    scatter_start(REJ)
    first_of_x = jnp.where(m < 2, 1.0, 0.0)
    r.vg[2:8, :] = r.vg[2:8, :] * first_of_x
    for j in range(n):
        r.gsv[j] = r.vg[:, j * vr : (j + 1) * vr].astype(BF)
    scatter_start(VEC)
    for kind in range(3):
        weight_grad(r.gsa.at[kind], r.xt, r.dp.at[kind], hw)
    scatter_start(ATT)
    scatter_pass()
    out_here.wait()
    out_there.wait_send()
    for q in range(CHUNKS):
        sum_end(7, q, ch)

        def last(i, q=q):
            at = aligned(q * ch + i * SUB, SUB)
            g = r.gb[at, :] + sum_rows(7, q, aligned(i * SUB, SUB))
            r.st[at, :] = g * r.keep[aligned(own0 + q * ch + i * SUB, SUB), :]

        loop(ch // SUB, last)
    in_here = pltpu.make_async_copy(r.st, r.ing.at[own_rows], r.osem.at[5])
    in_there = remote(r.st, r.ing.at[own_rows], r.osem.at[6], r.osem.at[7], core_peer)
    in_arrival = remote(r.st, r.ing.at[aligned(oth0, half)], r.osem.at[6], r.osem.at[7], core_peer)
    in_here.start()
    in_there.start()

    scatter_pass()
    def squares(value):
        value = value * value
        if value.ndim == 3:
            value = jnp.sum(value, axis=0)
        value = jnp.sum(value, axis=0, keepdims=True)
        return jnp.sum(value, axis=1, keepdims=True)

    swap_v = remote(r.vf.at[0], r.vf.at[1], r.vxs.at[2], r.vxr.at[2], core_peer)
    swap_w = remote(r.vf.at[2], r.vf.at[3], r.vxs.at[3], r.vxr.at[3], x_peer)
    total = jnp.zeros((1, 1), F32)
    while under_way:
        turn = under_way[0][1] if under_way[0][0] == ATT else 0
        if turn == 1:
            scatter_finish(NAR, r.gn)
            total = total + squares(r.gn[...])
            scatter_close(NAR)
            for region in range(5):
                gather_close(region)
        elif turn == 2:
            scatter_finish(VEC, r.vf.at[0])
            swap_v.start()
            scatter_finish(REJ, r.gr)
            total = total + squares(r.gr[...])
        elif turn == 3:
            swap_v.wait_recv()
            r.vf[2] = r.vf[0] + r.vf[1]
            swap_w.start()
            scatter_finish(EXP, r.ge)
            total = total + squares(r.ge[...])
            scatter_close(EXP)
            scatter_close(REJ)
        elif turn == 4:
            swap_w.wait_recv()
            r.vs[...] = r.vf[2] + r.vf[3]
            r.gv[...] = r.vs[pl.ds(columns * m, columns), :]
            total = total + squares(r.gv[...])
        scatter_pass()
    scatter_finish(ATT, r.ga)
    total = total + squares(r.ga[...])

    r.nm[m] = jnp.broadcast_to(total, (8, LANES))

    def model_copy(k, slot):
        return remote(r.nm.at[slot], r.nm.at[slot], r.nms.at[k], r.nmr.at[k], model_peers[k])

    for k in range(3):
        model_copy(k, m).start()
    for k in range(3):
        model_copy(k, model_peers[k][1]).wait_recv()
    r.nz[d] = jnp.sum(r.nm[...], axis=0)

    def line_copy(step, slot):
        here = r.nz.at[slot]
        return remote(here, here, r.nzs.at[0, step], r.nzr.at[0, step], z_peer(step))

    def cross_copy(step, slot):
        here = r.nz.at[slot]
        return remote(here, here, r.nzs.at[1, step], r.nzr.at[1, step], zy_peer(step))

    each(0, lines, lambda s: cross_copy(s, d).start())
    each(1, lines, lambda s: line_copy(s, d).start())
    each(0, lines, lambda s: cross_copy(s, z_from(s) + 1 - 2 * y).wait_recv())
    each(1, lines, lambda s: line_copy(s, z_from(s)).wait_recv())
    r.norm[...] = jnp.sqrt(jnp.sum(r.nz[...], axis=0))

    each(0, lines, lambda s: cross_copy(s, d).wait_send())
    each(1, lines, lambda s: line_copy(s, d).wait_send())
    for k in range(3):
        model_copy(k, m).wait_send()
    swap.wait_send()
    swap_x.wait_send()
    swap_v.wait_send()
    swap_w.wait_send()
    slots_out.wait_send()
    scatter_close(VEC)
    scatter_close(ATT)
    out_arrival.wait_recv()
    in_here.wait()
    in_there.wait_send()
    in_arrival.wait_recv()


def run_layers(
    n, tok, pos, cho, table, mcot, attend, rejoin, expand, narrow, vin
):
    rows, d_model = tok.shape
    vr = rejoin.shape[0]
    hw = rejoin.shape[1]
    uw = expand.shape[1]
    lines = n // 2
    half = rows // 2
    ch = half // CHUNKS
    heads = hw // HEAD_DIM
    wide = rows + SLOTS
    inputs = [
        ("tok", tok),
        ("pos", pos),
        ("cho", cho),
        ("table", table),
        ("mcot", mcot),
        ("attend", attend),
        ("rejoin", rejoin),
        ("expand", expand),
        ("narrow", narrow),
        ("vin", vin),
    ]
    outputs = [
        ("act", (rows, d_model), pl.ANY),
        ("ing", (rows, d_model), pl.ANY),
        ("ga", (3, vr, hw), pltpu.VMEM),
        ("gr", (vr, hw), pltpu.VMEM),
        ("ge", (vr, uw), pltpu.VMEM),
        ("gn", (vr, uw), pltpu.VMEM),
        ("gv", vin.shape, pltpu.VMEM),
        ("norm", (8, LANES), pltpu.VMEM),
    ]
    low = [
        ("wv", (n, 16, vr)),
        ("wa", (3, d_model, hw)),
        ("wr", (d_model, hw)),
        ("we", (d_model, uw)),
        ("wn", (d_model, uw)),
        ("gsv", (n, 16, vr)),
        ("gsa", (3, d_model, hw)),
        ("gsr", (d_model, hw)),
        ("gse", (d_model, uw)),
        ("gsn", (d_model, uw)),
        ("yv", (lines, 16, vr)),
        ("ya", (lines, 3, vr, hw)),
        ("yr", (lines, vr, hw)),
        ("ye", (lines, vr, uw)),
        ("yn", (lines, vr, uw)),
        ("zv", (lines, 16, vr)),
        ("za", (lines, 3, vr, hw)),
        ("zr", (lines, vr, hw)),
        ("ze", (lines, vr, uw)),
        ("zn", (lines, vr, uw)),
        ("cs", (2, CHUNKS, ch, d_model)),
        ("cr", (2, CHUNKS, ch, d_model)),
        ("xs", (2, CHUNKS, ch, d_model)),
        ("xr", (2, CHUNKS, ch, d_model)),
        ("vb", (4, 16, vr)),
        ("oh", (SLOTS, rows)),
        ("oht", (rows, SLOTS)),
        ("mc", (SLOTS, d_model)),
        ("xl", (rows, d_model)),
        ("normed", (rows, d_model)),
        ("low2", (rows, d_model)),
        ("xt", (d_model, 2 * rows)),
        ("nt", (d_model, wide)),
        ("l2t", (d_model, wide)),
        ("l1t", (d_model, wide)),
        ("act0", (wide, uw)),
        ("slope0", (rows, uw)),
        ("be", (wide, uw)),
        ("ctx", (wide, hw)),
        ("ctx1", (rows, hw)),
        ("dp", (3, 2 * rows, hw)),
        ("qz", (2, heads, rows, LANES)),
        ("qzt", (2, heads, LANES, rows)),
        ("kn", (2, rows, hw)),
        ("kt", (2, hw, rows)),
        ("vn", (2, rows, hw)),
        ("vvt", (hw, rows)),
        ("ct", (2, hw, rows)),
        ("p0", (heads, rows, rows)),
        ("dqt", (hw, rows)),
        ("slc", (SLOTS, uw)),
        ("low2c", (SLOTS, d_model)),
        ("slt", (SLOTS, d_model)),
        ("qc", (heads, SLOTS, LANES)),
        ("pc", (heads, rows, SLOTS)),
        ("cct", (hw, SLOTS)),
    ]
    full = [
        ("vt", (16, d_model)),
        ("vg", (16, d_model)),
        ("keep", (rows, 1)),
        ("st", (half, d_model)),
        ("gb", (half, d_model)),
        ("xh1", (2, half, d_model)),
        ("xh2", (2, half, d_model)),
        ("rs1", (2, half, 1)),
        ("rs2", (2, half, 1)),
        ("acc", (ch, d_model)),
        ("part", (SLOTS, TILE)),
        ("vf", (4, 16, vr)),
        ("vs", (16, vr)),
        ("nm", (4, 8, LANES)),
        ("nz", (n, 8, LANES)),
    ]
    sems = [
        ("agzs", (5, lines + 3)),
        ("agzr", (5, lines)),
        ("agys", (5, lines)),
        ("agyr", (5, lines)),
        ("rsys", (5, lines)),
        ("rsyr", (5, lines)),
        ("rszs", (5, lines)),
        ("rszr", (5, lines)),
        ("arcs", (8, CHUNKS, d_model // TILE)),
        ("arcr", (8, CHUNKS, d_model // TILE)),
        ("arxs", (8, CHUNKS, d_model // TILE)),
        ("arxr", (8, CHUNKS, d_model // TILE)),
        ("shs", (8, CHUNKS)),
        ("shr", (8, CHUNKS)),
        ("vxs", (4,)),
        ("vxr", (4,)),
        ("osem", (8,)),
        ("nms", (3,)),
        ("nmr", (3,)),
        ("nzs", (2, lines)),
        ("nzr", (2, lines)),
        ("ccs", (lines,)),
        ("ccr", (lines,)),
        ("cxs", (lines,)),
        ("cxr", (lines,)),
    ]
    names = (
        [name for name, _ in inputs]
        + [name for name, _, _ in outputs]
        + [name for name, _ in low]
        + [name for name, _ in full]
        + ["pb"]
        + [name for name, _ in sems]
    )
    sizes = (n, d_model, rows, hw, uw, vr)

    def body(*refs):
        layer_kernel(names, sizes, *refs)

    return pl.pallas_call(
        body,
        out_shape=[jax.ShapeDtypeStruct(shape, F32) for _, shape, _ in outputs],
        in_specs=[pl.BlockSpec(memory_space=pltpu.VMEM)] * len(inputs),
        out_specs=[pl.BlockSpec(memory_space=space) for _, _, space in outputs],
        scratch_shapes=[pltpu.VMEM(shape, BF) for _, shape in low]
        + [pltpu.VMEM(shape, F32) for _, shape in full]
        + [pltpu.VMEM((16, LANES), jnp.int32)]
        + [pltpu.SemaphoreType.DMA(shape) for _, shape in sems],
        compiler_params=pltpu.CompilerParams(
            collective_id=0, has_side_effects=True, vmem_limit_bytes=61 * 1024 * 1024
        ),
        cost_estimate=pl.CostEstimate(
            flops=20_000_000_000, bytes_accessed=20_000_000, transcendentals=4_000_000
        ),
    )(*[value for _, value in inputs])


def apply_update(weight, first_moment, second_moment, shadow, gradient, step_rate):
    momentum = 0.5 * first_moment + 0.5 * gradient
    variance = 0.5 * second_moment + 0.5 * gradient * gradient
    bias_fix = 1.0 - 0.5**STEP
    updated = weight - step_rate * (
        momentum / bias_fix / (jnp.sqrt(variance / bias_fix) + 1e-08) + 0.01 * weight
    )
    average = 0.999 * shadow + 0.001 * updated
    return (updated, momentum, variance, average, updated.astype(BF))


def update_kernel(rates, clip_limit, norm, act, ing, *refs):
    *refs, norm_out, act_out, ing_out = refs
    act_out[...] = act[...]
    ing_out[...] = ing[...]
    norm_out[...] = norm[0:1, 0:1]
    factor = jnp.minimum(1.0, clip_limit / (norm[0:1, 0:1] + 1e-06))
    ins, outs = refs[: 5 * len(rates)], refs[5 * len(rates) :]
    for index, rate in enumerate(rates):
        weight, first, second, shadow, gradient = ins[5 * index : 5 * index + 5]
        targets = outs[5 * index : 5 * index + 5]
        for part in range(weight.shape[0]) if len(weight.shape) == 3 else (slice(None),):
            results = apply_update(
                weight[part],
                first[part],
                second[part],
                shadow[part],
                gradient[part] * factor,
                rate,
            )
            for target, value in zip(targets, results, strict=True):
                target[part] = value


def run_update(groups, rates, norm, clip_limit, act, ing):
    vr = groups[1][0].shape[0]
    step = min(vr, 64)

    def spec(shape, whole):
        if whole:
            return pl.BlockSpec(shape, lambda i: (0, 0))
        if len(shape) == 3:
            return pl.BlockSpec((shape[0], step, shape[2]), lambda i: (0, i, 0))
        return pl.BlockSpec((step, shape[1]), lambda i: (i, 0))

    last = len(groups) - 1
    passed = pl.BlockSpec((act.shape[0] * step // vr, act.shape[1]), lambda i: (i, 0))
    specs = [spec(group[0].shape, k == last) for k, group in enumerate(groups)]

    def body(*refs):
        update_kernel(rates, clip_limit, *refs)

    flat = [value for group in groups for value in group]
    size = sum(value.size for value in flat) * 4
    outs = pl.pallas_call(
        body,
        grid=(vr // step,),
        in_specs=[spec(norm.shape, True)]
        + [passed] * 2
        + [one for one in specs for _ in range(5)],
        out_specs=[one for one in specs for _ in range(5)]
        + [spec((1, 1), True)]
        + [passed] * 2,
        out_shape=[
            jax.ShapeDtypeStruct(group[0].shape, kind)
            for group in groups
            for kind in (F32, F32, F32, F32, BF)
        ]
        + [jax.ShapeDtypeStruct(shape, F32) for shape in ((1, 1), act.shape, ing.shape)],
        compiler_params=pltpu.CompilerParams(vmem_limit_bytes=60 * 1024 * 1024),
        cost_estimate=pl.CostEstimate(flops=size, bytes_accessed=2 * size, transcendentals=0),
    )(norm, act, ing, *flat)
    groups_out = [outs[5 * k : 5 * k + 5] for k in range(len(groups))]
    return groups_out, outs[-3].reshape(()), *outs[-2:]


def per_device(
    tokens_in,
    masked_positions,
    replace_choice,
    replace_table,
    masked_cotangent,
    attend,
    attend_mean,
    attend_square,
    attend_shadow,
    rejoin,
    rejoin_mean,
    rejoin_square,
    rejoin_shadow,
    expand,
    expand_mean,
    expand_square,
    expand_shadow,
    narrow,
    narrow_mean,
    narrow_square,
    narrow_shadow,
    vectors,
    vectors_mean,
    vectors_square,
    vectors_shadow,
):
    n = lax.axis_size("dp")
    act, ing, ga, gr, ge, gn, gv, norm = run_layers(
        n,
        tokens_in,
        masked_positions,
        replace_choice,
        replace_table,
        masked_cotangent,
        attend.transpose(1, 0, 2),
        rejoin,
        expand,
        narrow,
        vectors.T,
    )
    d_model = tokens_in.shape[1]
    param_count = 4 * d_model * d_model + 2 * d_model * expand.shape[1] * 4 + 12 * d_model
    clip_limit = 0.001 * math.sqrt(param_count * tokens_in.shape[0] * n)
    cubes = [x.transpose(1, 0, 2) for x in (attend, attend_mean, attend_square, attend_shadow)]
    rows_of = [x.T for x in (vectors, vectors_mean, vectors_square, vectors_shadow)]
    new, gradient_norm, act, ing = run_update(
        (
            (*cubes, ga),
            (rejoin, rejoin_mean, rejoin_square, rejoin_shadow, gr),
            (expand, expand_mean, expand_square, expand_shadow, ge),
            (narrow, narrow_mean, narrow_square, narrow_shadow, gn),
            (*rows_of, gv),
        ),
        (0.04, 0.16, 0.04, 0.04, 0.5),
        norm,
        clip_limit,
        act,
        ing,
    )
    results = [act, ing, gradient_norm]
    results.extend(x.transpose(1, 0, 2) for x in new[0])
    for group in new[1:4]:
        results.extend(group)
    results.extend(x.T for x in new[4])
    return tuple(results)


def solution(mesh):
    row = P("dp", None)
    cube = P("dp", None, "mp")
    flat = P("dp", "mp")
    return jax.shard_map(
        per_device,
        mesh=mesh,
        in_specs=(row, row, row, P(), P("dp", None, None)) + (cube,) * 4 + (flat,) * 16,
        out_specs=(row, row, P()) + (cube,) * 5 + (flat,) * 20,
        check_vma=False,
    )
```

```python
import math
from types import SimpleNamespace

import jax
import jax.numpy as jnp
from jax import lax
from jax.experimental import pallas as pl
from jax.experimental.pallas import tpu as pltpu
from jax.sharding import PartitionSpec as P

HEAD_DIM = 64
SEQ_LEN = 512
DEPTH = 2
STEP = 7
EPS = 1e-05
BF = jnp.bfloat16
F32 = jnp.float32
MESH = pl.DeviceIdType.MESH
LANES = 128
TILE = 256
SLOTS = 128
CHUNKS = 2
SUB = 64
VEC, ATT, REJ, EXP, NAR = range(5)
GELU_A = 0.7978845608028654
GELU_B = 0.044715


def nn(former, latter):
    return jnp.dot(former, latter, preferred_element_type=F32)


def nt(former, latter):
    return lax.dot_general(former, latter, (((1,), (1,)), ((), ())), preferred_element_type=F32)


def low_transpose(block):
    return jnp.transpose(block.astype(F32), (1, 0)).astype(BF)


def loop(count, body):
    def step(index, carry):
        body(index)
        return carry

    lax.fori_loop(0, count, step, 0)


def each(first, last, body):
    if last - first <= 8:
        for index in range(first, last):
            body(index)
    else:

        def step(index, carry):
            body(index)
            return carry

        lax.fori_loop(first, last, step, 0)


def aligned(index, size):
    return pl.ds(pl.multiple_of(index, size), size)


def layer_kernel(names, sizes, *refs):
    r = SimpleNamespace(**dict(zip(names, refs, strict=True)))
    n, d_model, rows, hw, uw, vr = sizes
    r.doz, r.dozt = r.qz.at[1], r.qzt.at[1]
    half = rows // 2
    ch = half // CHUNKS
    lines = n // 2
    heads = hw // HEAD_DIM
    slot_half = SLOTS // 2

    d = lax.axis_index("dp")
    m = lax.axis_index("mp")
    z, y = d // 2, d % 2
    core = m % 2
    core_peer = (d, m + 1 - 2 * core)
    x_peer = (d, (m + 2) % 4)
    y_peer = (d + 1 - 2 * y, m)
    model_peers = (core_peer, x_peer, (d, 3 - m))
    own0 = core * half
    oth0 = half - own0

    weights = (r.wv, r.wa, r.wr, r.we, r.wn)
    grads = (r.gsv, r.gsa, r.gsr, r.gse, r.gsn)
    from_y = (r.yv, r.ya, r.yr, r.ye, r.yn)
    from_z = (r.zv, r.za, r.zr, r.ze, r.zn)

    def z_peer(step):
        return (((z + step) % lines) * 2 + y, m)

    def zy_peer(step):
        return (((z + step) % lines) * 2 + 1 - y, m)

    def z_from(step):
        return ((z + lines - step) % lines) * 2 + y

    def block(ref, region, index):
        if region == VEC:
            return ref.at[index]
        where = aligned(index * vr, vr)
        return ref.at[:, where, :] if region == ATT else ref.at[where, :]

    def remote(source, target, send, recv, device):
        return pltpu.make_async_remote_copy(
            src_ref=source,
            dst_ref=target,
            send_sem=send,
            recv_sem=recv,
            device_id=device,
            device_id_type=MESH,
        )

    barrier = pltpu.get_barrier_semaphore()

    def greet(peer):
        pl.semaphore_signal(barrier, inc=1, device_id=peer, device_id_type=MESH)

    for peer in model_peers:
        greet(peer)
    each(1, lines, lambda s: greet(z_peer(s)))
    each(0, lines, lambda s: greet(zy_peer(s)))

    relay = lines == 4
    last_line = lines - 1
    inner = jnp.logical_and(z > 0, z < last_line)
    far_end = (jnp.where(z == 1, 0, last_line) * 2 + y, m)
    near_mid = (jnp.where(z == 0, 1, last_line - 1) * 2 + y, m)

    def gather_z(region, step):
        piece = block(weights[region], region, d)
        return remote(
            piece, piece, r.agzs.at[region, step], r.agzr.at[region, step], z_peer(step)
        )

    def gather_z_arrival(region, step):
        piece = block(weights[region], region, z_from(step))
        return remote(
            piece, piece, r.agzs.at[region, step], r.agzr.at[region, step], z_peer(step)
        )

    def gather_onward(region, turn):
        piece = block(weights[region], region, z_from(gather_order(turn)))
        if turn == 3:
            target = far_end
            arrives_as = jnp.where(z == 1, 1, last_line)
        else:
            target = ((z + 3 - 2 * turn) * 2 + y, m)
            arrives_as = 2
        return remote(
            piece,
            piece,
            r.agzs.at[region, last_line + turn],
            r.agzr.at[region, arrives_as],
            target,
        )

    def gather_y(region, step):
        piece = block(weights[region], region, z_from(step))
        return remote(piece, piece, r.agys.at[region, step], r.agyr.at[region, step], y_peer)

    def gather_y_arrival(region, step):
        piece = block(weights[region], region, z_from(step) + 1 - 2 * y)
        return remote(piece, piece, r.agys.at[region, step], r.agyr.at[region, step], y_peer)

    def near(step, body):
        if not relay:
            body()
        elif step != 2:
            pl.when(z < last_line if step == 1 else z > 0)(body)

    def gather_start_z(region):
        for step in range(1, lines):
            near(step, lambda: gather_z(region, step).start())

    def gather_start_y(region):
        gather_y(region, 0).start()

    def gather_order(turn):
        if not relay or turn == 0:
            return turn
        if turn == 1:
            return jnp.where(z == 0, last_line, 1)
        if turn == 2:
            return jnp.where(inner, last_line, 2)
        return jnp.where(inner, 2, jnp.where(z == 0, 1, last_line))

    def gather_pass(region, turn):
        step = gather_order(turn)
        gather_z_arrival(region, step).wait_recv()
        if relay:
            pl.when(inner)(lambda: gather_onward(region, turn).start())
        gather_y(region, step).start()

    def gather_wait(region):
        each(0, lines, lambda s: gather_y_arrival(region, s).wait_recv())

    def gather_close(region):
        for step in range(1, lines):
            near(step, lambda: gather_z(region, step).wait_send())
        if relay:
            for turn in range(1, lines):
                pl.when(inner)(lambda: gather_onward(region, turn).wait_send())
        each(0, lines, lambda s: gather_y(region, s).wait_send())

    def scatter_y(region, step):
        owner = ((z + step) % lines) * 2 + 1 - y
        return remote(
            block(grads[region], region, owner),
            from_y[region].at[step],
            r.rsys.at[region, step],
            r.rsyr.at[region, step],
            y_peer,
        )

    def scatter_z(region, step):
        owner = ((z + step) % lines) * 2 + y
        return remote(
            block(grads[region], region, owner),
            from_z[region].at[step],
            r.rszs.at[region, step],
            r.rszr.at[region, step],
            z_peer(step),
        )

    def scatter_far(region, step):
        owner = ((z + step) % lines) * 2 + y
        return remote(
            block(grads[region], region, owner),
            from_z[region].at[0],
            r.rszs.at[region, step],
            r.rszr.at[region, 0],
            near_mid,
        )

    def scatter_order(turn):
        if not relay:
            return turn % lines
        if turn == 1:
            return jnp.where(z == 0, last_line, 1)
        if turn == 2:
            return jnp.where(z == 0, 1, last_line)
        return 2 if turn == 3 else 0

    def scatter_cross(step):
        owner = ((z + step) % lines) * 2 + 1 - y
        return remote(
            block(grads[REJ], REJ, owner),
            from_y[REJ].at[step],
            r.rsys.at[REJ, step],
            r.rsyr.at[REJ, step],
            z_peer(step),
        )

    def scatter_turn():
        piece = block(grads[REJ], REJ, d + 1 - 2 * y)
        total = piece[...].astype(F32)
        for step in range(1, lines):
            scatter_cross(step).wait_recv()
            total = total + from_y[REJ][step].astype(F32)
        piece[...] = total.astype(BF)
        scatter_y(REJ, 0).start()

    def scatter_start(region):
        if region == REJ:
            each(1, lines, lambda s: scatter_z(REJ, s).start())
            each(1, lines, lambda s: scatter_cross(s).start())
            return
        ready.append(region)
        scatter_next()

    ready = []
    order = (NAR, EXP, VEC, ATT)
    queue = [(region, turn) for region in order for turn in range(1, lines + 1)]
    under_way = []
    weight_of = {NAR: 4, EXP: 4, ATT: 3, VEC: 1}

    def scatter_next():
        while queue and queue[0][0] in ready:
            if sum(weight_of[region] for region, _ in under_way) > 4:
                break
            region, turn = queue.pop(0)
            scatter_y(region, scatter_order(turn)).start()
            under_way.append((region, turn))

    def scatter_pass():
        region, turn = under_way[0]
        step = scatter_order(turn)
        scatter_y(region, step).wait_recv()
        under_way.pop(0)
        scatter_next()
        if turn == lines:
            return
        piece = block(grads[region], region, ((z + step) % lines) * 2 + y)
        total = piece[...].astype(F32) + from_y[region][step].astype(F32)
        piece[...] = total.astype(BF)
        if not relay:
            scatter_z(region, step).start()
        elif turn == 1:
            pl.when(inner)(lambda: scatter_z(region, step).start())
            pl.when(jnp.logical_not(inner))(lambda: scatter_far(region, step).start())
        elif turn == 2:
            scatter_z(region, step).start()
        else:

            @pl.when(inner)
            def _():
                scatter_far(region, 0).wait_recv()
                piece[...] = (total + from_z[region][0].astype(F32)).astype(BF)

            scatter_z(region, step).start()

    def scatter_finish(region, out_ref):
        def one(step):
            scatter_z(region, step).wait_recv()
            out_ref[...] += from_z[region][step].astype(F32)

        if region == REJ:
            scatter_y(region, 0).wait_recv()
        piece = block(grads[region], region, d)
        out_ref[...] = piece[...].astype(F32) + from_y[region][0].astype(F32)
        for step in range(1, lines):
            if not relay or region == REJ or step == 2:
                one(step)
            else:
                pl.when(z > 0 if step == 1 else z < last_line)(lambda: one(step))

    def scatter_close(region):
        each(0, lines, lambda s: scatter_y(region, s).wait_send())
        each(1, lines, lambda s: scatter_z(region, s).wait_send())

    tiles = d_model // TILE

    def core_copy(k, q, count, j):
        where = (k % 2, q, slice(0, count), aligned(j * TILE, TILE))
        return remote(
            r.cs.at[where], r.cr.at[where], r.arcs.at[k, q, j], r.arcr.at[k, q, j], core_peer
        )

    def x_copy(k, q, count, j):
        where = (k % 2, q, slice(0, count), aligned(j * TILE, TILE))
        return remote(
            r.xs.at[where], r.xr.at[where], r.arxs.at[k, q, j], r.arxr.at[k, q, j], x_peer
        )

    def sum_begin(k, q, tile_of, count):
        b = k % 2

        def onward(j):
            cols = aligned(j * TILE, TILE)
            core_copy(k, q, count, j).wait_recv()
            r.xs[b, q, :count, cols] = (
                r.acc[:count, cols] + r.cr[b, q, :count, cols].astype(F32)
            ).astype(BF)
            x_copy(k, q, count, j).start()

        def one(j):
            cols = aligned(j * TILE, TILE)
            part = tile_of(cols)
            r.cs[b, q, :count, cols] = part[:count].astype(BF)
            core_copy(k, q, count, j).start()
            r.acc[:count, cols] = part[count:]
            pl.when(j > 0)(lambda: onward(j - 1))

        loop(tiles, one)
        onward(tiles - 1)

    def sum_end(k, q, count):
        for j in range(tiles):
            x_copy(k, q, count, j).wait()
            core_copy(k, q, count, j).wait_send()

    def sum_rows(k, q, where):
        b = k % 2
        return r.xs[b, q, where].astype(F32) + r.xr[b, q, where].astype(F32)

    def share(k, ref, q):
        where = aligned(own0 + q * ch, ch)
        return remote(ref.at[where], ref.at[where], r.shs.at[k, q], r.shr.at[k, q], core_peer)

    def share_arrival(k, ref, q):
        where = aligned(oth0 + q * ch, ch)
        return remote(ref.at[where], ref.at[where], r.shs.at[k, q], r.shr.at[k, q], core_peer)

    def share_wait(k, ref, q):
        share(k, ref, q).wait_send()
        share_arrival(k, ref, q).wait_recv()

    def both(ref, q, cols=slice(None)):
        return jnp.concatenate(
            [ref[aligned(oth0 + q * ch, ch), cols], ref[aligned(own0 + q * ch, ch), cols]],
            axis=0,
        )

    def put_both(ref, q, cols, value):
        ref[aligned(oth0 + q * ch, ch), cols] = value[:ch]
        ref[aligned(own0 + q * ch, ch), cols] = value[ch:]

    columns = r.vin.shape[0]
    r.vs[...] = jnp.zeros(r.vs.shape, F32)
    r.vs[pl.ds(columns * m, columns), :] = r.vin[...]
    r.vb[0] = r.vs[...].astype(BF)
    mine = aligned(d * vr, vr)
    r.wa[:, mine, :] = r.attend[...].astype(BF)
    r.wr[mine, :] = r.rejoin[...].astype(BF)
    pl.semaphore_wait(barrier, len(model_peers) + n - 1)
    swap = remote(r.vb.at[0], r.vb.at[1], r.vxs.at[0], r.vxr.at[0], core_peer)
    swap.start()
    gather_start_y(ATT)
    gather_start_z(ATT)
    gather_start_y(REJ)
    swap.wait_recv()
    r.vb[2] = r.vb[0] + r.vb[1]
    swap_x = remote(r.vb.at[2], r.vb.at[3], r.vxs.at[1], r.vxr.at[1], x_peer)
    swap_x.start()
    r.we[mine, :] = r.expand[...].astype(BF)
    r.wn[mine, :] = r.narrow[...].astype(BF)
    swap_x.wait_recv()
    r.wv[d] = r.vb[2] + r.vb[3]
    gather_start_y(VEC)

    r.pb[...] = jnp.full(r.pb.shape, SEQ_LEN, jnp.int32)
    slots = r.pos.shape[1]
    r.pb[0:1, 0:slots] = r.pos[...]
    r.pb[8:9, 0:slots] = r.cho[...]
    pos_row = jnp.broadcast_to(r.pb[0:1, :], (SLOTS, SLOTS))
    cho_row = jnp.broadcast_to(r.pb[8:9, :], (SLOTS, SLOTS))
    pos_col = jnp.transpose(pos_row.astype(F32), (1, 0)).astype(jnp.int32)
    cho_col = jnp.transpose(cho_row.astype(F32), (1, 0)).astype(jnp.int32)
    lane_iota = lax.broadcasted_iota(jnp.int32, (SLOTS, LANES), 1)
    row_iota = lax.broadcasted_iota(jnp.int32, (SLOTS, LANES), 0)
    for j in range(rows // LANES):
        r.oh[:, j * LANES : (j + 1) * LANES] = jnp.where(
            pos_col == lane_iota + j * LANES, 1.0, 0.0
        ).astype(BF)
        r.oht[j * LANES : (j + 1) * LANES, :] = jnp.where(
            pos_row == row_iota + j * LANES, 1.0, 0.0
        ).astype(BF)
    r.low2c[...] = jnp.zeros(r.low2c.shape, BF)
    r.low2c[0 : r.table.shape[0], :] = r.table[...]
    choice = jnp.where(cho_col == lane_iota, 1.0, 0.0).astype(BF)
    for j in range(d_model // TILE):
        r.slt[:, j * TILE : (j + 1) * TILE] = nn(
            choice, r.low2c[:, j * TILE : (j + 1) * TILE]
        ).astype(BF)
    r.mc[...] = jnp.zeros(r.mc.shape, BF)
    r.mc[0:slots, :] = r.mcot[...].reshape(slots, d_model)
    r.vg[...] = jnp.zeros(r.vg.shape, F32)

    gather_pass(ATT, 1)
    gather_start_y(EXP)

    def embed(i):
        where = aligned(i * SUB, SUB)
        hot = r.oht[where, :]
        keep = 1.0 - jnp.sum(hot.astype(F32), axis=1, keepdims=True)
        r.keep[where, :] = keep
        r.xl[where, :] = (r.tok[where, :].astype(F32) * keep + nn(hot, r.slt[...])).astype(BF)

    loop(rows // SUB, embed)
    r.st[...] = r.xl[aligned(own0, half), :].astype(F32)

    def transpose_into(target, lane0, source, row0, count):
        for i in range(count // LANES):
            target[:, lane0 + i * LANES : lane0 + (i + 1) * LANES] = low_transpose(
                source[row0 + i * LANES : row0 + (i + 1) * LANES, :]
            )

    for turn in range(2, lines - 1):
        gather_pass(ATT, turn)
    gather_start_z(VEC)
    gather_start_z(REJ)
    gather_pass(ATT, lines - 1)
    gather_start_z(EXP)
    for turn in range(1, lines):
        gather_pass(VEC, turn)
    for turn in range(1, lines):
        gather_pass(REJ, turn)
    gather_wait(VEC)
    gather_pass(EXP, 1)
    gather_wait(ATT)
    gather_start_y(NAR)
    gather_pass(EXP, 2)
    for j in range(n):
        r.vt[:, j * vr : (j + 1) * vr] = r.wv[j].astype(F32)

    def head_bias(row):
        return r.vt[row : row + 1, aligned(m * hw, hw)]

    half_mask = lax.broadcasted_iota(jnp.int32, (1, LANES), 1) < HEAD_DIM

    def lane_half(value, head):
        return jnp.where(half_mask if head % 2 == 0 else jnp.logical_not(half_mask), value, 0)

    def put_heads(ref, q, value):
        for head in range(heads):
            pair = (head // 2) * LANES
            piece = lane_half(value[:, pair : pair + LANES], head)
            ref[head, aligned(oth0 + q * ch, ch), :] = piece[:ch]
            ref[head, aligned(own0 + q * ch, ch), :] = piece[ch:]

    def put_heads_across(ref, q, across):
        for head in range(heads):
            at = (head % 2) * HEAD_DIM
            piece = across[head * HEAD_DIM : (head + 1) * HEAD_DIM, :]
            ref[head, at : at + HEAD_DIM, aligned(oth0 + q * ch, ch)] = piece[:, :ch]
            ref[head, at : at + HEAD_DIM, aligned(own0 + q * ch, ch)] = piece[:, ch:]

    def put_across(ref, q, across):
        ref[:, aligned(oth0 + q * ch, ch)] = across[:, :ch]
        ref[:, aligned(own0 + q * ch, ch)] = across[:, ch:]

    r.qzt[...] = jnp.zeros(r.qzt.shape, BF)

    def share_block(layer, head, lane0, width):
        if layer == 0:
            return r.p0.at[head, :, aligned(lane0, width)]
        return r.gse.at[
            (head // 2) * rows : (head // 2 + 1) * rows,
            aligned((head % 2) * rows + lane0, width),
        ]

    def both_lanes(ref, where, q):
        return jnp.concatenate(
            [ref[where, aligned(oth0 + q * ch, ch)], ref[where, aligned(own0 + q * ch, ch)]],
            axis=1,
        )

    def project(layer, q):
        x = both(r.xl, q)
        queries = (nn(x, r.wa[0]) + head_bias(0)).astype(BF) * jnp.asarray(0.125, BF)
        put_heads(r.qz.at[layer], q, queries)
        put_heads_across(r.qzt.at[layer], q, low_transpose(queries))
        keys = nn(x, r.wa[1]).astype(BF)
        put_both(r.kn.at[layer], q, slice(None), keys)
        put_across(r.kt.at[layer], q, low_transpose(keys))
        values = (nn(x, r.wa[2]) + head_bias(1)).astype(BF)
        put_both(r.vn.at[layer], q, slice(None), values)
        put_across(r.vvt, q, low_transpose(values))

    def attend_forward(layer, q):
        for head in range(heads):
            pair = slice((head // 2) * LANES, (head // 2 + 1) * LANES)
            across = both_lanes(r.qzt.at[layer, head], slice(None), q)
            scores = nn(r.kn[layer, :, pair], across)
            raised = jnp.exp(scores - jnp.max(scores, axis=0, keepdims=True))
            total = jnp.sum(raised, axis=0, keepdims=True)
            low = (raised * (1.0 / total)).astype(BF)
            share_block(layer, head, oth0 + q * ch, ch)[...] = low[:, :ch]
            share_block(layer, head, own0 + q * ch, ch)[...] = low[:, ch:]
            where = slice(head * HEAD_DIM, (head + 1) * HEAD_DIM)
            context = nn(r.vvt[where, :], low).astype(BF)
            r.ct[layer, where, aligned(oth0 + q * ch, ch)] = context[:, :ch]
            r.ct[layer, where, aligned(own0 + q * ch, ch)] = context[:, ch:]
        target = r.ctx if layer == 0 else r.ctx1
        put_both(target, q, slice(None), low_transpose(both_lanes(r.ct.at[layer], slice(None), q)))

    def first_norm(layer, q):
        def one(i):
            at = aligned(q * ch + i * SUB, SUB)
            total = sum_rows(2 * layer, q, aligned(i * SUB, SUB))
            res = r.st[at, :] + (total + r.vt[2:3, :])
            cen = res - jnp.mean(res, axis=1, keepdims=True)
            spread = lax.rsqrt(jnp.mean(cen * cen, axis=1, keepdims=True) + EPS)
            hat = cen * spread
            r.xh1[layer, at, :] = hat
            r.rs1[layer, at, :] = spread
            normed = hat * r.vt[4:5, :] + r.vt[5:6, :]
            r.st[at, :] = normed
            r.normed[aligned(own0 + q * ch + i * SUB, SUB), :] = normed.astype(BF)

        loop(ch // SUB, one)

    def second_norm(layer, q):
        def one(i):
            at = aligned(q * ch + i * SUB, SUB)
            total = sum_rows(2 * layer + 1, q, aligned(i * SUB, SUB))
            res = r.st[at, :] + (total + r.vt[3:4, :])
            cen = res - jnp.mean(res, axis=1, keepdims=True)
            spread = lax.rsqrt(jnp.mean(cen * cen, axis=1, keepdims=True) + EPS)
            hat = cen * spread
            r.xh2[layer, at, :] = hat
            r.rs2[layer, at, :] = spread
            out = hat * r.vt[6:7, :] + r.vt[7:8, :]
            r.st[at, :] = out
            if layer < DEPTH - 1:
                r.xl[aligned(own0 + q * ch + i * SUB, SUB), :] = out.astype(BF)

        loop(ch // SUB, one)

    def unit_act(layer):
        return r.act0 if layer == 0 else r.gsn

    def gelu(v):
        square = v * v
        t = jnp.tanh(GELU_A * v * (1.0 + GELU_B * square))
        return 0.5 * (1.0 + t), t, square

    def gelu_slope(v, gate, t, square):
        return gate + (0.5 * GELU_A) * v * (1.0 - t * t) * (1.0 + (3.0 * GELU_B) * square)

    def widen(layer, q):
        act = unit_act(layer)

        def one(j):
            cols = aligned(j * TILE, TILE)
            v = nn(both(r.normed, q), r.we[:, cols]) + r.vt[pl.ds(8 + m, 1), cols]
            gate, t, square = gelu(v)
            put_both(act, q, cols, (v * gate).astype(BF))
            if layer == 0:
                put_both(r.slope0, q, cols, gelu_slope(v, gate, t, square).astype(BF))

        loop(uw // TILE, one)

    def widen_slots():
        def one(j):
            cols = aligned(j * TILE, TILE)
            v = nn(r.low2c[...], r.we[:, cols]) + r.vt[pl.ds(8 + m, 1), cols]
            gate, t, square = gelu(v)
            r.act0[rows : rows + SLOTS, cols] = (v * gate).astype(BF)
            r.slc[:, cols] = gelu_slope(v, gate, t, square).astype(BF)

        loop(uw // TILE, one)

    def rejoin_sum(layer, q):
        ctx = r.ctx if layer == 0 else r.ctx1
        sum_begin(2 * layer, q, lambda cols: nt(both(ctx, q), r.wr[cols, :]), ch)

    def narrow_sum(layer, q):
        act = unit_act(layer)
        sum_begin(2 * layer + 1, q, lambda cols: nt(both(act, q), r.wn[cols, :]), ch)

    hot = r.oh[...]

    def pick(target, row0, source, source0, width):
        def one(j):
            cols = aligned(j * TILE, TILE)
            target[row0 : row0 + SLOTS, cols] = nn(
                hot, source[source0 : source0 + rows, cols]
            ).astype(BF)

        loop(width // TILE, one)

    by_columns = (2 * vr) % LANES == 0

    def column_core(step):
        cols = aligned((z_from(step) - y) * vr, 2 * vr)
        return remote(
            r.cs.at[1, :, :, cols],
            r.cr.at[1, :, :, cols],
            r.ccs.at[step],
            r.ccr.at[step],
            core_peer,
        )

    def column_x(step):
        cols = aligned((z_from(step) - y) * vr, 2 * vr)
        return remote(
            r.xs.at[1, :, :, cols], r.xr.at[1, :, :, cols], r.cxs.at[step], r.cxr.at[step], x_peer
        )

    def column_sum(step):
        cols = aligned((z_from(step) - y) * vr, 2 * vr)
        weight = r.wn[cols, :]
        away = nt(r.act0[aligned(oth0, half), :], weight).astype(BF)
        for q in range(CHUNKS):
            r.cs[1, q, :, cols] = away[q * ch : (q + 1) * ch]
        column_core(step).start()
        here = nt(r.act0[aligned(own0, half), :], weight)
        column_core(step).wait_recv()
        for q in range(CHUNKS):
            r.xs[1, q, :, cols] = (
                here[q * ch : (q + 1) * ch] + r.cr[1, q, :, cols].astype(F32)
            ).astype(BF)
        column_x(step).start()

    for layer in range(DEPTH):
        for q in range(CHUNKS):
            if layer > 0:
                share_wait(2 * layer - 1, r.xl, q)
            project(layer, q)
        for q in range(CHUNKS):
            attend_forward(layer, q)
            if layer > 0:
                rejoin_sum(layer, q)
            elif q == 0:
                for turn in range(3, lines):
                    gather_pass(EXP, turn)
                gather_start_z(NAR)
        if layer == 0:
            gather_wait(REJ)
            for q in range(CHUNKS):
                rejoin_sum(layer, q)
            gather_pass(NAR, 1)
            transpose_into(r.xt, 0, r.xl, 0, rows)
        else:
            transpose_into(r.xt, rows, r.xl, 0, rows)
        for q in range(CHUNKS):
            sum_end(2 * layer, q, ch)
            first_norm(layer, q)
            share(2 * layer, r.normed, q).start()
            if layer == 0:
                gather_pass(NAR, q + 2)
                if q == 0:
                    gather_wait(EXP)
            share_wait(2 * layer, r.normed, q)
            widen(layer, q)
            if layer > 0:
                narrow_sum(layer, q)
        if layer == 0:
            for turn in range(CHUNKS + 2, lines):
                gather_pass(NAR, turn)
            if by_columns:
                for turn in range(lines):
                    step = gather_order(turn)
                    gather_y_arrival(NAR, step).wait_recv()
                    column_sum(step)
                transpose_into(r.nt, 0, r.normed, 0, rows)
                for step in range(lines):
                    column_x(step).wait()
                    column_core(step).wait_send()
            else:
                transpose_into(r.nt, 0, r.normed, 0, rows)
                gather_wait(NAR)
                for q in range(CHUNKS):
                    narrow_sum(layer, q)
        else:
            pick(r.low2c, 0, r.normed, 0, d_model)
            widen_slots()
            transpose_into(r.nt, rows, r.low2c, 0, SLOTS)
        for q in range(CHUNKS):
            if not (layer == 0 and by_columns):
                sum_end(2 * layer + 1, q, ch)
            second_norm(layer, q)
            if layer < DEPTH - 1:
                share(2 * layer + 1, r.xl, q).start()

    own_rows = aligned(own0, half)
    out_here = pltpu.make_async_copy(r.st, r.act.at[own_rows], r.osem.at[0])
    out_there = remote(r.st, r.act.at[own_rows], r.osem.at[1], r.osem.at[2], core_peer)
    out_arrival = remote(
        r.st, r.act.at[aligned(oth0, half)], r.osem.at[1], r.osem.at[2], core_peer
    )
    out_here.start()
    out_there.start()

    def add_rows(row, value):
        r.vg[row : row + 1, :] += jnp.sum(value, axis=0, keepdims=True)

    def norm_pull(g, hat, spread, gain):
        scaled = g * gain
        mean = jnp.mean(scaled, axis=1, keepdims=True)
        inner = jnp.mean(scaled * hat, axis=1, keepdims=True)
        return spread * (scaled - mean - hat * inner)

    def second_pull(layer, q, gradient):
        def one(i):
            at = aligned(q * ch + i * SUB, SUB)
            g = gradient(i, at)
            hat = r.xh2[layer, at, :]
            add_rows(6, g * hat)
            add_rows(7, g)
            back = norm_pull(g, hat, r.rs2[layer, at, :], r.vt[6:7, :])
            add_rows(3, back)
            r.gb[at, :] = back
            r.low2[aligned(own0 + q * ch + i * SUB, SUB), :] = back.astype(BF)

        loop(ch // SUB, one)

    def first_pull(layer, q, gradient):
        def one(i):
            at = aligned(q * ch + i * SUB, SUB)
            g = gradient(i, at)
            hat = r.xh1[layer, at, :]
            add_rows(4, g * hat)
            add_rows(5, g)
            back = norm_pull(g, hat, r.rs1[layer, at, :], r.vt[4:5, :])
            add_rows(2, back)
            r.gb[at, :] = back
            r.xl[aligned(own0 + q * ch + i * SUB, SUB), :] = back.astype(BF)

        loop(ch // SUB, one)

    def hot_rows(at_start):
        return r.oht[aligned(own0 + at_start, SUB), :]

    def bias_sums(row0):
        for kind, row in ((0, 0), (2, 1)):
            cols = aligned(m * hw, hw)
            r.vg[row : row + 1, cols] += jnp.sum(
                r.dp[kind, row0 : row0 + rows, :].astype(F32), axis=0, keepdims=True
            )

    for q in range(CHUNKS):
        second_pull(1, q, lambda i, at: nn(hot_rows(q * ch + i * SUB), r.mc[...]))
        share(4, r.low2, q).start()
    for q in range(CHUNKS):
        share_wait(4, r.low2, q)
    pick(r.low2c, 0, r.low2, 0, d_model)

    def slot_units(j):
        cols = aligned(j * TILE, TILE)
        back = nn(r.low2c[...], r.wn[:, cols]) * r.slc[:, cols].astype(F32)
        back = back.astype(BF)
        r.be[rows : rows + SLOTS, cols] = back
        r.vg[pl.ds(8 + m, 1), cols] += jnp.sum(back.astype(F32), axis=0, keepdims=True)

    loop(uw // TILE, slot_units)
    slot_own = core * slot_half
    slot_oth = slot_half - slot_own

    def slot_tile(cols):
        part = nt(r.be[rows : rows + SLOTS, :], r.we[cols, :])
        r.part[...] = part
        return jnp.concatenate(
            [
                r.part[aligned(slot_oth, slot_half), :],
                r.part[aligned(slot_own, slot_half), :],
            ],
            axis=0,
        )

    sum_begin(4, 0, slot_tile, slot_half)
    transpose_into(r.l2t, rows, r.low2c, 0, SLOTS)
    for head in range(heads):
        r.qc[head] = nn(hot, r.qz[1, head]).astype(BF)
        source = r.gse[
            (head // 2) * rows : (head // 2 + 1) * rows,
            (head % 2) * rows : (head % 2 + 1) * rows,
        ]
        r.pc[head] = nn(source, r.oht[...]).astype(BF)
    r.cct[...] = nn(r.ct[1], r.oht[...]).astype(BF)
    sum_end(4, 0, slot_half)
    mine_slots = r.slt.at[aligned(slot_own, slot_half)]
    mine_slots[...] = sum_rows(4, 0, slice(0, slot_half)).astype(BF)
    slots_out = remote(mine_slots, mine_slots, r.osem.at[3], r.osem.at[4], core_peer)
    slots_in_ref = r.slt.at[aligned(slot_oth, slot_half)]
    slots_in = remote(slots_in_ref, slots_in_ref, r.osem.at[3], r.osem.at[4], core_peer)
    slots_out.start()
    slots_in.wait_recv()
    for q in range(CHUNKS):
        first_pull(
            1, q, lambda i, at: r.gb[at, :] + nn(hot_rows(q * ch + i * SUB), r.slt[...])
        )
        share(5, r.xl, q).start()

    for q in range(CHUNKS):
        share_wait(5, r.xl, q)
    pick(r.low2c, 0, r.xl, 0, d_model)
    low_ctx = nn(r.low2c[...], r.wr[...]).astype(BF)
    across = low_transpose(low_ctx)
    dq_across = []
    for pair in range(heads // 2):
        lanes = slice(pair * LANES, (pair + 1) * LANES)
        dv = jnp.zeros((rows, LANES), F32)
        dk = jnp.zeros((rows, LANES), F32)
        for head in (2 * pair, 2 * pair + 1):
            where = slice(head * HEAD_DIM, (head + 1) * HEAD_DIM)
            at = (head % 2) * HEAD_DIM
            r.dozt[head, at : at + HEAD_DIM, 0:SLOTS] = across[where, :]
            low = r.pc[head]
            dv += nn(low, lane_half(low_ctx[:, lanes], head))
            dp = nn(r.vn[1, :, lanes], r.dozt[head, :, 0:SLOTS])
            delta = jnp.sum(
                across[where, :].astype(F32) * r.cct[where, :].astype(F32), axis=0, keepdims=True
            )
            ds = (low.astype(F32) * (dp - delta)).astype(BF)
            dk += nn(ds, r.qc[head])
            dq_across.append(nn(r.kt[1, where, :], ds) * 0.125)
        r.dp[1, rows : 2 * rows, lanes] = dk.astype(BF)
        r.dp[2, rows : 2 * rows, lanes] = dv.astype(BF)
    dq = low_transpose(jnp.concatenate(dq_across, axis=0))
    r.dp[0, rows : 2 * rows, :] = nn(r.oht[...], dq).astype(BF)
    bias_sums(rows)

    def layer_rows(k, q, row0):
        def tile_of(cols):
            total = None
            for kind in range(3):
                lhs = jnp.concatenate(
                    [
                        r.dp[kind, aligned(row0 + oth0 + q * ch, ch), :],
                        r.dp[kind, aligned(row0 + own0 + q * ch, ch), :],
                    ],
                    axis=0,
                )
                part = nt(lhs, r.wa[kind, cols, :])
                total = part if total is None else total + part
            return total

        sum_begin(k, q, tile_of, ch)

    for q in range(CHUNKS):
        layer_rows(5, q, rows)
    transpose_into(r.l1t, rows, r.low2c, 0, SLOTS)

    def weight_grad_rows(target, across, latter, width, row0, count):
        at = aligned(row0, count)

        def one(j):
            cols = aligned(j * TILE, TILE)
            target[at, cols] = nn(across[at, :], latter[:, cols]).astype(BF)

        loop(width // TILE, one)

    def weight_grad(target, across, latter, width):
        loop(
            d_model // TILE,
            lambda i: weight_grad_rows(target, across, latter, width, i * TILE, TILE),
        )

    def transpose_both(target, source, q):
        for row0 in (oth0 + q * ch, own0 + q * ch):
            target[:, aligned(row0, ch)] = low_transpose(source[aligned(row0, ch), :])

    def units_back(q):
        def one(j):
            cols = aligned(j * TILE, TILE)
            slope = both(r.slope0, q, cols).astype(F32)
            back = (nn(both(r.low2, q), r.wn[:, cols]) * slope).astype(BF)
            put_both(r.be, q, cols, back)
            r.vg[pl.ds(8 + m, 1), cols] += jnp.sum(back.astype(F32), axis=0, keepdims=True)

        loop(uw // TILE, one)

    for q in range(CHUNKS):
        sum_end(5, q, ch)
        second_pull(
            0, q, lambda i, at: r.gb[at, :] + sum_rows(5, q, aligned(i * SUB, SUB))
        )
        share(6, r.low2, q).start()
        share_wait(6, r.low2, q)
        transpose_both(r.l2t, r.low2, q)
        if q == 0:
            units_back(q)
    if by_columns:
        for turn in range(1, lines + 1):
            owner = ((z + scatter_order(turn)) % lines) * 2 + 1 - y
            weight_grad_rows(r.gsn, r.l2t, r.act0, uw, owner * vr, vr)
            if turn <= 2:
                scatter_y(NAR, scatter_order(turn)).start()
                under_way.append(queue.pop(0))
        ready.append(NAR)
    else:
        weight_grad(r.gsn, r.l2t, r.act0, uw)
        scatter_start(NAR)
    for q in range(CHUNKS):
        if q > 0:
            units_back(q)
        sum_begin(6, q, lambda cols, q=q: nt(both(r.be, q), r.we[cols, :]), ch)
    if by_columns:
        each(
            0,
            lines,
            lambda s: weight_grad_rows(
                r.gsn, r.l2t, r.act0, uw, (((z + s) % lines) * 2 + y) * vr, vr
            ),
        )
    pick(r.ctx, rows, r.ctx1, 0, hw)
    weight_grad(r.gse, r.nt, r.be, uw)
    scatter_start(EXP)
    scatter_pass()
    for q in range(CHUNKS):
        sum_end(6, q, ch)
        first_pull(
            0, q, lambda i, at: r.gb[at, :] + sum_rows(6, q, aligned(i * SUB, SUB))
        )
        share(7, r.xl, q).start()
    scatter_pass()
    for q in range(CHUNKS):
        share_wait(7, r.xl, q)
        back = nn(both(r.xl, q), r.wr[...]).astype(BF)
        put_heads(r.doz, q, back)
        put_heads_across(r.dozt, q, low_transpose(back))

    def head_pair(pair):
        lanes = aligned(pair * LANES, LANES)
        dv = jnp.zeros((rows, LANES), F32)
        dk = jnp.zeros((rows, LANES), F32)
        for side in range(2):
            head = 2 * pair + side
            where = aligned(head * HEAD_DIM, HEAD_DIM)
            for part in range(rows // TILE):
                some = slice(part * TILE, (part + 1) * TILE)
                low = r.p0[head, :, some]
                dv += nn(low, r.doz[head, some, :])
                inner = r.dozt[head, side * HEAD_DIM : (side + 1) * HEAD_DIM, some]
                delta = jnp.sum(
                    inner.astype(F32) * r.ct[0, where, some].astype(F32), axis=0, keepdims=True
                )
                dp = nn(r.vn[0, :, lanes], r.dozt[head, :, some])
                ds = (low.astype(F32) * (dp - delta)).astype(BF)
                dk += nn(ds, r.qz[0, head, some, :])
                r.dqt[where, some] = (nn(r.kt[0, where, :], ds) * 0.125).astype(BF)
        r.dp[1, 0:rows, lanes] = dk.astype(BF)
        r.dp[2, 0:rows, lanes] = dv.astype(BF)

    for pair in range(heads // 2):
        head_pair(pair)
        scatter_pass()
    for i in range(rows // LANES):
        some = slice(i * LANES, (i + 1) * LANES)
        r.dp[0, some, :] = low_transpose(r.dqt[:, some])
    for q in range(CHUNKS):
        layer_rows(7, q, 0)
    scatter_pass()
    bias_sums(0)
    transpose_into(r.l1t, 0, r.xl, 0, rows)
    weight_grad(r.gsr, r.l1t, r.ctx, hw)
    scatter_start(REJ)
    first_of_x = jnp.where(m < 2, 1.0, 0.0)
    r.vg[2:8, :] = r.vg[2:8, :] * first_of_x
    for j in range(n):
        r.gsv[j] = r.vg[:, j * vr : (j + 1) * vr].astype(BF)
    scatter_start(VEC)
    for kind in range(3):
        weight_grad(r.gsa.at[kind], r.xt, r.dp.at[kind], hw)
    scatter_start(ATT)
    scatter_pass()
    out_here.wait()
    out_there.wait_send()
    for q in range(CHUNKS):
        sum_end(7, q, ch)

        def last(i, q=q):
            at = aligned(q * ch + i * SUB, SUB)
            g = r.gb[at, :] + sum_rows(7, q, aligned(i * SUB, SUB))
            r.st[at, :] = g * r.keep[aligned(own0 + q * ch + i * SUB, SUB), :]

        loop(ch // SUB, last)
    in_here = pltpu.make_async_copy(r.st, r.ing.at[own_rows], r.osem.at[5])
    in_there = remote(r.st, r.ing.at[own_rows], r.osem.at[6], r.osem.at[7], core_peer)
    in_arrival = remote(r.st, r.ing.at[aligned(oth0, half)], r.osem.at[6], r.osem.at[7], core_peer)
    in_here.start()
    in_there.start()
    scatter_turn()

    scatter_pass()
    def squares(value):
        value = value * value
        if value.ndim == 3:
            value = jnp.sum(value, axis=0)
        value = jnp.sum(value, axis=0, keepdims=True)
        return jnp.sum(value, axis=1, keepdims=True)

    swap_v = remote(r.vf.at[0], r.vf.at[1], r.vxs.at[2], r.vxr.at[2], core_peer)
    swap_w = remote(r.vf.at[2], r.vf.at[3], r.vxs.at[3], r.vxr.at[3], x_peer)
    total = jnp.zeros((1, 1), F32)
    while under_way:
        turn = under_way[0][1] if under_way[0][0] == ATT else 0
        if turn == 1:
            scatter_finish(NAR, r.gn)
            total = total + squares(r.gn[...])
            scatter_close(NAR)
            for region in range(5):
                gather_close(region)
        elif turn == 2:
            scatter_finish(VEC, r.vf.at[0])
            swap_v.start()
            scatter_finish(REJ, r.gr)
            total = total + squares(r.gr[...])
        elif turn == 3:
            swap_v.wait_recv()
            r.vf[2] = r.vf[0] + r.vf[1]
            swap_w.start()
            scatter_finish(EXP, r.ge)
            total = total + squares(r.ge[...])
            scatter_close(EXP)
            scatter_close(REJ)
        elif turn == 4:
            swap_w.wait_recv()
            r.vs[...] = r.vf[2] + r.vf[3]
            r.gv[...] = r.vs[pl.ds(columns * m, columns), :]
            total = total + squares(r.gv[...])
        scatter_pass()
    scatter_finish(ATT, r.ga)
    total = total + squares(r.ga[...])

    r.nm[m] = jnp.broadcast_to(total, (8, LANES))

    def model_copy(k, slot):
        return remote(r.nm.at[slot], r.nm.at[slot], r.nms.at[k], r.nmr.at[k], model_peers[k])

    for k in range(3):
        model_copy(k, m).start()
    for k in range(3):
        model_copy(k, model_peers[k][1]).wait_recv()
    r.nz[d] = jnp.sum(r.nm[...], axis=0)

    def line_copy(step, slot):
        here = r.nz.at[slot]
        return remote(here, here, r.nzs.at[0, step], r.nzr.at[0, step], z_peer(step))

    def cross_copy(step, slot):
        here = r.nz.at[slot]
        return remote(here, here, r.nzs.at[1, step], r.nzr.at[1, step], zy_peer(step))

    each(0, lines, lambda s: cross_copy(s, d).start())
    each(1, lines, lambda s: line_copy(s, d).start())
    each(0, lines, lambda s: cross_copy(s, z_from(s) + 1 - 2 * y).wait_recv())
    each(1, lines, lambda s: line_copy(s, z_from(s)).wait_recv())
    r.norm[...] = jnp.sqrt(jnp.sum(r.nz[...], axis=0))

    each(0, lines, lambda s: cross_copy(s, d).wait_send())
    each(1, lines, lambda s: line_copy(s, d).wait_send())
    for k in range(3):
        model_copy(k, m).wait_send()
    swap.wait_send()
    swap_x.wait_send()
    swap_v.wait_send()
    swap_w.wait_send()
    slots_out.wait_send()
    scatter_close(VEC)
    scatter_close(ATT)
    out_arrival.wait_recv()
    in_here.wait()
    in_there.wait_send()
    in_arrival.wait_recv()


def run_layers(
    n, tok, pos, cho, table, mcot, attend, rejoin, expand, narrow, vin
):
    rows, d_model = tok.shape
    vr = rejoin.shape[0]
    hw = rejoin.shape[1]
    uw = expand.shape[1]
    lines = n // 2
    half = rows // 2
    ch = half // CHUNKS
    heads = hw // HEAD_DIM
    wide = rows + SLOTS
    inputs = [
        ("tok", tok),
        ("pos", pos),
        ("cho", cho),
        ("table", table),
        ("mcot", mcot),
        ("attend", attend),
        ("rejoin", rejoin),
        ("expand", expand),
        ("narrow", narrow),
        ("vin", vin),
    ]
    outputs = [
        ("act", (rows, d_model), pl.ANY),
        ("ing", (rows, d_model), pl.ANY),
        ("ga", (3, vr, hw), pltpu.VMEM),
        ("gr", (vr, hw), pltpu.VMEM),
        ("ge", (vr, uw), pltpu.VMEM),
        ("gn", (vr, uw), pltpu.VMEM),
        ("gv", vin.shape, pltpu.VMEM),
        ("norm", (8, LANES), pltpu.VMEM),
    ]
    low = [
        ("wv", (n, 16, vr)),
        ("wa", (3, d_model, hw)),
        ("wr", (d_model, hw)),
        ("we", (d_model, uw)),
        ("wn", (d_model, uw)),
        ("gsv", (n, 16, vr)),
        ("gsa", (3, d_model, hw)),
        ("gsr", (d_model, hw)),
        ("gse", (d_model, uw)),
        ("gsn", (d_model, uw)),
        ("yv", (lines, 16, vr)),
        ("ya", (lines, 3, vr, hw)),
        ("yr", (lines, vr, hw)),
        ("ye", (lines, vr, uw)),
        ("yn", (lines, vr, uw)),
        ("zv", (lines, 16, vr)),
        ("za", (lines, 3, vr, hw)),
        ("zr", (lines, vr, hw)),
        ("ze", (lines, vr, uw)),
        ("zn", (lines, vr, uw)),
        ("cs", (2, CHUNKS, ch, d_model)),
        ("cr", (2, CHUNKS, ch, d_model)),
        ("xs", (2, CHUNKS, ch, d_model)),
        ("xr", (2, CHUNKS, ch, d_model)),
        ("vb", (4, 16, vr)),
        ("oh", (SLOTS, rows)),
        ("oht", (rows, SLOTS)),
        ("mc", (SLOTS, d_model)),
        ("xl", (rows, d_model)),
        ("normed", (rows, d_model)),
        ("low2", (rows, d_model)),
        ("xt", (d_model, 2 * rows)),
        ("nt", (d_model, wide)),
        ("l2t", (d_model, wide)),
        ("l1t", (d_model, wide)),
        ("act0", (wide, uw)),
        ("slope0", (rows, uw)),
        ("be", (wide, uw)),
        ("ctx", (wide, hw)),
        ("ctx1", (rows, hw)),
        ("dp", (3, 2 * rows, hw)),
        ("qz", (2, heads, rows, LANES)),
        ("qzt", (2, heads, LANES, rows)),
        ("kn", (2, rows, hw)),
        ("kt", (2, hw, rows)),
        ("vn", (2, rows, hw)),
        ("vvt", (hw, rows)),
        ("ct", (2, hw, rows)),
        ("p0", (heads, rows, rows)),
        ("dqt", (hw, rows)),
        ("slc", (SLOTS, uw)),
        ("low2c", (SLOTS, d_model)),
        ("slt", (SLOTS, d_model)),
        ("qc", (heads, SLOTS, LANES)),
        ("pc", (heads, rows, SLOTS)),
        ("cct", (hw, SLOTS)),
    ]
    full = [
        ("vt", (16, d_model)),
        ("vg", (16, d_model)),
        ("keep", (rows, 1)),
        ("st", (half, d_model)),
        ("gb", (half, d_model)),
        ("xh1", (2, half, d_model)),
        ("xh2", (2, half, d_model)),
        ("rs1", (2, half, 1)),
        ("rs2", (2, half, 1)),
        ("acc", (ch, d_model)),
        ("part", (SLOTS, TILE)),
        ("vf", (4, 16, vr)),
        ("vs", (16, vr)),
        ("nm", (4, 8, LANES)),
        ("nz", (n, 8, LANES)),
    ]
    sems = [
        ("agzs", (5, lines + 3)),
        ("agzr", (5, lines)),
        ("agys", (5, lines)),
        ("agyr", (5, lines)),
        ("rsys", (5, lines)),
        ("rsyr", (5, lines)),
        ("rszs", (5, lines)),
        ("rszr", (5, lines)),
        ("arcs", (8, CHUNKS, d_model // TILE)),
        ("arcr", (8, CHUNKS, d_model // TILE)),
        ("arxs", (8, CHUNKS, d_model // TILE)),
        ("arxr", (8, CHUNKS, d_model // TILE)),
        ("shs", (8, CHUNKS)),
        ("shr", (8, CHUNKS)),
        ("vxs", (4,)),
        ("vxr", (4,)),
        ("osem", (8,)),
        ("nms", (3,)),
        ("nmr", (3,)),
        ("nzs", (2, lines)),
        ("nzr", (2, lines)),
        ("ccs", (lines,)),
        ("ccr", (lines,)),
        ("cxs", (lines,)),
        ("cxr", (lines,)),
    ]
    names = (
        [name for name, _ in inputs]
        + [name for name, _, _ in outputs]
        + [name for name, _ in low]
        + [name for name, _ in full]
        + ["pb"]
        + [name for name, _ in sems]
    )
    sizes = (n, d_model, rows, hw, uw, vr)

    def body(*refs):
        layer_kernel(names, sizes, *refs)

    return pl.pallas_call(
        body,
        out_shape=[jax.ShapeDtypeStruct(shape, F32) for _, shape, _ in outputs],
        in_specs=[pl.BlockSpec(memory_space=pltpu.VMEM)] * len(inputs),
        out_specs=[pl.BlockSpec(memory_space=space) for _, _, space in outputs],
        scratch_shapes=[pltpu.VMEM(shape, BF) for _, shape in low]
        + [pltpu.VMEM(shape, F32) for _, shape in full]
        + [pltpu.VMEM((16, LANES), jnp.int32)]
        + [pltpu.SemaphoreType.DMA(shape) for _, shape in sems],
        compiler_params=pltpu.CompilerParams(
            collective_id=0, has_side_effects=True, vmem_limit_bytes=61 * 1024 * 1024
        ),
        cost_estimate=pl.CostEstimate(
            flops=20_000_000_000, bytes_accessed=20_000_000, transcendentals=4_000_000
        ),
    )(*[value for _, value in inputs])


def apply_update(weight, first_moment, second_moment, shadow, gradient, step_rate):
    momentum = 0.5 * first_moment + 0.5 * gradient
    variance = 0.5 * second_moment + 0.5 * gradient * gradient
    bias_fix = 1.0 - 0.5**STEP
    updated = weight - step_rate * (
        momentum / bias_fix / (jnp.sqrt(variance / bias_fix) + 1e-08) + 0.01 * weight
    )
    average = 0.999 * shadow + 0.001 * updated
    return (updated, momentum, variance, average, updated.astype(BF))


def update_kernel(rates, clip_limit, norm, act, ing, *refs):
    *refs, norm_out, act_out, ing_out = refs
    act_out[...] = act[...]
    ing_out[...] = ing[...]
    norm_out[...] = norm[0:1, 0:1]
    factor = jnp.minimum(1.0, clip_limit / (norm[0:1, 0:1] + 1e-06))
    ins, outs = refs[: 5 * len(rates)], refs[5 * len(rates) :]
    for index, rate in enumerate(rates):
        weight, first, second, shadow, gradient = ins[5 * index : 5 * index + 5]
        targets = outs[5 * index : 5 * index + 5]
        for part in range(weight.shape[0]) if len(weight.shape) == 3 else (slice(None),):
            results = apply_update(
                weight[part],
                first[part],
                second[part],
                shadow[part],
                gradient[part] * factor,
                rate,
            )
            for target, value in zip(targets, results, strict=True):
                target[part] = value


def run_update(groups, rates, norm, clip_limit, act, ing):
    vr = groups[1][0].shape[0]
    step = min(vr, 64)

    def spec(shape, whole):
        if whole:
            return pl.BlockSpec(shape, lambda i: (0, 0))
        if len(shape) == 3:
            return pl.BlockSpec((shape[0], step, shape[2]), lambda i: (0, i, 0))
        return pl.BlockSpec((step, shape[1]), lambda i: (i, 0))

    last = len(groups) - 1
    passed = pl.BlockSpec((act.shape[0] * step // vr, act.shape[1]), lambda i: (i, 0))
    specs = [spec(group[0].shape, k == last) for k, group in enumerate(groups)]

    def body(*refs):
        update_kernel(rates, clip_limit, *refs)

    flat = [value for group in groups for value in group]
    size = sum(value.size for value in flat) * 4
    outs = pl.pallas_call(
        body,
        grid=(vr // step,),
        in_specs=[spec(norm.shape, True)]
        + [passed] * 2
        + [one for one in specs for _ in range(5)],
        out_specs=[one for one in specs for _ in range(5)]
        + [spec((1, 1), True)]
        + [passed] * 2,
        out_shape=[
            jax.ShapeDtypeStruct(group[0].shape, kind)
            for group in groups
            for kind in (F32, F32, F32, F32, BF)
        ]
        + [jax.ShapeDtypeStruct(shape, F32) for shape in ((1, 1), act.shape, ing.shape)],
        compiler_params=pltpu.CompilerParams(vmem_limit_bytes=60 * 1024 * 1024),
        cost_estimate=pl.CostEstimate(flops=size, bytes_accessed=2 * size, transcendentals=0),
    )(norm, act, ing, *flat)
    groups_out = [outs[5 * k : 5 * k + 5] for k in range(len(groups))]
    return groups_out, outs[-3].reshape(()), *outs[-2:]


def per_device(
    tokens_in,
    masked_positions,
    replace_choice,
    replace_table,
    masked_cotangent,
    attend,
    attend_mean,
    attend_square,
    attend_shadow,
    rejoin,
    rejoin_mean,
    rejoin_square,
    rejoin_shadow,
    expand,
    expand_mean,
    expand_square,
    expand_shadow,
    narrow,
    narrow_mean,
    narrow_square,
    narrow_shadow,
    vectors,
    vectors_mean,
    vectors_square,
    vectors_shadow,
):
    n = lax.axis_size("dp")
    act, ing, ga, gr, ge, gn, gv, norm = run_layers(
        n,
        tokens_in,
        masked_positions,
        replace_choice,
        replace_table,
        masked_cotangent,
        attend.transpose(1, 0, 2),
        rejoin,
        expand,
        narrow,
        vectors.T,
    )
    d_model = tokens_in.shape[1]
    param_count = 4 * d_model * d_model + 2 * d_model * expand.shape[1] * 4 + 12 * d_model
    clip_limit = 0.001 * math.sqrt(param_count * tokens_in.shape[0] * n)
    cubes = [x.transpose(1, 0, 2) for x in (attend, attend_mean, attend_square, attend_shadow)]
    rows_of = [x.T for x in (vectors, vectors_mean, vectors_square, vectors_shadow)]
    new, gradient_norm, act, ing = run_update(
        (
            (*cubes, ga),
            (rejoin, rejoin_mean, rejoin_square, rejoin_shadow, gr),
            (expand, expand_mean, expand_square, expand_shadow, ge),
            (narrow, narrow_mean, narrow_square, narrow_shadow, gn),
            (*rows_of, gv),
        ),
        (0.04, 0.16, 0.04, 0.04, 0.5),
        norm,
        clip_limit,
        act,
        ing,
    )
    results = [act, ing, gradient_norm]
    results.extend(x.transpose(1, 0, 2) for x in new[0])
    for group in new[1:4]:
        results.extend(group)
    results.extend(x.T for x in new[4])
    return tuple(results)


def solution(mesh):
    row = P("dp", None)
    cube = P("dp", None, "mp")
    flat = P("dp", "mp")
    return jax.shard_map(
        per_device,
        mesh=mesh,
        in_specs=(row, row, row, P(), P("dp", None, None)) + (cube,) * 4 + (flat,) * 16,
        out_specs=(row, row, P()) + (cube,) * 5 + (flat,) * 20,
        check_vma=False,
    )
```

```python
import math
from types import SimpleNamespace

import jax
import jax.numpy as jnp
from jax import lax
from jax.experimental import pallas as pl
from jax.experimental.pallas import tpu as pltpu
from jax.sharding import PartitionSpec as P

HEAD_DIM = 64
SEQ_LEN = 512
DEPTH = 2
STEP = 7
EPS = 1e-05
BF = jnp.bfloat16
F32 = jnp.float32
MESH = pl.DeviceIdType.MESH
LANES = 128
TILE = 256
SLOTS = 128
CHUNKS = 2
SUB = 64
VEC, ATT, REJ, EXP, NAR = range(5)
GELU_A = 0.7978845608028654
GELU_B = 0.044715


def nn(former, latter):
    return jnp.dot(former, latter, preferred_element_type=F32)


def nt(former, latter):
    return lax.dot_general(former, latter, (((1,), (1,)), ((), ())), preferred_element_type=F32)


def low_transpose(block):
    return jnp.transpose(block.astype(F32), (1, 0)).astype(BF)


def loop(count, body):
    def step(index, carry):
        body(index)
        return carry

    lax.fori_loop(0, count, step, 0)


def each(first, last, body):
    if last - first <= 8:
        for index in range(first, last):
            body(index)
    else:

        def step(index, carry):
            body(index)
            return carry

        lax.fori_loop(first, last, step, 0)


def aligned(index, size):
    return pl.ds(pl.multiple_of(index, size), size)


def layer_kernel(names, sizes, *refs):
    r = SimpleNamespace(**dict(zip(names, refs, strict=True)))
    n, d_model, rows, hw, uw, vr = sizes
    r.doz, r.dozt = r.qz.at[1], r.qzt.at[1]
    half = rows // 2
    ch = half // CHUNKS
    lines = n // 2
    heads = hw // HEAD_DIM
    slot_half = SLOTS // 2

    d = lax.axis_index("dp")
    m = lax.axis_index("mp")
    z, y = d // 2, d % 2
    core = m % 2
    core_peer = (d, m + 1 - 2 * core)
    x_peer = (d, (m + 2) % 4)
    y_peer = (d + 1 - 2 * y, m)
    model_peers = (core_peer, x_peer, (d, 3 - m))
    own0 = core * half
    oth0 = half - own0

    weights = (r.wv, r.wa, r.wr, r.we, r.wn)
    grads = (r.gsv, r.gsa, r.gsr, r.gse, r.gsn)
    from_y = (r.yv, r.ya, r.yr, r.ye, r.yn)
    from_z = (r.zv, r.za, r.zr, r.ze, r.zn)

    def z_peer(step):
        return (((z + step) % lines) * 2 + y, m)

    def zy_peer(step):
        return (((z + step) % lines) * 2 + 1 - y, m)

    def z_from(step):
        return ((z + lines - step) % lines) * 2 + y

    def block(ref, region, index):
        if region == VEC:
            return ref.at[index]
        where = aligned(index * vr, vr)
        return ref.at[:, where, :] if region == ATT else ref.at[where, :]

    def remote(source, target, send, recv, device):
        return pltpu.make_async_remote_copy(
            src_ref=source,
            dst_ref=target,
            send_sem=send,
            recv_sem=recv,
            device_id=device,
            device_id_type=MESH,
        )

    loads = [
        pltpu.make_async_copy(source, target, r.lsem.at[k])
        for k, (source, target) in enumerate(
            ((r.expand, r.expand_in), (r.narrow, r.narrow_in), (r.tok, r.tok_in))
        )
    ]
    for load in loads:
        load.start()

    barrier = pltpu.get_barrier_semaphore()

    def greet(peer):
        pl.semaphore_signal(barrier, inc=1, device_id=peer, device_id_type=MESH)

    for peer in model_peers:
        greet(peer)
    each(1, lines, lambda s: greet(z_peer(s)))
    each(0, lines, lambda s: greet(zy_peer(s)))

    relay = lines == 4
    last_line = lines - 1
    inner = jnp.logical_and(z > 0, z < last_line)
    far_end = (jnp.where(z == 1, 0, last_line) * 2 + y, m)
    near_mid = (jnp.where(z == 0, 1, last_line - 1) * 2 + y, m)

    def gather_z(region, step):
        piece = block(weights[region], region, d)
        return remote(
            piece, piece, r.agzs.at[region, step], r.agzr.at[region, step], z_peer(step)
        )

    def gather_z_arrival(region, step):
        piece = block(weights[region], region, z_from(step))
        return remote(
            piece, piece, r.agzs.at[region, step], r.agzr.at[region, step], z_peer(step)
        )

    def gather_onward(region, turn):
        piece = block(weights[region], region, z_from(gather_order(turn)))
        if turn == 3:
            target = far_end
            arrives_as = jnp.where(z == 1, 1, last_line)
        else:
            target = ((z + 3 - 2 * turn) * 2 + y, m)
            arrives_as = 2
        return remote(
            piece,
            piece,
            r.agzs.at[region, last_line + turn],
            r.agzr.at[region, arrives_as],
            target,
        )

    def gather_y(region, step):
        piece = block(weights[region], region, z_from(step))
        return remote(piece, piece, r.agys.at[region, step], r.agyr.at[region, step], y_peer)

    def gather_y_arrival(region, step):
        piece = block(weights[region], region, z_from(step) + 1 - 2 * y)
        return remote(piece, piece, r.agys.at[region, step], r.agyr.at[region, step], y_peer)

    def near(step, body):
        if not relay:
            body()
        elif step != 2:
            pl.when(z < last_line if step == 1 else z > 0)(body)

    def gather_start_z(region):
        for step in range(1, lines):
            near(step, lambda: gather_z(region, step).start())

    def gather_start_y(region):
        gather_y(region, 0).start()

    def gather_order(turn):
        if not relay or turn == 0:
            return turn
        if turn == 1:
            return jnp.where(z == 0, last_line, 1)
        if turn == 2:
            return jnp.where(inner, last_line, 2)
        return jnp.where(inner, 2, jnp.where(z == 0, 1, last_line))

    def gather_pass(region, turn):
        step = gather_order(turn)
        gather_z_arrival(region, step).wait_recv()
        if relay:
            pl.when(inner)(lambda: gather_onward(region, turn).start())
        gather_y(region, step).start()

    def gather_wait(region):
        each(0, lines, lambda s: gather_y_arrival(region, s).wait_recv())

    def gather_close(region):
        for step in range(1, lines):
            near(step, lambda: gather_z(region, step).wait_send())
        if relay:
            for turn in range(1, lines):
                pl.when(inner)(lambda: gather_onward(region, turn).wait_send())
        each(0, lines, lambda s: gather_y(region, s).wait_send())

    def scatter_y(region, step):
        owner = ((z + step) % lines) * 2 + 1 - y
        return remote(
            block(grads[region], region, owner),
            from_y[region].at[step],
            r.rsys.at[region, step],
            r.rsyr.at[region, step],
            y_peer,
        )

    def scatter_z(region, step):
        owner = ((z + step) % lines) * 2 + y
        return remote(
            block(grads[region], region, owner),
            from_z[region].at[step],
            r.rszs.at[region, step],
            r.rszr.at[region, step],
            z_peer(step),
        )

    def scatter_far(region, step):
        owner = ((z + step) % lines) * 2 + y
        return remote(
            block(grads[region], region, owner),
            from_z[region].at[0],
            r.rszs.at[region, step],
            r.rszr.at[region, 0],
            near_mid,
        )

    def scatter_order(turn):
        if not relay:
            return turn % lines
        if turn == 1:
            return jnp.where(z == 0, last_line, 1)
        if turn == 2:
            return jnp.where(z == 0, 1, last_line)
        return 2 if turn == 3 else 0

    def scatter_cross(step):
        owner = ((z + step) % lines) * 2 + 1 - y
        return remote(
            block(grads[REJ], REJ, owner),
            from_y[REJ].at[step],
            r.rsys.at[REJ, step],
            r.rsyr.at[REJ, step],
            z_peer(step),
        )

    def scatter_turn():
        piece = block(grads[REJ], REJ, d + 1 - 2 * y)
        total = piece[...].astype(F32)
        for step in range(1, lines):
            scatter_cross(step).wait_recv()
            total = total + from_y[REJ][step].astype(F32)
        piece[...] = total.astype(BF)
        scatter_y(REJ, 0).start()

    def scatter_start(region):
        if region == REJ:
            each(1, lines, lambda s: scatter_z(REJ, s).start())
            each(1, lines, lambda s: scatter_cross(s).start())
            return
        ready.append(region)
        scatter_next()

    ready = []
    order = (NAR, EXP, VEC, ATT)
    queue = [(region, turn) for region in order for turn in range(1, lines + 1)]
    under_way = []
    weight_of = {NAR: 4, EXP: 4, ATT: 3, VEC: 1}

    def scatter_next():
        while queue and queue[0][0] in ready:
            if sum(weight_of[region] for region, _ in under_way) > 4:
                break
            region, turn = queue.pop(0)
            scatter_y(region, scatter_order(turn)).start()
            under_way.append((region, turn))

    def scatter_pass():
        region, turn = under_way[0]
        step = scatter_order(turn)
        scatter_y(region, step).wait_recv()
        under_way.pop(0)
        scatter_next()
        if turn == lines:
            return
        piece = block(grads[region], region, ((z + step) % lines) * 2 + y)
        total = piece[...].astype(F32) + from_y[region][step].astype(F32)
        piece[...] = total.astype(BF)
        if not relay:
            scatter_z(region, step).start()
        elif turn == 1:
            pl.when(inner)(lambda: scatter_z(region, step).start())
            pl.when(jnp.logical_not(inner))(lambda: scatter_far(region, step).start())
        elif turn == 2:
            scatter_z(region, step).start()
        else:

            @pl.when(inner)
            def _():
                scatter_far(region, 0).wait_recv()
                piece[...] = (total + from_z[region][0].astype(F32)).astype(BF)

            scatter_z(region, step).start()

    def scatter_finish(region, out_ref):
        def one(step):
            scatter_z(region, step).wait_recv()
            out_ref[...] += from_z[region][step].astype(F32)

        if region == REJ:
            scatter_y(region, 0).wait_recv()
        piece = block(grads[region], region, d)
        out_ref[...] = piece[...].astype(F32) + from_y[region][0].astype(F32)
        for step in range(1, lines):
            if not relay or region == REJ or step == 2:
                one(step)
            else:
                pl.when(z > 0 if step == 1 else z < last_line)(lambda: one(step))

    def scatter_close(region):
        each(0, lines, lambda s: scatter_y(region, s).wait_send())
        each(1, lines, lambda s: scatter_z(region, s).wait_send())

    tiles = d_model // TILE

    def core_copy(k, q, count, j):
        where = (k % 2, q, slice(0, count), aligned(j * TILE, TILE))
        return remote(
            r.cs.at[where], r.cr.at[where], r.arcs.at[k, q, j], r.arcr.at[k, q, j], core_peer
        )

    def x_copy(k, q, count, j):
        where = (k % 2, q, slice(0, count), aligned(j * TILE, TILE))
        return remote(
            r.xs.at[where], r.xr.at[where], r.arxs.at[k, q, j], r.arxr.at[k, q, j], x_peer
        )

    def sum_begin(k, q, tile_of, count):
        b = k % 2

        def onward(j):
            cols = aligned(j * TILE, TILE)
            core_copy(k, q, count, j).wait_recv()
            r.xs[b, q, :count, cols] = (
                r.acc[:count, cols] + r.cr[b, q, :count, cols].astype(F32)
            ).astype(BF)
            x_copy(k, q, count, j).start()

        def one(j):
            cols = aligned(j * TILE, TILE)
            part = tile_of(cols)
            r.cs[b, q, :count, cols] = part[:count].astype(BF)
            core_copy(k, q, count, j).start()
            r.acc[:count, cols] = part[count:]
            pl.when(j > 0)(lambda: onward(j - 1))

        loop(tiles, one)
        onward(tiles - 1)

    def sum_end(k, q, count):
        for j in range(tiles):
            x_copy(k, q, count, j).wait()
            core_copy(k, q, count, j).wait_send()

    def sum_rows(k, q, where):
        b = k % 2
        return r.xs[b, q, where].astype(F32) + r.xr[b, q, where].astype(F32)

    def share(k, ref, q):
        where = aligned(own0 + q * ch, ch)
        return remote(ref.at[where], ref.at[where], r.shs.at[k, q], r.shr.at[k, q], core_peer)

    def share_arrival(k, ref, q):
        where = aligned(oth0 + q * ch, ch)
        return remote(ref.at[where], ref.at[where], r.shs.at[k, q], r.shr.at[k, q], core_peer)

    def share_wait(k, ref, q):
        share(k, ref, q).wait_send()
        share_arrival(k, ref, q).wait_recv()

    def both(ref, q, cols=slice(None)):
        return jnp.concatenate(
            [ref[aligned(oth0 + q * ch, ch), cols], ref[aligned(own0 + q * ch, ch), cols]],
            axis=0,
        )

    def put_both(ref, q, cols, value):
        ref[aligned(oth0 + q * ch, ch), cols] = value[:ch]
        ref[aligned(own0 + q * ch, ch), cols] = value[ch:]

    columns = r.vin.shape[0]
    r.vs[...] = jnp.zeros(r.vs.shape, F32)
    r.vs[pl.ds(columns * m, columns), :] = r.vin[...]
    r.vb[0] = r.vs[...].astype(BF)
    mine = aligned(d * vr, vr)
    r.wa[:, mine, :] = r.attend[...].astype(BF)
    r.wr[mine, :] = r.rejoin[...].astype(BF)
    pl.semaphore_wait(barrier, len(model_peers) + n - 1)
    swap = remote(r.vb.at[0], r.vb.at[1], r.vxs.at[0], r.vxr.at[0], core_peer)
    swap.start()
    gather_start_y(ATT)
    gather_start_z(ATT)
    gather_start_y(REJ)
    swap.wait_recv()
    r.vb[2] = r.vb[0] + r.vb[1]
    swap_x = remote(r.vb.at[2], r.vb.at[3], r.vxs.at[1], r.vxr.at[1], x_peer)
    swap_x.start()
    loads[0].wait()
    r.we[mine, :] = r.expand_in[...].astype(BF)
    loads[1].wait()
    r.wn[mine, :] = r.narrow_in[...].astype(BF)
    loads[2].wait()
    swap_x.wait_recv()
    r.wv[d] = r.vb[2] + r.vb[3]
    gather_start_y(VEC)

    r.pb[...] = jnp.full(r.pb.shape, SEQ_LEN, jnp.int32)
    slots = r.pos.shape[1]
    r.pb[0:1, 0:slots] = r.pos[...]
    r.pb[8:9, 0:slots] = r.cho[...]
    pos_row = jnp.broadcast_to(r.pb[0:1, :], (SLOTS, SLOTS))
    cho_row = jnp.broadcast_to(r.pb[8:9, :], (SLOTS, SLOTS))
    pos_col = jnp.transpose(pos_row.astype(F32), (1, 0)).astype(jnp.int32)
    cho_col = jnp.transpose(cho_row.astype(F32), (1, 0)).astype(jnp.int32)
    lane_iota = lax.broadcasted_iota(jnp.int32, (SLOTS, LANES), 1)
    row_iota = lax.broadcasted_iota(jnp.int32, (SLOTS, LANES), 0)
    for j in range(rows // LANES):
        r.oh[:, j * LANES : (j + 1) * LANES] = jnp.where(
            pos_col == lane_iota + j * LANES, 1.0, 0.0
        ).astype(BF)
        r.oht[j * LANES : (j + 1) * LANES, :] = jnp.where(
            pos_row == row_iota + j * LANES, 1.0, 0.0
        ).astype(BF)
    r.low2c[...] = jnp.zeros(r.low2c.shape, BF)
    r.low2c[0 : r.table.shape[0], :] = r.table[...]
    choice = jnp.where(cho_col == lane_iota, 1.0, 0.0).astype(BF)
    for j in range(d_model // TILE):
        r.slt[:, j * TILE : (j + 1) * TILE] = nn(
            choice, r.low2c[:, j * TILE : (j + 1) * TILE]
        ).astype(BF)
    r.mc[...] = jnp.zeros(r.mc.shape, BF)
    r.mc[0:slots, :] = r.mcot[...].reshape(slots, d_model)
    r.vg[...] = jnp.zeros(r.vg.shape, F32)

    gather_pass(ATT, 1)
    gather_start_y(EXP)

    def embed(i):
        where = aligned(i * SUB, SUB)
        hot = r.oht[where, :]
        keep = 1.0 - jnp.sum(hot.astype(F32), axis=1, keepdims=True)
        r.keep[where, :] = keep
        r.xl[where, :] = (r.tok_in[where, :].astype(F32) * keep + nn(hot, r.slt[...])).astype(BF)

    loop(rows // SUB, embed)
    r.st[...] = r.xl[aligned(own0, half), :].astype(F32)

    def transpose_into(target, lane0, source, row0, count):
        for i in range(count // LANES):
            target[:, lane0 + i * LANES : lane0 + (i + 1) * LANES] = low_transpose(
                source[row0 + i * LANES : row0 + (i + 1) * LANES, :]
            )

    for turn in range(2, lines - 1):
        gather_pass(ATT, turn)
    gather_start_z(VEC)
    gather_start_z(REJ)
    gather_pass(ATT, lines - 1)
    gather_start_z(EXP)
    for turn in range(1, lines):
        gather_pass(VEC, turn)
    for turn in range(1, lines):
        gather_pass(REJ, turn)
    gather_wait(VEC)
    gather_pass(EXP, 1)
    gather_wait(ATT)
    gather_start_y(NAR)
    gather_pass(EXP, 2)
    for j in range(n):
        r.vt[:, j * vr : (j + 1) * vr] = r.wv[j].astype(F32)

    def head_bias(row):
        return r.vt[row : row + 1, aligned(m * hw, hw)]

    half_mask = lax.broadcasted_iota(jnp.int32, (1, LANES), 1) < HEAD_DIM

    def lane_half(value, head):
        return jnp.where(half_mask if head % 2 == 0 else jnp.logical_not(half_mask), value, 0)

    def put_heads(ref, q, value):
        for head in range(heads):
            pair = (head // 2) * LANES
            piece = lane_half(value[:, pair : pair + LANES], head)
            ref[head, aligned(oth0 + q * ch, ch), :] = piece[:ch]
            ref[head, aligned(own0 + q * ch, ch), :] = piece[ch:]

    def put_heads_across(ref, q, across):
        for head in range(heads):
            at = (head % 2) * HEAD_DIM
            piece = across[head * HEAD_DIM : (head + 1) * HEAD_DIM, :]
            ref[head, at : at + HEAD_DIM, aligned(oth0 + q * ch, ch)] = piece[:, :ch]
            ref[head, at : at + HEAD_DIM, aligned(own0 + q * ch, ch)] = piece[:, ch:]

    def put_across(ref, q, across):
        ref[:, aligned(oth0 + q * ch, ch)] = across[:, :ch]
        ref[:, aligned(own0 + q * ch, ch)] = across[:, ch:]

    r.qzt[...] = jnp.zeros(r.qzt.shape, BF)

    def share_block(layer, head, lane0, width):
        if layer == 0:
            return r.p0.at[head, :, aligned(lane0, width)]
        return r.gse.at[
            (head // 2) * rows : (head // 2 + 1) * rows,
            aligned((head % 2) * rows + lane0, width),
        ]

    def both_lanes(ref, where, q):
        return jnp.concatenate(
            [ref[where, aligned(oth0 + q * ch, ch)], ref[where, aligned(own0 + q * ch, ch)]],
            axis=1,
        )

    def project(layer, q):
        x = both(r.xl, q)
        queries = (nn(x, r.wa[0]) + head_bias(0)).astype(BF) * jnp.asarray(0.125, BF)
        put_heads(r.qz.at[layer], q, queries)
        put_heads_across(r.qzt.at[layer], q, low_transpose(queries))
        keys = nn(x, r.wa[1]).astype(BF)
        put_both(r.kn.at[layer], q, slice(None), keys)
        put_across(r.kt.at[layer], q, low_transpose(keys))
        values = (nn(x, r.wa[2]) + head_bias(1)).astype(BF)
        put_both(r.vn.at[layer], q, slice(None), values)
        put_across(r.vvt, q, low_transpose(values))

    def attend_forward(layer, q):
        for head in range(heads):
            pair = slice((head // 2) * LANES, (head // 2 + 1) * LANES)
            across = both_lanes(r.qzt.at[layer, head], slice(None), q)
            scores = nn(r.kn[layer, :, pair], across)
            raised = jnp.exp(scores - jnp.max(scores, axis=0, keepdims=True))
            total = jnp.sum(raised, axis=0, keepdims=True)
            low = (raised * (1.0 / total)).astype(BF)
            share_block(layer, head, oth0 + q * ch, ch)[...] = low[:, :ch]
            share_block(layer, head, own0 + q * ch, ch)[...] = low[:, ch:]
            where = slice(head * HEAD_DIM, (head + 1) * HEAD_DIM)
            context = nn(r.vvt[where, :], low).astype(BF)
            r.ct[layer, where, aligned(oth0 + q * ch, ch)] = context[:, :ch]
            r.ct[layer, where, aligned(own0 + q * ch, ch)] = context[:, ch:]
        target = r.ctx if layer == 0 else r.ctx1
        put_both(target, q, slice(None), low_transpose(both_lanes(r.ct.at[layer], slice(None), q)))

    def first_norm(layer, q):
        def one(i):
            at = aligned(q * ch + i * SUB, SUB)
            total = sum_rows(2 * layer, q, aligned(i * SUB, SUB))
            res = r.st[at, :] + (total + r.vt[2:3, :])
            cen = res - jnp.mean(res, axis=1, keepdims=True)
            spread = lax.rsqrt(jnp.mean(cen * cen, axis=1, keepdims=True) + EPS)
            hat = cen * spread
            r.xh1[layer, at, :] = hat
            r.rs1[layer, at, :] = spread
            normed = hat * r.vt[4:5, :] + r.vt[5:6, :]
            r.st[at, :] = normed
            r.normed[aligned(own0 + q * ch + i * SUB, SUB), :] = normed.astype(BF)

        loop(ch // SUB, one)

    def second_norm(layer, q):
        def one(i):
            at = aligned(q * ch + i * SUB, SUB)
            total = sum_rows(2 * layer + 1, q, aligned(i * SUB, SUB))
            res = r.st[at, :] + (total + r.vt[3:4, :])
            cen = res - jnp.mean(res, axis=1, keepdims=True)
            spread = lax.rsqrt(jnp.mean(cen * cen, axis=1, keepdims=True) + EPS)
            hat = cen * spread
            r.xh2[layer, at, :] = hat
            r.rs2[layer, at, :] = spread
            out = hat * r.vt[6:7, :] + r.vt[7:8, :]
            r.st[at, :] = out
            if layer < DEPTH - 1:
                r.xl[aligned(own0 + q * ch + i * SUB, SUB), :] = out.astype(BF)

        loop(ch // SUB, one)

    def unit_act(layer):
        return r.act0 if layer == 0 else r.gsn

    def gelu(v):
        square = v * v
        t = jnp.tanh(GELU_A * v * (1.0 + GELU_B * square))
        return 0.5 * (1.0 + t), t, square

    def gelu_slope(v, gate, t, square):
        return gate + (0.5 * GELU_A) * v * (1.0 - t * t) * (1.0 + (3.0 * GELU_B) * square)

    def widen(layer, q):
        act = unit_act(layer)

        def one(j):
            cols = aligned(j * TILE, TILE)
            v = nn(both(r.normed, q), r.we[:, cols]) + r.vt[pl.ds(8 + m, 1), cols]
            gate, t, square = gelu(v)
            put_both(act, q, cols, (v * gate).astype(BF))
            if layer == 0:
                put_both(r.slope0, q, cols, gelu_slope(v, gate, t, square).astype(BF))

        loop(uw // TILE, one)

    def widen_slots():
        def one(j):
            cols = aligned(j * TILE, TILE)
            v = nn(r.low2c[...], r.we[:, cols]) + r.vt[pl.ds(8 + m, 1), cols]
            gate, t, square = gelu(v)
            r.act0[rows : rows + SLOTS, cols] = (v * gate).astype(BF)
            r.slc[:, cols] = gelu_slope(v, gate, t, square).astype(BF)

        loop(uw // TILE, one)

    def rejoin_sum(layer, q):
        ctx = r.ctx if layer == 0 else r.ctx1
        sum_begin(2 * layer, q, lambda cols: nt(both(ctx, q), r.wr[cols, :]), ch)

    def narrow_sum(layer, q):
        act = unit_act(layer)
        sum_begin(2 * layer + 1, q, lambda cols: nt(both(act, q), r.wn[cols, :]), ch)

    hot = r.oh[...]

    def pick(target, row0, source, source0, width):
        def one(j):
            cols = aligned(j * TILE, TILE)
            target[row0 : row0 + SLOTS, cols] = nn(
                hot, source[source0 : source0 + rows, cols]
            ).astype(BF)

        loop(width // TILE, one)

    by_columns = (2 * vr) % LANES == 0

    def column_core(step):
        cols = aligned((z_from(step) - y) * vr, 2 * vr)
        return remote(
            r.cs.at[1, :, :, cols],
            r.cr.at[1, :, :, cols],
            r.ccs.at[step],
            r.ccr.at[step],
            core_peer,
        )

    def column_x(step):
        cols = aligned((z_from(step) - y) * vr, 2 * vr)
        return remote(
            r.xs.at[1, :, :, cols], r.xr.at[1, :, :, cols], r.cxs.at[step], r.cxr.at[step], x_peer
        )

    def column_sum(step):
        cols = aligned((z_from(step) - y) * vr, 2 * vr)
        weight = r.wn[cols, :]
        away = nt(r.act0[aligned(oth0, half), :], weight).astype(BF)
        for q in range(CHUNKS):
            r.cs[1, q, :, cols] = away[q * ch : (q + 1) * ch]
        column_core(step).start()
        here = nt(r.act0[aligned(own0, half), :], weight)
        column_core(step).wait_recv()
        for q in range(CHUNKS):
            r.xs[1, q, :, cols] = (
                here[q * ch : (q + 1) * ch] + r.cr[1, q, :, cols].astype(F32)
            ).astype(BF)
        column_x(step).start()

    for layer in range(DEPTH):
        for q in range(CHUNKS):
            if layer > 0:
                share_wait(2 * layer - 1, r.xl, q)
            project(layer, q)
        for q in range(CHUNKS):
            attend_forward(layer, q)
            if layer > 0:
                rejoin_sum(layer, q)
            elif q == 0:
                for turn in range(3, lines):
                    gather_pass(EXP, turn)
                gather_start_z(NAR)
        if layer == 0:
            gather_wait(REJ)
            for q in range(CHUNKS):
                rejoin_sum(layer, q)
            gather_pass(NAR, 1)
            transpose_into(r.xt, 0, r.xl, 0, rows)
        else:
            transpose_into(r.xt, rows, r.xl, 0, rows)
        for q in range(CHUNKS):
            sum_end(2 * layer, q, ch)
            first_norm(layer, q)
            share(2 * layer, r.normed, q).start()
            if layer == 0:
                gather_pass(NAR, q + 2)
                if q == 0:
                    gather_wait(EXP)
            share_wait(2 * layer, r.normed, q)
            widen(layer, q)
            if layer > 0:
                narrow_sum(layer, q)
        if layer == 0:
            for turn in range(CHUNKS + 2, lines):
                gather_pass(NAR, turn)
            if by_columns:
                for turn in range(lines):
                    step = gather_order(turn)
                    gather_y_arrival(NAR, step).wait_recv()
                    column_sum(step)
                transpose_into(r.nt, 0, r.normed, 0, rows)
                for step in range(lines):
                    column_x(step).wait()
                    column_core(step).wait_send()
            else:
                transpose_into(r.nt, 0, r.normed, 0, rows)
                gather_wait(NAR)
                for q in range(CHUNKS):
                    narrow_sum(layer, q)
        else:
            pick(r.low2c, 0, r.normed, 0, d_model)
            widen_slots()
            transpose_into(r.nt, rows, r.low2c, 0, SLOTS)
        for q in range(CHUNKS):
            if not (layer == 0 and by_columns):
                sum_end(2 * layer + 1, q, ch)
            second_norm(layer, q)
            if layer < DEPTH - 1:
                share(2 * layer + 1, r.xl, q).start()

    own_rows = aligned(own0, half)
    out_here = pltpu.make_async_copy(r.st, r.act.at[own_rows], r.osem.at[0])
    out_there = remote(r.st, r.act.at[own_rows], r.osem.at[1], r.osem.at[2], core_peer)
    out_arrival = remote(
        r.st, r.act.at[aligned(oth0, half)], r.osem.at[1], r.osem.at[2], core_peer
    )
    out_here.start()
    out_there.start()

    def add_rows(row, value):
        r.vg[row : row + 1, :] += jnp.sum(value, axis=0, keepdims=True)

    def norm_pull(g, hat, spread, gain):
        scaled = g * gain
        mean = jnp.mean(scaled, axis=1, keepdims=True)
        inner = jnp.mean(scaled * hat, axis=1, keepdims=True)
        return spread * (scaled - mean - hat * inner)

    def second_pull(layer, q, gradient):
        def one(i):
            at = aligned(q * ch + i * SUB, SUB)
            g = gradient(i, at)
            hat = r.xh2[layer, at, :]
            add_rows(6, g * hat)
            add_rows(7, g)
            back = norm_pull(g, hat, r.rs2[layer, at, :], r.vt[6:7, :])
            add_rows(3, back)
            r.gb[at, :] = back
            r.low2[aligned(own0 + q * ch + i * SUB, SUB), :] = back.astype(BF)

        loop(ch // SUB, one)

    def first_pull(layer, q, gradient):
        def one(i):
            at = aligned(q * ch + i * SUB, SUB)
            g = gradient(i, at)
            hat = r.xh1[layer, at, :]
            add_rows(4, g * hat)
            add_rows(5, g)
            back = norm_pull(g, hat, r.rs1[layer, at, :], r.vt[4:5, :])
            add_rows(2, back)
            r.gb[at, :] = back
            r.xl[aligned(own0 + q * ch + i * SUB, SUB), :] = back.astype(BF)

        loop(ch // SUB, one)

    def hot_rows(at_start):
        return r.oht[aligned(own0 + at_start, SUB), :]

    def bias_sums(row0):
        for kind, row in ((0, 0), (2, 1)):
            cols = aligned(m * hw, hw)
            r.vg[row : row + 1, cols] += jnp.sum(
                r.dp[kind, row0 : row0 + rows, :].astype(F32), axis=0, keepdims=True
            )

    for q in range(CHUNKS):
        second_pull(1, q, lambda i, at: nn(hot_rows(q * ch + i * SUB), r.mc[...]))
        share(4, r.low2, q).start()
    for q in range(CHUNKS):
        share_wait(4, r.low2, q)
    pick(r.low2c, 0, r.low2, 0, d_model)

    def slot_units(j):
        cols = aligned(j * TILE, TILE)
        back = nn(r.low2c[...], r.wn[:, cols]) * r.slc[:, cols].astype(F32)
        back = back.astype(BF)
        r.be[rows : rows + SLOTS, cols] = back
        r.vg[pl.ds(8 + m, 1), cols] += jnp.sum(back.astype(F32), axis=0, keepdims=True)

    loop(uw // TILE, slot_units)
    slot_own = core * slot_half
    slot_oth = slot_half - slot_own

    def slot_tile(cols):
        part = nt(r.be[rows : rows + SLOTS, :], r.we[cols, :])
        r.part[...] = part
        return jnp.concatenate(
            [
                r.part[aligned(slot_oth, slot_half), :],
                r.part[aligned(slot_own, slot_half), :],
            ],
            axis=0,
        )

    sum_begin(4, 0, slot_tile, slot_half)
    transpose_into(r.l2t, rows, r.low2c, 0, SLOTS)
    for head in range(heads):
        r.qc[head] = nn(hot, r.qz[1, head]).astype(BF)
        source = r.gse[
            (head // 2) * rows : (head // 2 + 1) * rows,
            (head % 2) * rows : (head % 2 + 1) * rows,
        ]
        r.pc[head] = nn(source, r.oht[...]).astype(BF)
    r.cct[...] = nn(r.ct[1], r.oht[...]).astype(BF)
    sum_end(4, 0, slot_half)
    mine_slots = r.slt.at[aligned(slot_own, slot_half)]
    mine_slots[...] = sum_rows(4, 0, slice(0, slot_half)).astype(BF)
    slots_out = remote(mine_slots, mine_slots, r.osem.at[3], r.osem.at[4], core_peer)
    slots_in_ref = r.slt.at[aligned(slot_oth, slot_half)]
    slots_in = remote(slots_in_ref, slots_in_ref, r.osem.at[3], r.osem.at[4], core_peer)
    slots_out.start()
    slots_in.wait_recv()
    for q in range(CHUNKS):
        first_pull(
            1, q, lambda i, at: r.gb[at, :] + nn(hot_rows(q * ch + i * SUB), r.slt[...])
        )
        share(5, r.xl, q).start()

    for q in range(CHUNKS):
        share_wait(5, r.xl, q)
    pick(r.low2c, 0, r.xl, 0, d_model)
    low_ctx = nn(r.low2c[...], r.wr[...]).astype(BF)
    across = low_transpose(low_ctx)
    dq_across = []
    for pair in range(heads // 2):
        lanes = slice(pair * LANES, (pair + 1) * LANES)
        dv = jnp.zeros((rows, LANES), F32)
        dk = jnp.zeros((rows, LANES), F32)
        for head in (2 * pair, 2 * pair + 1):
            where = slice(head * HEAD_DIM, (head + 1) * HEAD_DIM)
            at = (head % 2) * HEAD_DIM
            r.dozt[head, at : at + HEAD_DIM, 0:SLOTS] = across[where, :]
            low = r.pc[head]
            dv += nn(low, lane_half(low_ctx[:, lanes], head))
            dp = nn(r.vn[1, :, lanes], r.dozt[head, :, 0:SLOTS])
            delta = jnp.sum(
                across[where, :].astype(F32) * r.cct[where, :].astype(F32), axis=0, keepdims=True
            )
            ds = (low.astype(F32) * (dp - delta)).astype(BF)
            dk += nn(ds, r.qc[head])
            dq_across.append(nn(r.kt[1, where, :], ds) * 0.125)
        r.dp[1, rows : 2 * rows, lanes] = dk.astype(BF)
        r.dp[2, rows : 2 * rows, lanes] = dv.astype(BF)
    dq = low_transpose(jnp.concatenate(dq_across, axis=0))
    r.dp[0, rows : 2 * rows, :] = nn(r.oht[...], dq).astype(BF)
    bias_sums(rows)

    def layer_rows(k, q, row0):
        def tile_of(cols):
            total = None
            for kind in range(3):
                lhs = jnp.concatenate(
                    [
                        r.dp[kind, aligned(row0 + oth0 + q * ch, ch), :],
                        r.dp[kind, aligned(row0 + own0 + q * ch, ch), :],
                    ],
                    axis=0,
                )
                part = nt(lhs, r.wa[kind, cols, :])
                total = part if total is None else total + part
            return total

        sum_begin(k, q, tile_of, ch)

    for q in range(CHUNKS):
        layer_rows(5, q, rows)
    transpose_into(r.l1t, rows, r.low2c, 0, SLOTS)

    def weight_grad_rows(target, across, latter, width, row0, count):
        at = aligned(row0, count)

        def one(j):
            cols = aligned(j * TILE, TILE)
            target[at, cols] = nn(across[at, :], latter[:, cols]).astype(BF)

        loop(width // TILE, one)

    def weight_grad(target, across, latter, width):
        loop(
            d_model // TILE,
            lambda i: weight_grad_rows(target, across, latter, width, i * TILE, TILE),
        )

    def transpose_both(target, source, q):
        for row0 in (oth0 + q * ch, own0 + q * ch):
            target[:, aligned(row0, ch)] = low_transpose(source[aligned(row0, ch), :])

    def units_back(q):
        def one(j):
            cols = aligned(j * TILE, TILE)
            slope = both(r.slope0, q, cols).astype(F32)
            back = (nn(both(r.low2, q), r.wn[:, cols]) * slope).astype(BF)
            put_both(r.be, q, cols, back)
            r.vg[pl.ds(8 + m, 1), cols] += jnp.sum(back.astype(F32), axis=0, keepdims=True)

        loop(uw // TILE, one)

    for q in range(CHUNKS):
        sum_end(5, q, ch)
        second_pull(
            0, q, lambda i, at: r.gb[at, :] + sum_rows(5, q, aligned(i * SUB, SUB))
        )
        share(6, r.low2, q).start()
        share_wait(6, r.low2, q)
        transpose_both(r.l2t, r.low2, q)
        if q == 0:
            units_back(q)
    if by_columns:
        for turn in range(1, lines + 1):
            owner = ((z + scatter_order(turn)) % lines) * 2 + 1 - y
            weight_grad_rows(r.gsn, r.l2t, r.act0, uw, owner * vr, vr)
            if turn <= 2:
                scatter_y(NAR, scatter_order(turn)).start()
                under_way.append(queue.pop(0))
        ready.append(NAR)
    else:
        weight_grad(r.gsn, r.l2t, r.act0, uw)
        scatter_start(NAR)
    for q in range(CHUNKS):
        if q > 0:
            units_back(q)
        sum_begin(6, q, lambda cols, q=q: nt(both(r.be, q), r.we[cols, :]), ch)
    if by_columns:
        each(
            0,
            lines,
            lambda s: weight_grad_rows(
                r.gsn, r.l2t, r.act0, uw, (((z + s) % lines) * 2 + y) * vr, vr
            ),
        )
    pick(r.ctx, rows, r.ctx1, 0, hw)
    weight_grad(r.gse, r.nt, r.be, uw)
    scatter_start(EXP)
    scatter_pass()
    for q in range(CHUNKS):
        sum_end(6, q, ch)
        first_pull(
            0, q, lambda i, at: r.gb[at, :] + sum_rows(6, q, aligned(i * SUB, SUB))
        )
        share(7, r.xl, q).start()
    scatter_pass()
    for q in range(CHUNKS):
        share_wait(7, r.xl, q)
        back = nn(both(r.xl, q), r.wr[...]).astype(BF)
        put_heads(r.doz, q, back)
        put_heads_across(r.dozt, q, low_transpose(back))

    def head_pair(pair):
        lanes = aligned(pair * LANES, LANES)
        dv = jnp.zeros((rows, LANES), F32)
        dk = jnp.zeros((rows, LANES), F32)
        for side in range(2):
            head = 2 * pair + side
            where = aligned(head * HEAD_DIM, HEAD_DIM)
            for part in range(rows // TILE):
                some = slice(part * TILE, (part + 1) * TILE)
                low = r.p0[head, :, some]
                dv += nn(low, r.doz[head, some, :])
                inner = r.dozt[head, side * HEAD_DIM : (side + 1) * HEAD_DIM, some]
                delta = jnp.sum(
                    inner.astype(F32) * r.ct[0, where, some].astype(F32), axis=0, keepdims=True
                )
                dp = nn(r.vn[0, :, lanes], r.dozt[head, :, some])
                ds = (low.astype(F32) * (dp - delta)).astype(BF)
                dk += nn(ds, r.qz[0, head, some, :])
                r.dqt[where, some] = (nn(r.kt[0, where, :], ds) * 0.125).astype(BF)
        r.dp[1, 0:rows, lanes] = dk.astype(BF)
        r.dp[2, 0:rows, lanes] = dv.astype(BF)

    for pair in range(heads // 2):
        head_pair(pair)
        scatter_pass()
    for i in range(rows // LANES):
        some = slice(i * LANES, (i + 1) * LANES)
        r.dp[0, some, :] = low_transpose(r.dqt[:, some])
    for q in range(CHUNKS):
        layer_rows(7, q, 0)
    scatter_pass()
    bias_sums(0)
    transpose_into(r.l1t, 0, r.xl, 0, rows)
    weight_grad(r.gsr, r.l1t, r.ctx, hw)
    scatter_start(REJ)
    first_of_x = jnp.where(m < 2, 1.0, 0.0)
    r.vg[2:8, :] = r.vg[2:8, :] * first_of_x
    for j in range(n):
        r.gsv[j] = r.vg[:, j * vr : (j + 1) * vr].astype(BF)
    scatter_start(VEC)
    for kind in range(3):
        weight_grad(r.gsa.at[kind], r.xt, r.dp.at[kind], hw)
    scatter_start(ATT)
    scatter_pass()
    out_here.wait()
    out_there.wait_send()
    for q in range(CHUNKS):
        sum_end(7, q, ch)

        def last(i, q=q):
            at = aligned(q * ch + i * SUB, SUB)
            g = r.gb[at, :] + sum_rows(7, q, aligned(i * SUB, SUB))
            r.st[at, :] = g * r.keep[aligned(own0 + q * ch + i * SUB, SUB), :]

        loop(ch // SUB, last)
    in_here = pltpu.make_async_copy(r.st, r.ing.at[own_rows], r.osem.at[5])
    in_there = remote(r.st, r.ing.at[own_rows], r.osem.at[6], r.osem.at[7], core_peer)
    in_arrival = remote(r.st, r.ing.at[aligned(oth0, half)], r.osem.at[6], r.osem.at[7], core_peer)
    in_here.start()
    in_there.start()
    scatter_turn()

    scatter_pass()
    def squares(value):
        value = value * value
        if value.ndim == 3:
            value = jnp.sum(value, axis=0)
        value = jnp.sum(value, axis=0, keepdims=True)
        return jnp.sum(value, axis=1, keepdims=True)

    swap_v = remote(r.vf.at[0], r.vf.at[1], r.vxs.at[2], r.vxr.at[2], core_peer)
    swap_w = remote(r.vf.at[2], r.vf.at[3], r.vxs.at[3], r.vxr.at[3], x_peer)
    total = jnp.zeros((1, 1), F32)
    while under_way:
        turn = under_way[0][1] if under_way[0][0] == ATT else 0
        if turn == 1:
            scatter_finish(NAR, r.gn)
            total = total + squares(r.gn[...])
            scatter_close(NAR)
            for region in range(5):
                gather_close(region)
        elif turn == 2:
            scatter_finish(VEC, r.vf.at[0])
            swap_v.start()
            scatter_finish(REJ, r.gr)
            total = total + squares(r.gr[...])
        elif turn == 3:
            swap_v.wait_recv()
            r.vf[2] = r.vf[0] + r.vf[1]
            swap_w.start()
            scatter_finish(EXP, r.ge)
            total = total + squares(r.ge[...])
            scatter_close(EXP)
            scatter_close(REJ)
        elif turn == 4:
            swap_w.wait_recv()
            r.vs[...] = r.vf[2] + r.vf[3]
            r.gv[...] = r.vs[pl.ds(columns * m, columns), :]
            total = total + squares(r.gv[...])
        scatter_pass()
    scatter_finish(ATT, r.ga)
    total = total + squares(r.ga[...])

    r.nm[m] = jnp.broadcast_to(total, (8, LANES))

    def model_copy(k, slot):
        return remote(r.nm.at[slot], r.nm.at[slot], r.nms.at[k], r.nmr.at[k], model_peers[k])

    for k in range(3):
        model_copy(k, m).start()
    for k in range(3):
        model_copy(k, model_peers[k][1]).wait_recv()
    r.nz[d] = jnp.sum(r.nm[...], axis=0)

    def line_copy(step, slot):
        here = r.nz.at[slot]
        return remote(here, here, r.nzs.at[0, step], r.nzr.at[0, step], z_peer(step))

    def cross_copy(step, slot):
        here = r.nz.at[slot]
        return remote(here, here, r.nzs.at[1, step], r.nzr.at[1, step], zy_peer(step))

    each(0, lines, lambda s: cross_copy(s, d).start())
    each(1, lines, lambda s: line_copy(s, d).start())
    each(0, lines, lambda s: cross_copy(s, z_from(s) + 1 - 2 * y).wait_recv())
    each(1, lines, lambda s: line_copy(s, z_from(s)).wait_recv())
    r.norm[...] = jnp.sqrt(jnp.sum(r.nz[...], axis=0))

    each(0, lines, lambda s: cross_copy(s, d).wait_send())
    each(1, lines, lambda s: line_copy(s, d).wait_send())
    for k in range(3):
        model_copy(k, m).wait_send()
    swap.wait_send()
    swap_x.wait_send()
    swap_v.wait_send()
    swap_w.wait_send()
    slots_out.wait_send()
    scatter_close(VEC)
    scatter_close(ATT)
    out_arrival.wait_recv()
    in_here.wait()
    in_there.wait_send()
    in_arrival.wait_recv()


def run_layers(
    n, tok, pos, cho, table, mcot, attend, rejoin, expand, narrow, vin
):
    rows, d_model = tok.shape
    vr = rejoin.shape[0]
    hw = rejoin.shape[1]
    uw = expand.shape[1]
    lines = n // 2
    half = rows // 2
    ch = half // CHUNKS
    heads = hw // HEAD_DIM
    wide = rows + SLOTS
    inputs = [
        ("tok", tok),
        ("pos", pos),
        ("cho", cho),
        ("table", table),
        ("mcot", mcot),
        ("attend", attend),
        ("rejoin", rejoin),
        ("expand", expand),
        ("narrow", narrow),
        ("vin", vin),
    ]
    outputs = [
        ("act", (rows, d_model), pl.ANY),
        ("ing", (rows, d_model), pl.ANY),
        ("ga", (3, vr, hw), pltpu.VMEM),
        ("gr", (vr, hw), pltpu.VMEM),
        ("ge", (vr, uw), pltpu.VMEM),
        ("gn", (vr, uw), pltpu.VMEM),
        ("gv", vin.shape, pltpu.VMEM),
        ("norm", (8, LANES), pltpu.VMEM),
    ]
    low = [
        ("wv", (n, 16, vr)),
        ("wa", (3, d_model, hw)),
        ("wr", (d_model, hw)),
        ("we", (d_model, uw)),
        ("wn", (d_model, uw)),
        ("gsv", (n, 16, vr)),
        ("gsa", (3, d_model, hw)),
        ("gsr", (d_model, hw)),
        ("gse", (d_model, uw)),
        ("gsn", (d_model, uw)),
        ("yv", (lines, 16, vr)),
        ("ya", (lines, 3, vr, hw)),
        ("yr", (lines, vr, hw)),
        ("ye", (lines, vr, uw)),
        ("yn", (lines, vr, uw)),
        ("zv", (lines, 16, vr)),
        ("za", (lines, 3, vr, hw)),
        ("zr", (lines, vr, hw)),
        ("ze", (lines, vr, uw)),
        ("zn", (lines, vr, uw)),
        ("cs", (2, CHUNKS, ch, d_model)),
        ("cr", (2, CHUNKS, ch, d_model)),
        ("xs", (2, CHUNKS, ch, d_model)),
        ("xr", (2, CHUNKS, ch, d_model)),
        ("vb", (4, 16, vr)),
        ("oh", (SLOTS, rows)),
        ("oht", (rows, SLOTS)),
        ("mc", (SLOTS, d_model)),
        ("xl", (rows, d_model)),
        ("normed", (rows, d_model)),
        ("low2", (rows, d_model)),
        ("xt", (d_model, 2 * rows)),
        ("nt", (d_model, wide)),
        ("l2t", (d_model, wide)),
        ("l1t", (d_model, wide)),
        ("act0", (wide, uw)),
        ("slope0", (rows, uw)),
        ("be", (wide, uw)),
        ("ctx", (wide, hw)),
        ("ctx1", (rows, hw)),
        ("dp", (3, 2 * rows, hw)),
        ("qz", (2, heads, rows, LANES)),
        ("qzt", (2, heads, LANES, rows)),
        ("kn", (2, rows, hw)),
        ("kt", (2, hw, rows)),
        ("vn", (2, rows, hw)),
        ("vvt", (hw, rows)),
        ("ct", (2, hw, rows)),
        ("p0", (heads, rows, rows)),
        ("dqt", (hw, rows)),
        ("slc", (SLOTS, uw)),
        ("low2c", (SLOTS, d_model)),
        ("slt", (SLOTS, d_model)),
        ("qc", (heads, SLOTS, LANES)),
        ("pc", (heads, rows, SLOTS)),
        ("cct", (hw, SLOTS)),
        ("tok_in", (rows, d_model)),
    ]
    full = [
        ("vt", (16, d_model)),
        ("vg", (16, d_model)),
        ("keep", (rows, 1)),
        ("st", (half, d_model)),
        ("gb", (half, d_model)),
        ("xh1", (2, half, d_model)),
        ("xh2", (2, half, d_model)),
        ("rs1", (2, half, 1)),
        ("rs2", (2, half, 1)),
        ("acc", (ch, d_model)),
        ("part", (SLOTS, TILE)),
        ("vf", (4, 16, vr)),
        ("vs", (16, vr)),
        ("expand_in", (vr, uw)),
        ("narrow_in", (vr, uw)),
        ("nm", (4, 8, LANES)),
        ("nz", (n, 8, LANES)),
    ]
    sems = [
        ("agzs", (5, lines + 3)),
        ("agzr", (5, lines)),
        ("agys", (5, lines)),
        ("agyr", (5, lines)),
        ("rsys", (5, lines)),
        ("rsyr", (5, lines)),
        ("rszs", (5, lines)),
        ("rszr", (5, lines)),
        ("arcs", (8, CHUNKS, d_model // TILE)),
        ("arcr", (8, CHUNKS, d_model // TILE)),
        ("arxs", (8, CHUNKS, d_model // TILE)),
        ("arxr", (8, CHUNKS, d_model // TILE)),
        ("shs", (8, CHUNKS)),
        ("shr", (8, CHUNKS)),
        ("vxs", (4,)),
        ("vxr", (4,)),
        ("osem", (8,)),
        ("lsem", (3,)),
        ("nms", (3,)),
        ("nmr", (3,)),
        ("nzs", (2, lines)),
        ("nzr", (2, lines)),
        ("ccs", (lines,)),
        ("ccr", (lines,)),
        ("cxs", (lines,)),
        ("cxr", (lines,)),
    ]
    names = (
        [name for name, _ in inputs]
        + [name for name, _, _ in outputs]
        + [name for name, _ in low]
        + [name for name, _ in full]
        + ["pb"]
        + [name for name, _ in sems]
    )
    sizes = (n, d_model, rows, hw, uw, vr)

    def body(*refs):
        layer_kernel(names, sizes, *refs)

    return pl.pallas_call(
        body,
        out_shape=[jax.ShapeDtypeStruct(shape, F32) for _, shape, _ in outputs],
        in_specs=[
            pl.BlockSpec(
                memory_space=pl.ANY if name in ("tok", "expand", "narrow") else pltpu.VMEM
            )
            for name, _ in inputs
        ],
        out_specs=[pl.BlockSpec(memory_space=space) for _, _, space in outputs],
        scratch_shapes=[pltpu.VMEM(shape, BF) for _, shape in low]
        + [pltpu.VMEM(shape, F32) for _, shape in full]
        + [pltpu.VMEM((16, LANES), jnp.int32)]
        + [pltpu.SemaphoreType.DMA(shape) for _, shape in sems],
        compiler_params=pltpu.CompilerParams(
            collective_id=0, has_side_effects=True, vmem_limit_bytes=61 * 1024 * 1024
        ),
        cost_estimate=pl.CostEstimate(
            flops=20_000_000_000, bytes_accessed=20_000_000, transcendentals=4_000_000
        ),
    )(*[value for _, value in inputs])


def apply_update(weight, first_moment, second_moment, shadow, gradient, step_rate):
    momentum = 0.5 * first_moment + 0.5 * gradient
    variance = 0.5 * second_moment + 0.5 * gradient * gradient
    bias_fix = 1.0 - 0.5**STEP
    updated = weight - step_rate * (
        momentum / bias_fix / (jnp.sqrt(variance / bias_fix) + 1e-08) + 0.01 * weight
    )
    average = 0.999 * shadow + 0.001 * updated
    return (updated, momentum, variance, average, updated.astype(BF))


def update_kernel(rates, clip_limit, norm, act, ing, *refs):
    *refs, norm_out, act_out, ing_out = refs
    act_out[...] = act[...]
    ing_out[...] = ing[...]
    norm_out[...] = norm[0:1, 0:1]
    factor = jnp.minimum(1.0, clip_limit / (norm[0:1, 0:1] + 1e-06))
    ins, outs = refs[: 5 * len(rates)], refs[5 * len(rates) :]
    for index, rate in enumerate(rates):
        weight, first, second, shadow, gradient = ins[5 * index : 5 * index + 5]
        targets = outs[5 * index : 5 * index + 5]
        for part in range(weight.shape[0]) if len(weight.shape) == 3 else (slice(None),):
            results = apply_update(
                weight[part],
                first[part],
                second[part],
                shadow[part],
                gradient[part] * factor,
                rate,
            )
            for target, value in zip(targets, results, strict=True):
                target[part] = value


def run_update(groups, rates, norm, clip_limit, act, ing):
    vr = groups[1][0].shape[0]
    step = min(vr, 64)

    def spec(shape, whole):
        if whole:
            return pl.BlockSpec(shape, lambda i: (0, 0))
        if len(shape) == 3:
            return pl.BlockSpec((shape[0], step, shape[2]), lambda i: (0, i, 0))
        return pl.BlockSpec((step, shape[1]), lambda i: (i, 0))

    last = len(groups) - 1
    passed = pl.BlockSpec((act.shape[0] * step // vr, act.shape[1]), lambda i: (i, 0))
    specs = [spec(group[0].shape, k == last) for k, group in enumerate(groups)]

    def body(*refs):
        update_kernel(rates, clip_limit, *refs)

    flat = [value for group in groups for value in group]
    size = sum(value.size for value in flat) * 4
    outs = pl.pallas_call(
        body,
        grid=(vr // step,),
        in_specs=[spec(norm.shape, True)]
        + [passed] * 2
        + [one for one in specs for _ in range(5)],
        out_specs=[one for one in specs for _ in range(5)]
        + [spec((1, 1), True)]
        + [passed] * 2,
        out_shape=[
            jax.ShapeDtypeStruct(group[0].shape, kind)
            for group in groups
            for kind in (F32, F32, F32, F32, BF)
        ]
        + [jax.ShapeDtypeStruct(shape, F32) for shape in ((1, 1), act.shape, ing.shape)],
        compiler_params=pltpu.CompilerParams(vmem_limit_bytes=60 * 1024 * 1024),
        cost_estimate=pl.CostEstimate(flops=size, bytes_accessed=2 * size, transcendentals=0),
    )(norm, act, ing, *flat)
    groups_out = [outs[5 * k : 5 * k + 5] for k in range(len(groups))]
    return groups_out, outs[-3].reshape(()), *outs[-2:]


def per_device(
    tokens_in,
    masked_positions,
    replace_choice,
    replace_table,
    masked_cotangent,
    attend,
    attend_mean,
    attend_square,
    attend_shadow,
    rejoin,
    rejoin_mean,
    rejoin_square,
    rejoin_shadow,
    expand,
    expand_mean,
    expand_square,
    expand_shadow,
    narrow,
    narrow_mean,
    narrow_square,
    narrow_shadow,
    vectors,
    vectors_mean,
    vectors_square,
    vectors_shadow,
):
    n = lax.axis_size("dp")
    act, ing, ga, gr, ge, gn, gv, norm = run_layers(
        n,
        tokens_in,
        masked_positions,
        replace_choice,
        replace_table,
        masked_cotangent,
        attend.transpose(1, 0, 2),
        rejoin,
        expand,
        narrow,
        vectors.T,
    )
    d_model = tokens_in.shape[1]
    param_count = 4 * d_model * d_model + 2 * d_model * expand.shape[1] * 4 + 12 * d_model
    clip_limit = 0.001 * math.sqrt(param_count * tokens_in.shape[0] * n)
    cubes = [x.transpose(1, 0, 2) for x in (attend, attend_mean, attend_square, attend_shadow)]
    rows_of = [x.T for x in (vectors, vectors_mean, vectors_square, vectors_shadow)]
    new, gradient_norm, act, ing = run_update(
        (
            (*cubes, ga),
            (rejoin, rejoin_mean, rejoin_square, rejoin_shadow, gr),
            (expand, expand_mean, expand_square, expand_shadow, ge),
            (narrow, narrow_mean, narrow_square, narrow_shadow, gn),
            (*rows_of, gv),
        ),
        (0.04, 0.16, 0.04, 0.04, 0.5),
        norm,
        clip_limit,
        act,
        ing,
    )
    results = [act, ing, gradient_norm]
    results.extend(x.transpose(1, 0, 2) for x in new[0])
    for group in new[1:4]:
        results.extend(group)
    results.extend(x.T for x in new[4])
    return tuple(results)


def solution(mesh):
    row = P("dp", None)
    cube = P("dp", None, "mp")
    flat = P("dp", "mp")
    return jax.shard_map(
        per_device,
        mesh=mesh,
        in_specs=(row, row, row, P(), P("dp", None, None)) + (cube,) * 4 + (flat,) * 16,
        out_specs=(row, row, P()) + (cube,) * 5 + (flat,) * 20,
        check_vma=False,
    )
```

```python
import math
from types import SimpleNamespace

import jax
import jax.numpy as jnp
from jax import lax
from jax.experimental import pallas as pl
from jax.experimental.pallas import tpu as pltpu
from jax.sharding import PartitionSpec as P

HEAD_DIM = 64
SEQ_LEN = 512
DEPTH = 2
STEP = 7
EPS = 1e-05
BF = jnp.bfloat16
F32 = jnp.float32
MESH = pl.DeviceIdType.MESH
LANES = 128
TILE = 256
SLOTS = 128
CHUNKS = 2
SUB = 64
VEC, ATT, REJ, EXP, NAR = range(5)
GELU_A = 0.7978845608028654
GELU_B = 0.044715


def nn(former, latter):
    return jnp.dot(former, latter, preferred_element_type=F32)


def nt(former, latter):
    return lax.dot_general(former, latter, (((1,), (1,)), ((), ())), preferred_element_type=F32)


def low_transpose(block):
    return jnp.transpose(block.astype(F32), (1, 0)).astype(BF)


def loop(count, body):
    def step(index, carry):
        body(index)
        return carry

    lax.fori_loop(0, count, step, 0)


def each(first, last, body):
    if last - first <= 8:
        for index in range(first, last):
            body(index)
    else:

        def step(index, carry):
            body(index)
            return carry

        lax.fori_loop(first, last, step, 0)


def aligned(index, size):
    return pl.ds(pl.multiple_of(index, size), size)


def layer_kernel(names, sizes, *refs):
    r = SimpleNamespace(**dict(zip(names, refs, strict=True)))
    n, d_model, rows, hw, uw, vr = sizes
    r.doz, r.dozt = r.qz.at[1], r.qzt.at[1]
    half = rows // 2
    ch = half // CHUNKS
    lines = n // 2
    heads = hw // HEAD_DIM
    slot_half = SLOTS // 2

    d = lax.axis_index("dp")
    m = lax.axis_index("mp")
    z, y = d // 2, d % 2
    core = m % 2
    core_peer = (d, m + 1 - 2 * core)
    x_peer = (d, (m + 2) % 4)
    y_peer = (d + 1 - 2 * y, m)
    model_peers = (core_peer, x_peer, (d, 3 - m))
    own0 = core * half
    oth0 = half - own0

    weights = (r.wv, r.wa, r.wr, r.we, r.wn)
    grads = (r.gsv, r.gsa, r.gsr, r.gse, r.gsn)
    from_y = (r.yv, r.ya, r.yr, r.ye, r.yn)
    from_z = (r.zv, r.za, r.zr, r.ze, r.zn)

    def z_peer(step):
        return (((z + step) % lines) * 2 + y, m)

    def zy_peer(step):
        return (((z + step) % lines) * 2 + 1 - y, m)

    def z_from(step):
        return ((z + lines - step) % lines) * 2 + y

    def block(ref, region, index):
        if region == VEC:
            return ref.at[index]
        where = aligned(index * vr, vr)
        return ref.at[:, where, :] if region == ATT else ref.at[where, :]

    def remote(source, target, send, recv, device):
        return pltpu.make_async_remote_copy(
            src_ref=source,
            dst_ref=target,
            send_sem=send,
            recv_sem=recv,
            device_id=device,
            device_id_type=MESH,
        )

    loads = [
        pltpu.make_async_copy(source, target, r.lsem.at[k])
        for k, (source, target) in enumerate(
            ((r.expand, r.expand_in), (r.narrow, r.narrow_in), (r.tok, r.tok_in))
        )
    ]
    for load in loads:
        load.start()

    barrier = pltpu.get_barrier_semaphore()

    def greet(peer):
        pl.semaphore_signal(barrier, inc=1, device_id=peer, device_id_type=MESH)

    for peer in model_peers:
        greet(peer)
    each(1, lines, lambda s: greet(z_peer(s)))
    each(0, lines, lambda s: greet(zy_peer(s)))

    relay = lines == 4
    last_line = lines - 1
    inner = jnp.logical_and(z > 0, z < last_line)
    far_end = (jnp.where(z == 1, 0, last_line) * 2 + y, m)
    near_mid = (jnp.where(z == 0, 1, last_line - 1) * 2 + y, m)

    def gather_z(region, step):
        piece = block(weights[region], region, d)
        return remote(
            piece, piece, r.agzs.at[region, step], r.agzr.at[region, step], z_peer(step)
        )

    def gather_z_arrival(region, step):
        piece = block(weights[region], region, z_from(step))
        return remote(
            piece, piece, r.agzs.at[region, step], r.agzr.at[region, step], z_peer(step)
        )

    def gather_onward(region, turn):
        piece = block(weights[region], region, z_from(gather_order(turn)))
        if turn == 3:
            target = far_end
            arrives_as = jnp.where(z == 1, 1, last_line)
        else:
            target = ((z + 3 - 2 * turn) * 2 + y, m)
            arrives_as = 2
        return remote(
            piece,
            piece,
            r.agzs.at[region, last_line + turn],
            r.agzr.at[region, arrives_as],
            target,
        )

    def gather_y(region, step):
        piece = block(weights[region], region, z_from(step))
        return remote(piece, piece, r.agys.at[region, step], r.agyr.at[region, step], y_peer)

    def gather_y_arrival(region, step):
        piece = block(weights[region], region, z_from(step) + 1 - 2 * y)
        return remote(piece, piece, r.agys.at[region, step], r.agyr.at[region, step], y_peer)

    def near(step, body):
        if not relay:
            body()
        elif step != 2:
            pl.when(z < last_line if step == 1 else z > 0)(body)

    def gather_start_z(region):
        for step in range(1, lines):
            near(step, lambda: gather_z(region, step).start())

    def gather_start_y(region):
        gather_y(region, 0).start()

    def gather_order(turn):
        if not relay or turn == 0:
            return turn
        if turn == 1:
            return jnp.where(z == 0, last_line, 1)
        if turn == 2:
            return jnp.where(inner, last_line, 2)
        return jnp.where(inner, 2, jnp.where(z == 0, 1, last_line))

    def gather_pass(region, turn):
        step = gather_order(turn)
        gather_z_arrival(region, step).wait_recv()
        if relay:
            pl.when(inner)(lambda: gather_onward(region, turn).start())
        gather_y(region, step).start()

    def gather_wait(region):
        each(0, lines, lambda s: gather_y_arrival(region, s).wait_recv())

    def gather_close(region):
        for step in range(1, lines):
            near(step, lambda: gather_z(region, step).wait_send())
        if relay:
            for turn in range(1, lines):
                pl.when(inner)(lambda: gather_onward(region, turn).wait_send())
        each(0, lines, lambda s: gather_y(region, s).wait_send())

    def scatter_y(region, step):
        owner = ((z + step) % lines) * 2 + 1 - y
        return remote(
            block(grads[region], region, owner),
            from_y[region].at[step],
            r.rsys.at[region, step],
            r.rsyr.at[region, step],
            y_peer,
        )

    def scatter_z(region, step):
        owner = ((z + step) % lines) * 2 + y
        return remote(
            block(grads[region], region, owner),
            from_z[region].at[step],
            r.rszs.at[region, step],
            r.rszr.at[region, step],
            z_peer(step),
        )

    def scatter_far(region, step):
        owner = ((z + step) % lines) * 2 + y
        return remote(
            block(grads[region], region, owner),
            from_z[region].at[0],
            r.rszs.at[region, step],
            r.rszr.at[region, 0],
            near_mid,
        )

    def scatter_order(turn):
        if not relay:
            return turn % lines
        if turn == 1:
            return jnp.where(z == 0, last_line, 1)
        if turn == 2:
            return jnp.where(z == 0, 1, last_line)
        return 2 if turn == 3 else 0

    def scatter_cross(step):
        owner = ((z + step) % lines) * 2 + 1 - y
        return remote(
            block(grads[REJ], REJ, owner),
            from_y[REJ].at[step],
            r.rsys.at[REJ, step],
            r.rsyr.at[REJ, step],
            z_peer(step),
        )

    def scatter_turn():
        piece = block(grads[REJ], REJ, d + 1 - 2 * y)
        total = piece[...].astype(F32)
        for step in range(1, lines):
            scatter_cross(step).wait_recv()
            total = total + from_y[REJ][step].astype(F32)
        piece[...] = total.astype(BF)
        scatter_y(REJ, 0).start()

    def scatter_start(region):
        if region == REJ:
            each(1, lines, lambda s: scatter_z(REJ, s).start())
            each(1, lines, lambda s: scatter_cross(s).start())
            return
        ready.append(region)
        scatter_next()

    ready = []
    order = (NAR, EXP, VEC, ATT)
    queue = [(region, turn) for region in order for turn in range(1, lines + 1)]
    under_way = []
    weight_of = {NAR: 4, EXP: 4, ATT: 3, VEC: 1}

    def scatter_next():
        while queue and queue[0][0] in ready:
            if sum(weight_of[region] for region, _ in under_way) > 8:
                break
            region, turn = queue.pop(0)
            scatter_y(region, scatter_order(turn)).start()
            under_way.append((region, turn))

    def scatter_pass():
        region, turn = under_way[0]
        step = scatter_order(turn)
        scatter_y(region, step).wait_recv()
        under_way.pop(0)
        scatter_next()
        if turn == lines:
            return
        piece = block(grads[region], region, ((z + step) % lines) * 2 + y)
        total = piece[...].astype(F32) + from_y[region][step].astype(F32)
        piece[...] = total.astype(BF)
        if not relay:
            scatter_z(region, step).start()
        elif turn == 1:
            pl.when(inner)(lambda: scatter_z(region, step).start())
            pl.when(jnp.logical_not(inner))(lambda: scatter_far(region, step).start())
        elif turn == 2:
            scatter_z(region, step).start()
        else:

            @pl.when(inner)
            def _():
                scatter_far(region, 0).wait_recv()
                piece[...] = (total + from_z[region][0].astype(F32)).astype(BF)

            scatter_z(region, step).start()

    def scatter_finish(region, out_ref):
        def one(step):
            scatter_z(region, step).wait_recv()
            out_ref[...] += from_z[region][step].astype(F32)

        if region == REJ:
            scatter_y(region, 0).wait_recv()
        piece = block(grads[region], region, d)
        out_ref[...] = piece[...].astype(F32) + from_y[region][0].astype(F32)
        for step in range(1, lines):
            if not relay or region == REJ or step == 2:
                one(step)
            else:
                pl.when(z > 0 if step == 1 else z < last_line)(lambda: one(step))

    def scatter_close(region):
        each(0, lines, lambda s: scatter_y(region, s).wait_send())
        each(1, lines, lambda s: scatter_z(region, s).wait_send())

    tiles = d_model // TILE

    def core_copy(k, q, count, j):
        where = (k % 2, q, slice(0, count), aligned(j * TILE, TILE))
        return remote(
            r.cs.at[where], r.cr.at[where], r.arcs.at[k, q, j], r.arcr.at[k, q, j], core_peer
        )

    def x_copy(k, q, count, j):
        where = (k % 2, q, slice(0, count), aligned(j * TILE, TILE))
        return remote(
            r.xs.at[where], r.xr.at[where], r.arxs.at[k, q, j], r.arxr.at[k, q, j], x_peer
        )

    def sum_begin(k, q, tile_of, count):
        b = k % 2

        def onward(j):
            cols = aligned(j * TILE, TILE)
            core_copy(k, q, count, j).wait_recv()
            r.xs[b, q, :count, cols] = (
                r.acc[:count, cols] + r.cr[b, q, :count, cols].astype(F32)
            ).astype(BF)
            x_copy(k, q, count, j).start()

        def one(j):
            cols = aligned(j * TILE, TILE)
            part = tile_of(cols)
            r.cs[b, q, :count, cols] = part[:count].astype(BF)
            core_copy(k, q, count, j).start()
            r.acc[:count, cols] = part[count:]
            pl.when(j > 0)(lambda: onward(j - 1))

        loop(tiles, one)
        onward(tiles - 1)

    def sum_end(k, q, count):
        for j in range(tiles):
            x_copy(k, q, count, j).wait()
            core_copy(k, q, count, j).wait_send()

    def sum_rows(k, q, where):
        b = k % 2
        return r.xs[b, q, where].astype(F32) + r.xr[b, q, where].astype(F32)

    def share(k, ref, q):
        where = aligned(own0 + q * ch, ch)
        return remote(ref.at[where], ref.at[where], r.shs.at[k, q], r.shr.at[k, q], core_peer)

    def share_arrival(k, ref, q):
        where = aligned(oth0 + q * ch, ch)
        return remote(ref.at[where], ref.at[where], r.shs.at[k, q], r.shr.at[k, q], core_peer)

    def share_wait(k, ref, q):
        share(k, ref, q).wait_send()
        share_arrival(k, ref, q).wait_recv()

    def both(ref, q, cols=slice(None)):
        return jnp.concatenate(
            [ref[aligned(oth0 + q * ch, ch), cols], ref[aligned(own0 + q * ch, ch), cols]],
            axis=0,
        )

    def put_both(ref, q, cols, value):
        ref[aligned(oth0 + q * ch, ch), cols] = value[:ch]
        ref[aligned(own0 + q * ch, ch), cols] = value[ch:]

    columns = r.vin.shape[0]
    r.vs[...] = jnp.zeros(r.vs.shape, F32)
    r.vs[pl.ds(columns * m, columns), :] = r.vin[...]
    r.vb[0] = r.vs[...].astype(BF)
    mine = aligned(d * vr, vr)
    r.wa[:, mine, :] = r.attend[...].astype(BF)
    r.wr[mine, :] = r.rejoin[...].astype(BF)
    pl.semaphore_wait(barrier, len(model_peers) + n - 1)
    swap = remote(r.vb.at[0], r.vb.at[1], r.vxs.at[0], r.vxr.at[0], core_peer)
    swap.start()
    gather_start_y(ATT)
    gather_start_z(ATT)
    gather_start_y(REJ)
    swap.wait_recv()
    r.vb[2] = r.vb[0] + r.vb[1]
    swap_x = remote(r.vb.at[2], r.vb.at[3], r.vxs.at[1], r.vxr.at[1], x_peer)
    swap_x.start()
    loads[0].wait()
    r.we[mine, :] = r.expand_in[...].astype(BF)
    loads[1].wait()
    r.wn[mine, :] = r.narrow_in[...].astype(BF)
    loads[2].wait()
    swap_x.wait_recv()
    r.wv[d] = r.vb[2] + r.vb[3]
    gather_start_y(VEC)

    r.pb[...] = jnp.full(r.pb.shape, SEQ_LEN, jnp.int32)
    slots = r.pos.shape[1]
    r.pb[0:1, 0:slots] = r.pos[...]
    r.pb[8:9, 0:slots] = r.cho[...]
    pos_row = jnp.broadcast_to(r.pb[0:1, :], (SLOTS, SLOTS))
    cho_row = jnp.broadcast_to(r.pb[8:9, :], (SLOTS, SLOTS))
    pos_col = jnp.transpose(pos_row.astype(F32), (1, 0)).astype(jnp.int32)
    cho_col = jnp.transpose(cho_row.astype(F32), (1, 0)).astype(jnp.int32)
    lane_iota = lax.broadcasted_iota(jnp.int32, (SLOTS, LANES), 1)
    row_iota = lax.broadcasted_iota(jnp.int32, (SLOTS, LANES), 0)
    for j in range(rows // LANES):
        r.oh[:, j * LANES : (j + 1) * LANES] = jnp.where(
            pos_col == lane_iota + j * LANES, 1.0, 0.0
        ).astype(BF)
        r.oht[j * LANES : (j + 1) * LANES, :] = jnp.where(
            pos_row == row_iota + j * LANES, 1.0, 0.0
        ).astype(BF)
    r.low2c[...] = jnp.zeros(r.low2c.shape, BF)
    r.low2c[0 : r.table.shape[0], :] = r.table[...]
    choice = jnp.where(cho_col == lane_iota, 1.0, 0.0).astype(BF)
    for j in range(d_model // TILE):
        r.slt[:, j * TILE : (j + 1) * TILE] = nn(
            choice, r.low2c[:, j * TILE : (j + 1) * TILE]
        ).astype(BF)
    r.mc[...] = jnp.zeros(r.mc.shape, BF)
    r.mc[0:slots, :] = r.mcot[...].reshape(slots, d_model)
    r.vg[...] = jnp.zeros(r.vg.shape, F32)

    gather_pass(ATT, 1)
    gather_start_y(EXP)

    def embed(i):
        where = aligned(i * SUB, SUB)
        hot = r.oht[where, :]
        keep = 1.0 - jnp.sum(hot.astype(F32), axis=1, keepdims=True)
        r.keep[where, :] = keep
        r.xl[where, :] = (r.tok_in[where, :].astype(F32) * keep + nn(hot, r.slt[...])).astype(BF)

    loop(rows // SUB, embed)
    r.st[...] = r.xl[aligned(own0, half), :].astype(F32)

    def transpose_into(target, lane0, source, row0, count):
        for i in range(count // LANES):
            target[:, lane0 + i * LANES : lane0 + (i + 1) * LANES] = low_transpose(
                source[row0 + i * LANES : row0 + (i + 1) * LANES, :]
            )

    for turn in range(2, lines - 1):
        gather_pass(ATT, turn)
    gather_start_z(VEC)
    gather_start_z(REJ)
    gather_pass(ATT, lines - 1)
    gather_start_z(EXP)
    for turn in range(1, lines):
        gather_pass(VEC, turn)
    for turn in range(1, lines):
        gather_pass(REJ, turn)
    gather_wait(VEC)
    gather_pass(EXP, 1)
    gather_wait(ATT)
    gather_start_y(NAR)
    gather_pass(EXP, 2)
    for j in range(n):
        r.vt[:, j * vr : (j + 1) * vr] = r.wv[j].astype(F32)

    def head_bias(row):
        return r.vt[row : row + 1, aligned(m * hw, hw)]

    half_mask = lax.broadcasted_iota(jnp.int32, (1, LANES), 1) < HEAD_DIM

    def lane_half(value, head):
        return jnp.where(half_mask if head % 2 == 0 else jnp.logical_not(half_mask), value, 0)

    def put_heads(ref, q, value):
        for head in range(heads):
            pair = (head // 2) * LANES
            piece = lane_half(value[:, pair : pair + LANES], head)
            ref[head, aligned(oth0 + q * ch, ch), :] = piece[:ch]
            ref[head, aligned(own0 + q * ch, ch), :] = piece[ch:]

    def put_heads_across(ref, q, across):
        for head in range(heads):
            at = (head % 2) * HEAD_DIM
            piece = across[head * HEAD_DIM : (head + 1) * HEAD_DIM, :]
            ref[head, at : at + HEAD_DIM, aligned(oth0 + q * ch, ch)] = piece[:, :ch]
            ref[head, at : at + HEAD_DIM, aligned(own0 + q * ch, ch)] = piece[:, ch:]

    def put_across(ref, q, across):
        ref[:, aligned(oth0 + q * ch, ch)] = across[:, :ch]
        ref[:, aligned(own0 + q * ch, ch)] = across[:, ch:]

    r.qzt[...] = jnp.zeros(r.qzt.shape, BF)

    def share_block(layer, head, lane0, width):
        if layer == 0:
            return r.p0.at[head, :, aligned(lane0, width)]
        return r.gse.at[
            (head // 2) * rows : (head // 2 + 1) * rows,
            aligned((head % 2) * rows + lane0, width),
        ]

    def both_lanes(ref, where, q):
        return jnp.concatenate(
            [ref[where, aligned(oth0 + q * ch, ch)], ref[where, aligned(own0 + q * ch, ch)]],
            axis=1,
        )

    def project(layer, q):
        x = both(r.xl, q)
        queries = (nn(x, r.wa[0]) + head_bias(0)).astype(BF) * jnp.asarray(0.125, BF)
        put_heads(r.qz.at[layer], q, queries)
        put_heads_across(r.qzt.at[layer], q, low_transpose(queries))
        keys = nn(x, r.wa[1]).astype(BF)
        put_both(r.kn.at[layer], q, slice(None), keys)
        put_across(r.kt.at[layer], q, low_transpose(keys))
        values = (nn(x, r.wa[2]) + head_bias(1)).astype(BF)
        put_both(r.vn.at[layer], q, slice(None), values)
        put_across(r.vvt, q, low_transpose(values))

    def attend_forward(layer, q):
        for head in range(heads):
            pair = slice((head // 2) * LANES, (head // 2 + 1) * LANES)
            across = both_lanes(r.qzt.at[layer, head], slice(None), q)
            scores = nn(r.kn[layer, :, pair], across)
            raised = jnp.exp(scores - jnp.max(scores, axis=0, keepdims=True))
            total = jnp.sum(raised, axis=0, keepdims=True)
            low = (raised * (1.0 / total)).astype(BF)
            share_block(layer, head, oth0 + q * ch, ch)[...] = low[:, :ch]
            share_block(layer, head, own0 + q * ch, ch)[...] = low[:, ch:]
            where = slice(head * HEAD_DIM, (head + 1) * HEAD_DIM)
            context = nn(r.vvt[where, :], low).astype(BF)
            r.ct[layer, where, aligned(oth0 + q * ch, ch)] = context[:, :ch]
            r.ct[layer, where, aligned(own0 + q * ch, ch)] = context[:, ch:]
        target = r.ctx if layer == 0 else r.ctx1
        put_both(target, q, slice(None), low_transpose(both_lanes(r.ct.at[layer], slice(None), q)))

    def first_norm(layer, q):
        def one(i):
            at = aligned(q * ch + i * SUB, SUB)
            total = sum_rows(2 * layer, q, aligned(i * SUB, SUB))
            res = r.st[at, :] + (total + r.vt[2:3, :])
            cen = res - jnp.mean(res, axis=1, keepdims=True)
            spread = lax.rsqrt(jnp.mean(cen * cen, axis=1, keepdims=True) + EPS)
            hat = cen * spread
            r.xh1[layer, at, :] = hat
            r.rs1[layer, at, :] = spread
            normed = hat * r.vt[4:5, :] + r.vt[5:6, :]
            r.st[at, :] = normed
            r.normed[aligned(own0 + q * ch + i * SUB, SUB), :] = normed.astype(BF)

        loop(ch // SUB, one)

    def second_norm(layer, q):
        def one(i):
            at = aligned(q * ch + i * SUB, SUB)
            total = sum_rows(2 * layer + 1, q, aligned(i * SUB, SUB))
            res = r.st[at, :] + (total + r.vt[3:4, :])
            cen = res - jnp.mean(res, axis=1, keepdims=True)
            spread = lax.rsqrt(jnp.mean(cen * cen, axis=1, keepdims=True) + EPS)
            hat = cen * spread
            r.xh2[layer, at, :] = hat
            r.rs2[layer, at, :] = spread
            out = hat * r.vt[6:7, :] + r.vt[7:8, :]
            r.st[at, :] = out
            if layer < DEPTH - 1:
                r.xl[aligned(own0 + q * ch + i * SUB, SUB), :] = out.astype(BF)

        loop(ch // SUB, one)

    def unit_act(layer):
        return r.act0 if layer == 0 else r.gsn

    def gelu(v):
        square = v * v
        t = jnp.tanh(GELU_A * v * (1.0 + GELU_B * square))
        return 0.5 * (1.0 + t), t, square

    def gelu_slope(v, gate, t, square):
        return gate + (0.5 * GELU_A) * v * (1.0 - t * t) * (1.0 + (3.0 * GELU_B) * square)

    def widen(layer, q):
        act = unit_act(layer)

        def one(j):
            cols = aligned(j * TILE, TILE)
            v = nn(both(r.normed, q), r.we[:, cols]) + r.vt[pl.ds(8 + m, 1), cols]
            gate, t, square = gelu(v)
            put_both(act, q, cols, (v * gate).astype(BF))
            if layer == 0:
                put_both(r.slope0, q, cols, gelu_slope(v, gate, t, square).astype(BF))

        loop(uw // TILE, one)

    def widen_slots():
        def one(j):
            cols = aligned(j * TILE, TILE)
            v = nn(r.low2c[...], r.we[:, cols]) + r.vt[pl.ds(8 + m, 1), cols]
            gate, t, square = gelu(v)
            r.act0[rows : rows + SLOTS, cols] = (v * gate).astype(BF)
            r.slc[:, cols] = gelu_slope(v, gate, t, square).astype(BF)

        loop(uw // TILE, one)

    def rejoin_sum(layer, q):
        ctx = r.ctx if layer == 0 else r.ctx1
        sum_begin(2 * layer, q, lambda cols: nt(both(ctx, q), r.wr[cols, :]), ch)

    def narrow_sum(layer, q):
        act = unit_act(layer)
        sum_begin(2 * layer + 1, q, lambda cols: nt(both(act, q), r.wn[cols, :]), ch)

    hot = r.oh[...]

    def pick(target, row0, source, source0, width):
        def one(j):
            cols = aligned(j * TILE, TILE)
            target[row0 : row0 + SLOTS, cols] = nn(
                hot, source[source0 : source0 + rows, cols]
            ).astype(BF)

        loop(width // TILE, one)

    by_columns = (2 * vr) % LANES == 0

    def column_core(step):
        cols = aligned((z_from(step) - y) * vr, 2 * vr)
        return remote(
            r.cs.at[1, :, :, cols],
            r.cr.at[1, :, :, cols],
            r.ccs.at[step],
            r.ccr.at[step],
            core_peer,
        )

    def column_x(step):
        cols = aligned((z_from(step) - y) * vr, 2 * vr)
        return remote(
            r.xs.at[1, :, :, cols], r.xr.at[1, :, :, cols], r.cxs.at[step], r.cxr.at[step], x_peer
        )

    def column_sum(step):
        cols = aligned((z_from(step) - y) * vr, 2 * vr)
        weight = r.wn[cols, :]
        away = nt(r.act0[aligned(oth0, half), :], weight).astype(BF)
        for q in range(CHUNKS):
            r.cs[1, q, :, cols] = away[q * ch : (q + 1) * ch]
        column_core(step).start()
        here = nt(r.act0[aligned(own0, half), :], weight)
        column_core(step).wait_recv()
        for q in range(CHUNKS):
            r.xs[1, q, :, cols] = (
                here[q * ch : (q + 1) * ch] + r.cr[1, q, :, cols].astype(F32)
            ).astype(BF)
        column_x(step).start()

    for layer in range(DEPTH):
        for q in range(CHUNKS):
            if layer > 0:
                share_wait(2 * layer - 1, r.xl, q)
            project(layer, q)
        for q in range(CHUNKS):
            attend_forward(layer, q)
            if layer > 0:
                rejoin_sum(layer, q)
            elif q == 0:
                for turn in range(3, lines):
                    gather_pass(EXP, turn)
                gather_start_z(NAR)
        if layer == 0:
            gather_wait(REJ)
            for q in range(CHUNKS):
                rejoin_sum(layer, q)
            gather_pass(NAR, 1)
            transpose_into(r.xt, 0, r.xl, 0, rows)
        else:
            transpose_into(r.xt, rows, r.xl, 0, rows)
        for q in range(CHUNKS):
            sum_end(2 * layer, q, ch)
            first_norm(layer, q)
            share(2 * layer, r.normed, q).start()
            if layer == 0:
                gather_pass(NAR, q + 2)
                if q == 0:
                    gather_wait(EXP)
            share_wait(2 * layer, r.normed, q)
            widen(layer, q)
            if layer > 0:
                narrow_sum(layer, q)
        if layer == 0:
            for turn in range(CHUNKS + 2, lines):
                gather_pass(NAR, turn)
            if by_columns:
                for turn in range(lines):
                    step = gather_order(turn)
                    gather_y_arrival(NAR, step).wait_recv()
                    column_sum(step)
                transpose_into(r.nt, 0, r.normed, 0, rows)
                for step in range(lines):
                    column_x(step).wait()
                    column_core(step).wait_send()
            else:
                transpose_into(r.nt, 0, r.normed, 0, rows)
                gather_wait(NAR)
                for q in range(CHUNKS):
                    narrow_sum(layer, q)
        else:
            pick(r.low2c, 0, r.normed, 0, d_model)
            widen_slots()
            transpose_into(r.nt, rows, r.low2c, 0, SLOTS)
        for q in range(CHUNKS):
            if not (layer == 0 and by_columns):
                sum_end(2 * layer + 1, q, ch)
            second_norm(layer, q)
            if layer < DEPTH - 1:
                share(2 * layer + 1, r.xl, q).start()

    own_rows = aligned(own0, half)
    out_here = pltpu.make_async_copy(r.st, r.act.at[own_rows], r.osem.at[0])
    out_there = remote(r.st, r.act.at[own_rows], r.osem.at[1], r.osem.at[2], core_peer)
    out_arrival = remote(
        r.st, r.act.at[aligned(oth0, half)], r.osem.at[1], r.osem.at[2], core_peer
    )
    out_here.start()
    out_there.start()

    def add_rows(row, value):
        r.vg[row : row + 1, :] += jnp.sum(value, axis=0, keepdims=True)

    def norm_pull(g, hat, spread, gain):
        scaled = g * gain
        mean = jnp.mean(scaled, axis=1, keepdims=True)
        inner = jnp.mean(scaled * hat, axis=1, keepdims=True)
        return spread * (scaled - mean - hat * inner)

    def second_pull(layer, q, gradient):
        def one(i):
            at = aligned(q * ch + i * SUB, SUB)
            g = gradient(i, at)
            hat = r.xh2[layer, at, :]
            add_rows(6, g * hat)
            add_rows(7, g)
            back = norm_pull(g, hat, r.rs2[layer, at, :], r.vt[6:7, :])
            add_rows(3, back)
            r.gb[at, :] = back
            r.low2[aligned(own0 + q * ch + i * SUB, SUB), :] = back.astype(BF)

        loop(ch // SUB, one)

    def first_pull(layer, q, gradient):
        def one(i):
            at = aligned(q * ch + i * SUB, SUB)
            g = gradient(i, at)
            hat = r.xh1[layer, at, :]
            add_rows(4, g * hat)
            add_rows(5, g)
            back = norm_pull(g, hat, r.rs1[layer, at, :], r.vt[4:5, :])
            add_rows(2, back)
            r.gb[at, :] = back
            r.xl[aligned(own0 + q * ch + i * SUB, SUB), :] = back.astype(BF)

        loop(ch // SUB, one)

    def hot_rows(at_start):
        return r.oht[aligned(own0 + at_start, SUB), :]

    def bias_sums(row0):
        for kind, row in ((0, 0), (2, 1)):
            cols = aligned(m * hw, hw)
            r.vg[row : row + 1, cols] += jnp.sum(
                r.dp[kind, row0 : row0 + rows, :].astype(F32), axis=0, keepdims=True
            )

    for q in range(CHUNKS):
        second_pull(1, q, lambda i, at: nn(hot_rows(q * ch + i * SUB), r.mc[...]))
        share(4, r.low2, q).start()
    for q in range(CHUNKS):
        share_wait(4, r.low2, q)
    pick(r.low2c, 0, r.low2, 0, d_model)

    def slot_units(j):
        cols = aligned(j * TILE, TILE)
        back = nn(r.low2c[...], r.wn[:, cols]) * r.slc[:, cols].astype(F32)
        back = back.astype(BF)
        r.be[rows : rows + SLOTS, cols] = back
        r.vg[pl.ds(8 + m, 1), cols] += jnp.sum(back.astype(F32), axis=0, keepdims=True)

    loop(uw // TILE, slot_units)
    slot_own = core * slot_half
    slot_oth = slot_half - slot_own

    def slot_tile(cols):
        part = nt(r.be[rows : rows + SLOTS, :], r.we[cols, :])
        r.part[...] = part
        return jnp.concatenate(
            [
                r.part[aligned(slot_oth, slot_half), :],
                r.part[aligned(slot_own, slot_half), :],
            ],
            axis=0,
        )

    sum_begin(4, 0, slot_tile, slot_half)
    transpose_into(r.l2t, rows, r.low2c, 0, SLOTS)
    for head in range(heads):
        r.qc[head] = nn(hot, r.qz[1, head]).astype(BF)
        source = r.gse[
            (head // 2) * rows : (head // 2 + 1) * rows,
            (head % 2) * rows : (head % 2 + 1) * rows,
        ]
        r.pc[head] = nn(source, r.oht[...]).astype(BF)
    r.cct[...] = nn(r.ct[1], r.oht[...]).astype(BF)
    sum_end(4, 0, slot_half)
    mine_slots = r.slt.at[aligned(slot_own, slot_half)]
    mine_slots[...] = sum_rows(4, 0, slice(0, slot_half)).astype(BF)
    slots_out = remote(mine_slots, mine_slots, r.osem.at[3], r.osem.at[4], core_peer)
    slots_in_ref = r.slt.at[aligned(slot_oth, slot_half)]
    slots_in = remote(slots_in_ref, slots_in_ref, r.osem.at[3], r.osem.at[4], core_peer)
    slots_out.start()
    slots_in.wait_recv()
    for q in range(CHUNKS):
        first_pull(
            1, q, lambda i, at: r.gb[at, :] + nn(hot_rows(q * ch + i * SUB), r.slt[...])
        )
        share(5, r.xl, q).start()

    for q in range(CHUNKS):
        share_wait(5, r.xl, q)
    pick(r.low2c, 0, r.xl, 0, d_model)
    low_ctx = nn(r.low2c[...], r.wr[...]).astype(BF)
    across = low_transpose(low_ctx)
    dq_across = []
    for pair in range(heads // 2):
        lanes = slice(pair * LANES, (pair + 1) * LANES)
        dv = jnp.zeros((rows, LANES), F32)
        dk = jnp.zeros((rows, LANES), F32)
        for head in (2 * pair, 2 * pair + 1):
            where = slice(head * HEAD_DIM, (head + 1) * HEAD_DIM)
            at = (head % 2) * HEAD_DIM
            r.dozt[head, at : at + HEAD_DIM, 0:SLOTS] = across[where, :]
            low = r.pc[head]
            dv += nn(low, lane_half(low_ctx[:, lanes], head))
            dp = nn(r.vn[1, :, lanes], r.dozt[head, :, 0:SLOTS])
            delta = jnp.sum(
                across[where, :].astype(F32) * r.cct[where, :].astype(F32), axis=0, keepdims=True
            )
            ds = (low.astype(F32) * (dp - delta)).astype(BF)
            dk += nn(ds, r.qc[head])
            dq_across.append(nn(r.kt[1, where, :], ds) * 0.125)
        r.dp[1, rows : 2 * rows, lanes] = dk.astype(BF)
        r.dp[2, rows : 2 * rows, lanes] = dv.astype(BF)
    dq = low_transpose(jnp.concatenate(dq_across, axis=0))
    r.dp[0, rows : 2 * rows, :] = nn(r.oht[...], dq).astype(BF)
    bias_sums(rows)

    def layer_rows(k, q, row0):
        def tile_of(cols):
            total = None
            for kind in range(3):
                lhs = jnp.concatenate(
                    [
                        r.dp[kind, aligned(row0 + oth0 + q * ch, ch), :],
                        r.dp[kind, aligned(row0 + own0 + q * ch, ch), :],
                    ],
                    axis=0,
                )
                part = nt(lhs, r.wa[kind, cols, :])
                total = part if total is None else total + part
            return total

        sum_begin(k, q, tile_of, ch)

    for q in range(CHUNKS):
        layer_rows(5, q, rows)
    transpose_into(r.l1t, rows, r.low2c, 0, SLOTS)

    def weight_grad_rows(target, across, latter, width, row0, count):
        at = aligned(row0, count)

        def one(j):
            cols = aligned(j * TILE, TILE)
            target[at, cols] = nn(across[at, :], latter[:, cols]).astype(BF)

        loop(width // TILE, one)

    def weight_grad(target, across, latter, width):
        loop(
            d_model // TILE,
            lambda i: weight_grad_rows(target, across, latter, width, i * TILE, TILE),
        )

    def transpose_both(target, source, q):
        for row0 in (oth0 + q * ch, own0 + q * ch):
            target[:, aligned(row0, ch)] = low_transpose(source[aligned(row0, ch), :])

    def units_back(q):
        def one(j):
            cols = aligned(j * TILE, TILE)
            slope = both(r.slope0, q, cols).astype(F32)
            back = (nn(both(r.low2, q), r.wn[:, cols]) * slope).astype(BF)
            put_both(r.be, q, cols, back)
            r.vg[pl.ds(8 + m, 1), cols] += jnp.sum(back.astype(F32), axis=0, keepdims=True)

        loop(uw // TILE, one)

    for q in range(CHUNKS):
        sum_end(5, q, ch)
        second_pull(
            0, q, lambda i, at: r.gb[at, :] + sum_rows(5, q, aligned(i * SUB, SUB))
        )
        share(6, r.low2, q).start()
        share_wait(6, r.low2, q)
        transpose_both(r.l2t, r.low2, q)
        if q == 0:
            units_back(q)
    if by_columns:
        for turn in range(1, lines + 1):
            owner = ((z + scatter_order(turn)) % lines) * 2 + 1 - y
            weight_grad_rows(r.gsn, r.l2t, r.act0, uw, owner * vr, vr)
            if turn <= 2:
                scatter_y(NAR, scatter_order(turn)).start()
                under_way.append(queue.pop(0))
        ready.append(NAR)
    else:
        weight_grad(r.gsn, r.l2t, r.act0, uw)
        scatter_start(NAR)
    for q in range(CHUNKS):
        if q > 0:
            units_back(q)
        sum_begin(6, q, lambda cols, q=q: nt(both(r.be, q), r.we[cols, :]), ch)
    if by_columns:
        each(
            0,
            lines,
            lambda s: weight_grad_rows(
                r.gsn, r.l2t, r.act0, uw, (((z + s) % lines) * 2 + y) * vr, vr
            ),
        )
    pick(r.ctx, rows, r.ctx1, 0, hw)
    weight_grad(r.gse, r.nt, r.be, uw)
    scatter_start(EXP)
    scatter_pass()
    for q in range(CHUNKS):
        sum_end(6, q, ch)
        first_pull(
            0, q, lambda i, at: r.gb[at, :] + sum_rows(6, q, aligned(i * SUB, SUB))
        )
        share(7, r.xl, q).start()
    scatter_pass()
    for q in range(CHUNKS):
        share_wait(7, r.xl, q)
        back = nn(both(r.xl, q), r.wr[...]).astype(BF)
        put_heads(r.doz, q, back)
        put_heads_across(r.dozt, q, low_transpose(back))

    def head_pair(pair):
        lanes = aligned(pair * LANES, LANES)
        dv = jnp.zeros((rows, LANES), F32)
        dk = jnp.zeros((rows, LANES), F32)
        for side in range(2):
            head = 2 * pair + side
            where = aligned(head * HEAD_DIM, HEAD_DIM)
            for part in range(rows // TILE):
                some = slice(part * TILE, (part + 1) * TILE)
                low = r.p0[head, :, some]
                dv += nn(low, r.doz[head, some, :])
                inner = r.dozt[head, side * HEAD_DIM : (side + 1) * HEAD_DIM, some]
                delta = jnp.sum(
                    inner.astype(F32) * r.ct[0, where, some].astype(F32), axis=0, keepdims=True
                )
                dp = nn(r.vn[0, :, lanes], r.dozt[head, :, some])
                ds = (low.astype(F32) * (dp - delta)).astype(BF)
                dk += nn(ds, r.qz[0, head, some, :])
                r.dqt[where, some] = (nn(r.kt[0, where, :], ds) * 0.125).astype(BF)
        r.dp[1, 0:rows, lanes] = dk.astype(BF)
        r.dp[2, 0:rows, lanes] = dv.astype(BF)

    for pair in range(heads // 2):
        head_pair(pair)
        scatter_pass()
    for i in range(rows // LANES):
        some = slice(i * LANES, (i + 1) * LANES)
        r.dp[0, some, :] = low_transpose(r.dqt[:, some])
    for q in range(CHUNKS):
        layer_rows(7, q, 0)
    scatter_pass()
    bias_sums(0)
    transpose_into(r.l1t, 0, r.xl, 0, rows)
    weight_grad(r.gsr, r.l1t, r.ctx, hw)
    scatter_start(REJ)
    first_of_x = jnp.where(m < 2, 1.0, 0.0)
    r.vg[2:8, :] = r.vg[2:8, :] * first_of_x
    for j in range(n):
        r.gsv[j] = r.vg[:, j * vr : (j + 1) * vr].astype(BF)
    scatter_start(VEC)
    for kind in range(3):
        weight_grad(r.gsa.at[kind], r.xt, r.dp.at[kind], hw)
    scatter_start(ATT)
    scatter_pass()
    out_here.wait()
    out_there.wait_send()
    for q in range(CHUNKS):
        sum_end(7, q, ch)

        def last(i, q=q):
            at = aligned(q * ch + i * SUB, SUB)
            g = r.gb[at, :] + sum_rows(7, q, aligned(i * SUB, SUB))
            r.st[at, :] = g * r.keep[aligned(own0 + q * ch + i * SUB, SUB), :]

        loop(ch // SUB, last)
    in_here = pltpu.make_async_copy(r.st, r.ing.at[own_rows], r.osem.at[5])
    in_there = remote(r.st, r.ing.at[own_rows], r.osem.at[6], r.osem.at[7], core_peer)
    in_arrival = remote(r.st, r.ing.at[aligned(oth0, half)], r.osem.at[6], r.osem.at[7], core_peer)
    in_here.start()
    in_there.start()
    scatter_turn()

    scatter_pass()
    def squares(value):
        value = value * value
        if value.ndim == 3:
            value = jnp.sum(value, axis=0)
        value = jnp.sum(value, axis=0, keepdims=True)
        return jnp.sum(value, axis=1, keepdims=True)

    swap_v = remote(r.vf.at[0], r.vf.at[1], r.vxs.at[2], r.vxr.at[2], core_peer)
    swap_w = remote(r.vf.at[2], r.vf.at[3], r.vxs.at[3], r.vxr.at[3], x_peer)
    total = jnp.zeros((1, 1), F32)
    while under_way:
        turn = under_way[0][1] if under_way[0][0] == ATT else 0
        if turn == 1:
            scatter_finish(NAR, r.gn)
            total = total + squares(r.gn[...])
            scatter_close(NAR)
            for region in range(5):
                gather_close(region)
        elif turn == 2:
            scatter_finish(VEC, r.vf.at[0])
            swap_v.start()
            scatter_finish(REJ, r.gr)
            total = total + squares(r.gr[...])
        elif turn == 3:
            swap_v.wait_recv()
            r.vf[2] = r.vf[0] + r.vf[1]
            swap_w.start()
            scatter_finish(EXP, r.ge)
            total = total + squares(r.ge[...])
            scatter_close(EXP)
            scatter_close(REJ)
        elif turn == 4:
            swap_w.wait_recv()
            r.vs[...] = r.vf[2] + r.vf[3]
            r.gv[...] = r.vs[pl.ds(columns * m, columns), :]
            total = total + squares(r.gv[...])
        scatter_pass()
    scatter_finish(ATT, r.ga)
    total = total + squares(r.ga[...])

    r.nm[m] = jnp.broadcast_to(total, (8, LANES))

    def model_copy(k, slot):
        return remote(r.nm.at[slot], r.nm.at[slot], r.nms.at[k], r.nmr.at[k], model_peers[k])

    for k in range(3):
        model_copy(k, m).start()
    for k in range(3):
        model_copy(k, model_peers[k][1]).wait_recv()
    r.nz[d] = jnp.sum(r.nm[...], axis=0)

    def line_copy(step, slot):
        here = r.nz.at[slot]
        return remote(here, here, r.nzs.at[0, step], r.nzr.at[0, step], z_peer(step))

    def cross_copy(step, slot):
        here = r.nz.at[slot]
        return remote(here, here, r.nzs.at[1, step], r.nzr.at[1, step], zy_peer(step))

    each(0, lines, lambda s: cross_copy(s, d).start())
    each(1, lines, lambda s: line_copy(s, d).start())
    each(0, lines, lambda s: cross_copy(s, z_from(s) + 1 - 2 * y).wait_recv())
    each(1, lines, lambda s: line_copy(s, z_from(s)).wait_recv())
    r.norm[...] = jnp.sqrt(jnp.sum(r.nz[...], axis=0))

    each(0, lines, lambda s: cross_copy(s, d).wait_send())
    each(1, lines, lambda s: line_copy(s, d).wait_send())
    for k in range(3):
        model_copy(k, m).wait_send()
    swap.wait_send()
    swap_x.wait_send()
    swap_v.wait_send()
    swap_w.wait_send()
    slots_out.wait_send()
    scatter_close(VEC)
    scatter_close(ATT)
    out_arrival.wait_recv()
    in_here.wait()
    in_there.wait_send()
    in_arrival.wait_recv()


def run_layers(
    n, tok, pos, cho, table, mcot, attend, rejoin, expand, narrow, vin
):
    rows, d_model = tok.shape
    vr = rejoin.shape[0]
    hw = rejoin.shape[1]
    uw = expand.shape[1]
    lines = n // 2
    half = rows // 2
    ch = half // CHUNKS
    heads = hw // HEAD_DIM
    wide = rows + SLOTS
    inputs = [
        ("tok", tok),
        ("pos", pos),
        ("cho", cho),
        ("table", table),
        ("mcot", mcot),
        ("attend", attend),
        ("rejoin", rejoin),
        ("expand", expand),
        ("narrow", narrow),
        ("vin", vin),
    ]
    outputs = [
        ("act", (rows, d_model), pl.ANY),
        ("ing", (rows, d_model), pl.ANY),
        ("ga", (3, vr, hw), pltpu.VMEM),
        ("gr", (vr, hw), pltpu.VMEM),
        ("ge", (vr, uw), pltpu.VMEM),
        ("gn", (vr, uw), pltpu.VMEM),
        ("gv", vin.shape, pltpu.VMEM),
        ("norm", (8, LANES), pltpu.VMEM),
    ]
    low = [
        ("wv", (n, 16, vr)),
        ("wa", (3, d_model, hw)),
        ("wr", (d_model, hw)),
        ("we", (d_model, uw)),
        ("wn", (d_model, uw)),
        ("gsv", (n, 16, vr)),
        ("gsa", (3, d_model, hw)),
        ("gsr", (d_model, hw)),
        ("gse", (d_model, uw)),
        ("gsn", (d_model, uw)),
        ("yv", (lines, 16, vr)),
        ("ya", (lines, 3, vr, hw)),
        ("yr", (lines, vr, hw)),
        ("ye", (lines, vr, uw)),
        ("yn", (lines, vr, uw)),
        ("zv", (lines, 16, vr)),
        ("za", (lines, 3, vr, hw)),
        ("zr", (lines, vr, hw)),
        ("ze", (lines, vr, uw)),
        ("zn", (lines, vr, uw)),
        ("cs", (2, CHUNKS, ch, d_model)),
        ("cr", (2, CHUNKS, ch, d_model)),
        ("xs", (2, CHUNKS, ch, d_model)),
        ("xr", (2, CHUNKS, ch, d_model)),
        ("vb", (4, 16, vr)),
        ("oh", (SLOTS, rows)),
        ("oht", (rows, SLOTS)),
        ("mc", (SLOTS, d_model)),
        ("xl", (rows, d_model)),
        ("normed", (rows, d_model)),
        ("low2", (rows, d_model)),
        ("xt", (d_model, 2 * rows)),
        ("nt", (d_model, wide)),
        ("l2t", (d_model, wide)),
        ("l1t", (d_model, wide)),
        ("act0", (wide, uw)),
        ("slope0", (rows, uw)),
        ("be", (wide, uw)),
        ("ctx", (wide, hw)),
        ("ctx1", (rows, hw)),
        ("dp", (3, 2 * rows, hw)),
        ("qz", (2, heads, rows, LANES)),
        ("qzt", (2, heads, LANES, rows)),
        ("kn", (2, rows, hw)),
        ("kt", (2, hw, rows)),
        ("vn", (2, rows, hw)),
        ("vvt", (hw, rows)),
        ("ct", (2, hw, rows)),
        ("p0", (heads, rows, rows)),
        ("dqt", (hw, rows)),
        ("slc", (SLOTS, uw)),
        ("low2c", (SLOTS, d_model)),
        ("slt", (SLOTS, d_model)),
        ("qc", (heads, SLOTS, LANES)),
        ("pc", (heads, rows, SLOTS)),
        ("cct", (hw, SLOTS)),
        ("tok_in", (rows, d_model)),
    ]
    full = [
        ("vt", (16, d_model)),
        ("vg", (16, d_model)),
        ("keep", (rows, 1)),
        ("st", (half, d_model)),
        ("gb", (half, d_model)),
        ("xh1", (2, half, d_model)),
        ("xh2", (2, half, d_model)),
        ("rs1", (2, half, 1)),
        ("rs2", (2, half, 1)),
        ("acc", (ch, d_model)),
        ("part", (SLOTS, TILE)),
        ("vf", (4, 16, vr)),
        ("vs", (16, vr)),
        ("expand_in", (vr, uw)),
        ("narrow_in", (vr, uw)),
        ("nm", (4, 8, LANES)),
        ("nz", (n, 8, LANES)),
    ]
    sems = [
        ("agzs", (5, lines + 3)),
        ("agzr", (5, lines)),
        ("agys", (5, lines)),
        ("agyr", (5, lines)),
        ("rsys", (5, lines)),
        ("rsyr", (5, lines)),
        ("rszs", (5, lines)),
        ("rszr", (5, lines)),
        ("arcs", (8, CHUNKS, d_model // TILE)),
        ("arcr", (8, CHUNKS, d_model // TILE)),
        ("arxs", (8, CHUNKS, d_model // TILE)),
        ("arxr", (8, CHUNKS, d_model // TILE)),
        ("shs", (8, CHUNKS)),
        ("shr", (8, CHUNKS)),
        ("vxs", (4,)),
        ("vxr", (4,)),
        ("osem", (8,)),
        ("lsem", (3,)),
        ("nms", (3,)),
        ("nmr", (3,)),
        ("nzs", (2, lines)),
        ("nzr", (2, lines)),
        ("ccs", (lines,)),
        ("ccr", (lines,)),
        ("cxs", (lines,)),
        ("cxr", (lines,)),
    ]
    names = (
        [name for name, _ in inputs]
        + [name for name, _, _ in outputs]
        + [name for name, _ in low]
        + [name for name, _ in full]
        + ["pb"]
        + [name for name, _ in sems]
    )
    sizes = (n, d_model, rows, hw, uw, vr)

    def body(*refs):
        layer_kernel(names, sizes, *refs)

    return pl.pallas_call(
        body,
        out_shape=[jax.ShapeDtypeStruct(shape, F32) for _, shape, _ in outputs],
        in_specs=[
            pl.BlockSpec(
                memory_space=pl.ANY if name in ("tok", "expand", "narrow") else pltpu.VMEM
            )
            for name, _ in inputs
        ],
        out_specs=[pl.BlockSpec(memory_space=space) for _, _, space in outputs],
        scratch_shapes=[pltpu.VMEM(shape, BF) for _, shape in low]
        + [pltpu.VMEM(shape, F32) for _, shape in full]
        + [pltpu.VMEM((16, LANES), jnp.int32)]
        + [pltpu.SemaphoreType.DMA(shape) for _, shape in sems],
        compiler_params=pltpu.CompilerParams(
            collective_id=0, has_side_effects=True, vmem_limit_bytes=61 * 1024 * 1024
        ),
        cost_estimate=pl.CostEstimate(
            flops=20_000_000_000, bytes_accessed=20_000_000, transcendentals=4_000_000
        ),
    )(*[value for _, value in inputs])


def apply_update(weight, first_moment, second_moment, shadow, gradient, step_rate):
    momentum = 0.5 * first_moment + 0.5 * gradient
    variance = 0.5 * second_moment + 0.5 * gradient * gradient
    bias_fix = 1.0 - 0.5**STEP
    updated = weight - step_rate * (
        momentum / bias_fix / (jnp.sqrt(variance / bias_fix) + 1e-08) + 0.01 * weight
    )
    average = 0.999 * shadow + 0.001 * updated
    return (updated, momentum, variance, average, updated.astype(BF))


def update_kernel(rates, clip_limit, norm, act, ing, *refs):
    *refs, norm_out, act_out, ing_out = refs
    act_out[...] = act[...]
    ing_out[...] = ing[...]
    norm_out[...] = norm[0:1, 0:1]
    factor = jnp.minimum(1.0, clip_limit / (norm[0:1, 0:1] + 1e-06))
    ins, outs = refs[: 5 * len(rates)], refs[5 * len(rates) :]
    for index, rate in enumerate(rates):
        weight, first, second, shadow, gradient = ins[5 * index : 5 * index + 5]
        targets = outs[5 * index : 5 * index + 5]
        for part in range(weight.shape[0]) if len(weight.shape) == 3 else (slice(None),):
            results = apply_update(
                weight[part],
                first[part],
                second[part],
                shadow[part],
                gradient[part] * factor,
                rate,
            )
            for target, value in zip(targets, results, strict=True):
                target[part] = value


def run_update(groups, rates, norm, clip_limit, act, ing):
    vr = groups[1][0].shape[0]
    step = min(vr, 64)

    def spec(shape, whole):
        if whole:
            return pl.BlockSpec(shape, lambda i: (0, 0))
        if len(shape) == 3:
            return pl.BlockSpec((shape[0], step, shape[2]), lambda i: (0, i, 0))
        return pl.BlockSpec((step, shape[1]), lambda i: (i, 0))

    last = len(groups) - 1
    passed = pl.BlockSpec((act.shape[0] * step // vr, act.shape[1]), lambda i: (i, 0))
    specs = [spec(group[0].shape, k == last) for k, group in enumerate(groups)]

    def body(*refs):
        update_kernel(rates, clip_limit, *refs)

    flat = [value for group in groups for value in group]
    size = sum(value.size for value in flat) * 4
    outs = pl.pallas_call(
        body,
        grid=(vr // step,),
        in_specs=[spec(norm.shape, True)]
        + [passed] * 2
        + [one for one in specs for _ in range(5)],
        out_specs=[one for one in specs for _ in range(5)]
        + [spec((1, 1), True)]
        + [passed] * 2,
        out_shape=[
            jax.ShapeDtypeStruct(group[0].shape, kind)
            for group in groups
            for kind in (F32, F32, F32, F32, BF)
        ]
        + [jax.ShapeDtypeStruct(shape, F32) for shape in ((1, 1), act.shape, ing.shape)],
        compiler_params=pltpu.CompilerParams(vmem_limit_bytes=60 * 1024 * 1024),
        cost_estimate=pl.CostEstimate(flops=size, bytes_accessed=2 * size, transcendentals=0),
    )(norm, act, ing, *flat)
    groups_out = [outs[5 * k : 5 * k + 5] for k in range(len(groups))]
    return groups_out, outs[-3].reshape(()), *outs[-2:]


def per_device(
    tokens_in,
    masked_positions,
    replace_choice,
    replace_table,
    masked_cotangent,
    attend,
    attend_mean,
    attend_square,
    attend_shadow,
    rejoin,
    rejoin_mean,
    rejoin_square,
    rejoin_shadow,
    expand,
    expand_mean,
    expand_square,
    expand_shadow,
    narrow,
    narrow_mean,
    narrow_square,
    narrow_shadow,
    vectors,
    vectors_mean,
    vectors_square,
    vectors_shadow,
):
    n = lax.axis_size("dp")
    act, ing, ga, gr, ge, gn, gv, norm = run_layers(
        n,
        tokens_in,
        masked_positions,
        replace_choice,
        replace_table,
        masked_cotangent,
        attend.transpose(1, 0, 2),
        rejoin,
        expand,
        narrow,
        vectors.T,
    )
    d_model = tokens_in.shape[1]
    param_count = 4 * d_model * d_model + 2 * d_model * expand.shape[1] * 4 + 12 * d_model
    clip_limit = 0.001 * math.sqrt(param_count * tokens_in.shape[0] * n)
    cubes = [x.transpose(1, 0, 2) for x in (attend, attend_mean, attend_square, attend_shadow)]
    rows_of = [x.T for x in (vectors, vectors_mean, vectors_square, vectors_shadow)]
    new, gradient_norm, act, ing = run_update(
        (
            (*cubes, ga),
            (rejoin, rejoin_mean, rejoin_square, rejoin_shadow, gr),
            (expand, expand_mean, expand_square, expand_shadow, ge),
            (narrow, narrow_mean, narrow_square, narrow_shadow, gn),
            (*rows_of, gv),
        ),
        (0.04, 0.16, 0.04, 0.04, 0.5),
        norm,
        clip_limit,
        act,
        ing,
    )
    results = [act, ing, gradient_norm]
    results.extend(x.transpose(1, 0, 2) for x in new[0])
    for group in new[1:4]:
        results.extend(group)
    results.extend(x.T for x in new[4])
    return tuple(results)


def solution(mesh):
    row = P("dp", None)
    cube = P("dp", None, "mp")
    flat = P("dp", "mp")
    return jax.shard_map(
        per_device,
        mesh=mesh,
        in_specs=(row, row, row, P(), P("dp", None, None)) + (cube,) * 4 + (flat,) * 16,
        out_specs=(row, row, P()) + (cube,) * 5 + (flat,) * 20,
        check_vma=False,
    )
```
